32 devices in a mesh: lon: 16 (over z, y, core), lat: 2 (over x).
Axes of the slice: x: 2, y: 2, z: 4, core: 2. Of those that a mesh axis runs over, the one named last changes fastest.
Arguments:
- target: float32 [3, 32, 16384], P(None, 'lat', 'lon'), may hold values from -6 to 6
- grad_x: float32 [2, 3, 32, 16384], P(None, None, 'lat', 'lon'), may hold values from -6 to 6
- grad_y: float32 [2, 3, 32, 16384], P(None, None, 'lat', 'lon'), may hold values from -6 to 6
- labels: int32 [32, 16384], P('lat', 'lon'), may hold values from 0 to 1
- sweeps: int32 [3], replicated, may hold values from 2 to 4
Outputs:
- stitched: float32 [3, 32, 16384], P(None, 'lat', 'lon')
The draws below stay inside these ranges and needn't reach their ends.
All inputs are finite; a program needn't handle non-finite values.
Results may differ from the reference program's by a relative error of at most 0.0004.
Values sent between devices are 32-bit elements; how exact they have to be, the bound alone decides.
No kernel may reach another device: no remote copies, remote signals or barrier semaphores. Data moves between devices by JAX's collectives and lax.ppermute only.
A program may use at most 64 MiB of HBM per device.

```python
import jax
import jax.numpy as jnp
from jax import lax

SOURCES = 2
LEVELS = 3
MAXS = 4
NY = 32
NX = 16384


def gradient_field(key):
    noise_key = jax.random.fold_in(key, 0)
    shape = (SOURCES, 3, NY, NX)
    return jnp.clip(0.5 * jax.random.normal(noise_key, shape, jnp.float32), -6.0, 6.0)


def draw_grad_x(key, part):
    return gradient_field(jax.random.fold_in(key, 101))


def draw_grad_y(key, part):
    return gradient_field(jax.random.fold_in(key, 202))


def plant(entries, key, least, top_value):
    place = [jax.random.randint(jax.random.fold_in(key, axis), (), 0, length) for axis, length in enumerate(entries.shape)]
    longest = entries.shape.index(max(entries.shape))
    neighbour = place[:longest] + [(place[longest] + 1) % entries.shape[longest]] + place[longest + 1:]
    return entries.at[tuple(place)].set(least).at[tuple(neighbour)].set(top_value)


def block_scale(rng, dims, cuts, low, top_value):
    factor_of, own = 1.0, jax.random.fold_in(rng, 6)
    for dim, shards_of in cuts:
        draws = jnp.exp(jax.random.uniform(jax.random.fold_in(own, dim), (shards_of,), jnp.float32, low / len(cuts), top_value / len(cuts)))
        factor_of = factor_of * jnp.repeat(draws, dims[dim] // shards_of).reshape([-1 if axis == dim else 1 for axis in range(len(dims))])
    return factor_of


def centred(key, shape, scale, most, shards=(), held_as=jnp.bfloat16):
    values = jax.random.normal(key, shape, jnp.float32) * scale
    if len(shards) > 0:
        values = block_scale(key, shape, shards, -0.22, 0.18) * values
    return jnp.clip(values, min=-most, max=most).astype(held_as)


def setup_inputs(seed: int = 0) -> dict:
    key_of = jax.random.split(jax.random.key(seed), 6)
    return {
        "target": centred(key_of[0], (3, NY, NX), 1.0, 6.0, ((1, 2), (2, 16)), jnp.float32),
        "grad_x": draw_grad_x(jax.random.fold_in(key_of[5], 71), 0),
        "grad_y": draw_grad_y(jax.random.fold_in(key_of[5], 71), 0),
        "labels": plant(jax.random.randint(key_of[3], (NY, NX), 0, SOURCES), jax.random.fold_in(key_of[3], 1), 0, SOURCES - 1).astype(jnp.int32),
        "sweeps": jax.random.randint(key_of[4], (LEVELS,), 2, MAXS + 1).astype(jnp.int32),
    }


screening = 0.02
damping = 0.8


def wrap_pad(field, width):
    field = jnp.concatenate([field[:, :, -width:], field, field[:, :, :width]], axis=2)
    return jnp.pad(field, ((0, 0), (width, width), (0, 0)))


def stencil(padded, scale):
    inner = padded[:, 1:-1, 1:-1]
    beside = padded[:, :-2, 1:-1] + padded[:, 2:, 1:-1] + padded[:, 1:-1, :-2] + padded[:, 1:-1, 2:]
    return (screening + 4.0 * scale) * inner - scale * beside


def smooth(field, right, count, scale):
    diag = screening + 4.0 * scale

    def sweep(step, value):
        return value + damping * (right - stencil(wrap_pad(value, 1), scale)) / diag

    return lax.fori_loop(0, count, sweep, field)


def restrict(field):
    chans, rows, cols = field.shape
    return field.reshape(chans, rows // 2, 2, cols // 2, 2).mean(axis=(2, 4))


def prolong_from(padded):
    center = padded[:, 1:-1, 1:-1]
    north = padded[:, :-2, 1:-1]
    south = padded[:, 2:, 1:-1]
    west = padded[:, 1:-1, :-2]
    east = padded[:, 1:-1, 2:]
    f00 = 0.5625 * center + 0.1875 * north + 0.1875 * west + 0.0625 * padded[:, :-2, :-2]
    f01 = 0.5625 * center + 0.1875 * north + 0.1875 * east + 0.0625 * padded[:, :-2, 2:]
    f10 = 0.5625 * center + 0.1875 * south + 0.1875 * west + 0.0625 * padded[:, 2:, :-2]
    f11 = 0.5625 * center + 0.1875 * south + 0.1875 * east + 0.0625 * padded[:, 2:, 2:]
    stacked = jnp.stack([jnp.stack([f00, f01], -1), jnp.stack([f10, f11], -1)], 2)
    chans, rows, two, cols, other = stacked.shape
    return stacked.reshape(chans, rows * 2, cols * 2)


def cycle(level, field, right, sweeps):
    scale = 0.25 ** level
    count = sweeps[level]
    field = smooth(field, right, count, scale)
    if level + 1 == LEVELS:
        return field
    resid = right - stencil(wrap_pad(field, 1), scale)
    coarse = restrict(resid)
    fix = cycle(level + 1, jnp.zeros_like(coarse), coarse, sweeps)
    field = field + prolong_from(wrap_pad(fix, 1))
    return smooth(field, right, count, scale)


def reference(target, grad_x, grad_y, labels, sweeps):
    sel_x = jnp.zeros_like(target)
    sel_y = jnp.zeros_like(target)
    for source in range(SOURCES):
        picked = (labels == source)[None, :, :]
        sel_x = jnp.where(picked, grad_x[source], sel_x)
        sel_y = jnp.where(picked, grad_y[source], sel_y)
    west = jnp.roll(sel_x, 1, axis=2)
    north = jnp.concatenate([jnp.zeros_like(sel_y[:, :1, :]), sel_y[:, :-1, :]], axis=1)
    right = screening * target - ((sel_x - west) + (sel_y - north))
    return cycle(0, target, right, sweeps)
```

```python
import functools

import jax
import jax.numpy as jnp
from jax import lax
from jax.experimental import pallas as pl
from jax.experimental.pallas import tpu as pltpu
from jax.sharding import PartitionSpec as P

SCREENING = 0.02
DAMPING = 0.8
LANES = 128
HALF = LANES // 2
VMEM = pl.BlockSpec(memory_space=pltpu.VMEM)
SMEM = pl.BlockSpec(memory_space=pltpu.SMEM)


def diagonal(scale):
    return SCREENING + 4.0 * scale


def rows_of(value):
    return lax.broadcasted_iota(jnp.int32, value.shape, 0)


def north_of(value):
    return jnp.where(rows_of(value) == 0, 0.0, pltpu.roll(value, 1, 0))


def south_of(value):
    last = value.shape[0] - 1
    return jnp.where(rows_of(value) == last, 0.0, pltpu.roll(value, last, 0))


def west_of(value):
    return pltpu.roll(value, 1, 1)


def east_of(value):
    return pltpu.roll(value, value.shape[1] - 1, 1)


def around(value):
    return (north_of(value) + south_of(value)) + (west_of(value) + east_of(value))


def sweep(value, right, scale, inside):
    diag = diagonal(scale)
    value = (1.0 - DAMPING) * value + (DAMPING / diag) * right + (DAMPING * scale / diag) * around(value)
    return value if inside is None else value * inside


def residual(value, right, scale):
    return right - diagonal(scale) * value + scale * around(value)


def two_parts(value):
    high = value.astype(jnp.bfloat16)
    return high, (value - high.astype(jnp.float32)).astype(jnp.bfloat16)


def moved(value, places):
    high, low = two_parts(value)
    dot = functools.partial(jnp.dot, preferred_element_type=jnp.float32)
    return dot(high, places) + dot(low, places)


def places_of(shape, wanted):
    source = lax.broadcasted_iota(jnp.int32, shape, 0)
    target = lax.broadcasted_iota(jnp.int32, shape, 1)
    return wanted(source, target).astype(jnp.float32).astype(jnp.bfloat16)


def halo_coarse(fine):
    return jnp.where(fine < HALF, fine // 2, HALF + fine // 2)


def pair_columns(fields):
    own = places_of((2 * LANES, LANES), lambda source, target: source // 2 == target)
    halo = places_of((LANES, LANES), lambda source, target: halo_coarse(source) == target)
    rows, cols = fields[0].shape
    blocks = (cols - LANES) // (2 * LANES)
    cut = [f[:, k * 2 * LANES:(k + 1) * 2 * LANES] for f in fields for k in range(blocks)]
    packed = moved(jnp.concatenate(cut, 0), own)
    edges = moved(jnp.concatenate([f[:, cols - LANES:] for f in fields], 0), halo)
    out = []
    for i in range(len(fields)):
        parts = [packed[(i * blocks + k) * rows:(i * blocks + k + 1) * rows] for k in range(blocks)]
        out.append(jnp.concatenate(parts + [edges[i * rows:(i + 1) * rows]], 1))
    return out


def spread_columns(fields):
    own = places_of((2 * LANES, 2 * LANES), lambda source, target: source == target // 2 + LANES * (target % 2))
    halo = places_of((2 * LANES, LANES), lambda source, target: source == halo_coarse(target) + LANES * (target % 2))
    rows, cols = fields[0].shape
    blocks = (cols - LANES) // LANES
    west = [0.75 * f + 0.25 * west_of(f) for f in fields]
    east = [0.75 * f + 0.25 * east_of(f) for f in fields]

    def cut(k):
        span = slice(k * LANES, (k + 1) * LANES)
        return [jnp.concatenate([w[:, span], e[:, span]], 1) for w, e in zip(west, east)]

    own_cut = [cut(k) for k in range(blocks)]
    packed = moved(jnp.concatenate([own_cut[k][i] for i in range(len(fields)) for k in range(blocks)], 0), own)
    edges = moved(jnp.concatenate(cut(blocks), 0), halo)
    out = []
    for i in range(len(fields)):
        parts = [packed[(i * blocks + k) * rows:(i * blocks + k + 1) * rows] for k in range(blocks)]
        out.append(jnp.concatenate(parts + [edges[i * rows:(i + 1) * rows]], 1))
    return out


def restrict(fields, paired_ref):
    rows = fields[0].shape[0]
    out = []
    for i, paired in enumerate(pair_columns(fields)):
        halves = []
        for k, tile in enumerate(tiles(paired)):
            paired_ref[i, k] = tile
            north = paired_ref[i, k, pl.ds(0, rows // 2, stride=2), :]
            south = paired_ref[i, k, pl.ds(1, rows // 2, stride=2), :]
            halves.append(0.25 * (north + south))
        out.append(jnp.concatenate(halves, 1))
    return out


def prolong(fields, fine_ref, first):
    rows = fields[0].shape[0]
    norths = [0.75 * f + 0.25 * north_of(f) for f in fields]
    souths = [0.75 * f + 0.25 * south_of(f) for f in fields]
    spread = spread_columns(norths + souths)
    for i in range(len(fields)):
        for k, (north, south) in enumerate(zip(tiles(spread[i]), tiles(spread[len(fields) + i]))):
            fine_ref[i, k, pl.ds(first, rows, stride=2), :] = north
            fine_ref[i, k, pl.ds(first + 1, rows, stride=2), :] = south


def wide_rows(fine_ref, chan, start, rows):
    return jnp.concatenate([fine_ref[chan, k, pl.ds(start, rows), :] for k in range(fine_ref.shape[1])], 1)


def selected(grad, labels):
    out = jnp.zeros(grad.shape[1:], jnp.float32)
    for source in range(grad.shape[0]):
        out = jnp.where((labels == source)[None], grad[source], out)
    return out


def edge_kernel(*refs):
    first, last, out_ref = refs[:4], refs[4:8], refs[8]
    inner = lax.broadcasted_iota(jnp.int32, (1, 1, LANES), 2) < HALF
    target, grad_x, grad_y, labels = (
        jnp.where(inner if f.ndim > 2 else inner[0], f[...], l[...]) for f, l in zip(first, last)
    )
    chans = target.shape[0]
    out_ref[:chans] = target
    out_ref[chans:2 * chans] = selected(grad_x, labels)
    out_ref[2 * chans:] = selected(grad_y, labels)


def edges(target, grad_x, grad_y, labels):
    chans, rows, cols = target.shape
    tile = cols // LANES - 1
    arrays = (target, grad_x, grad_y, labels)

    def spec(array, place):
        lead = (0,) * (array.ndim - 1)
        return pl.BlockSpec(array.shape[:-1] + (LANES,), lambda _: lead + (place,))

    return pl.pallas_call(
        edge_kernel,
        grid=(1,),
        in_specs=[spec(a, 0) for a in arrays] + [spec(a, tile) for a in arrays],
        out_specs=pl.BlockSpec((3 * chans, rows, LANES), lambda _: (0, 0, 0)),
        out_shape=jax.ShapeDtypeStruct((3 * chans, rows, LANES), jnp.float32),
        name="edges",
    )(*arrays, *arrays)


def window_of(rows, parts):
    spare = 8
    return rows + (2 * spare if parts > 2 else spare if parts == 2 else 0)


def own_start(parts, place):
    return 0 if parts == 1 else 8 * place if parts == 2 else 8


def band_mask(window, parts, place, rows):
    if parts <= 2:
        return None
    row = lax.broadcasted_iota(jnp.int32, (window, 1), 0) + place * rows - 8
    return ((row >= 0) & (row < parts * rows)).astype(jnp.float32)


def tiles(value):
    return [value[:, k * LANES:(k + 1) * LANES] for k in range(value.shape[1] // LANES)]


def pack(value8, right4, coarse12):
    out = tiles(value8)
    halves = tiles(right4) + tiles(coarse12[8:])
    if len(halves) % 2:
        halves.append(halves[-1])
    out += tiles(coarse12[:8])
    out += [jnp.concatenate([halves[k], halves[k + 1]], 0) for k in range(0, len(halves), 2)]
    return out


def packed_tiles(fine_tiles, coarse_tiles):
    return fine_tiles + coarse_tiles + (fine_tiles + coarse_tiles + 1) // 2


def unpack(tile, fine_tiles, coarse_tiles):
    value8 = jnp.concatenate([tile(k) for k in range(fine_tiles)], 1)
    top = jnp.concatenate([tile(fine_tiles + k) for k in range(coarse_tiles)], 1)
    halves = []
    for k in range(fine_tiles + coarse_tiles, packed_tiles(fine_tiles, coarse_tiles)):
        both = tile(k)
        halves += [both[:4], both[4:]]
    right4 = jnp.concatenate(halves[:fine_tiles], 1)
    bottom = jnp.concatenate(halves[fine_tiles:fine_tiles + coarse_tiles], 1)
    return value8, right4, jnp.concatenate([top, bottom], 0)


def down_kernel(parts, sweeps, target, grad_x, grad_y, labels, even, odd, *refs):
    if parts == 2:
        packed_ref, *refs = refs
    value_ref, right_ref, coarse_ref, v_ref, b_ref, paired_ref = refs
    chans, rows, cols = target.shape
    window = value_ref.shape[1]
    place = lax.axis_index("lat")
    second = lax.axis_index("lon") % 2 == 1
    start = own_start(parts, place)
    if parts == 2:
        start = pl.multiple_of(start, 8)
    inside = band_mask(window, parts, place, rows)
    inner = lax.broadcasted_iota(jnp.int32, (rows, LANES), 1) < HALF
    marks = labels[...]
    count = sweeps[0]
    scale = 1.0

    def halo(chan):
        a, b = even[chan], odd[chan]
        return jnp.where(inner != second, a, b)

    def chosen(grad, chan):
        out = jnp.zeros((rows, cols), jnp.float32)
        for source in range(grad.shape[0]):
            out = jnp.where(marks == source, grad[source, chan], out)
        return out

    if window > rows:
        v_ref[...] = jnp.zeros_like(v_ref)
        b_ref[...] = jnp.zeros_like(b_ref)
    resid = []
    for chan in range(chans):
        own = jnp.concatenate([target[chan], halo(chan)], 1)
        sel_x = jnp.concatenate([chosen(grad_x, chan), halo(chans + chan)], 1)
        sel_y = jnp.concatenate([chosen(grad_y, chan), halo(2 * chans + chan)], 1)
        right = SCREENING * own - ((sel_x - west_of(sel_x)) + (sel_y - north_of(sel_y)))
        v_ref[chan, pl.ds(start, rows), :] = own
        b_ref[chan, pl.ds(start, rows), :] = right
        if window > rows:
            below = pltpu.roll(sel_y[rows - 8:], 1, 0)
            b_ref[chan, pl.ds(start + rows, 8), :] = jnp.where(rows_of(below) == 0, below, 0.0)
        right = b_ref[chan, :window, :]
        if inside is not None:
            right = right * inside
        right_ref[chan] = right
        value = lax.fori_loop(
            0, count, lambda _, v, chan=chan: sweep(v, right_ref[chan], scale, inside), v_ref[chan, :window, :]
        )
        value_ref[chan] = value
        left = residual(value, right, scale)
        resid.append(left if inside is None else left * inside)
    coarse = restrict(resid, paired_ref)
    for chan in range(chans):
        coarse_ref[chan] = coarse[chan]
        if parts == 2:
            north = place == 0
            value8 = jnp.where(north, value_ref[chan, 12:20, :], value_ref[chan, 4:12, :])
            right4 = jnp.where(north, right_ref[chan, 13:17, :], right_ref[chan, 8:12, :])
            for k, tile in enumerate(pack(value8, right4, coarse[chan])):
                packed_ref[chan, k] = tile


def down(parts, sweeps, target, grad_x, grad_y, labels, even, odd):
    chans, rows, cols = target.shape
    window = window_of(rows, parts)
    wide, half = cols + LANES, cols // 2 + LANES
    f32 = functools.partial(jax.ShapeDtypeStruct, dtype=jnp.float32)
    outs = [f32((chans, window, wide)), f32((chans, window, wide)), f32((chans, window // 2, half))]
    if parts == 2:
        outs.insert(0, f32((chans, packed_tiles(wide // LANES, half // LANES), 8, LANES)))
    spare = 8 if window > rows else 0
    return pl.pallas_call(
        functools.partial(down_kernel, parts),
        in_specs=[SMEM] + [VMEM] * 6,
        out_specs=[VMEM] * len(outs),
        out_shape=outs,
        scratch_shapes=[
            pltpu.VMEM((chans, window + spare, wide), jnp.float32),
            pltpu.VMEM((chans, window + spare, wide), jnp.float32),
            pltpu.VMEM((chans, half // LANES, window, LANES), jnp.float32),
        ],
        compiler_params=pltpu.CompilerParams(vmem_limit_bytes=32 * 2**20),
        name="down",
    )(sweeps, target, grad_x, grad_y, labels, even, odd)


def joined(place, own, other, height):
    gap = jnp.zeros((height - own.shape[0], own.shape[1]), jnp.float32)
    top, bottom = (lambda v: jnp.concatenate([v, gap], 0)), (lambda v: jnp.concatenate([gap, v], 0))
    return jnp.where(place == 0, top(own) + bottom(other), bottom(own) + top(other))


def up_kernel(parts, sweeps, value_ref, right_ref, coarse_ref, *refs):
    if parts == 2:
        packed_ref, *refs = refs
    out_ref, b0_ref, b1_ref, b2_ref, pair_ref, fix1_ref, fix0_ref = refs
    chans, rows, cols = out_ref.shape
    window, wide = value_ref.shape[1:]
    half = b1_ref.shape[2]
    place = lax.axis_index("lat")
    inside = band_mask(window, parts, place, rows)
    north = place == 0

    def widened(value, upper, lower):
        def at(first):
            last = window - first - value.shape[0]
            pads = [jnp.zeros((n, wide), jnp.float32) for n in (first, last)]
            return jnp.concatenate([pads[0], value, pads[1]], 0)

        return jnp.where(north, at(upper), at(lower))

    def received(chan):
        return unpack(lambda k: packed_ref[chan, k], wide // LANES, half // LANES)

    for chan in range(chans):
        if parts == 2:
            b1_ref[chan] = joined(place, coarse_ref[chan], received(chan)[2], b1_ref.shape[1])
        else:
            b1_ref[chan] = coarse_ref[chan]

    def smoothed(values, right_ref, count, scale, inside=None):
        def step(_, values):
            return tuple(sweep(v, right_ref[i], scale, inside) for i, v in enumerate(values))

        return lax.fori_loop(0, count, step, tuple(values))

    def from_zero(right_ref, count, scale):
        first = [(DAMPING / diagonal(scale)) * right_ref[i] for i in range(chans)]
        return smoothed(first, right_ref, count - 1, scale)

    mid = from_zero(b1_ref, sweeps[1], 0.25)
    low = restrict([residual(mid[i], b1_ref[i], 0.25) for i in range(chans)], pair_ref)
    for i in range(chans):
        b2_ref[i] = low[i]
    fix2 = from_zero(b2_ref, sweeps[2], 0.0625)
    prolong(fix2, fix1_ref, 0)
    mid = smoothed([mid[i] + wide_rows(fix1_ref, i, 0, mid[i].shape[0]) for i in range(chans)], b1_ref, sweeps[1], 0.25)
    spare = 8 if parts > 2 else 0
    if spare:
        fix0_ref[...] = jnp.zeros_like(fix0_ref)
    prolong(mid, fix0_ref, spare)
    start = own_start(parts, place)
    shown = 0 if parts == 1 else pl.multiple_of((8 if parts == 2 else rows) * place, 8)
    for i in range(chans):
        value = value_ref[i] + wide_rows(fix0_ref, i, shown, window)
        if parts == 2:
            value8, right4, _ = received(i)
            value = value + widened(value8, 12, 4)
            b0_ref[i] = right_ref[i] + widened(right4, 16, 5)
        else:
            b0_ref[i] = right_ref[i]
        value = lax.fori_loop(0, sweeps[0], lambda _, v, i=i: sweep(v, b0_ref[i], 1.0, inside), value)
        if parts == 2:
            out_ref[i] = jnp.where(place == 0, value[:rows, :cols], value[8:8 + rows, :cols])
        else:
            out_ref[i] = value[start:start + rows, :cols]


def up(parts, shape, sweeps, value, right, coarse, *packed):
    chans, rows, cols = shape
    window, wide = value.shape[1:]
    full = parts * rows
    f32 = functools.partial(pltpu.VMEM, dtype=jnp.float32)
    spare = 16 if parts > 2 else 0
    return pl.pallas_call(
        functools.partial(up_kernel, parts),
        in_specs=[SMEM] + [VMEM] * (3 + len(packed)),
        out_specs=VMEM,
        out_shape=jax.ShapeDtypeStruct(shape, jnp.float32),
        scratch_shapes=[
            f32(value.shape),
            f32((chans, full // 2, cols // 2 + LANES)),
            f32((chans, full // 4, cols // 4 + LANES)),
            f32((chans, cols // 4 // LANES + 1, full // 2, LANES)),
            f32((chans, cols // 2 // LANES + 1, full // 2, LANES)),
            f32((chans, wide // LANES, full + spare, LANES)),
        ],
        compiler_params=pltpu.CompilerParams(vmem_limit_bytes=48 * 2**20),
        name="up",
    )(sweeps, value, right, coarse, *packed)


def local(target, grad_x, grad_y, labels, sweeps):
    parts, around_globe = lax.axis_size("lat"), lax.axis_size("lon")
    tile = edges(target, grad_x, grad_y, labels)
    swap_odd = [(i, (i + 1 if i % 2 else i - 1) % around_globe) for i in range(around_globe)]
    swap_even = [(i, i - 1 if i % 2 else i + 1) for i in range(around_globe)]
    odd = lax.ppermute(tile, "lon", swap_odd)
    even = lax.ppermute(tile, "lon", swap_even)
    found = down(parts, sweeps, target, grad_x, grad_y, labels, even, odd)
    if parts == 2:
        packed, value, right, coarse = found
        packed = lax.ppermute(packed, "lat", [(0, 1), (1, 0)])
        return up(parts, target.shape, sweeps, value, right, coarse, packed)
    value, right, coarse = found
    if parts > 2:
        rows = target.shape[1]
        southward = [(i, i + 1) for i in range(parts - 1)]
        northward = [(i + 1, i) for i in range(parts - 1)]

        def shared(field):
            north = lax.ppermute(field[:, rows:], "lat", southward)
            south = lax.ppermute(field[:, :16], "lat", northward)
            zeros = jnp.zeros_like(field[:, :16])
            return field + jnp.concatenate([north, zeros], 1) + jnp.concatenate([zeros, south], 1)

        value, right = shared(value), shared(right)
        every = lax.all_gather(coarse, "lat")
        step = rows // 2
        total = jnp.zeros((coarse.shape[0], parts * step + 8, coarse.shape[2]), jnp.float32)
        for i in range(parts):
            total = total.at[:, i * step:i * step + step + 8].add(every[i])
        coarse = total[:, 4:-4]
    return up(parts, target.shape, sweeps, value, right, coarse)


def solution(mesh):
    in_specs = (
        P(None, "lat", "lon"),
        P(None, None, "lat", "lon"),
        P(None, None, "lat", "lon"),
        P("lat", "lon"),
        P(),
    )
    out_specs = P(None, "lat", "lon")
    return jax.shard_map(local, mesh=mesh, in_specs=in_specs, out_specs=out_specs, check_vma=False)
```

```python
import functools

import jax
import jax.numpy as jnp
from jax import lax
from jax.experimental import pallas as pl
from jax.experimental.pallas import tpu as pltpu
from jax.sharding import PartitionSpec as P

SCREENING = 0.02
DAMPING = 0.8
LANES = 128
HALF = LANES // 2
VMEM = pl.BlockSpec(memory_space=pltpu.VMEM)
SMEM = pl.BlockSpec(memory_space=pltpu.SMEM)


def diagonal(scale):
    return SCREENING + 4.0 * scale


def rows_of(value):
    return lax.broadcasted_iota(jnp.int32, value.shape, 0)


def north_of(value):
    return jnp.where(rows_of(value) == 0, 0.0, pltpu.roll(value, 1, 0))


def south_of(value):
    last = value.shape[0] - 1
    return jnp.where(rows_of(value) == last, 0.0, pltpu.roll(value, last, 0))


def west_of(value):
    return pltpu.roll(value, 1, 1)


def east_of(value):
    return pltpu.roll(value, value.shape[1] - 1, 1)


def around(value):
    return (north_of(value) + south_of(value)) + (west_of(value) + east_of(value))


def sweep(value, right, scale, inside):
    diag = diagonal(scale)
    value = (1.0 - DAMPING) * value + (DAMPING / diag) * right + (DAMPING * scale / diag) * around(value)
    return value if inside is None else value * inside


def residual(value, right, scale):
    return right - diagonal(scale) * value + scale * around(value)


def two_parts(value):
    high = value.astype(jnp.bfloat16)
    return high, (value - high.astype(jnp.float32)).astype(jnp.bfloat16)


def moved(value, places):
    high, low = two_parts(value)
    dot = functools.partial(jnp.dot, preferred_element_type=jnp.float32)
    return dot(high, places) + dot(low, places)


def places_of(shape, wanted):
    source = lax.broadcasted_iota(jnp.int32, shape, 0)
    target = lax.broadcasted_iota(jnp.int32, shape, 1)
    return wanted(source, target).astype(jnp.float32).astype(jnp.bfloat16)


def halo_coarse(fine):
    return jnp.where(fine < HALF, fine // 2, HALF + fine // 2)


def pair_columns(fields):
    own = places_of((2 * LANES, LANES), lambda source, target: source // 2 == target)
    halo = places_of((LANES, LANES), lambda source, target: halo_coarse(source) == target)
    rows, cols = fields[0].shape
    blocks = (cols - LANES) // (2 * LANES)
    cut = [f[:, k * 2 * LANES:(k + 1) * 2 * LANES] for f in fields for k in range(blocks)]
    packed = moved(jnp.concatenate(cut, 0), own)
    edges = moved(jnp.concatenate([f[:, cols - LANES:] for f in fields], 0), halo)
    out = []
    for i in range(len(fields)):
        parts = [packed[(i * blocks + k) * rows:(i * blocks + k + 1) * rows] for k in range(blocks)]
        out.append(jnp.concatenate(parts + [edges[i * rows:(i + 1) * rows]], 1))
    return out


def spread_columns(fields):
    own = places_of((2 * LANES, 2 * LANES), lambda source, target: source == target // 2 + LANES * (target % 2))
    halo = places_of((2 * LANES, LANES), lambda source, target: source == halo_coarse(target) + LANES * (target % 2))
    rows, cols = fields[0].shape
    blocks = (cols - LANES) // LANES
    west = [0.75 * f + 0.25 * west_of(f) for f in fields]
    east = [0.75 * f + 0.25 * east_of(f) for f in fields]

    def cut(k):
        span = slice(k * LANES, (k + 1) * LANES)
        return [jnp.concatenate([w[:, span], e[:, span]], 1) for w, e in zip(west, east)]

    own_cut = [cut(k) for k in range(blocks)]
    packed = moved(jnp.concatenate([own_cut[k][i] for i in range(len(fields)) for k in range(blocks)], 0), own)
    edges = moved(jnp.concatenate(cut(blocks), 0), halo)
    out = []
    for i in range(len(fields)):
        parts = [packed[(i * blocks + k) * rows:(i * blocks + k + 1) * rows] for k in range(blocks)]
        out.append(jnp.concatenate(parts + [edges[i * rows:(i + 1) * rows]], 1))
    return out


def restrict(fields, paired_ref):
    rows = fields[0].shape[0]
    out = []
    for i, paired in enumerate(pair_columns(fields)):
        halves = []
        for k, tile in enumerate(tiles(paired)):
            paired_ref[i, k] = tile
            north = paired_ref[i, k, pl.ds(0, rows // 2, stride=2), :]
            south = paired_ref[i, k, pl.ds(1, rows // 2, stride=2), :]
            halves.append(0.25 * (north + south))
        out.append(jnp.concatenate(halves, 1))
    return out


def prolong(fields, fine_ref, first):
    rows = fields[0].shape[0]
    norths = [0.75 * f + 0.25 * north_of(f) for f in fields]
    souths = [0.75 * f + 0.25 * south_of(f) for f in fields]
    spread = spread_columns(norths + souths)
    for i in range(len(fields)):
        for k, (north, south) in enumerate(zip(tiles(spread[i]), tiles(spread[len(fields) + i]))):
            fine_ref[i, k, pl.ds(first, rows, stride=2), :] = north
            fine_ref[i, k, pl.ds(first + 1, rows, stride=2), :] = south


def wide_rows(fine_ref, chan, start, rows):
    return jnp.concatenate([fine_ref[chan, k, pl.ds(start, rows), :] for k in range(fine_ref.shape[1])], 1)


def window_of(rows, parts):
    spare = 8
    return rows + (2 * spare if parts > 2 else spare if parts == 2 else 0)


def own_start(parts, place):
    return 0 if parts == 1 else 8 * place if parts == 2 else 8


def band_mask(window, parts, place, rows):
    if parts <= 2:
        return None
    row = lax.broadcasted_iota(jnp.int32, (window, 1), 0) + place * rows - 8
    return ((row >= 0) & (row < parts * rows)).astype(jnp.float32)


def tiles(value):
    return [value[:, k * LANES:(k + 1) * LANES] for k in range(value.shape[1] // LANES)]


def lanes_of(tile):
    return lax.broadcasted_iota(jnp.int32, tile.shape, len(tile.shape) - 1)


def pack(value8, right4, coarse12):
    out = tiles(value8)
    halves = tiles(right4) + tiles(coarse12[8:])
    if len(halves) % 2:
        halves.append(halves[-1])
    out += tiles(coarse12[:8])
    out += [jnp.concatenate([halves[k], halves[k + 1]], 0) for k in range(0, len(halves), 2)]
    return out


def packed_tiles(fine_tiles, coarse_tiles):
    return fine_tiles + coarse_tiles + (fine_tiles + coarse_tiles + 1) // 2


def unpack(tile, fine_tiles, coarse_tiles):
    value8 = jnp.concatenate([tile(k) for k in range(fine_tiles)], 1)
    top = jnp.concatenate([tile(fine_tiles + k) for k in range(coarse_tiles)], 1)
    halves = []
    for k in range(fine_tiles + coarse_tiles, packed_tiles(fine_tiles, coarse_tiles)):
        both = tile(k)
        halves += [both[:4], both[4:]]
    right4 = jnp.concatenate(halves[:fine_tiles], 1)
    bottom = jnp.concatenate(halves[fine_tiles:fine_tiles + coarse_tiles], 1)
    return value8, right4, jnp.concatenate([top, bottom], 0)


def eastward(value):
    own = value[..., -2 * LANES:-LANES]
    return jnp.where(lanes_of(own) < HALF, value[..., -LANES:], own)


def westward(value):
    own = value[..., :LANES]
    return jnp.where(lanes_of(own) < HALF, own, value[..., -LANES:])


def with_edges(value, from_west, from_east):
    inner = lanes_of(from_west) < HALF
    first = value[..., :LANES] + jnp.where(inner, from_west, 0.0)
    last = value[..., -2 * LANES:-LANES] + jnp.where(inner, 0.0, from_east)
    halo = value[..., -LANES:] + jnp.where(inner, from_east, from_west)
    return jnp.concatenate([first, value[..., LANES:-2 * LANES], last, halo], value.ndim - 1)


VALUE_AT, RIGHT_AT = 48, 80


def taller(value, rows):
    missing = rows - value.shape[0]
    return jnp.concatenate([value, jnp.zeros((missing, value.shape[1]), value.dtype)], 0) if missing else value


def three_in_one(value, right, coarse, rows):
    value, right, coarse = (taller(v, rows) for v in (value, right, coarse))
    lane = lanes_of(value)
    at = lambda first: (lane >= first) & (lane < first + 16)
    out = jnp.where(at(VALUE_AT), pltpu.roll(value, VALUE_AT + 8, 1), coarse)
    return jnp.where(at(RIGHT_AT), pltpu.roll(right, RIGHT_AT + 8, 1), out)


def one_to_three(tile, value_rows, right_rows, coarse_rows):
    lane = lanes_of(tile)
    ends = lambda width: (lane < width) | (lane >= LANES - width)
    value = jnp.where(ends(8), pltpu.roll(tile, LANES - VALUE_AT - 8, 1), 0.0)
    right = jnp.where(ends(8), pltpu.roll(tile, LANES - RIGHT_AT - 8, 1), 0.0)
    coarse = jnp.where(ends(32), tile, 0.0)
    return value[:value_rows], right[:right_rows], coarse[:coarse_rows]


def down_kernel(parts, sweeps, target, grad_x, grad_y, labels, *refs):
    outs, scratch = refs[:8 if parts == 2 else 3], refs[8 if parts == 2 else 3:]
    value_ref, right_ref, coarse_ref = outs[:3]
    target_v, grad_x_v, grad_y_v, labels_v, v_ref, b_ref, paired_ref, sems = scratch
    chans, rows, cols = target.shape
    window = value_ref.shape[1]
    place = lax.axis_index("lat")
    second = lax.axis_index("lon") % 2 == 1
    start = own_start(parts, place)
    if parts == 2:
        start = pl.multiple_of(start, 8)
    inside = band_mask(window, parts, place, rows)
    count = sweeps[0]
    scale = 1.0

    marks_copy = pltpu.make_async_copy(labels, labels_v, sems.at[chans, 0])
    marks_copy.start()
    copies = []
    for chan in range(chans):
        copies.append([
            pltpu.make_async_copy(target.at[chan], target_v.at[chan], sems.at[chan, 0]),
            pltpu.make_async_copy(grad_x.at[:, chan], grad_x_v.at[:, chan], sems.at[chan, 1]),
            pltpu.make_async_copy(grad_y.at[:, chan], grad_y_v.at[:, chan], sems.at[chan, 2]),
        ])
        for copy in copies[-1]:
            copy.start()
    if window > rows:
        v_ref[...] = jnp.zeros_like(v_ref)
        b_ref[...] = jnp.zeros_like(b_ref)
    marks_copy.wait()

    def chosen(grad, chan):
        marks = labels_v[...]
        out = jnp.zeros((rows, cols), jnp.float32)
        for source in range(grad.shape[0]):
            out = jnp.where(marks == source, grad[source, chan], out)
        return out

    blank = jnp.zeros((rows, LANES), jnp.float32)
    resid = []
    for chan in range(chans):
        for copy in copies[chan]:
            copy.wait()
        own = jnp.concatenate([target_v[chan], blank], 1)
        sel_x = jnp.concatenate([chosen(grad_x_v, chan), blank], 1)
        sel_y = jnp.concatenate([chosen(grad_y_v, chan), blank], 1)
        right = SCREENING * own - ((sel_x - west_of(sel_x)) + (sel_y - north_of(sel_y)))
        v_ref[chan, pl.ds(start, rows), :] = own
        b_ref[chan, pl.ds(start, rows), :] = right
        if window > rows:
            below = pltpu.roll(sel_y[rows - 8:], 1, 0)
            b_ref[chan, pl.ds(start + rows, 8), :] = jnp.where(rows_of(below) == 0, below, 0.0)
        right = b_ref[chan, :window, :]
        if inside is not None:
            right = right * inside
        right_ref[chan] = right
        value = lax.fori_loop(
            0, count, lambda _, v, chan=chan: sweep(v, right_ref[chan], scale, inside), v_ref[chan, :window, :]
        )
        value_ref[chan] = value
        left = residual(value, right, scale)
        resid.append(left if inside is None else left * inside)
    coarse = restrict(resid, paired_ref)
    for chan in range(chans):
        coarse_ref[chan] = coarse[chan]
        if parts == 2:
            packed_ref, odd_ref, even_ref, odd_across, even_across = outs[3:]
            north = place == 0
            value, right = value_ref[chan], right_ref[chan]
            value8 = jnp.where(north, value[12:20], value[4:12])
            right4 = jnp.where(north, right[13:17], right[8:12])
            for k, tile in enumerate(pack(value8, right4, coarse[chan])):
                packed_ref[chan, k] = tile
            for height, odd, even, fields in (
                (window, odd_ref, even_ref, (value, right, coarse[chan])),
                (16, odd_across, even_across, (value8, right4, coarse[chan])),
            ):
                east = three_in_one(*[eastward(f) for f in fields], height)
                west = three_in_one(*[westward(f) for f in fields], height)
                odd[chan] = jnp.where(second, east, west)
                even[chan] = jnp.where(second, west, east)


def down(parts, sweeps, target, grad_x, grad_y, labels):
    chans, rows, cols = target.shape
    window = window_of(rows, parts)
    wide, half = cols + LANES, cols // 2 + LANES
    f32 = functools.partial(jax.ShapeDtypeStruct, dtype=jnp.float32)
    outs = [f32((chans, window, wide)), f32((chans, window, wide)), f32((chans, window // 2, half))]
    if parts == 2:
        outs.append(f32((chans, packed_tiles(wide // LANES, half // LANES), 8, LANES)))
        outs += [f32((chans, window, LANES))] * 2 + [f32((chans, 16, LANES))] * 2
    spare = 8 if window > rows else 0
    return pl.pallas_call(
        functools.partial(down_kernel, parts),
        in_specs=[SMEM] + [pl.BlockSpec(memory_space=pl.ANY)] * 4,
        out_specs=[VMEM] * len(outs),
        out_shape=outs,
        scratch_shapes=[
            pltpu.VMEM(target.shape, jnp.float32),
            pltpu.VMEM(grad_x.shape, jnp.float32),
            pltpu.VMEM(grad_y.shape, jnp.float32),
            pltpu.VMEM(labels.shape, jnp.int32),
            pltpu.VMEM((chans, window + spare, wide), jnp.float32),
            pltpu.VMEM((chans, window + spare, wide), jnp.float32),
            pltpu.VMEM((chans, half // LANES, window, LANES), jnp.float32),
            pltpu.SemaphoreType.DMA((chans + 1, 3)),
        ],
        compiler_params=pltpu.CompilerParams(vmem_limit_bytes=32 * 2**20),
        name="down",
    )(sweeps, target, grad_x, grad_y, labels)


def joined(place, own, other, height):
    gap = jnp.zeros((height - own.shape[0], own.shape[1]), jnp.float32)
    top, bottom = (lambda v: jnp.concatenate([v, gap], 0)), (lambda v: jnp.concatenate([gap, v], 0))
    return jnp.where(place == 0, top(own) + bottom(other), bottom(own) + top(other))


def up_kernel(parts, sweeps, value_ref, right_ref, coarse_ref, *refs):
    if parts == 2:
        packed_ref, *edge_refs = refs[:5]
        refs = refs[5:]
    out_ref, b0_ref, b1_ref, b2_ref, pair_ref, fix1_ref, fix0_ref = refs
    chans, rows, cols = out_ref.shape
    window, wide = value_ref.shape[1:]
    half = b1_ref.shape[2]
    place = lax.axis_index("lat")
    inside = band_mask(window, parts, place, rows)
    north = place == 0

    def widened(value, upper, lower):
        def at(first):
            last = window - first - value.shape[0]
            pads = [jnp.zeros((n, wide), jnp.float32) for n in (first, last)]
            return jnp.concatenate([pads[0], value, pads[1]], 0)

        return jnp.where(north, at(upper), at(lower))

    second = lax.axis_index("lon") % 2 == 1

    def sides(odd_ref, even_ref, chan, *heights):
        odd, even = odd_ref[chan], even_ref[chan]
        west = one_to_three(jnp.where(second, even, odd), *heights)
        east = one_to_three(jnp.where(second, odd, even), *heights)
        return list(zip(west, east))

    def own_part(chan, which):
        field = (value_ref, right_ref, coarse_ref)[which][chan]
        if parts != 2:
            return field
        return with_edges(field, *sides(*edge_refs[:2], chan, window, window, window // 2)[which])

    def other_part(chan, which):
        field = unpack(lambda k: packed_ref[chan, k], wide // LANES, half // LANES)[which]
        return with_edges(field, *sides(*edge_refs[2:], chan, 8, 4, 12)[which])

    for chan in range(chans):
        if parts == 2:
            b1_ref[chan] = joined(place, own_part(chan, 2), other_part(chan, 2), b1_ref.shape[1])
        else:
            b1_ref[chan] = coarse_ref[chan]

    def smoothed(values, right_ref, count, scale, inside=None):
        def step(_, values):
            return tuple(sweep(v, right_ref[i], scale, inside) for i, v in enumerate(values))

        return lax.fori_loop(0, count, step, tuple(values))

    def from_zero(right_ref, count, scale):
        first = [(DAMPING / diagonal(scale)) * right_ref[i] for i in range(chans)]
        return smoothed(first, right_ref, count - 1, scale)

    mid = from_zero(b1_ref, sweeps[1], 0.25)
    low = restrict([residual(mid[i], b1_ref[i], 0.25) for i in range(chans)], pair_ref)
    for i in range(chans):
        b2_ref[i] = low[i]
    fix2 = from_zero(b2_ref, sweeps[2], 0.0625)
    prolong(fix2, fix1_ref, 0)
    mid = smoothed([mid[i] + wide_rows(fix1_ref, i, 0, mid[i].shape[0]) for i in range(chans)], b1_ref, sweeps[1], 0.25)
    spare = 8 if parts > 2 else 0
    if spare:
        fix0_ref[...] = jnp.zeros_like(fix0_ref)
    prolong(mid, fix0_ref, spare)
    start = own_start(parts, place)
    shown = 0 if parts == 1 else pl.multiple_of((8 if parts == 2 else rows) * place, 8)
    for i in range(chans):
        value = own_part(i, 0) + wide_rows(fix0_ref, i, shown, window)
        right = own_part(i, 1)
        if parts == 2:
            value = value + widened(other_part(i, 0), 12, 4)
            right = right + widened(other_part(i, 1), 16, 5)
        b0_ref[i] = right
        value = lax.fori_loop(0, sweeps[0], lambda _, v, i=i: sweep(v, b0_ref[i], 1.0, inside), value)
        if parts == 2:
            out_ref[i] = jnp.where(place == 0, value[:rows, :cols], value[8:8 + rows, :cols])
        else:
            out_ref[i] = value[start:start + rows, :cols]


def up(parts, shape, sweeps, value, right, coarse, *packed):
    chans, rows, cols = shape
    window, wide = value.shape[1:]
    full = parts * rows
    f32 = functools.partial(pltpu.VMEM, dtype=jnp.float32)
    spare = 16 if parts > 2 else 0
    return pl.pallas_call(
        functools.partial(up_kernel, parts),
        in_specs=[SMEM] + [VMEM] * (3 + len(packed)),
        out_specs=VMEM,
        out_shape=jax.ShapeDtypeStruct(shape, jnp.float32),
        scratch_shapes=[
            f32(value.shape),
            f32((chans, full // 2, cols // 2 + LANES)),
            f32((chans, full // 4, cols // 4 + LANES)),
            f32((chans, cols // 4 // LANES + 1, full // 2, LANES)),
            f32((chans, cols // 2 // LANES + 1, full // 2, LANES)),
            f32((chans, wide // LANES, full + spare, LANES)),
        ],
        compiler_params=pltpu.CompilerParams(vmem_limit_bytes=48 * 2**20),
        name="up",
    )(sweeps, value, right, coarse, *packed)


def local(target, grad_x, grad_y, labels, sweeps):
    parts, around_globe = lax.axis_size("lat"), lax.axis_size("lon")
    value, right, coarse, *sent = down(parts, sweeps, target, grad_x, grad_y, labels)
    if parts == 2:
        odd = [(i, (i + 1 if i % 2 else i - 1) % around_globe) for i in range(around_globe)]
        even = [(i, i - 1 if i % 2 else i + 1) for i in range(around_globe)]

        def across(pairs):
            return [(2 * i + k, 2 * j + 1 - k) for i, j in pairs for k in range(2)]

        packed, odd_edge, even_edge, odd_across, even_across = sent
        packed = lax.ppermute(packed, "lat", [(0, 1), (1, 0)])
        odd_edge = lax.ppermute(odd_edge, "lon", odd)
        odd_across = lax.ppermute(odd_across, ("lon", "lat"), across(odd))
        even_edge = lax.ppermute(even_edge, "lon", even)
        even_across = lax.ppermute(even_across, ("lon", "lat"), across(even))
        received = (packed, odd_edge, even_edge, odd_across, even_across)
        return up(parts, target.shape, sweeps, value, right, coarse, *received)

    def shared_lon(field):
        from_west = lax.ppermute(eastward(field), "lon", [(i, (i + 1) % around_globe) for i in range(around_globe)])
        from_east = lax.ppermute(westward(field), "lon", [((i + 1) % around_globe, i) for i in range(around_globe)])
        return with_edges(field, from_west, from_east)

    value, right, coarse = (shared_lon(f) for f in (value, right, coarse))
    if parts > 2:
        rows = target.shape[1]
        southward = [(i, i + 1) for i in range(parts - 1)]
        northward = [(i + 1, i) for i in range(parts - 1)]

        def shared_lat(field):
            north = lax.ppermute(field[:, rows:], "lat", southward)
            south = lax.ppermute(field[:, :16], "lat", northward)
            zeros = jnp.zeros_like(field[:, :16])
            return field + jnp.concatenate([north, zeros], 1) + jnp.concatenate([zeros, south], 1)

        value, right = shared_lat(value), shared_lat(right)
        every = lax.all_gather(coarse, "lat")
        step = rows // 2
        total = jnp.zeros((coarse.shape[0], parts * step + 8, coarse.shape[2]), jnp.float32)
        for i in range(parts):
            total = total.at[:, i * step:i * step + step + 8].add(every[i])
        coarse = total[:, 4:-4]
    return up(parts, target.shape, sweeps, value, right, coarse)


def solution(mesh):
    in_specs = (
        P(None, "lat", "lon"),
        P(None, None, "lat", "lon"),
        P(None, None, "lat", "lon"),
        P("lat", "lon"),
        P(),
    )
    out_specs = P(None, "lat", "lon")
    return jax.shard_map(local, mesh=mesh, in_specs=in_specs, out_specs=out_specs, check_vma=False)
```

```python
import functools

import jax
import jax.numpy as jnp
from jax import lax
from jax.experimental import pallas as pl
from jax.experimental.pallas import tpu as pltpu
from jax.sharding import PartitionSpec as P

SCREENING = 0.02
DAMPING = 0.8
LANES = 128
HALF = LANES // 2
VMEM = pl.BlockSpec(memory_space=pltpu.VMEM)
HBM = pl.BlockSpec(memory_space=pltpu.HBM)


def diagonal(scale):
    return SCREENING + 4.0 * scale


def rows_of(value):
    return lax.broadcasted_iota(jnp.int32, value.shape, 0)


def north_of(value):
    return jnp.where(rows_of(value) == 0, 0.0, pltpu.roll(value, 1, 0))


def south_of(value):
    last = value.shape[0] - 1
    return jnp.where(rows_of(value) == last, 0.0, pltpu.roll(value, last, 0))


def west_of(value):
    return pltpu.roll(value, 1, 1)


def east_of(value):
    return pltpu.roll(value, value.shape[1] - 1, 1)


def around(value):
    return (north_of(value) + south_of(value)) + (west_of(value) + east_of(value))


def sweep(value, right, scale, inside):
    diag = diagonal(scale)
    value = (1.0 - DAMPING) * value + (DAMPING / diag) * right + (DAMPING * scale / diag) * around(value)
    return value if inside is None else value * inside


def residual(value, right, scale):
    return right - diagonal(scale) * value + scale * around(value)


def two_parts(value):
    high = value.astype(jnp.bfloat16)
    return high, (value - high.astype(jnp.float32)).astype(jnp.bfloat16)


def moved(value, places):
    high, low = two_parts(value)
    dot = functools.partial(jnp.dot, preferred_element_type=jnp.float32)
    return dot(high, places) + dot(low, places)


def places_of(shape, wanted):
    source = lax.broadcasted_iota(jnp.int32, shape, 0)
    target = lax.broadcasted_iota(jnp.int32, shape, 1)
    return wanted(source, target).astype(jnp.float32).astype(jnp.bfloat16)


def halo_coarse(fine):
    return jnp.where(fine < HALF, fine // 2, HALF + fine // 2)


def pair_columns(fields):
    own = places_of((2 * LANES, LANES), lambda source, target: source // 2 == target)
    halo = places_of((LANES, LANES), lambda source, target: halo_coarse(source) == target)
    rows, cols = fields[0].shape
    blocks = (cols - LANES) // (2 * LANES)
    cut = [f[:, k * 2 * LANES:(k + 1) * 2 * LANES] for f in fields for k in range(blocks)]
    packed = moved(jnp.concatenate(cut, 0), own)
    edges = moved(jnp.concatenate([f[:, cols - LANES:] for f in fields], 0), halo)
    out = []
    for i in range(len(fields)):
        parts = [packed[(i * blocks + k) * rows:(i * blocks + k + 1) * rows] for k in range(blocks)]
        out.append(jnp.concatenate(parts + [edges[i * rows:(i + 1) * rows]], 1))
    return out


def spread_columns(fields):
    own = places_of((2 * LANES, 2 * LANES), lambda source, target: source == target // 2 + LANES * (target % 2))
    halo = places_of((2 * LANES, LANES), lambda source, target: source == halo_coarse(target) + LANES * (target % 2))
    rows, cols = fields[0].shape
    blocks = (cols - LANES) // LANES
    west = [0.75 * f + 0.25 * west_of(f) for f in fields]
    east = [0.75 * f + 0.25 * east_of(f) for f in fields]

    def cut(k):
        span = slice(k * LANES, (k + 1) * LANES)
        return [jnp.concatenate([w[:, span], e[:, span]], 1) for w, e in zip(west, east)]

    own_cut = [cut(k) for k in range(blocks)]
    packed = moved(jnp.concatenate([own_cut[k][i] for i in range(len(fields)) for k in range(blocks)], 0), own)
    edges = moved(jnp.concatenate(cut(blocks), 0), halo)
    out = []
    for i in range(len(fields)):
        parts = [packed[(i * blocks + k) * rows:(i * blocks + k + 1) * rows] for k in range(blocks)]
        out.append(jnp.concatenate(parts + [edges[i * rows:(i + 1) * rows]], 1))
    return out


def restrict(fields, paired_ref):
    rows = fields[0].shape[0]
    out = []
    for i, paired in enumerate(pair_columns(fields)):
        halves = []
        for k, tile in enumerate(tiles(paired)):
            paired_ref[i, k] = tile
            north = paired_ref[i, k, pl.ds(0, rows // 2, stride=2), :]
            south = paired_ref[i, k, pl.ds(1, rows // 2, stride=2), :]
            halves.append(0.25 * (north + south))
        out.append(jnp.concatenate(halves, 1))
    return out


def prolong(fields, fine_ref, first):
    rows = fields[0].shape[0]
    norths = [0.75 * f + 0.25 * north_of(f) for f in fields]
    souths = [0.75 * f + 0.25 * south_of(f) for f in fields]
    spread = spread_columns(norths + souths)
    for i in range(len(fields)):
        for k, (north, south) in enumerate(zip(tiles(spread[i]), tiles(spread[len(fields) + i]))):
            fine_ref[i, k, pl.ds(first, rows, stride=2), :] = north
            fine_ref[i, k, pl.ds(first + 1, rows, stride=2), :] = south


def wide_rows(fine_ref, chan, start, rows):
    return jnp.concatenate([fine_ref[chan, k, pl.ds(start, rows), :] for k in range(fine_ref.shape[1])], 1)


def window_of(rows, parts):
    spare = 8
    return rows + (2 * spare if parts > 2 else spare if parts == 2 else 0)


def own_start(parts, place):
    return 0 if parts == 1 else 8 * place if parts == 2 else 8


def band_mask(window, parts, place, rows):
    if parts <= 2:
        return None
    row = lax.broadcasted_iota(jnp.int32, (window, 1), 0) + place * rows - 8
    return ((row >= 0) & (row < parts * rows)).astype(jnp.float32)


def tiles(value):
    return [value[:, k * LANES:(k + 1) * LANES] for k in range(value.shape[1] // LANES)]


def lanes_of(tile):
    return lax.broadcasted_iota(jnp.int32, tile.shape, len(tile.shape) - 1)


def pack(value8, right4, coarse12):
    out = tiles(value8)
    halves = tiles(right4) + tiles(coarse12[8:])
    if len(halves) % 2:
        halves.append(halves[-1])
    out += tiles(coarse12[:8])
    out += [jnp.concatenate([halves[k], halves[k + 1]], 0) for k in range(0, len(halves), 2)]
    return out


def packed_tiles(fine_tiles, coarse_tiles):
    return fine_tiles + coarse_tiles + (fine_tiles + coarse_tiles + 1) // 2


def unpack(tile, fine_tiles, coarse_tiles):
    value8 = jnp.concatenate([tile(k) for k in range(fine_tiles)], 1)
    top = jnp.concatenate([tile(fine_tiles + k) for k in range(coarse_tiles)], 1)
    halves = []
    for k in range(fine_tiles + coarse_tiles, packed_tiles(fine_tiles, coarse_tiles)):
        both = tile(k)
        halves += [both[:4], both[4:]]
    right4 = jnp.concatenate(halves[:fine_tiles], 1)
    bottom = jnp.concatenate(halves[fine_tiles:fine_tiles + coarse_tiles], 1)
    return value8, right4, jnp.concatenate([top, bottom], 0)


def eastward(value):
    own = value[..., -2 * LANES:-LANES]
    return jnp.where(lanes_of(own) < HALF, value[..., -LANES:], own)


def westward(value):
    own = value[..., :LANES]
    return jnp.where(lanes_of(own) < HALF, own, value[..., -LANES:])


def with_edges(value, from_west, from_east):
    inner = lanes_of(from_west) < HALF
    first = value[..., :LANES] + jnp.where(inner, from_west, 0.0)
    last = value[..., -2 * LANES:-LANES] + jnp.where(inner, 0.0, from_east)
    halo = value[..., -LANES:] + jnp.where(inner, from_east, from_west)
    return jnp.concatenate([first, value[..., LANES:-2 * LANES], last, halo], value.ndim - 1)


VALUE_AT, RIGHT_AT = 48, 80


def taller(value, rows):
    missing = rows - value.shape[0]
    return jnp.concatenate([value, jnp.zeros((missing, value.shape[1]), value.dtype)], 0) if missing else value


def three_in_one(value, right, coarse, rows):
    value, right, coarse = (taller(v, rows) for v in (value, right, coarse))
    lane = lanes_of(value)
    at = lambda first: (lane >= first) & (lane < first + 16)
    out = jnp.where(at(VALUE_AT), pltpu.roll(value, VALUE_AT + 8, 1), coarse)
    return jnp.where(at(RIGHT_AT), pltpu.roll(right, RIGHT_AT + 8, 1), out)


def one_to_three(tile, value_rows, right_rows, coarse_rows):
    lane = lanes_of(tile)
    ends = lambda width: (lane < width) | (lane >= LANES - width)
    value = jnp.where(ends(8), pltpu.roll(tile, LANES - VALUE_AT - 8, 1), 0.0)
    right = jnp.where(ends(8), pltpu.roll(tile, LANES - RIGHT_AT - 8, 1), 0.0)
    coarse = jnp.where(ends(32), tile, 0.0)
    return value[:value_rows], right[:right_rows], coarse[:coarse_rows]


def down_kernel(parts, sweeps_hbm, target, grad_x, grad_y, labels, *refs):
    outs, scratch = refs[:8 if parts == 2 else 3], refs[8 if parts == 2 else 3:]
    value_ref, right_ref, coarse_ref = outs[:3]
    sweeps, target_v, grad_x_v, grad_y_v, labels_v, v_ref, b_ref, paired_ref, sems = scratch
    chans, rows, cols = target.shape
    window = value_ref.shape[1]
    place = lax.axis_index("lat")
    second = lax.axis_index("lon") % 2 == 1
    start = own_start(parts, place)
    if parts == 2:
        start = pl.multiple_of(start, 8)
    inside = band_mask(window, parts, place, rows)
    scale = 1.0

    first_copies = [
        pltpu.make_async_copy(labels, labels_v, sems.at[chans, 0]),
        pltpu.make_async_copy(sweeps_hbm, sweeps, sems.at[chans, 1]),
    ]
    for copy in first_copies:
        copy.start()
    copies = []
    for chan in range(chans):
        copies.append([
            pltpu.make_async_copy(target.at[chan], target_v.at[chan], sems.at[chan, 0]),
            pltpu.make_async_copy(grad_x.at[:, chan], grad_x_v.at[:, chan], sems.at[chan, 1]),
            pltpu.make_async_copy(grad_y.at[:, chan], grad_y_v.at[:, chan], sems.at[chan, 2]),
        ])
        for copy in copies[-1]:
            copy.start()
    if window > rows:
        v_ref[...] = jnp.zeros_like(v_ref)
        b_ref[...] = jnp.zeros_like(b_ref)
    for copy in first_copies:
        copy.wait()
    count = sweeps[0]

    def chosen(grad, chan):
        marks = labels_v[...]
        out = jnp.zeros((rows, cols), jnp.float32)
        for source in range(grad.shape[0]):
            out = jnp.where(marks == source, grad[source, chan], out)
        return out

    blank = jnp.zeros((rows, LANES), jnp.float32)
    resid = []
    for chan in range(chans):
        for copy in copies[chan]:
            copy.wait()
        own = jnp.concatenate([target_v[chan], blank], 1)
        sel_x = jnp.concatenate([chosen(grad_x_v, chan), blank], 1)
        sel_y = jnp.concatenate([chosen(grad_y_v, chan), blank], 1)
        right = SCREENING * own - ((sel_x - west_of(sel_x)) + (sel_y - north_of(sel_y)))
        v_ref[chan, pl.ds(start, rows), :] = own
        b_ref[chan, pl.ds(start, rows), :] = right
        if window > rows:
            below = pltpu.roll(sel_y[rows - 8:], 1, 0)
            b_ref[chan, pl.ds(start + rows, 8), :] = jnp.where(rows_of(below) == 0, below, 0.0)
        right = b_ref[chan, :window, :]
        if inside is not None:
            right = right * inside
        right_ref[chan] = right
        value = lax.fori_loop(
            0, count, lambda _, v, chan=chan: sweep(v, right_ref[chan], scale, inside), v_ref[chan, :window, :]
        )
        value_ref[chan] = value
        left = residual(value, right, scale)
        resid.append(left if inside is None else left * inside)
    coarse = restrict(resid, paired_ref)
    for chan in range(chans):
        coarse_ref[chan] = coarse[chan]
        if parts == 2:
            packed_ref, odd_ref, even_ref, odd_across, even_across = outs[3:]
            north = place == 0
            value, right = value_ref[chan], right_ref[chan]
            value8 = jnp.where(north, value[12:20], value[4:12])
            right4 = jnp.where(north, right[13:17], right[8:12])
            for k, tile in enumerate(pack(value8, right4, coarse[chan])):
                packed_ref[chan, k] = tile
            for height, odd, even, fields in (
                (window, odd_ref, even_ref, (value, right, coarse[chan])),
                (16, odd_across, even_across, (value8, right4, coarse[chan])),
            ):
                east = three_in_one(*[eastward(f) for f in fields], height)
                west = three_in_one(*[westward(f) for f in fields], height)
                odd[chan] = jnp.where(second, east, west)
                even[chan] = jnp.where(second, west, east)


def down(parts, sweeps, target, grad_x, grad_y, labels):
    chans, rows, cols = target.shape
    window = window_of(rows, parts)
    wide, half = cols + LANES, cols // 2 + LANES
    f32 = functools.partial(jax.ShapeDtypeStruct, dtype=jnp.float32)
    outs = [f32((chans, window, wide)), f32((chans, window, wide)), f32((chans, window // 2, half))]
    if parts == 2:
        outs.append(f32((chans, packed_tiles(wide // LANES, half // LANES), 8, LANES)))
        outs += [f32((chans, window, LANES))] * 2 + [f32((chans, 16, LANES))] * 2
    spare = 8 if window > rows else 0
    return pl.pallas_call(
        functools.partial(down_kernel, parts),
        in_specs=[HBM] * 5,
        out_specs=[VMEM] * len(outs),
        out_shape=outs,
        scratch_shapes=[
            pltpu.SMEM(sweeps.shape, jnp.int32),
            pltpu.VMEM(target.shape, jnp.float32),
            pltpu.VMEM(grad_x.shape, jnp.float32),
            pltpu.VMEM(grad_y.shape, jnp.float32),
            pltpu.VMEM(labels.shape, jnp.int32),
            pltpu.VMEM((chans, window + spare, wide), jnp.float32),
            pltpu.VMEM((chans, window + spare, wide), jnp.float32),
            pltpu.VMEM((chans, half // LANES, window, LANES), jnp.float32),
            pltpu.SemaphoreType.DMA((chans + 1, 3)),
        ],
        compiler_params=pltpu.CompilerParams(vmem_limit_bytes=32 * 2**20),
        name="down",
    )(sweeps, target, grad_x, grad_y, labels)


def joined(place, own, other, height):
    gap = jnp.zeros((height - own.shape[0], own.shape[1]), jnp.float32)
    top, bottom = (lambda v: jnp.concatenate([v, gap], 0)), (lambda v: jnp.concatenate([gap, v], 0))
    return jnp.where(place == 0, top(own) + bottom(other), bottom(own) + top(other))


def up_kernel(parts, sweeps_hbm, value_ref, right_ref, coarse_ref, *refs):
    if parts == 2:
        packed_ref, *edge_refs = refs[:5]
        refs = refs[5:]
    out_ref, sweeps, b0_ref, b1_ref, b2_ref, pair_ref, fix1_ref, fix0_ref, sem = refs
    sweeps_copy = pltpu.make_async_copy(sweeps_hbm, sweeps, sem)
    sweeps_copy.start()
    chans, rows, cols = out_ref.shape
    window, wide = value_ref.shape[1:]
    half = b1_ref.shape[2]
    place = lax.axis_index("lat")
    inside = band_mask(window, parts, place, rows)
    north = place == 0

    def widened(value, upper, lower):
        def at(first):
            last = window - first - value.shape[0]
            pads = [jnp.zeros((n, wide), jnp.float32) for n in (first, last)]
            return jnp.concatenate([pads[0], value, pads[1]], 0)

        return jnp.where(north, at(upper), at(lower))

    second = lax.axis_index("lon") % 2 == 1

    def sides(odd_ref, even_ref, chan, *heights):
        odd, even = odd_ref[chan], even_ref[chan]
        west = one_to_three(jnp.where(second, even, odd), *heights)
        east = one_to_three(jnp.where(second, odd, even), *heights)
        return list(zip(west, east))

    def own_part(chan, which):
        field = (value_ref, right_ref, coarse_ref)[which][chan]
        if parts != 2:
            return field
        return with_edges(field, *sides(*edge_refs[:2], chan, window, window, window // 2)[which])

    def other_part(chan, which):
        field = unpack(lambda k: packed_ref[chan, k], wide // LANES, half // LANES)[which]
        return with_edges(field, *sides(*edge_refs[2:], chan, 8, 4, 12)[which])

    for chan in range(chans):
        if parts == 2:
            b1_ref[chan] = joined(place, own_part(chan, 2), other_part(chan, 2), b1_ref.shape[1])
        else:
            b1_ref[chan] = coarse_ref[chan]

    def smoothed(values, right_ref, count, scale, inside=None):
        def step(_, values):
            return tuple(sweep(v, right_ref[i], scale, inside) for i, v in enumerate(values))

        return lax.fori_loop(0, count, step, tuple(values))

    def from_zero(right_ref, count, scale):
        first = [(DAMPING / diagonal(scale)) * right_ref[i] for i in range(chans)]
        return smoothed(first, right_ref, count - 1, scale)

    sweeps_copy.wait()
    mid = from_zero(b1_ref, sweeps[1], 0.25)
    low = restrict([residual(mid[i], b1_ref[i], 0.25) for i in range(chans)], pair_ref)
    for i in range(chans):
        b2_ref[i] = low[i]
    fix2 = from_zero(b2_ref, sweeps[2], 0.0625)
    prolong(fix2, fix1_ref, 0)
    mid = smoothed([mid[i] + wide_rows(fix1_ref, i, 0, mid[i].shape[0]) for i in range(chans)], b1_ref, sweeps[1], 0.25)
    spare = 8 if parts > 2 else 0
    if spare:
        fix0_ref[...] = jnp.zeros_like(fix0_ref)
    prolong(mid, fix0_ref, spare)
    start = own_start(parts, place)
    shown = 0 if parts == 1 else pl.multiple_of((8 if parts == 2 else rows) * place, 8)
    for i in range(chans):
        value = own_part(i, 0) + wide_rows(fix0_ref, i, shown, window)
        right = own_part(i, 1)
        if parts == 2:
            value = value + widened(other_part(i, 0), 12, 4)
            right = right + widened(other_part(i, 1), 16, 5)
        b0_ref[i] = right
        value = lax.fori_loop(0, sweeps[0], lambda _, v, i=i: sweep(v, b0_ref[i], 1.0, inside), value)
        if parts == 2:
            out_ref[i] = jnp.where(place == 0, value[:rows, :cols], value[8:8 + rows, :cols])
        else:
            out_ref[i] = value[start:start + rows, :cols]


def up(parts, shape, sweeps, value, right, coarse, *packed):
    chans, rows, cols = shape
    window, wide = value.shape[1:]
    full = parts * rows
    f32 = functools.partial(pltpu.VMEM, dtype=jnp.float32)
    spare = 16 if parts > 2 else 0
    return pl.pallas_call(
        functools.partial(up_kernel, parts),
        in_specs=[HBM] + [VMEM] * (3 + len(packed)),
        out_specs=VMEM,
        out_shape=jax.ShapeDtypeStruct(shape, jnp.float32),
        scratch_shapes=[
            pltpu.SMEM(sweeps.shape, jnp.int32),
            f32(value.shape),
            f32((chans, full // 2, cols // 2 + LANES)),
            f32((chans, full // 4, cols // 4 + LANES)),
            f32((chans, cols // 4 // LANES + 1, full // 2, LANES)),
            f32((chans, cols // 2 // LANES + 1, full // 2, LANES)),
            f32((chans, wide // LANES, full + spare, LANES)),
            pltpu.SemaphoreType.DMA,
        ],
        compiler_params=pltpu.CompilerParams(vmem_limit_bytes=48 * 2**20),
        name="up",
    )(sweeps, value, right, coarse, *packed)


def local(target, grad_x, grad_y, labels, sweeps):
    parts, around_globe = lax.axis_size("lat"), lax.axis_size("lon")
    value, right, coarse, *sent = down(parts, sweeps, target, grad_x, grad_y, labels)
    if parts == 2:
        odd = [(i, (i + 1 if i % 2 else i - 1) % around_globe) for i in range(around_globe)]
        even = [(i, i - 1 if i % 2 else i + 1) for i in range(around_globe)]

        def across(pairs):
            return [(2 * i + k, 2 * j + 1 - k) for i, j in pairs for k in range(2)]

        packed, odd_edge, even_edge, odd_across, even_across = sent
        packed = lax.ppermute(packed, "lat", [(0, 1), (1, 0)])
        odd_edge = lax.ppermute(odd_edge, "lon", odd)
        odd_across = lax.ppermute(odd_across, ("lon", "lat"), across(odd))
        even_edge = lax.ppermute(even_edge, "lon", even)
        even_across = lax.ppermute(even_across, ("lon", "lat"), across(even))
        received = (packed, odd_edge, even_edge, odd_across, even_across)
        return up(parts, target.shape, sweeps, value, right, coarse, *received)

    def shared_lon(field):
        from_west = lax.ppermute(eastward(field), "lon", [(i, (i + 1) % around_globe) for i in range(around_globe)])
        from_east = lax.ppermute(westward(field), "lon", [((i + 1) % around_globe, i) for i in range(around_globe)])
        return with_edges(field, from_west, from_east)

    value, right, coarse = (shared_lon(f) for f in (value, right, coarse))
    if parts > 2:
        rows = target.shape[1]
        southward = [(i, i + 1) for i in range(parts - 1)]
        northward = [(i + 1, i) for i in range(parts - 1)]

        def shared_lat(field):
            north = lax.ppermute(field[:, rows:], "lat", southward)
            south = lax.ppermute(field[:, :16], "lat", northward)
            zeros = jnp.zeros_like(field[:, :16])
            return field + jnp.concatenate([north, zeros], 1) + jnp.concatenate([zeros, south], 1)

        value, right = shared_lat(value), shared_lat(right)
        every = lax.all_gather(coarse, "lat")
        step = rows // 2
        total = jnp.zeros((coarse.shape[0], parts * step + 8, coarse.shape[2]), jnp.float32)
        for i in range(parts):
            total = total.at[:, i * step:i * step + step + 8].add(every[i])
        coarse = total[:, 4:-4]
    return up(parts, target.shape, sweeps, value, right, coarse)


def solution(mesh):
    in_specs = (
        P(None, "lat", "lon"),
        P(None, None, "lat", "lon"),
        P(None, None, "lat", "lon"),
        P("lat", "lon"),
        P(),
    )
    out_specs = P(None, "lat", "lon")
    return jax.shard_map(local, mesh=mesh, in_specs=in_specs, out_specs=out_specs, check_vma=False)
```

```python
import functools

import jax
import jax.numpy as jnp
from jax import lax
from jax.experimental import pallas as pl
from jax.experimental.pallas import tpu as pltpu
from jax.sharding import PartitionSpec as P

SCREENING = 0.02
DAMPING = 0.8
LANES = 128
HALF = LANES // 2
VMEM = pl.BlockSpec(memory_space=pltpu.VMEM)
HBM = pl.BlockSpec(memory_space=pltpu.HBM)


def in_hbm(array):
    return pltpu.with_memory_space_constraint(array, pltpu.HBM)


def diagonal(scale):
    return SCREENING + 4.0 * scale


def rows_of(value):
    return lax.broadcasted_iota(jnp.int32, value.shape, 0)


def north_of(value):
    return jnp.where(rows_of(value) == 0, 0.0, pltpu.roll(value, 1, 0))


def south_of(value):
    last = value.shape[0] - 1
    return jnp.where(rows_of(value) == last, 0.0, pltpu.roll(value, last, 0))


def west_of(value):
    return pltpu.roll(value, 1, 1)


def east_of(value):
    return pltpu.roll(value, value.shape[1] - 1, 1)


def around(value):
    return (north_of(value) + south_of(value)) + (west_of(value) + east_of(value))


def sweep(value, right, scale, inside):
    diag = diagonal(scale)
    value = (1.0 - DAMPING) * value + (DAMPING / diag) * right + (DAMPING * scale / diag) * around(value)
    return value if inside is None else value * inside


def residual(value, right, scale):
    return right - diagonal(scale) * value + scale * around(value)


def two_parts(value):
    high = value.astype(jnp.bfloat16)
    return high, (value - high.astype(jnp.float32)).astype(jnp.bfloat16)


def moved(value, places):
    high, low = two_parts(value)
    dot = functools.partial(jnp.dot, preferred_element_type=jnp.float32)
    return dot(high, places) + dot(low, places)


def places_of(shape, wanted):
    source = lax.broadcasted_iota(jnp.int32, shape, 0)
    target = lax.broadcasted_iota(jnp.int32, shape, 1)
    return wanted(source, target).astype(jnp.float32).astype(jnp.bfloat16)


def halo_coarse(fine):
    return jnp.where(fine < HALF, fine // 2, HALF + fine // 2)


def pair_columns(fields):
    own = places_of((2 * LANES, LANES), lambda source, target: source // 2 == target)
    halo = places_of((LANES, LANES), lambda source, target: halo_coarse(source) == target)
    rows, cols = fields[0].shape
    blocks = (cols - LANES) // (2 * LANES)
    cut = [f[:, k * 2 * LANES:(k + 1) * 2 * LANES] for f in fields for k in range(blocks)]
    packed = moved(jnp.concatenate(cut, 0), own)
    edges = moved(jnp.concatenate([f[:, cols - LANES:] for f in fields], 0), halo)
    out = []
    for i in range(len(fields)):
        parts = [packed[(i * blocks + k) * rows:(i * blocks + k + 1) * rows] for k in range(blocks)]
        out.append(jnp.concatenate(parts + [edges[i * rows:(i + 1) * rows]], 1))
    return out


def spread_columns(fields):
    own = places_of((2 * LANES, 2 * LANES), lambda source, target: source == target // 2 + LANES * (target % 2))
    halo = places_of((2 * LANES, LANES), lambda source, target: source == halo_coarse(target) + LANES * (target % 2))
    rows, cols = fields[0].shape
    blocks = (cols - LANES) // LANES
    west = [0.75 * f + 0.25 * west_of(f) for f in fields]
    east = [0.75 * f + 0.25 * east_of(f) for f in fields]

    def cut(k):
        span = slice(k * LANES, (k + 1) * LANES)
        return [jnp.concatenate([w[:, span], e[:, span]], 1) for w, e in zip(west, east)]

    own_cut = [cut(k) for k in range(blocks)]
    packed = moved(jnp.concatenate([own_cut[k][i] for i in range(len(fields)) for k in range(blocks)], 0), own)
    edges = moved(jnp.concatenate(cut(blocks), 0), halo)
    out = []
    for i in range(len(fields)):
        parts = [packed[(i * blocks + k) * rows:(i * blocks + k + 1) * rows] for k in range(blocks)]
        out.append(jnp.concatenate(parts + [edges[i * rows:(i + 1) * rows]], 1))
    return out


def restrict(fields, paired_ref):
    rows = fields[0].shape[0]
    out = []
    for i, paired in enumerate(pair_columns(fields)):
        halves = []
        for k, tile in enumerate(tiles(paired)):
            paired_ref[i, k] = tile
            north = paired_ref[i, k, pl.ds(0, rows // 2, stride=2), :]
            south = paired_ref[i, k, pl.ds(1, rows // 2, stride=2), :]
            halves.append(0.25 * (north + south))
        out.append(jnp.concatenate(halves, 1))
    return out


def prolong(fields, fine_ref, first):
    rows = fields[0].shape[0]
    norths = [0.75 * f + 0.25 * north_of(f) for f in fields]
    souths = [0.75 * f + 0.25 * south_of(f) for f in fields]
    spread = spread_columns(norths + souths)
    for i in range(len(fields)):
        for k, (north, south) in enumerate(zip(tiles(spread[i]), tiles(spread[len(fields) + i]))):
            fine_ref[i, k, pl.ds(first, rows, stride=2), :] = north
            fine_ref[i, k, pl.ds(first + 1, rows, stride=2), :] = south


def wide_rows(fine_ref, chan, start, rows):
    return jnp.concatenate([fine_ref[chan, k, pl.ds(start, rows), :] for k in range(fine_ref.shape[1])], 1)


def window_of(rows, parts):
    spare = 8
    return rows + (2 * spare if parts > 2 else spare if parts == 2 else 0)


def own_start(parts, place):
    return 0 if parts == 1 else 8 * place if parts == 2 else 8


def band_mask(window, parts, place, rows):
    if parts <= 2:
        return None
    row = lax.broadcasted_iota(jnp.int32, (window, 1), 0) + place * rows - 8
    return ((row >= 0) & (row < parts * rows)).astype(jnp.float32)


def tiles(value):
    return [value[:, k * LANES:(k + 1) * LANES] for k in range(value.shape[1] // LANES)]


def lanes_of(tile):
    return lax.broadcasted_iota(jnp.int32, tile.shape, len(tile.shape) - 1)


def pack(value8, right4, coarse12):
    out = tiles(value8)
    halves = tiles(right4) + tiles(coarse12[8:])
    if len(halves) % 2:
        halves.append(halves[-1])
    out += tiles(coarse12[:8])
    out += [jnp.concatenate([halves[k], halves[k + 1]], 0) for k in range(0, len(halves), 2)]
    return out


def packed_tiles(fine_tiles, coarse_tiles):
    return fine_tiles + coarse_tiles + (fine_tiles + coarse_tiles + 1) // 2


def unpack(tile, fine_tiles, coarse_tiles):
    value8 = jnp.concatenate([tile(k) for k in range(fine_tiles)], 1)
    top = jnp.concatenate([tile(fine_tiles + k) for k in range(coarse_tiles)], 1)
    halves = []
    for k in range(fine_tiles + coarse_tiles, packed_tiles(fine_tiles, coarse_tiles)):
        both = tile(k)
        halves += [both[:4], both[4:]]
    right4 = jnp.concatenate(halves[:fine_tiles], 1)
    bottom = jnp.concatenate(halves[fine_tiles:fine_tiles + coarse_tiles], 1)
    return value8, right4, jnp.concatenate([top, bottom], 0)


def eastward(value):
    own = value[..., -2 * LANES:-LANES]
    return jnp.where(lanes_of(own) < HALF, value[..., -LANES:], own)


def westward(value):
    own = value[..., :LANES]
    return jnp.where(lanes_of(own) < HALF, own, value[..., -LANES:])


def with_edges(value, from_west, from_east):
    inner = lanes_of(from_west) < HALF
    first = value[..., :LANES] + jnp.where(inner, from_west, 0.0)
    last = value[..., -2 * LANES:-LANES] + jnp.where(inner, 0.0, from_east)
    halo = value[..., -LANES:] + jnp.where(inner, from_east, from_west)
    return jnp.concatenate([first, value[..., LANES:-2 * LANES], last, halo], value.ndim - 1)


VALUE_AT, RIGHT_AT = 48, 80


def taller(value, rows):
    missing = rows - value.shape[0]
    return jnp.concatenate([value, jnp.zeros((missing, value.shape[1]), value.dtype)], 0) if missing else value


def three_in_one(value, right, coarse, rows):
    value, right, coarse = (taller(v, rows) for v in (value, right, coarse))
    lane = lanes_of(value)
    at = lambda first: (lane >= first) & (lane < first + 16)
    out = jnp.where(at(VALUE_AT), pltpu.roll(value, VALUE_AT + 8, 1), coarse)
    return jnp.where(at(RIGHT_AT), pltpu.roll(right, RIGHT_AT + 8, 1), out)


def one_to_three(tile, value_rows, right_rows, coarse_rows):
    lane = lanes_of(tile)
    ends = lambda width: (lane < width) | (lane >= LANES - width)
    value = jnp.where(ends(8), pltpu.roll(tile, LANES - VALUE_AT - 8, 1), 0.0)
    right = jnp.where(ends(8), pltpu.roll(tile, LANES - RIGHT_AT - 8, 1), 0.0)
    coarse = jnp.where(ends(32), tile, 0.0)
    return value[:value_rows], right[:right_rows], coarse[:coarse_rows]


def down_kernel(parts, sweeps_hbm, target, grad_x, grad_y, labels, *refs):
    outs, scratch = refs[:8 if parts == 2 else 3], refs[8 if parts == 2 else 3:]
    value_ref, right_ref, coarse_ref = outs[:3]
    sweeps, target_v, grad_x_v, grad_y_v, labels_v, v_ref, b_ref, paired_ref, sems = scratch
    chans, rows, cols = target.shape
    window = value_ref.shape[1]
    place = lax.axis_index("lat")
    second = lax.axis_index("lon") % 2 == 1
    start = own_start(parts, place)
    if parts == 2:
        start = pl.multiple_of(start, 8)
    inside = band_mask(window, parts, place, rows)
    scale = 1.0

    first_copies = [
        pltpu.make_async_copy(labels, labels_v, sems.at[chans, 0]),
        pltpu.make_async_copy(sweeps_hbm, sweeps, sems.at[chans, 1]),
    ]
    for copy in first_copies:
        copy.start()
    copies = []
    for chan in range(chans):
        copies.append([
            pltpu.make_async_copy(target.at[chan], target_v.at[chan], sems.at[chan, 0]),
            pltpu.make_async_copy(grad_x.at[:, chan], grad_x_v.at[:, chan], sems.at[chan, 1]),
            pltpu.make_async_copy(grad_y.at[:, chan], grad_y_v.at[:, chan], sems.at[chan, 2]),
        ])
        for copy in copies[-1]:
            copy.start()
    if window > rows:
        v_ref[...] = jnp.zeros_like(v_ref)
        b_ref[...] = jnp.zeros_like(b_ref)
    for copy in first_copies:
        copy.wait()
    count = sweeps[0]

    def chosen(grad, chan):
        marks = labels_v[...]
        out = jnp.zeros((rows, cols), jnp.float32)
        for source in range(grad.shape[0]):
            out = jnp.where(marks == source, grad[source, chan], out)
        return out

    blank = jnp.zeros((rows, LANES), jnp.float32)
    resid = []
    for chan in range(chans):
        for copy in copies[chan]:
            copy.wait()
        own = jnp.concatenate([target_v[chan], blank], 1)
        sel_x = jnp.concatenate([chosen(grad_x_v, chan), blank], 1)
        sel_y = jnp.concatenate([chosen(grad_y_v, chan), blank], 1)
        right = SCREENING * own - ((sel_x - west_of(sel_x)) + (sel_y - north_of(sel_y)))
        v_ref[chan, pl.ds(start, rows), :] = own
        b_ref[chan, pl.ds(start, rows), :] = right
        if window > rows:
            below = pltpu.roll(sel_y[rows - 8:], 1, 0)
            b_ref[chan, pl.ds(start + rows, 8), :] = jnp.where(rows_of(below) == 0, below, 0.0)
        right = b_ref[chan, :window, :]
        if inside is not None:
            right = right * inside
        right_ref[chan] = right
        value = lax.fori_loop(
            0, count, lambda _, v, chan=chan: sweep(v, right_ref[chan], scale, inside), v_ref[chan, :window, :]
        )
        value_ref[chan] = value
        left = residual(value, right, scale)
        resid.append(left if inside is None else left * inside)
    coarse = restrict(resid, paired_ref)
    for chan in range(chans):
        coarse_ref[chan] = coarse[chan]
        if parts == 2:
            packed_ref, odd_ref, even_ref, odd_across, even_across = outs[3:]
            north = place == 0
            value, right = value_ref[chan], right_ref[chan]
            value8 = jnp.where(north, value[12:20], value[4:12])
            right4 = jnp.where(north, right[13:17], right[8:12])
            for k, tile in enumerate(pack(value8, right4, coarse[chan])):
                packed_ref[chan, k] = tile
            for height, odd, even, fields in (
                (window, odd_ref, even_ref, (value, right, coarse[chan])),
                (16, odd_across, even_across, (value8, right4, coarse[chan])),
            ):
                east = three_in_one(*[eastward(f) for f in fields], height)
                west = three_in_one(*[westward(f) for f in fields], height)
                odd[chan] = jnp.where(second, east, west)
                even[chan] = jnp.where(second, west, east)


def down(parts, sweeps, target, grad_x, grad_y, labels):
    chans, rows, cols = target.shape
    window = window_of(rows, parts)
    wide, half = cols + LANES, cols // 2 + LANES
    f32 = functools.partial(jax.ShapeDtypeStruct, dtype=jnp.float32)
    outs = [f32((chans, window, wide)), f32((chans, window, wide)), f32((chans, window // 2, half))]
    if parts == 2:
        outs.append(f32((chans, packed_tiles(wide // LANES, half // LANES), 8, LANES)))
        outs += [f32((chans, window, LANES))] * 2 + [f32((chans, 16, LANES))] * 2
    spare = 8 if window > rows else 0
    return pl.pallas_call(
        functools.partial(down_kernel, parts),
        in_specs=[HBM] * 5,
        out_specs=[VMEM] * len(outs),
        out_shape=outs,
        scratch_shapes=[
            pltpu.SMEM(sweeps.shape, jnp.int32),
            pltpu.VMEM(target.shape, jnp.float32),
            pltpu.VMEM(grad_x.shape, jnp.float32),
            pltpu.VMEM(grad_y.shape, jnp.float32),
            pltpu.VMEM(labels.shape, jnp.int32),
            pltpu.VMEM((chans, window + spare, wide), jnp.float32),
            pltpu.VMEM((chans, window + spare, wide), jnp.float32),
            pltpu.VMEM((chans, half // LANES, window, LANES), jnp.float32),
            pltpu.SemaphoreType.DMA((chans + 1, 3)),
        ],
        compiler_params=pltpu.CompilerParams(vmem_limit_bytes=32 * 2**20),
        name="down",
    )(*(in_hbm(a) for a in (sweeps, target, grad_x, grad_y, labels)))


def joined(place, own, other, height):
    gap = jnp.zeros((height - own.shape[0], own.shape[1]), jnp.float32)
    top, bottom = (lambda v: jnp.concatenate([v, gap], 0)), (lambda v: jnp.concatenate([gap, v], 0))
    return jnp.where(place == 0, top(own) + bottom(other), bottom(own) + top(other))


def up_kernel(parts, sweeps_hbm, value_ref, right_ref, coarse_ref, *refs):
    if parts == 2:
        packed_ref, *edge_refs = refs[:5]
        refs = refs[5:]
    out_ref, sweeps, b0_ref, b1_ref, b2_ref, pair_ref, fix1_ref, fix0_ref, sem = refs
    sweeps_copy = pltpu.make_async_copy(sweeps_hbm, sweeps, sem)
    sweeps_copy.start()
    chans, rows, cols = out_ref.shape
    window, wide = value_ref.shape[1:]
    half = b1_ref.shape[2]
    place = lax.axis_index("lat")
    inside = band_mask(window, parts, place, rows)
    north = place == 0

    def widened(value, upper, lower):
        def at(first):
            last = window - first - value.shape[0]
            pads = [jnp.zeros((n, wide), jnp.float32) for n in (first, last)]
            return jnp.concatenate([pads[0], value, pads[1]], 0)

        return jnp.where(north, at(upper), at(lower))

    second = lax.axis_index("lon") % 2 == 1

    def sides(odd_ref, even_ref, chan, *heights):
        odd, even = odd_ref[chan], even_ref[chan]
        west = one_to_three(jnp.where(second, even, odd), *heights)
        east = one_to_three(jnp.where(second, odd, even), *heights)
        return list(zip(west, east))

    def own_part(chan, which):
        field = (value_ref, right_ref, coarse_ref)[which][chan]
        if parts != 2:
            return field
        return with_edges(field, *sides(*edge_refs[:2], chan, window, window, window // 2)[which])

    def other_part(chan, which):
        field = unpack(lambda k: packed_ref[chan, k], wide // LANES, half // LANES)[which]
        return with_edges(field, *sides(*edge_refs[2:], chan, 8, 4, 12)[which])

    for chan in range(chans):
        if parts == 2:
            b1_ref[chan] = joined(place, own_part(chan, 2), other_part(chan, 2), b1_ref.shape[1])
        else:
            b1_ref[chan] = coarse_ref[chan]

    def smoothed(values, right_ref, count, scale, inside=None):
        def step(_, values):
            return tuple(sweep(v, right_ref[i], scale, inside) for i, v in enumerate(values))

        return lax.fori_loop(0, count, step, tuple(values))

    def from_zero(right_ref, count, scale):
        first = [(DAMPING / diagonal(scale)) * right_ref[i] for i in range(chans)]
        return smoothed(first, right_ref, count - 1, scale)

    sweeps_copy.wait()
    mid = from_zero(b1_ref, sweeps[1], 0.25)
    low = restrict([residual(mid[i], b1_ref[i], 0.25) for i in range(chans)], pair_ref)
    for i in range(chans):
        b2_ref[i] = low[i]
    fix2 = from_zero(b2_ref, sweeps[2], 0.0625)
    prolong(fix2, fix1_ref, 0)
    mid = smoothed([mid[i] + wide_rows(fix1_ref, i, 0, mid[i].shape[0]) for i in range(chans)], b1_ref, sweeps[1], 0.25)
    spare = 8 if parts > 2 else 0
    if spare:
        fix0_ref[...] = jnp.zeros_like(fix0_ref)
    prolong(mid, fix0_ref, spare)
    start = own_start(parts, place)
    shown = 0 if parts == 1 else pl.multiple_of((8 if parts == 2 else rows) * place, 8)
    for i in range(chans):
        value = own_part(i, 0) + wide_rows(fix0_ref, i, shown, window)
        right = own_part(i, 1)
        if parts == 2:
            value = value + widened(other_part(i, 0), 12, 4)
            right = right + widened(other_part(i, 1), 16, 5)
        b0_ref[i] = right
        value = lax.fori_loop(0, sweeps[0], lambda _, v, i=i: sweep(v, b0_ref[i], 1.0, inside), value)
        if parts == 2:
            out_ref[i] = jnp.where(place == 0, value[:rows, :cols], value[8:8 + rows, :cols])
        else:
            out_ref[i] = value[start:start + rows, :cols]


def up(parts, shape, sweeps, value, right, coarse, *packed):
    chans, rows, cols = shape
    window, wide = value.shape[1:]
    full = parts * rows
    f32 = functools.partial(pltpu.VMEM, dtype=jnp.float32)
    spare = 16 if parts > 2 else 0
    return pl.pallas_call(
        functools.partial(up_kernel, parts),
        in_specs=[HBM] + [VMEM] * (3 + len(packed)),
        out_specs=VMEM,
        out_shape=jax.ShapeDtypeStruct(shape, jnp.float32),
        scratch_shapes=[
            pltpu.SMEM(sweeps.shape, jnp.int32),
            f32(value.shape),
            f32((chans, full // 2, cols // 2 + LANES)),
            f32((chans, full // 4, cols // 4 + LANES)),
            f32((chans, cols // 4 // LANES + 1, full // 2, LANES)),
            f32((chans, cols // 2 // LANES + 1, full // 2, LANES)),
            f32((chans, wide // LANES, full + spare, LANES)),
            pltpu.SemaphoreType.DMA,
        ],
        compiler_params=pltpu.CompilerParams(vmem_limit_bytes=48 * 2**20),
        name="up",
    )(in_hbm(sweeps), value, right, coarse, *packed)


def local(target, grad_x, grad_y, labels, sweeps):
    parts, around_globe = lax.axis_size("lat"), lax.axis_size("lon")
    value, right, coarse, *sent = down(parts, sweeps, target, grad_x, grad_y, labels)
    if parts == 2:
        odd = [(i, (i + 1 if i % 2 else i - 1) % around_globe) for i in range(around_globe)]
        even = [(i, i - 1 if i % 2 else i + 1) for i in range(around_globe)]

        def across(pairs):
            return [(2 * i + k, 2 * j + 1 - k) for i, j in pairs for k in range(2)]

        packed, odd_edge, even_edge, odd_across, even_across = sent
        packed = lax.ppermute(packed, "lat", [(0, 1), (1, 0)])
        odd_edge = lax.ppermute(odd_edge, "lon", odd)
        odd_across = lax.ppermute(odd_across, ("lon", "lat"), across(odd))
        even_edge = lax.ppermute(even_edge, "lon", even)
        even_across = lax.ppermute(even_across, ("lon", "lat"), across(even))
        received = (packed, odd_edge, even_edge, odd_across, even_across)
        return up(parts, target.shape, sweeps, value, right, coarse, *received)

    def shared_lon(field):
        from_west = lax.ppermute(eastward(field), "lon", [(i, (i + 1) % around_globe) for i in range(around_globe)])
        from_east = lax.ppermute(westward(field), "lon", [((i + 1) % around_globe, i) for i in range(around_globe)])
        return with_edges(field, from_west, from_east)

    value, right, coarse = (shared_lon(f) for f in (value, right, coarse))
    if parts > 2:
        rows = target.shape[1]
        southward = [(i, i + 1) for i in range(parts - 1)]
        northward = [(i + 1, i) for i in range(parts - 1)]

        def shared_lat(field):
            north = lax.ppermute(field[:, rows:], "lat", southward)
            south = lax.ppermute(field[:, :16], "lat", northward)
            zeros = jnp.zeros_like(field[:, :16])
            return field + jnp.concatenate([north, zeros], 1) + jnp.concatenate([zeros, south], 1)

        value, right = shared_lat(value), shared_lat(right)
        every = lax.all_gather(coarse, "lat")
        step = rows // 2
        total = jnp.zeros((coarse.shape[0], parts * step + 8, coarse.shape[2]), jnp.float32)
        for i in range(parts):
            total = total.at[:, i * step:i * step + step + 8].add(every[i])
        coarse = total[:, 4:-4]
    return up(parts, target.shape, sweeps, value, right, coarse)


def solution(mesh):
    in_specs = (
        P(None, "lat", "lon"),
        P(None, None, "lat", "lon"),
        P(None, None, "lat", "lon"),
        P("lat", "lon"),
        P(),
    )
    out_specs = P(None, "lat", "lon")
    return jax.shard_map(local, mesh=mesh, in_specs=in_specs, out_specs=out_specs, check_vma=False)
```

```python
import functools

import jax
import jax.numpy as jnp
from jax import lax
from jax.experimental import pallas as pl
from jax.experimental.pallas import tpu as pltpu
from jax.sharding import PartitionSpec as P

SCREENING = 0.02
DAMPING = 0.8
LANES = 128
HALF = LANES // 2
VMEM = pl.BlockSpec(memory_space=pltpu.VMEM)
HBM = pl.BlockSpec(memory_space=pltpu.HBM)


def in_hbm(array):
    return pltpu.with_memory_space_constraint(array, pltpu.HBM)


def diagonal(scale):
    return SCREENING + 4.0 * scale


def rows_of(value):
    return lax.broadcasted_iota(jnp.int32, value.shape, 0)


def north_of(value):
    return jnp.where(rows_of(value) == 0, 0.0, pltpu.roll(value, 1, 0))


def south_of(value):
    last = value.shape[0] - 1
    return jnp.where(rows_of(value) == last, 0.0, pltpu.roll(value, last, 0))


def west_of(value):
    return pltpu.roll(value, 1, 1)


def east_of(value):
    return pltpu.roll(value, value.shape[1] - 1, 1)


def around(value):
    return (north_of(value) + south_of(value)) + (west_of(value) + east_of(value))


def sweep(value, right, scale, inside):
    diag = diagonal(scale)
    value = (1.0 - DAMPING) * value + (DAMPING / diag) * right + (DAMPING * scale / diag) * around(value)
    return value if inside is None else value * inside


def residual(value, right, scale):
    return right - diagonal(scale) * value + scale * around(value)


def two_parts(value):
    high = value.astype(jnp.bfloat16)
    return high, (value - high.astype(jnp.float32)).astype(jnp.bfloat16)


def moved(value, places):
    high, low = two_parts(value)
    dot = functools.partial(jnp.dot, preferred_element_type=jnp.float32)
    return dot(high, places) + dot(low, places)


def places_of(shape, wanted):
    source = lax.broadcasted_iota(jnp.int32, shape, 0)
    target = lax.broadcasted_iota(jnp.int32, shape, 1)
    return wanted(source, target).astype(jnp.float32).astype(jnp.bfloat16)


def halo_coarse(fine):
    return jnp.where(fine < HALF, fine // 2, HALF + fine // 2)


def pair_columns(fields):
    own = places_of((2 * LANES, LANES), lambda source, target: source // 2 == target)
    halo = places_of((LANES, LANES), lambda source, target: halo_coarse(source) == target)
    rows, cols = fields[0].shape
    blocks = (cols - LANES) // (2 * LANES)
    cut = [f[:, k * 2 * LANES:(k + 1) * 2 * LANES] for f in fields for k in range(blocks)]
    packed = moved(jnp.concatenate(cut, 0), own)
    edges = moved(jnp.concatenate([f[:, cols - LANES:] for f in fields], 0), halo)
    out = []
    for i in range(len(fields)):
        parts = [packed[(i * blocks + k) * rows:(i * blocks + k + 1) * rows] for k in range(blocks)]
        out.append(jnp.concatenate(parts + [edges[i * rows:(i + 1) * rows]], 1))
    return out


def spread_columns(fields):
    own = places_of((2 * LANES, 2 * LANES), lambda source, target: source == target // 2 + LANES * (target % 2))
    halo = places_of((2 * LANES, LANES), lambda source, target: source == halo_coarse(target) + LANES * (target % 2))
    rows, cols = fields[0].shape
    blocks = (cols - LANES) // LANES
    west = [0.75 * f + 0.25 * west_of(f) for f in fields]
    east = [0.75 * f + 0.25 * east_of(f) for f in fields]

    def cut(k):
        span = slice(k * LANES, (k + 1) * LANES)
        return [jnp.concatenate([w[:, span], e[:, span]], 1) for w, e in zip(west, east)]

    own_cut = [cut(k) for k in range(blocks)]
    packed = moved(jnp.concatenate([own_cut[k][i] for i in range(len(fields)) for k in range(blocks)], 0), own)
    edges = moved(jnp.concatenate(cut(blocks), 0), halo)
    out = []
    for i in range(len(fields)):
        parts = [packed[(i * blocks + k) * rows:(i * blocks + k + 1) * rows] for k in range(blocks)]
        out.append(jnp.concatenate(parts + [edges[i * rows:(i + 1) * rows]], 1))
    return out


def restrict(fields, paired_ref):
    rows = fields[0].shape[0]
    out = []
    for i, paired in enumerate(pair_columns(fields)):
        halves = []
        for k, tile in enumerate(tiles(paired)):
            paired_ref[i, k] = tile
            north = paired_ref[i, k, pl.ds(0, rows // 2, stride=2), :]
            south = paired_ref[i, k, pl.ds(1, rows // 2, stride=2), :]
            halves.append(0.25 * (north + south))
        out.append(jnp.concatenate(halves, 1))
    return out


def prolong(fields, fine_ref, first):
    rows = fields[0].shape[0]
    norths = [0.75 * f + 0.25 * north_of(f) for f in fields]
    souths = [0.75 * f + 0.25 * south_of(f) for f in fields]
    spread = spread_columns(norths + souths)
    for i in range(len(fields)):
        for k, (north, south) in enumerate(zip(tiles(spread[i]), tiles(spread[len(fields) + i]))):
            fine_ref[i, k, pl.ds(first, rows, stride=2), :] = north
            fine_ref[i, k, pl.ds(first + 1, rows, stride=2), :] = south


def wide_rows(fine_ref, chan, start, rows):
    return jnp.concatenate([fine_ref[chan, k, pl.ds(start, rows), :] for k in range(fine_ref.shape[1])], 1)


def window_of(rows, parts):
    spare = 8
    return rows + (2 * spare if parts > 2 else spare if parts == 2 else 0)


def own_start(parts, place):
    return 0 if parts == 1 else 8 * place if parts == 2 else 8


def band_mask(window, parts, place, rows):
    if parts <= 2:
        return None
    row = lax.broadcasted_iota(jnp.int32, (window, 1), 0) + place * rows - 8
    return ((row >= 0) & (row < parts * rows)).astype(jnp.float32)


def tiles(value):
    return [value[:, k * LANES:(k + 1) * LANES] for k in range(value.shape[1] // LANES)]


def lanes_of(tile):
    return lax.broadcasted_iota(jnp.int32, tile.shape, len(tile.shape) - 1)


def pack(value8, right4, coarse12):
    out = tiles(value8)
    halves = tiles(right4) + tiles(coarse12[8:])
    if len(halves) % 2:
        halves.append(halves[-1])
    out += tiles(coarse12[:8])
    out += [jnp.concatenate([halves[k], halves[k + 1]], 0) for k in range(0, len(halves), 2)]
    return out


def packed_tiles(fine_tiles, coarse_tiles):
    return fine_tiles + coarse_tiles + (fine_tiles + coarse_tiles + 1) // 2


def unpack(tile, fine_tiles, coarse_tiles):
    value8 = jnp.concatenate([tile(k) for k in range(fine_tiles)], 1)
    top = jnp.concatenate([tile(fine_tiles + k) for k in range(coarse_tiles)], 1)
    halves = []
    for k in range(fine_tiles + coarse_tiles, packed_tiles(fine_tiles, coarse_tiles)):
        both = tile(k)
        halves += [both[:4], both[4:]]
    right4 = jnp.concatenate(halves[:fine_tiles], 1)
    bottom = jnp.concatenate(halves[fine_tiles:fine_tiles + coarse_tiles], 1)
    return value8, right4, jnp.concatenate([top, bottom], 0)


def eastward(value):
    own = value[..., -2 * LANES:-LANES]
    return jnp.where(lanes_of(own) < HALF, value[..., -LANES:], own)


def westward(value):
    own = value[..., :LANES]
    return jnp.where(lanes_of(own) < HALF, own, value[..., -LANES:])


def with_edges(value, from_west, from_east):
    inner = lanes_of(from_west) < HALF
    first = value[..., :LANES] + jnp.where(inner, from_west, 0.0)
    last = value[..., -2 * LANES:-LANES] + jnp.where(inner, 0.0, from_east)
    halo = value[..., -LANES:] + jnp.where(inner, from_east, from_west)
    return jnp.concatenate([first, value[..., LANES:-2 * LANES], last, halo], value.ndim - 1)


VALUE_AT, RIGHT_AT = 48, 80


def taller(value, rows):
    missing = rows - value.shape[0]
    return jnp.concatenate([value, jnp.zeros((missing, value.shape[1]), value.dtype)], 0) if missing else value


def three_in_one(value, right, coarse, rows):
    value, right, coarse = (taller(v, rows) for v in (value, right, coarse))
    lane = lanes_of(value)
    at = lambda first: (lane >= first) & (lane < first + 16)
    out = jnp.where(at(VALUE_AT), pltpu.roll(value, VALUE_AT + 8, 1), coarse)
    return jnp.where(at(RIGHT_AT), pltpu.roll(right, RIGHT_AT + 8, 1), out)


def one_to_three(tile, value_rows, right_rows, coarse_rows):
    lane = lanes_of(tile)
    ends = lambda width: (lane < width) | (lane >= LANES - width)
    value = jnp.where(ends(8), pltpu.roll(tile, LANES - VALUE_AT - 8, 1), 0.0)
    right = jnp.where(ends(8), pltpu.roll(tile, LANES - RIGHT_AT - 8, 1), 0.0)
    coarse = jnp.where(ends(32), tile, 0.0)
    return value[:value_rows], right[:right_rows], coarse[:coarse_rows]


def down_kernel(parts, sweeps_hbm, target, grad_x, grad_y, labels, *refs):
    outs, scratch = refs[:8 if parts == 2 else 3], refs[8 if parts == 2 else 3:]
    value_ref, right_ref, coarse_ref = outs[:3]
    sweeps, target_v, grad_x_v, grad_y_v, labels_v, v_ref, b_ref, paired_ref, sems = scratch
    chans, rows, cols = target.shape
    window = value_ref.shape[1]
    place = lax.axis_index("lat")
    start = own_start(parts, place)
    if parts == 2:
        start = pl.multiple_of(start, 8)
    inside = band_mask(window, parts, place, rows)
    scale = 1.0

    first_copies = [
        pltpu.make_async_copy(labels, labels_v, sems.at[chans, 0]),
        pltpu.make_async_copy(sweeps_hbm, sweeps, sems.at[chans, 1]),
    ]
    for copy in first_copies:
        copy.start()
    copies = []
    for chan in range(chans):
        copies.append([
            pltpu.make_async_copy(target.at[chan], target_v.at[chan], sems.at[chan, 0]),
            pltpu.make_async_copy(grad_x.at[:, chan], grad_x_v.at[:, chan], sems.at[chan, 1]),
            pltpu.make_async_copy(grad_y.at[:, chan], grad_y_v.at[:, chan], sems.at[chan, 2]),
        ])
        for copy in copies[-1]:
            copy.start()
    if window > rows:
        v_ref[...] = jnp.zeros_like(v_ref)
        b_ref[...] = jnp.zeros_like(b_ref)
    for copy in first_copies:
        copy.wait()
    count = sweeps[0]

    def chosen(grad, chan):
        marks = labels_v[...]
        out = jnp.zeros((rows, cols), jnp.float32)
        for source in range(grad.shape[0]):
            out = jnp.where(marks == source, grad[source, chan], out)
        return out

    blank = jnp.zeros((rows, LANES), jnp.float32)
    resid = []
    for chan in range(chans):
        for copy in copies[chan]:
            copy.wait()
        own = jnp.concatenate([target_v[chan], blank], 1)
        sel_x = jnp.concatenate([chosen(grad_x_v, chan), blank], 1)
        sel_y = jnp.concatenate([chosen(grad_y_v, chan), blank], 1)
        right = SCREENING * own - ((sel_x - west_of(sel_x)) + (sel_y - north_of(sel_y)))
        v_ref[chan, pl.ds(start, rows), :] = own
        b_ref[chan, pl.ds(start, rows), :] = right
        if window > rows:
            below = pltpu.roll(sel_y[rows - 8:], 1, 0)
            b_ref[chan, pl.ds(start + rows, 8), :] = jnp.where(rows_of(below) == 0, below, 0.0)
        right = b_ref[chan, :window, :]
        if inside is not None:
            right = right * inside
        right_ref[chan] = right
        value = lax.fori_loop(
            0, count, lambda _, v, chan=chan: sweep(v, right_ref[chan], scale, inside), v_ref[chan, :window, :]
        )
        value_ref[chan] = value
        left = residual(value, right, scale)
        resid.append(left if inside is None else left * inside)
    coarse = restrict(resid, paired_ref)
    for chan in range(chans):
        coarse_ref[chan] = coarse[chan]
        if parts == 2:
            packed_ref, east_ref, west_ref, east_across, west_across = outs[3:]
            north = place == 0
            value, right = value_ref[chan], right_ref[chan]
            value8 = jnp.where(north, value[12:20], value[4:12])
            right4 = jnp.where(north, right[13:17], right[8:12])
            for k, tile in enumerate(pack(value8, right4, coarse[chan])):
                packed_ref[chan, k] = tile
            for height, east, west, fields in (
                (window, east_ref, west_ref, (value, right, coarse[chan])),
                (16, east_across, west_across, (value8, right4, coarse[chan])),
            ):
                east[chan] = three_in_one(*[eastward(f) for f in fields], height)
                west[chan] = three_in_one(*[westward(f) for f in fields], height)


def down(parts, sweeps, target, grad_x, grad_y, labels):
    chans, rows, cols = target.shape
    window = window_of(rows, parts)
    wide, half = cols + LANES, cols // 2 + LANES
    f32 = functools.partial(jax.ShapeDtypeStruct, dtype=jnp.float32)
    outs = [f32((chans, window, wide)), f32((chans, window, wide)), f32((chans, window // 2, half))]
    if parts == 2:
        outs.append(f32((chans, packed_tiles(wide // LANES, half // LANES), 8, LANES)))
        outs += [f32((chans, window, LANES))] * 2 + [f32((chans, 16, LANES))] * 2
    spare = 8 if window > rows else 0
    return pl.pallas_call(
        functools.partial(down_kernel, parts),
        in_specs=[HBM] * 5,
        out_specs=[VMEM] * len(outs),
        out_shape=outs,
        scratch_shapes=[
            pltpu.SMEM(sweeps.shape, jnp.int32),
            pltpu.VMEM(target.shape, jnp.float32),
            pltpu.VMEM(grad_x.shape, jnp.float32),
            pltpu.VMEM(grad_y.shape, jnp.float32),
            pltpu.VMEM(labels.shape, jnp.int32),
            pltpu.VMEM((chans, window + spare, wide), jnp.float32),
            pltpu.VMEM((chans, window + spare, wide), jnp.float32),
            pltpu.VMEM((chans, half // LANES, window, LANES), jnp.float32),
            pltpu.SemaphoreType.DMA((chans + 1, 3)),
        ],
        compiler_params=pltpu.CompilerParams(vmem_limit_bytes=32 * 2**20),
        name="down",
    )(*(in_hbm(a) for a in (sweeps, target, grad_x, grad_y, labels)))


def joined(place, own, other, height):
    gap = jnp.zeros((height - own.shape[0], own.shape[1]), jnp.float32)
    top, bottom = (lambda v: jnp.concatenate([v, gap], 0)), (lambda v: jnp.concatenate([gap, v], 0))
    return jnp.where(place == 0, top(own) + bottom(other), bottom(own) + top(other))


def up_kernel(parts, sweeps_hbm, value_ref, right_ref, coarse_ref, *refs):
    if parts == 2:
        packed_ref, *edge_refs = refs[:5]
        refs = refs[5:]
    out_ref, sweeps, b0_ref, b1_ref, b2_ref, pair_ref, fix1_ref, fix0_ref, sem = refs
    sweeps_copy = pltpu.make_async_copy(sweeps_hbm, sweeps, sem)
    sweeps_copy.start()
    chans, rows, cols = out_ref.shape
    window, wide = value_ref.shape[1:]
    half = b1_ref.shape[2]
    place = lax.axis_index("lat")
    inside = band_mask(window, parts, place, rows)
    north = place == 0

    def widened(value, upper, lower):
        def at(first):
            last = window - first - value.shape[0]
            pads = [jnp.zeros((n, wide), jnp.float32) for n in (first, last)]
            return jnp.concatenate([pads[0], value, pads[1]], 0)

        return jnp.where(north, at(upper), at(lower))

    def sides(west_ref, east_ref, chan, *heights):
        return list(zip(one_to_three(west_ref[chan], *heights), one_to_three(east_ref[chan], *heights)))

    def own_part(chan, which):
        field = (value_ref, right_ref, coarse_ref)[which][chan]
        if parts != 2:
            return field
        return with_edges(field, *sides(*edge_refs[:2], chan, window, window, window // 2)[which])

    def other_part(chan, which):
        field = unpack(lambda k: packed_ref[chan, k], wide // LANES, half // LANES)[which]
        return with_edges(field, *sides(*edge_refs[2:], chan, 8, 4, 12)[which])

    for chan in range(chans):
        if parts == 2:
            b1_ref[chan] = joined(place, own_part(chan, 2), other_part(chan, 2), b1_ref.shape[1])
        else:
            b1_ref[chan] = coarse_ref[chan]

    def smoothed(values, right_ref, count, scale, inside=None):
        def step(_, values):
            return tuple(sweep(v, right_ref[i], scale, inside) for i, v in enumerate(values))

        return lax.fori_loop(0, count, step, tuple(values))

    def from_zero(right_ref, count, scale):
        first = [(DAMPING / diagonal(scale)) * right_ref[i] for i in range(chans)]
        return smoothed(first, right_ref, count - 1, scale)

    sweeps_copy.wait()
    mid = from_zero(b1_ref, sweeps[1], 0.25)
    low = restrict([residual(mid[i], b1_ref[i], 0.25) for i in range(chans)], pair_ref)
    for i in range(chans):
        b2_ref[i] = low[i]
    fix2 = from_zero(b2_ref, sweeps[2], 0.0625)
    prolong(fix2, fix1_ref, 0)
    mid = smoothed([mid[i] + wide_rows(fix1_ref, i, 0, mid[i].shape[0]) for i in range(chans)], b1_ref, sweeps[1], 0.25)
    spare = 8 if parts > 2 else 0
    if spare:
        fix0_ref[...] = jnp.zeros_like(fix0_ref)
    prolong(mid, fix0_ref, spare)
    start = own_start(parts, place)
    shown = 0 if parts == 1 else pl.multiple_of((8 if parts == 2 else rows) * place, 8)
    for i in range(chans):
        value = own_part(i, 0) + wide_rows(fix0_ref, i, shown, window)
        right = own_part(i, 1)
        if parts == 2:
            value = value + widened(other_part(i, 0), 12, 4)
            right = right + widened(other_part(i, 1), 16, 5)
        b0_ref[i] = right
        value = lax.fori_loop(0, sweeps[0], lambda _, v, i=i: sweep(v, b0_ref[i], 1.0, inside), value)
        if parts == 2:
            out_ref[i] = jnp.where(place == 0, value[:rows, :cols], value[8:8 + rows, :cols])
        else:
            out_ref[i] = value[start:start + rows, :cols]


def up(parts, shape, sweeps, value, right, coarse, *packed):
    chans, rows, cols = shape
    window, wide = value.shape[1:]
    full = parts * rows
    f32 = functools.partial(pltpu.VMEM, dtype=jnp.float32)
    spare = 16 if parts > 2 else 0
    return pl.pallas_call(
        functools.partial(up_kernel, parts),
        in_specs=[HBM] + [VMEM] * (3 + len(packed)),
        out_specs=VMEM,
        out_shape=jax.ShapeDtypeStruct(shape, jnp.float32),
        scratch_shapes=[
            pltpu.SMEM(sweeps.shape, jnp.int32),
            f32(value.shape),
            f32((chans, full // 2, cols // 2 + LANES)),
            f32((chans, full // 4, cols // 4 + LANES)),
            f32((chans, cols // 4 // LANES + 1, full // 2, LANES)),
            f32((chans, cols // 2 // LANES + 1, full // 2, LANES)),
            f32((chans, wide // LANES, full + spare, LANES)),
            pltpu.SemaphoreType.DMA,
        ],
        compiler_params=pltpu.CompilerParams(vmem_limit_bytes=48 * 2**20),
        name="up",
    )(in_hbm(sweeps), value, right, coarse, *packed)


def local(target, grad_x, grad_y, labels, sweeps):
    parts, around_globe = lax.axis_size("lat"), lax.axis_size("lon")
    value, right, coarse, *sent = down(parts, sweeps, target, grad_x, grad_y, labels)
    if parts == 2:
        eastward_pairs = [(i, (i + 1) % around_globe) for i in range(around_globe)]
        westward_pairs = [(j, i) for i, j in eastward_pairs]

        def across(pairs):
            return [(2 * i + k, 2 * j + 1 - k) for i, j in pairs for k in range(2)]

        packed, east, west, east_across, west_across = sent
        packed = lax.ppermute(packed, "lat", [(0, 1), (1, 0)])
        from_west = lax.ppermute(east, "lon", eastward_pairs)
        across_west = lax.ppermute(east_across, ("lon", "lat"), across(eastward_pairs))
        from_east = lax.ppermute(west, "lon", westward_pairs)
        across_east = lax.ppermute(west_across, ("lon", "lat"), across(westward_pairs))
        received = (packed, from_west, from_east, across_west, across_east)
        return up(parts, target.shape, sweeps, value, right, coarse, *received)

    def shared_lon(field):
        from_west = lax.ppermute(eastward(field), "lon", [(i, (i + 1) % around_globe) for i in range(around_globe)])
        from_east = lax.ppermute(westward(field), "lon", [((i + 1) % around_globe, i) for i in range(around_globe)])
        return with_edges(field, from_west, from_east)

    value, right, coarse = (shared_lon(f) for f in (value, right, coarse))
    if parts > 2:
        rows = target.shape[1]
        southward = [(i, i + 1) for i in range(parts - 1)]
        northward = [(i + 1, i) for i in range(parts - 1)]

        def shared_lat(field):
            north = lax.ppermute(field[:, rows:], "lat", southward)
            south = lax.ppermute(field[:, :16], "lat", northward)
            zeros = jnp.zeros_like(field[:, :16])
            return field + jnp.concatenate([north, zeros], 1) + jnp.concatenate([zeros, south], 1)

        value, right = shared_lat(value), shared_lat(right)
        every = lax.all_gather(coarse, "lat")
        step = rows // 2
        total = jnp.zeros((coarse.shape[0], parts * step + 8, coarse.shape[2]), jnp.float32)
        for i in range(parts):
            total = total.at[:, i * step:i * step + step + 8].add(every[i])
        coarse = total[:, 4:-4]
    return up(parts, target.shape, sweeps, value, right, coarse)


def solution(mesh):
    in_specs = (
        P(None, "lat", "lon"),
        P(None, None, "lat", "lon"),
        P(None, None, "lat", "lon"),
        P("lat", "lon"),
        P(),
    )
    out_specs = P(None, "lat", "lon")
    return jax.shard_map(local, mesh=mesh, in_specs=in_specs, out_specs=out_specs, check_vma=False)
```

```python
import functools

import jax
import jax.numpy as jnp
from jax import lax
from jax.experimental import pallas as pl
from jax.experimental.pallas import tpu as pltpu
from jax.sharding import PartitionSpec as P

SCREENING = 0.02
DAMPING = 0.8
LANES = 128
HALF = LANES // 2
VMEM = pl.BlockSpec(memory_space=pltpu.VMEM)
HBM = pl.BlockSpec(memory_space=pltpu.HBM)


def in_hbm(array):
    return pltpu.with_memory_space_constraint(array, pltpu.HBM)


def diagonal(scale):
    return SCREENING + 4.0 * scale


def rows_of(value):
    return lax.broadcasted_iota(jnp.int32, value.shape, 0)


def north_of(value):
    return jnp.where(rows_of(value) == 0, 0.0, pltpu.roll(value, 1, 0))


def south_of(value):
    last = value.shape[0] - 1
    return jnp.where(rows_of(value) == last, 0.0, pltpu.roll(value, last, 0))


def west_of(value):
    return pltpu.roll(value, 1, 1)


def east_of(value):
    return pltpu.roll(value, value.shape[1] - 1, 1)


def around(value):
    return (north_of(value) + south_of(value)) + (west_of(value) + east_of(value))


def sweep(value, right, scale, inside):
    diag = diagonal(scale)
    value = (1.0 - DAMPING) * value + (DAMPING / diag) * right + (DAMPING * scale / diag) * around(value)
    return value if inside is None else value * inside


def residual(value, right, scale):
    return right - diagonal(scale) * value + scale * around(value)


def two_parts(value):
    high = value.astype(jnp.bfloat16)
    return high, (value - high.astype(jnp.float32)).astype(jnp.bfloat16)


def moved(value, places):
    high, low = two_parts(value)
    dot = functools.partial(jnp.dot, preferred_element_type=jnp.float32)
    return dot(high, places) + dot(low, places)


def places_of(shape, wanted):
    source = lax.broadcasted_iota(jnp.int32, shape, 0)
    target = lax.broadcasted_iota(jnp.int32, shape, 1)
    return wanted(source, target).astype(jnp.float32).astype(jnp.bfloat16)


def halo_coarse(fine):
    return jnp.where(fine < HALF, fine // 2, HALF + fine // 2)


def pair_columns(fields):
    own = places_of((2 * LANES, LANES), lambda source, target: source // 2 == target)
    halo = places_of((LANES, LANES), lambda source, target: halo_coarse(source) == target)
    rows, cols = fields[0].shape
    blocks = (cols - LANES) // (2 * LANES)
    cut = [f[:, k * 2 * LANES:(k + 1) * 2 * LANES] for f in fields for k in range(blocks)]
    packed = moved(jnp.concatenate(cut, 0), own)
    edges = moved(jnp.concatenate([f[:, cols - LANES:] for f in fields], 0), halo)
    out = []
    for i in range(len(fields)):
        parts = [packed[(i * blocks + k) * rows:(i * blocks + k + 1) * rows] for k in range(blocks)]
        out.append(jnp.concatenate(parts + [edges[i * rows:(i + 1) * rows]], 1))
    return out


def spread_columns(fields):
    own = places_of((2 * LANES, 2 * LANES), lambda source, target: source == target // 2 + LANES * (target % 2))
    halo = places_of((2 * LANES, LANES), lambda source, target: source == halo_coarse(target) + LANES * (target % 2))
    rows, cols = fields[0].shape
    blocks = (cols - LANES) // LANES
    west = [0.75 * f + 0.25 * west_of(f) for f in fields]
    east = [0.75 * f + 0.25 * east_of(f) for f in fields]

    def cut(k):
        span = slice(k * LANES, (k + 1) * LANES)
        return [jnp.concatenate([w[:, span], e[:, span]], 1) for w, e in zip(west, east)]

    own_cut = [cut(k) for k in range(blocks)]
    packed = moved(jnp.concatenate([own_cut[k][i] for i in range(len(fields)) for k in range(blocks)], 0), own)
    edges = moved(jnp.concatenate(cut(blocks), 0), halo)
    out = []
    for i in range(len(fields)):
        parts = [packed[(i * blocks + k) * rows:(i * blocks + k + 1) * rows] for k in range(blocks)]
        out.append(jnp.concatenate(parts + [edges[i * rows:(i + 1) * rows]], 1))
    return out


def restrict(fields, paired_ref):
    rows = fields[0].shape[0]
    out = []
    for i, paired in enumerate(pair_columns(fields)):
        halves = []
        for k, tile in enumerate(tiles(paired)):
            paired_ref[i, k] = tile
            north = paired_ref[i, k, pl.ds(0, rows // 2, stride=2), :]
            south = paired_ref[i, k, pl.ds(1, rows // 2, stride=2), :]
            halves.append(0.25 * (north + south))
        out.append(jnp.concatenate(halves, 1))
    return out


def prolong(fields, fine_ref, first):
    rows = fields[0].shape[0]
    norths = [0.75 * f + 0.25 * north_of(f) for f in fields]
    souths = [0.75 * f + 0.25 * south_of(f) for f in fields]
    spread = spread_columns(norths + souths)
    for i in range(len(fields)):
        for k, (north, south) in enumerate(zip(tiles(spread[i]), tiles(spread[len(fields) + i]))):
            fine_ref[i, k, pl.ds(first, rows, stride=2), :] = north
            fine_ref[i, k, pl.ds(first + 1, rows, stride=2), :] = south


def wide_rows(fine_ref, chan, start, rows):
    return jnp.concatenate([fine_ref[chan, k, pl.ds(start, rows), :] for k in range(fine_ref.shape[1])], 1)


def window_of(rows, parts):
    spare = 8
    return rows + (2 * spare if parts > 2 else spare if parts == 2 else 0)


def own_start(parts, place):
    return 0 if parts == 1 else 8 * place if parts == 2 else 8


def band_mask(window, parts, place, rows):
    if parts <= 2:
        return None
    row = lax.broadcasted_iota(jnp.int32, (window, 1), 0) + place * rows - 8
    return ((row >= 0) & (row < parts * rows)).astype(jnp.float32)


def tiles(value):
    return [value[:, k * LANES:(k + 1) * LANES] for k in range(value.shape[1] // LANES)]


def lanes_of(tile):
    return lax.broadcasted_iota(jnp.int32, tile.shape, len(tile.shape) - 1)


def pack(value8, right4, coarse12):
    out = tiles(value8)
    halves = tiles(right4) + tiles(coarse12[8:])
    if len(halves) % 2:
        halves.append(halves[-1])
    out += tiles(coarse12[:8])
    out += [jnp.concatenate([halves[k], halves[k + 1]], 0) for k in range(0, len(halves), 2)]
    return out


def packed_tiles(fine_tiles, coarse_tiles):
    return fine_tiles + coarse_tiles + (fine_tiles + coarse_tiles + 1) // 2


def unpack(tile, fine_tiles, coarse_tiles):
    value8 = jnp.concatenate([tile(k) for k in range(fine_tiles)], 1)
    top = jnp.concatenate([tile(fine_tiles + k) for k in range(coarse_tiles)], 1)
    halves = []
    for k in range(fine_tiles + coarse_tiles, packed_tiles(fine_tiles, coarse_tiles)):
        both = tile(k)
        halves += [both[:4], both[4:]]
    right4 = jnp.concatenate(halves[:fine_tiles], 1)
    bottom = jnp.concatenate(halves[fine_tiles:fine_tiles + coarse_tiles], 1)
    return value8, right4, jnp.concatenate([top, bottom], 0)


def eastward(value):
    own = value[..., -2 * LANES:-LANES]
    return jnp.where(lanes_of(own) < HALF, value[..., -LANES:], own)


def westward(value):
    own = value[..., :LANES]
    return jnp.where(lanes_of(own) < HALF, own, value[..., -LANES:])


def with_edges(value, from_west, from_east):
    inner = lanes_of(from_west) < HALF
    first = value[..., :LANES] + jnp.where(inner, from_west, 0.0)
    last = value[..., -2 * LANES:-LANES] + jnp.where(inner, 0.0, from_east)
    halo = value[..., -LANES:] + jnp.where(inner, from_east, from_west)
    return jnp.concatenate([first, value[..., LANES:-2 * LANES], last, halo], value.ndim - 1)


VALUE_AT, RIGHT_AT = 48, 80


def taller(value, rows):
    missing = rows - value.shape[0]
    return jnp.concatenate([value, jnp.zeros((missing, value.shape[1]), value.dtype)], 0) if missing else value


def three_in_one(value, right, coarse, rows):
    value, right, coarse = (taller(v, rows) for v in (value, right, coarse))
    lane = lanes_of(value)
    at = lambda first: (lane >= first) & (lane < first + 16)
    out = jnp.where(at(VALUE_AT), pltpu.roll(value, VALUE_AT + 8, 1), coarse)
    return jnp.where(at(RIGHT_AT), pltpu.roll(right, RIGHT_AT + 8, 1), out)


def one_to_three(tile, value_rows, right_rows, coarse_rows):
    lane = lanes_of(tile)
    ends = lambda width: (lane < width) | (lane >= LANES - width)
    value = jnp.where(ends(8), pltpu.roll(tile, LANES - VALUE_AT - 8, 1), 0.0)
    right = jnp.where(ends(8), pltpu.roll(tile, LANES - RIGHT_AT - 8, 1), 0.0)
    coarse = jnp.where(ends(32), tile, 0.0)
    return value[:value_rows], right[:right_rows], coarse[:coarse_rows]


def down_kernel(parts, sweeps_hbm, target, grad_x, grad_y, labels, *refs):
    outs, scratch = refs[:8 if parts == 2 else 3], refs[8 if parts == 2 else 3:]
    value_ref, right_ref, coarse_ref = outs[:3]
    sweeps, target_v, grad_x_v, grad_y_v, labels_v, v_ref, b_ref, paired_ref, sems = scratch
    chans, rows, cols = target.shape
    window = value_ref.shape[1]
    place = lax.axis_index("lat")
    start = own_start(parts, place)
    if parts == 2:
        start = pl.multiple_of(start, 8)
    inside = band_mask(window, parts, place, rows)
    scale = 1.0

    first_copies = [
        pltpu.make_async_copy(labels, labels_v, sems.at[chans, 0]),
        pltpu.make_async_copy(sweeps_hbm, sweeps, sems.at[chans, 1]),
    ]
    for copy in first_copies:
        copy.start()
    copies = []
    for chan in range(chans):
        copies.append([
            pltpu.make_async_copy(target.at[chan], target_v.at[chan], sems.at[chan, 0]),
            pltpu.make_async_copy(grad_x.at[:, chan], grad_x_v.at[:, chan], sems.at[chan, 1]),
            pltpu.make_async_copy(grad_y.at[:, chan], grad_y_v.at[:, chan], sems.at[chan, 2]),
        ])
        for copy in copies[-1]:
            copy.start()
    if window > rows:
        v_ref[...] = jnp.zeros_like(v_ref)
        b_ref[...] = jnp.zeros_like(b_ref)
    for copy in first_copies:
        copy.wait()
    count = sweeps[0]

    def chosen(grad, chan):
        marks = labels_v[...]
        out = jnp.zeros((rows, cols), jnp.float32)
        for source in range(grad.shape[0]):
            out = jnp.where(marks == source, grad[source, chan], out)
        return out

    blank = jnp.zeros((rows, LANES), jnp.float32)
    resid = []
    for chan in range(chans):
        for copy in copies[chan]:
            copy.wait()
        own = jnp.concatenate([target_v[chan], blank], 1)
        sel_x = jnp.concatenate([chosen(grad_x_v, chan), blank], 1)
        sel_y = jnp.concatenate([chosen(grad_y_v, chan), blank], 1)
        right = SCREENING * own - ((sel_x - west_of(sel_x)) + (sel_y - north_of(sel_y)))
        v_ref[chan, pl.ds(start, rows), :] = own
        b_ref[chan, pl.ds(start, rows), :] = right
        if window > rows:
            below = pltpu.roll(sel_y[rows - 8:], 1, 0)
            b_ref[chan, pl.ds(start + rows, 8), :] = jnp.where(rows_of(below) == 0, below, 0.0)
        right = b_ref[chan, :window, :]
        if inside is not None:
            right = right * inside
        right_ref[chan] = right
        value = lax.fori_loop(
            0, count, lambda _, v, chan=chan: sweep(v, right_ref[chan], scale, inside), v_ref[chan, :window, :]
        )
        value_ref[chan] = value
        left = residual(value, right, scale)
        resid.append(left if inside is None else left * inside)
    coarse = restrict(resid, paired_ref)
    for chan in range(chans):
        coarse_ref[chan] = coarse[chan]
        if parts == 2:
            packed_ref, east_ref, east_across, west_ref, west_across = outs[3:]
            north = place == 0
            value, right = value_ref[chan], right_ref[chan]
            value8 = jnp.where(north, value[12:20], value[4:12])
            right4 = jnp.where(north, right[13:17], right[8:12])
            for k, tile in enumerate(pack(value8, right4, coarse[chan])):
                packed_ref[chan, k] = tile
            for height, east, west, fields in (
                (window, east_ref, west_ref, (value, right, coarse[chan])),
                (window, east_across, west_across, (value8, right4, coarse[chan])),
            ):
                east[chan] = three_in_one(*[eastward(f) for f in fields], height)
                west[chan] = three_in_one(*[westward(f) for f in fields], height)


def down(parts, sweeps, target, grad_x, grad_y, labels):
    chans, rows, cols = target.shape
    window = window_of(rows, parts)
    wide, half = cols + LANES, cols // 2 + LANES
    f32 = functools.partial(jax.ShapeDtypeStruct, dtype=jnp.float32)
    outs = [f32((chans, window, wide)), f32((chans, window, wide)), f32((chans, window // 2, half))]
    if parts == 2:
        outs.append(f32((chans, packed_tiles(wide // LANES, half // LANES), 8, LANES)))
        outs += [f32((chans, window, LANES))] * 4
    spare = 8 if window > rows else 0
    return pl.pallas_call(
        functools.partial(down_kernel, parts),
        in_specs=[HBM] * 5,
        out_specs=[VMEM] * len(outs),
        out_shape=outs,
        scratch_shapes=[
            pltpu.SMEM(sweeps.shape, jnp.int32),
            pltpu.VMEM(target.shape, jnp.float32),
            pltpu.VMEM(grad_x.shape, jnp.float32),
            pltpu.VMEM(grad_y.shape, jnp.float32),
            pltpu.VMEM(labels.shape, jnp.int32),
            pltpu.VMEM((chans, window + spare, wide), jnp.float32),
            pltpu.VMEM((chans, window + spare, wide), jnp.float32),
            pltpu.VMEM((chans, half // LANES, window, LANES), jnp.float32),
            pltpu.SemaphoreType.DMA((chans + 1, 3)),
        ],
        compiler_params=pltpu.CompilerParams(vmem_limit_bytes=32 * 2**20),
        name="down",
    )(*(in_hbm(a) for a in (sweeps, target, grad_x, grad_y, labels)))


def joined(place, own, other, height):
    gap = jnp.zeros((height - own.shape[0], own.shape[1]), jnp.float32)
    top, bottom = (lambda v: jnp.concatenate([v, gap], 0)), (lambda v: jnp.concatenate([gap, v], 0))
    return jnp.where(place == 0, top(own) + bottom(other), bottom(own) + top(other))


def up_kernel(parts, sweeps_hbm, value_ref, right_ref, coarse_ref, *refs):
    if parts == 2:
        packed_ref, *edge_refs = refs[:5]
        refs = refs[5:]
    out_ref, sweeps, b0_ref, b1_ref, b2_ref, pair_ref, fix1_ref, fix0_ref, sem = refs
    sweeps_copy = pltpu.make_async_copy(sweeps_hbm, sweeps, sem)
    sweeps_copy.start()
    chans, rows, cols = out_ref.shape
    window, wide = value_ref.shape[1:]
    half = b1_ref.shape[2]
    place = lax.axis_index("lat")
    inside = band_mask(window, parts, place, rows)
    north = place == 0

    def widened(value, upper, lower):
        def at(first):
            last = window - first - value.shape[0]
            pads = [jnp.zeros((n, wide), jnp.float32) for n in (first, last)]
            return jnp.concatenate([pads[0], value, pads[1]], 0)

        return jnp.where(north, at(upper), at(lower))

    def sides(west_ref, east_ref, chan, *heights):
        return list(zip(one_to_three(west_ref[chan], *heights), one_to_three(east_ref[chan], *heights)))

    def own_part(chan, which):
        field = (value_ref, right_ref, coarse_ref)[which][chan]
        if parts != 2:
            return field
        return with_edges(field, *sides(edge_refs[0], edge_refs[2], chan, window, window, window // 2)[which])

    def other_part(chan, which):
        field = unpack(lambda k: packed_ref[chan, k], wide // LANES, half // LANES)[which]
        return with_edges(field, *sides(edge_refs[1], edge_refs[3], chan, 8, 4, 12)[which])

    for chan in range(chans):
        if parts == 2:
            b1_ref[chan] = joined(place, own_part(chan, 2), other_part(chan, 2), b1_ref.shape[1])
        else:
            b1_ref[chan] = coarse_ref[chan]

    def smoothed(values, right_ref, count, scale, inside=None):
        def step(_, values):
            return tuple(sweep(v, right_ref[i], scale, inside) for i, v in enumerate(values))

        return lax.fori_loop(0, count, step, tuple(values))

    def from_zero(right_ref, count, scale):
        first = [(DAMPING / diagonal(scale)) * right_ref[i] for i in range(chans)]
        return smoothed(first, right_ref, count - 1, scale)

    sweeps_copy.wait()
    mid = from_zero(b1_ref, sweeps[1], 0.25)
    low = restrict([residual(mid[i], b1_ref[i], 0.25) for i in range(chans)], pair_ref)
    for i in range(chans):
        b2_ref[i] = low[i]
    fix2 = from_zero(b2_ref, sweeps[2], 0.0625)
    prolong(fix2, fix1_ref, 0)
    mid = smoothed([mid[i] + wide_rows(fix1_ref, i, 0, mid[i].shape[0]) for i in range(chans)], b1_ref, sweeps[1], 0.25)
    spare = 8 if parts > 2 else 0
    if spare:
        fix0_ref[...] = jnp.zeros_like(fix0_ref)
    prolong(mid, fix0_ref, spare)
    start = own_start(parts, place)
    shown = 0 if parts == 1 else pl.multiple_of((8 if parts == 2 else rows) * place, 8)
    for i in range(chans):
        value = own_part(i, 0) + wide_rows(fix0_ref, i, shown, window)
        right = own_part(i, 1)
        if parts == 2:
            value = value + widened(other_part(i, 0), 12, 4)
            right = right + widened(other_part(i, 1), 16, 5)
        b0_ref[i] = right
        value = lax.fori_loop(0, sweeps[0], lambda _, v, i=i: sweep(v, b0_ref[i], 1.0, inside), value)
        if parts == 2:
            out_ref[i] = jnp.where(place == 0, value[:rows, :cols], value[8:8 + rows, :cols])
        else:
            out_ref[i] = value[start:start + rows, :cols]


def up(parts, shape, sweeps, value, right, coarse, *packed):
    chans, rows, cols = shape
    window, wide = value.shape[1:]
    full = parts * rows
    f32 = functools.partial(pltpu.VMEM, dtype=jnp.float32)
    spare = 16 if parts > 2 else 0
    return pl.pallas_call(
        functools.partial(up_kernel, parts),
        in_specs=[HBM] + [VMEM] * (3 + len(packed)),
        out_specs=VMEM,
        out_shape=jax.ShapeDtypeStruct(shape, jnp.float32),
        scratch_shapes=[
            pltpu.SMEM(sweeps.shape, jnp.int32),
            f32(value.shape),
            f32((chans, full // 2, cols // 2 + LANES)),
            f32((chans, full // 4, cols // 4 + LANES)),
            f32((chans, cols // 4 // LANES + 1, full // 2, LANES)),
            f32((chans, cols // 2 // LANES + 1, full // 2, LANES)),
            f32((chans, wide // LANES, full + spare, LANES)),
            pltpu.SemaphoreType.DMA,
        ],
        compiler_params=pltpu.CompilerParams(vmem_limit_bytes=48 * 2**20),
        name="up",
    )(in_hbm(sweeps), value, right, coarse, *packed)


def local(target, grad_x, grad_y, labels, sweeps):
    parts, around_globe = lax.axis_size("lat"), lax.axis_size("lon")
    value, right, coarse, *sent = down(parts, sweeps, target, grad_x, grad_y, labels)
    if parts == 2:
        eastward_pairs = [(i, (i + 1) % around_globe) for i in range(around_globe)]
        westward_pairs = [(j, i) for i, j in eastward_pairs]

        def across(pairs):
            return [(2 * i + k, 2 * j + 1 - k) for i, j in pairs for k in range(2)]

        packed, east, east_across, west, west_across = sent
        packed = lax.ppermute(packed, "lat", [(0, 1), (1, 0)])
        from_west = lax.ppermute(east, "lon", eastward_pairs)
        across_west = lax.ppermute(east_across, ("lon", "lat"), across(eastward_pairs))
        from_east = lax.ppermute(west, "lon", westward_pairs)
        across_east = lax.ppermute(west_across, ("lon", "lat"), across(westward_pairs))
        received = (packed, from_west, across_west, from_east, across_east)
        return up(parts, target.shape, sweeps, value, right, coarse, *received)

    def shared_lon(field):
        from_west = lax.ppermute(eastward(field), "lon", [(i, (i + 1) % around_globe) for i in range(around_globe)])
        from_east = lax.ppermute(westward(field), "lon", [((i + 1) % around_globe, i) for i in range(around_globe)])
        return with_edges(field, from_west, from_east)

    value, right, coarse = (shared_lon(f) for f in (value, right, coarse))
    if parts > 2:
        rows = target.shape[1]
        southward = [(i, i + 1) for i in range(parts - 1)]
        northward = [(i + 1, i) for i in range(parts - 1)]

        def shared_lat(field):
            north = lax.ppermute(field[:, rows:], "lat", southward)
            south = lax.ppermute(field[:, :16], "lat", northward)
            zeros = jnp.zeros_like(field[:, :16])
            return field + jnp.concatenate([north, zeros], 1) + jnp.concatenate([zeros, south], 1)

        value, right = shared_lat(value), shared_lat(right)
        every = lax.all_gather(coarse, "lat")
        step = rows // 2
        total = jnp.zeros((coarse.shape[0], parts * step + 8, coarse.shape[2]), jnp.float32)
        for i in range(parts):
            total = total.at[:, i * step:i * step + step + 8].add(every[i])
        coarse = total[:, 4:-4]
    return up(parts, target.shape, sweeps, value, right, coarse)


def solution(mesh):
    in_specs = (
        P(None, "lat", "lon"),
        P(None, None, "lat", "lon"),
        P(None, None, "lat", "lon"),
        P("lat", "lon"),
        P(),
    )
    out_specs = P(None, "lat", "lon")
    return jax.shard_map(local, mesh=mesh, in_specs=in_specs, out_specs=out_specs, check_vma=False)
```

```python
import functools

import jax
import jax.numpy as jnp
from jax import lax
from jax.experimental import pallas as pl
from jax.experimental.pallas import tpu as pltpu
from jax.sharding import PartitionSpec as P

SCREENING = 0.02
DAMPING = 0.8
LANES = 128
HALF = LANES // 2
VMEM = pl.BlockSpec(memory_space=pltpu.VMEM)
HBM = pl.BlockSpec(memory_space=pltpu.HBM)


def in_hbm(array):
    return pltpu.with_memory_space_constraint(array, pltpu.HBM)


def diagonal(scale):
    return SCREENING + 4.0 * scale


def rows_of(value):
    return lax.broadcasted_iota(jnp.int32, value.shape, 0)


def north_of(value):
    return jnp.where(rows_of(value) == 0, 0.0, pltpu.roll(value, 1, 0))


def south_of(value):
    last = value.shape[0] - 1
    return jnp.where(rows_of(value) == last, 0.0, pltpu.roll(value, last, 0))


def west_of(value):
    return pltpu.roll(value, 1, 1)


def east_of(value):
    return pltpu.roll(value, value.shape[1] - 1, 1)


def around(value):
    return (north_of(value) + south_of(value)) + (west_of(value) + east_of(value))


def sweep(value, right, scale, inside):
    diag = diagonal(scale)
    value = (1.0 - DAMPING) * value + (DAMPING / diag) * right + (DAMPING * scale / diag) * around(value)
    return value if inside is None else value * inside


def residual(value, right, scale):
    return right - diagonal(scale) * value + scale * around(value)


def two_parts(value):
    high = value.astype(jnp.bfloat16)
    return high, (value - high.astype(jnp.float32)).astype(jnp.bfloat16)


def moved(value, places):
    high, low = two_parts(value)
    dot = functools.partial(jnp.dot, preferred_element_type=jnp.float32)
    return dot(high, places) + dot(low, places)


def places_of(shape, wanted):
    source = lax.broadcasted_iota(jnp.int32, shape, 0)
    target = lax.broadcasted_iota(jnp.int32, shape, 1)
    return wanted(source, target).astype(jnp.float32).astype(jnp.bfloat16)


def halo_coarse(fine):
    return jnp.where(fine < HALF, fine // 2, HALF + fine // 2)


def pair_columns(fields):
    own = places_of((2 * LANES, LANES), lambda source, target: source // 2 == target)
    halo = places_of((LANES, LANES), lambda source, target: halo_coarse(source) == target)
    rows, cols = fields[0].shape
    blocks = (cols - LANES) // (2 * LANES)
    cut = [f[:, k * 2 * LANES:(k + 1) * 2 * LANES] for f in fields for k in range(blocks)]
    packed = moved(jnp.concatenate(cut, 0), own)
    edges = moved(jnp.concatenate([f[:, cols - LANES:] for f in fields], 0), halo)
    out = []
    for i in range(len(fields)):
        parts = [packed[(i * blocks + k) * rows:(i * blocks + k + 1) * rows] for k in range(blocks)]
        out.append(jnp.concatenate(parts + [edges[i * rows:(i + 1) * rows]], 1))
    return out


def spread_columns(fields):
    own = places_of((2 * LANES, 2 * LANES), lambda source, target: source == target // 2 + LANES * (target % 2))
    halo = places_of((2 * LANES, LANES), lambda source, target: source == halo_coarse(target) + LANES * (target % 2))
    rows, cols = fields[0].shape
    blocks = (cols - LANES) // LANES
    west = [0.75 * f + 0.25 * west_of(f) for f in fields]
    east = [0.75 * f + 0.25 * east_of(f) for f in fields]

    def cut(k):
        span = slice(k * LANES, (k + 1) * LANES)
        return [jnp.concatenate([w[:, span], e[:, span]], 1) for w, e in zip(west, east)]

    own_cut = [cut(k) for k in range(blocks)]
    packed = moved(jnp.concatenate([own_cut[k][i] for i in range(len(fields)) for k in range(blocks)], 0), own)
    edges = moved(jnp.concatenate(cut(blocks), 0), halo)
    out = []
    for i in range(len(fields)):
        parts = [packed[(i * blocks + k) * rows:(i * blocks + k + 1) * rows] for k in range(blocks)]
        out.append(jnp.concatenate(parts + [edges[i * rows:(i + 1) * rows]], 1))
    return out


def restrict(fields, paired_ref):
    rows = fields[0].shape[0]
    out = []
    for i, paired in enumerate(pair_columns(fields)):
        halves = []
        for k, tile in enumerate(tiles(paired)):
            paired_ref[i, k] = tile
            north = paired_ref[i, k, pl.ds(0, rows // 2, stride=2), :]
            south = paired_ref[i, k, pl.ds(1, rows // 2, stride=2), :]
            halves.append(0.25 * (north + south))
        out.append(jnp.concatenate(halves, 1))
    return out


def prolong(fields, fine_ref, first):
    rows = fields[0].shape[0]
    norths = [0.75 * f + 0.25 * north_of(f) for f in fields]
    souths = [0.75 * f + 0.25 * south_of(f) for f in fields]
    spread = spread_columns(norths + souths)
    for i in range(len(fields)):
        for k, (north, south) in enumerate(zip(tiles(spread[i]), tiles(spread[len(fields) + i]))):
            fine_ref[i, k, pl.ds(first, rows, stride=2), :] = north
            fine_ref[i, k, pl.ds(first + 1, rows, stride=2), :] = south


def wide_rows(fine_ref, chan, start, rows):
    return jnp.concatenate([fine_ref[chan, k, pl.ds(start, rows), :] for k in range(fine_ref.shape[1])], 1)


def window_of(rows, parts):
    spare = 8
    return rows + (2 * spare if parts > 2 else spare if parts == 2 else 0)


def own_start(parts, place):
    return 0 if parts == 1 else 8 * place if parts == 2 else 8


def band_mask(window, parts, place, rows):
    if parts <= 2:
        return None
    row = lax.broadcasted_iota(jnp.int32, (window, 1), 0) + place * rows - 8
    return ((row >= 0) & (row < parts * rows)).astype(jnp.float32)


def tiles(value):
    return [value[:, k * LANES:(k + 1) * LANES] for k in range(value.shape[1] // LANES)]


def lanes_of(tile):
    return lax.broadcasted_iota(jnp.int32, tile.shape, len(tile.shape) - 1)


def pack(value8, right4, coarse12):
    out = tiles(value8)
    halves = tiles(right4) + tiles(coarse12[8:])
    if len(halves) % 2:
        halves.append(halves[-1])
    out += tiles(coarse12[:8])
    out += [jnp.concatenate([halves[k], halves[k + 1]], 0) for k in range(0, len(halves), 2)]
    return out


def packed_tiles(fine_tiles, coarse_tiles):
    return fine_tiles + coarse_tiles + (fine_tiles + coarse_tiles + 1) // 2


def unpack(tile, fine_tiles, coarse_tiles):
    value8 = jnp.concatenate([tile(k) for k in range(fine_tiles)], 1)
    top = jnp.concatenate([tile(fine_tiles + k) for k in range(coarse_tiles)], 1)
    halves = []
    for k in range(fine_tiles + coarse_tiles, packed_tiles(fine_tiles, coarse_tiles)):
        both = tile(k)
        halves += [both[:4], both[4:]]
    right4 = jnp.concatenate(halves[:fine_tiles], 1)
    bottom = jnp.concatenate(halves[fine_tiles:fine_tiles + coarse_tiles], 1)
    return value8, right4, jnp.concatenate([top, bottom], 0)


def eastward(value):
    own = value[..., -2 * LANES:-LANES]
    return jnp.where(lanes_of(own) < HALF, value[..., -LANES:], own)


def westward(value):
    own = value[..., :LANES]
    return jnp.where(lanes_of(own) < HALF, own, value[..., -LANES:])


def with_edges(value, from_west, from_east):
    inner = lanes_of(from_west) < HALF
    first = value[..., :LANES] + jnp.where(inner, from_west, 0.0)
    last = value[..., -2 * LANES:-LANES] + jnp.where(inner, 0.0, from_east)
    halo = value[..., -LANES:] + jnp.where(inner, from_east, from_west)
    return jnp.concatenate([first, value[..., LANES:-2 * LANES], last, halo], value.ndim - 1)


VALUE_AT, RIGHT_AT = 48, 80


def taller(value, rows):
    missing = rows - value.shape[0]
    return jnp.concatenate([value, jnp.zeros((missing, value.shape[1]), value.dtype)], 0) if missing else value


def three_in_one(value, right, coarse, rows):
    value, right, coarse = (taller(v, rows) for v in (value, right, coarse))
    lane = lanes_of(value)
    at = lambda first: (lane >= first) & (lane < first + 16)
    out = jnp.where(at(VALUE_AT), pltpu.roll(value, VALUE_AT + 8, 1), coarse)
    return jnp.where(at(RIGHT_AT), pltpu.roll(right, RIGHT_AT + 8, 1), out)


def one_to_three(tile, value_rows, right_rows, coarse_rows):
    lane = lanes_of(tile)
    ends = lambda width: (lane < width) | (lane >= LANES - width)
    value = jnp.where(ends(8), pltpu.roll(tile, LANES - VALUE_AT - 8, 1), 0.0)
    right = jnp.where(ends(8), pltpu.roll(tile, LANES - RIGHT_AT - 8, 1), 0.0)
    coarse = jnp.where(ends(32), tile, 0.0)
    return value[:value_rows], right[:right_rows], coarse[:coarse_rows]


def down_kernel(parts, sweeps_hbm, target, grad_x, grad_y, labels, *refs):
    outs, scratch = refs[:8 if parts == 2 else 3], refs[8 if parts == 2 else 3:]
    value_ref, right_ref, coarse_ref = outs[:3]
    sweeps, target_v, grad_x_v, grad_y_v, labels_v, v_ref, b_ref, paired_ref, sems = scratch
    chans, rows, cols = target.shape
    window = value_ref.shape[1]
    place = lax.axis_index("lat")
    start = own_start(parts, place)
    if parts == 2:
        start = pl.multiple_of(start, 8)
    inside = band_mask(window, parts, place, rows)
    scale = 1.0

    first_copies = [
        pltpu.make_async_copy(labels, labels_v, sems.at[chans, 0]),
        pltpu.make_async_copy(sweeps_hbm, sweeps, sems.at[chans, 1]),
    ]
    for copy in first_copies:
        copy.start()
    copies = []
    for chan in range(chans):
        copies.append([
            pltpu.make_async_copy(target.at[chan], target_v.at[chan], sems.at[chan, 0]),
            pltpu.make_async_copy(grad_x.at[:, chan], grad_x_v.at[:, chan], sems.at[chan, 1]),
            pltpu.make_async_copy(grad_y.at[:, chan], grad_y_v.at[:, chan], sems.at[chan, 2]),
        ])
        for copy in copies[-1]:
            copy.start()
    if window > rows:
        v_ref[...] = jnp.zeros_like(v_ref)
        b_ref[...] = jnp.zeros_like(b_ref)
    for copy in first_copies:
        copy.wait()
    count = sweeps[0]

    def chosen(grad, chan):
        marks = labels_v[...]
        out = jnp.zeros((rows, cols), jnp.float32)
        for source in range(grad.shape[0]):
            out = jnp.where(marks == source, grad[source, chan], out)
        return out

    blank = jnp.zeros((rows, LANES), jnp.float32)
    resid = []
    for chan in range(chans):
        for copy in copies[chan]:
            copy.wait()
        own = jnp.concatenate([target_v[chan], blank], 1)
        sel_x = jnp.concatenate([chosen(grad_x_v, chan), blank], 1)
        sel_y = jnp.concatenate([chosen(grad_y_v, chan), blank], 1)
        right = SCREENING * own - ((sel_x - west_of(sel_x)) + (sel_y - north_of(sel_y)))
        v_ref[chan, pl.ds(start, rows), :] = own
        b_ref[chan, pl.ds(start, rows), :] = right
        if window > rows:
            below = pltpu.roll(sel_y[rows - 8:], 1, 0)
            b_ref[chan, pl.ds(start + rows, 8), :] = jnp.where(rows_of(below) == 0, below, 0.0)
        right = b_ref[chan, :window, :]
        if inside is not None:
            right = right * inside
        right_ref[chan] = right
        value = lax.fori_loop(
            0, count, lambda _, v, chan=chan: sweep(v, right_ref[chan], scale, inside), v_ref[chan, :window, :]
        )
        value_ref[chan] = value
        left = residual(value, right, scale)
        resid.append(left if inside is None else left * inside)
    coarse = restrict(resid, paired_ref)
    for chan in range(chans):
        coarse_ref[chan] = coarse[chan]
        if parts == 2:
            packed_ref, east_ref, east_across, west_ref, west_across = outs[3:]
            north = place == 0
            value, right = value_ref[chan], right_ref[chan]
            value8 = jnp.where(north, value[12:20], value[4:12])
            right4 = jnp.where(north, right[13:17], right[8:12])
            for k, tile in enumerate(pack(value8, right4, coarse[chan])):
                packed_ref[chan, k] = tile
            for height, east, west, fields in (
                (window, east_ref, west_ref, (value, right, coarse[chan])),
                (window, east_across, west_across, (value8, right4, coarse[chan])),
            ):
                east[chan] = three_in_one(*[eastward(f) for f in fields], height)
                west[chan] = three_in_one(*[westward(f) for f in fields], height)


def down(parts, sweeps, target, grad_x, grad_y, labels):
    chans, rows, cols = target.shape
    window = window_of(rows, parts)
    wide, half = cols + LANES, cols // 2 + LANES
    f32 = functools.partial(jax.ShapeDtypeStruct, dtype=jnp.float32)
    outs = [f32((chans, window, wide)), f32((chans, window, wide)), f32((chans, window // 2, half))]
    if parts == 2:
        outs.append(f32((chans, packed_tiles(wide // LANES, half // LANES), 8, LANES)))
        outs += [f32((chans, window, LANES))] * 4
    spare = 8 if window > rows else 0
    return pl.pallas_call(
        functools.partial(down_kernel, parts),
        in_specs=[HBM] * 5,
        out_specs=[VMEM] * len(outs),
        out_shape=outs,
        scratch_shapes=[
            pltpu.SMEM(sweeps.shape, jnp.int32),
            pltpu.VMEM(target.shape, jnp.float32),
            pltpu.VMEM(grad_x.shape, jnp.float32),
            pltpu.VMEM(grad_y.shape, jnp.float32),
            pltpu.VMEM(labels.shape, jnp.int32),
            pltpu.VMEM((chans, window + spare, wide), jnp.float32),
            pltpu.VMEM((chans, window + spare, wide), jnp.float32),
            pltpu.VMEM((chans, half // LANES, window, LANES), jnp.float32),
            pltpu.SemaphoreType.DMA((chans + 1, 3)),
        ],
        compiler_params=pltpu.CompilerParams(vmem_limit_bytes=32 * 2**20),
        name="down",
    )(*(in_hbm(a) for a in (sweeps, target, grad_x, grad_y, labels)))


def joined(place, own, other, height):
    gap = jnp.zeros((height - own.shape[0], own.shape[1]), jnp.float32)
    top, bottom = (lambda v: jnp.concatenate([v, gap], 0)), (lambda v: jnp.concatenate([gap, v], 0))
    return jnp.where(place == 0, top(own) + bottom(other), bottom(own) + top(other))


def up_kernel(parts, sweeps_hbm, value_ref, right_ref, coarse_ref, *refs):
    if parts == 2:
        packed_ref, *edge_refs = refs[:5]
        refs = refs[5:]
    out_ref, sweeps, b0_ref, b1_ref, b2_ref, pair_ref, fix1_ref, fix0_ref, sem = refs
    sweeps_copy = pltpu.make_async_copy(sweeps_hbm, sweeps, sem)
    sweeps_copy.start()
    chans, rows, cols = out_ref.shape
    window, wide = value_ref.shape[1:]
    half = b1_ref.shape[2]
    place = lax.axis_index("lat")
    inside = band_mask(window, parts, place, rows)
    north = place == 0

    def widened(value, upper, lower):
        def at(first):
            last = window - first - value.shape[0]
            pads = [jnp.zeros((n, wide), jnp.float32) for n in (first, last)]
            return jnp.concatenate([pads[0], value, pads[1]], 0)

        return jnp.where(north, at(upper), at(lower))

    def sides(west_ref, east_ref, chan, *heights):
        return list(zip(one_to_three(west_ref[chan], *heights), one_to_three(east_ref[chan], *heights)))

    def own_part(chan, which):
        field = (value_ref, right_ref, coarse_ref)[which][chan]
        if parts != 2:
            return field
        return with_edges(field, *sides(edge_refs[0], edge_refs[2], chan, window, window, window // 2)[which])

    def other_part(chan, which):
        field = unpack(lambda k: packed_ref[1 - place, chan, k], wide // LANES, half // LANES)[which]
        return with_edges(field, *sides(edge_refs[1], edge_refs[3], chan, 8, 4, 12)[which])

    for chan in range(chans):
        if parts == 2:
            b1_ref[chan] = joined(place, own_part(chan, 2), other_part(chan, 2), b1_ref.shape[1])
        else:
            b1_ref[chan] = coarse_ref[chan]

    def smoothed(values, right_ref, count, scale, inside=None):
        def step(_, values):
            return tuple(sweep(v, right_ref[i], scale, inside) for i, v in enumerate(values))

        return lax.fori_loop(0, count, step, tuple(values))

    def from_zero(right_ref, count, scale):
        first = [(DAMPING / diagonal(scale)) * right_ref[i] for i in range(chans)]
        return smoothed(first, right_ref, count - 1, scale)

    sweeps_copy.wait()
    mid = from_zero(b1_ref, sweeps[1], 0.25)
    low = restrict([residual(mid[i], b1_ref[i], 0.25) for i in range(chans)], pair_ref)
    for i in range(chans):
        b2_ref[i] = low[i]
    fix2 = from_zero(b2_ref, sweeps[2], 0.0625)
    prolong(fix2, fix1_ref, 0)
    mid = smoothed([mid[i] + wide_rows(fix1_ref, i, 0, mid[i].shape[0]) for i in range(chans)], b1_ref, sweeps[1], 0.25)
    spare = 8 if parts > 2 else 0
    if spare:
        fix0_ref[...] = jnp.zeros_like(fix0_ref)
    prolong(mid, fix0_ref, spare)
    start = own_start(parts, place)
    shown = 0 if parts == 1 else pl.multiple_of((8 if parts == 2 else rows) * place, 8)
    for i in range(chans):
        value = own_part(i, 0) + wide_rows(fix0_ref, i, shown, window)
        right = own_part(i, 1)
        if parts == 2:
            value = value + widened(other_part(i, 0), 12, 4)
            right = right + widened(other_part(i, 1), 16, 5)
        b0_ref[i] = right
        value = lax.fori_loop(0, sweeps[0], lambda _, v, i=i: sweep(v, b0_ref[i], 1.0, inside), value)
        if parts == 2:
            out_ref[i] = jnp.where(place == 0, value[:rows, :cols], value[8:8 + rows, :cols])
        else:
            out_ref[i] = value[start:start + rows, :cols]


def up(parts, shape, sweeps, value, right, coarse, *packed):
    chans, rows, cols = shape
    window, wide = value.shape[1:]
    full = parts * rows
    f32 = functools.partial(pltpu.VMEM, dtype=jnp.float32)
    spare = 16 if parts > 2 else 0
    return pl.pallas_call(
        functools.partial(up_kernel, parts),
        in_specs=[HBM] + [VMEM] * (3 + len(packed)),
        out_specs=VMEM,
        out_shape=jax.ShapeDtypeStruct(shape, jnp.float32),
        scratch_shapes=[
            pltpu.SMEM(sweeps.shape, jnp.int32),
            f32(value.shape),
            f32((chans, full // 2, cols // 2 + LANES)),
            f32((chans, full // 4, cols // 4 + LANES)),
            f32((chans, cols // 4 // LANES + 1, full // 2, LANES)),
            f32((chans, cols // 2 // LANES + 1, full // 2, LANES)),
            f32((chans, wide // LANES, full + spare, LANES)),
            pltpu.SemaphoreType.DMA,
        ],
        compiler_params=pltpu.CompilerParams(vmem_limit_bytes=48 * 2**20),
        name="up",
    )(in_hbm(sweeps), value, right, coarse, *packed)


def local(target, grad_x, grad_y, labels, sweeps):
    parts, around_globe = lax.axis_size("lat"), lax.axis_size("lon")
    value, right, coarse, *sent = down(parts, sweeps, target, grad_x, grad_y, labels)
    if parts == 2:
        eastward_pairs = [(i, (i + 1) % around_globe) for i in range(around_globe)]
        westward_pairs = [(j, i) for i, j in eastward_pairs]

        def across(pairs):
            return [(2 * i + k, 2 * j + 1 - k) for i, j in pairs for k in range(2)]

        packed, east, east_across, west, west_across = sent
        packed = lax.all_gather(packed, "lat")
        from_west = lax.ppermute(east, "lon", eastward_pairs)
        across_west = lax.ppermute(east_across, ("lon", "lat"), across(eastward_pairs))
        from_east = lax.ppermute(west, "lon", westward_pairs)
        across_east = lax.ppermute(west_across, ("lon", "lat"), across(westward_pairs))
        received = (packed, from_west, across_west, from_east, across_east)
        return up(parts, target.shape, sweeps, value, right, coarse, *received)

    def shared_lon(field):
        from_west = lax.ppermute(eastward(field), "lon", [(i, (i + 1) % around_globe) for i in range(around_globe)])
        from_east = lax.ppermute(westward(field), "lon", [((i + 1) % around_globe, i) for i in range(around_globe)])
        return with_edges(field, from_west, from_east)

    value, right, coarse = (shared_lon(f) for f in (value, right, coarse))
    if parts > 2:
        rows = target.shape[1]
        southward = [(i, i + 1) for i in range(parts - 1)]
        northward = [(i + 1, i) for i in range(parts - 1)]

        def shared_lat(field):
            north = lax.ppermute(field[:, rows:], "lat", southward)
            south = lax.ppermute(field[:, :16], "lat", northward)
            zeros = jnp.zeros_like(field[:, :16])
            return field + jnp.concatenate([north, zeros], 1) + jnp.concatenate([zeros, south], 1)

        value, right = shared_lat(value), shared_lat(right)
        every = lax.all_gather(coarse, "lat")
        step = rows // 2
        total = jnp.zeros((coarse.shape[0], parts * step + 8, coarse.shape[2]), jnp.float32)
        for i in range(parts):
            total = total.at[:, i * step:i * step + step + 8].add(every[i])
        coarse = total[:, 4:-4]
    return up(parts, target.shape, sweeps, value, right, coarse)


def solution(mesh):
    in_specs = (
        P(None, "lat", "lon"),
        P(None, None, "lat", "lon"),
        P(None, None, "lat", "lon"),
        P("lat", "lon"),
        P(),
    )
    out_specs = P(None, "lat", "lon")
    return jax.shard_map(local, mesh=mesh, in_specs=in_specs, out_specs=out_specs, check_vma=False)
```

```python
import functools

import jax
import jax.numpy as jnp
from jax import lax
from jax.experimental import pallas as pl
from jax.experimental.pallas import tpu as pltpu
from jax.sharding import PartitionSpec as P

SCREENING = 0.02
DAMPING = 0.8
LANES = 128
HALF = LANES // 2
SUBLANES = 8
VMEM = pl.BlockSpec(memory_space=pltpu.VMEM)
HBM = pl.BlockSpec(memory_space=pltpu.HBM)
F32 = functools.partial(jax.ShapeDtypeStruct, dtype=jnp.float32)
SCRATCH = functools.partial(pltpu.VMEM, dtype=jnp.float32)


def in_hbm(array):
    return pltpu.with_memory_space_constraint(array, pltpu.HBM)


def diagonal(scale):
    return SCREENING + 4.0 * scale


def rows_of(value):
    return lax.broadcasted_iota(jnp.int32, value.shape, 0)


def lanes_of(tile):
    return lax.broadcasted_iota(jnp.int32, tile.shape, len(tile.shape) - 1)


def tiles(value):
    return [value[:, k * LANES:(k + 1) * LANES] for k in range(value.shape[1] // LANES)]


def row_before(value):
    return jnp.where(rows_of(value) == 0, 0.0, pltpu.roll(value, 1, 0))


def row_after(value):
    last = value.shape[0] - 1
    return jnp.where(rows_of(value) == last, 0.0, pltpu.roll(value, last, 0))


def norths(planes):
    return [row_before(planes[-1])] + list(planes[:-1])


def souths(planes):
    return list(planes[1:]) + [row_after(planes[0])]


def west_of(value):
    return pltpu.roll(value, 1, 1)


def east_of(value):
    return pltpu.roll(value, value.shape[1] - 1, 1)


def around(planes):
    return [
        (north + south) + (west_of(value) + east_of(value))
        for value, north, south in zip(planes, norths(planes), souths(planes))
    ]


def sweep(planes, scaled, scale, inside=None):
    beside = DAMPING * scale / diagonal(scale)
    planes = [
        (1.0 - DAMPING) * value + (right + beside * total) for value, right, total in zip(planes, scaled, around(planes))
    ]
    return tuple(planes if inside is None else [value * mask for value, mask in zip(planes, inside)])


def residual(planes, right, scale):
    return [b - diagonal(scale) * value + scale * total for value, b, total in zip(planes, right, around(planes))]


def load_planes(ref, start, count, height):
    def plane(first):
        rows = pl.ds(first, height, stride=count) if count > 1 else pl.ds(first, height)
        return jnp.concatenate([ref[k, rows, :] for k in range(ref.shape[0])], 1)

    return [plane(start + t) for t in range(count)]


def store_planes(ref, start, planes):
    count, height = len(planes), planes[0].shape[0]
    for t, plane in enumerate(planes):
        rows = pl.ds(start + t, height, stride=count) if count > 1 else pl.ds(start + t, height)
        for k, tile in enumerate(tiles(plane)):
            ref[k, rows, :] = tile


def places_of(shape, wanted):
    source = lax.broadcasted_iota(jnp.int32, shape, 0)
    target = lax.broadcasted_iota(jnp.int32, shape, 1)
    return wanted(source, target).astype(jnp.float32).astype(jnp.bfloat16)


def halo_coarse(fine):
    return jnp.where(fine < HALF, fine // 2, HALF + fine // 2)


def pairing():
    own = places_of((2 * LANES, LANES), lambda source, target: source // 2 == target)
    halo = places_of((LANES, LANES), lambda source, target: halo_coarse(source) == target)
    return own, halo


def spreading():
    own = places_of((2 * LANES, 2 * LANES), lambda source, target: source == target // 2 + LANES * (target % 2))
    halo = places_of((2 * LANES, LANES), lambda source, target: source == halo_coarse(target) + LANES * (target % 2))
    return own, halo


def moved(value, places):
    high = value.astype(jnp.bfloat16)
    low = (value - high.astype(jnp.float32)).astype(jnp.bfloat16)
    dot = functools.partial(jnp.dot, preferred_element_type=jnp.float32)
    return dot(high, places) + dot(low, places)


def moved_blocks(own_blocks, halo_blocks, places):
    rows, count = halo_blocks[0].shape[0], len(own_blocks[0])
    packed = moved(jnp.concatenate([block for blocks in own_blocks for block in blocks], 0), places[0])
    edges = moved(jnp.concatenate(halo_blocks, 0), places[1])
    out = []
    for i in range(len(own_blocks)):
        parts = [packed[(i * count + k) * rows:(i * count + k + 1) * rows] for k in range(count)]
        out.append(jnp.concatenate(parts + [edges[i * rows:(i + 1) * rows]], 1))
    return out


def pair_columns(fields, places):
    cols = fields[0].shape[1] - LANES
    width = 2 * LANES
    own = [[f[:, k * width:(k + 1) * width] for k in range(cols // width)] for f in fields]
    return moved_blocks(own, [f[:, cols:] for f in fields], places)


def spread_columns(fields, places):
    cut = [list(zip(tiles(0.75 * f + 0.25 * west_of(f)), tiles(0.75 * f + 0.25 * east_of(f)))) for f in fields]
    blocks = [[jnp.concatenate(both, 1) for both in field] for field in cut]
    return moved_blocks([b[:-1] for b in blocks], [b[-1] for b in blocks], places)


def prolong(fields, places):
    halves = [
        half
        for planes in fields
        for value, north, south in zip(planes, norths(planes), souths(planes))
        for half in (0.75 * value + 0.25 * north, 0.75 * value + 0.25 * south)
    ]
    spread = spread_columns(halves, places)
    count = 2 * len(fields[0])
    return [spread[i * count:(i + 1) * count] for i in range(len(fields))]


def window_of(rows, parts):
    return rows + (2 * SUBLANES if parts > 2 else SUBLANES if parts == 2 else 0)


def own_start(parts, place):
    return 0 if parts == 1 else pl.multiple_of(SUBLANES * place, SUBLANES) if parts == 2 else SUBLANES


def band_masks(window, parts, place, rows):
    if parts <= 2:
        return None
    count = window // SUBLANES
    first = place * rows - SUBLANES
    row = [first + t + count * lax.broadcasted_iota(jnp.int32, (SUBLANES, 1), 0) for t in range(count)]
    return [((r >= 0) & (r < parts * rows)).astype(jnp.float32) for r in row]


def eastward(own_last, halo):
    return jnp.where(lanes_of(halo) < HALF, halo, own_last)


def westward(own_first, halo):
    return jnp.where(lanes_of(halo) < HALF, own_first, halo)


def with_edges(parts, from_west, from_east):
    inner = lanes_of(from_west) < HALF
    first = parts[0] + jnp.where(inner, from_west, 0.0)
    last = parts[-2] + jnp.where(inner, 0.0, from_east)
    halo = parts[-1] + jnp.where(inner, from_east, from_west)
    return [first] + list(parts[1:-2]) + [last, halo]


COARSE_WIDTH, FINE_WIDTH, REACH = 32, 8, 4
TO_EAST, TO_WEST = -24, -8


def in_window(lane, start, width):
    start = start % LANES
    end = start + width
    return (lane >= start) & (lane < end) if end <= LANES else (lane >= start) | (lane < end - LANES)


def slots(value_rows, right_rows, coarse_rows, coarse_start):
    out, at = [], 0
    for which, rows, start, width in (
        (2, coarse_rows, coarse_start, COARSE_WIDTH),
        (0, value_rows, -REACH, FINE_WIDTH),
        (1, right_rows, -REACH, FINE_WIDTH),
    ):
        for first in range(0, rows, SUBLANES):
            out.append((which, first, min(SUBLANES, rows - first), start, width, at))
            at += width
    assert at <= LANES
    return out


def bundle(fields, coarse_start):
    out = jnp.zeros((SUBLANES, LANES), jnp.float32)
    lane = lanes_of(out)
    for which, first, rows, start, width, at in slots(*(f.shape[0] for f in fields), coarse_start):
        piece = fields[which][first:first + rows]
        if rows < SUBLANES:
            piece = jnp.concatenate([piece, jnp.zeros((SUBLANES - rows, LANES), jnp.float32)], 0)
        out = jnp.where(in_window(lane, at, width), pltpu.roll(piece, (at - start) % LANES, 1), out)
    return out


def unbundle(tile, heights, coarse_start):
    lane = lanes_of(tile)
    pieces = ([], [], [])
    for which, first, rows, start, width, at in slots(*heights, coarse_start):
        piece = jnp.where(in_window(lane, start, width), pltpu.roll(tile, (start - at) % LANES, 1), 0.0)
        pieces[which].append(piece[:rows])
    return [jnp.concatenate(p, 0) if len(p) > 1 else p[0] for p in pieces]


VALUE_ROWS, RIGHT_ROWS, COARSE_ROWS = 8, 4, 12
ACROSS = (VALUE_ROWS, RIGHT_ROWS, COARSE_ROWS)


def pack(value, right, coarse):
    halves = right[:-1] + [c[SUBLANES:] for c in coarse[:-1]]
    joined = [jnp.concatenate(halves[k:k + 2], 0) for k in range(0, len(halves), 2)]
    return value[:-1] + [c[:SUBLANES] for c in coarse[:-1]] + joined + [bundle([value[-1], right[-1], coarse[-1]], TO_WEST)]


def packed_tiles(fine, coarse):
    return fine + coarse + (fine + coarse) // 2 + 1


def unpack(tile, fine, coarse):
    halves = []
    for k in range(fine + coarse, fine + coarse + (fine + coarse) // 2):
        both = tile(k)
        halves += [both[:4], both[4:]]
    value = [tile(k) for k in range(fine)]
    right = halves[:fine]
    low = [jnp.concatenate([tile(fine + k), halves[fine + k]], 0) for k in range(coarse)]
    ends = unbundle(tile(packed_tiles(fine, coarse) - 1), ACROSS, TO_WEST)
    return [field + [end] for field, end in zip((value, right, low), ends)]


def down_kernel(parts, sweeps_hbm, target, grad_x, grad_y, labels, *refs):
    sent = 5 if parts == 2 else 0
    value_ref, right_ref, coarse_ref = refs[:3]
    sent_refs = refs[3:3 + sent]
    sweeps, target_v, grad_x_v, grad_y_v, labels_v, v_ref, b_ref, scaled_ref, resid_ref, sems = refs[3 + sent:]
    chans, rows, cols = target.shape
    window = value_ref.shape[2]
    count = window // SUBLANES
    place = lax.axis_index("lat")
    start = own_start(parts, place)
    inside = band_masks(window, parts, place, rows)
    scale = 1.0

    first_copies = [
        pltpu.make_async_copy(labels, labels_v, sems.at[chans, 0]),
        pltpu.make_async_copy(sweeps_hbm, sweeps, sems.at[chans, 1]),
    ]
    for copy in first_copies:
        copy.start()
    copies = []
    for chan in range(chans):
        copies.append([
            pltpu.make_async_copy(target.at[chan], target_v.at[chan], sems.at[chan, 0]),
            pltpu.make_async_copy(grad_x.at[:, chan], grad_x_v.at[:, chan], sems.at[chan, 1]),
            pltpu.make_async_copy(grad_y.at[:, chan], grad_y_v.at[:, chan], sems.at[chan, 2]),
        ])
        for copy in copies[-1]:
            copy.start()
    if window > rows:
        v_ref[...] = jnp.zeros_like(v_ref)
        b_ref[...] = jnp.zeros_like(b_ref)
    places = pairing()
    for copy in first_copies:
        copy.wait()

    def chosen(grad, chan):
        marks = labels_v[...]
        out = jnp.zeros((rows, cols), jnp.float32)
        for source in range(grad.shape[0]):
            out = jnp.where(marks == source, grad[source, chan], out)
        return out

    blank = jnp.zeros((rows, LANES), jnp.float32)
    paired = []
    for chan in range(chans):
        for copy in copies[chan]:
            copy.wait()
        own = jnp.concatenate([target_v[chan], blank], 1)
        sel_x = jnp.concatenate([chosen(grad_x_v, chan), blank], 1)
        sel_y = jnp.concatenate([chosen(grad_y_v, chan), blank], 1)
        right = SCREENING * own - ((sel_x - west_of(sel_x)) + (sel_y - row_before(sel_y)))
        below = pltpu.roll(sel_y[rows - SUBLANES:], 1, 0)
        below = jnp.where(rows_of(below) == 0, below, 0.0)
        for k, (v, b, s) in enumerate(zip(tiles(own), tiles(right), tiles(below))):
            v_ref[chan, k, pl.ds(start, rows), :] = v
            b_ref[chan, k, pl.ds(start, rows), :] = b
            if window > rows:
                b_ref[chan, k, pl.ds(start + rows, SUBLANES), :] = s
        planes = load_planes(v_ref.at[chan], 0, count, SUBLANES)
        right = load_planes(b_ref.at[chan], 0, count, SUBLANES)
        if inside is not None:
            right = [b * mask for b, mask in zip(right, inside)]
        store_planes(right_ref.at[chan], 0, right)
        for t in range(count):
            scaled_ref[t] = (DAMPING / diagonal(scale)) * right[t]

        def step(_, planes):
            return sweep(planes, [scaled_ref[t] for t in range(count)], scale, inside)

        planes = lax.fori_loop(0, sweeps[0], step, tuple(planes))
        store_planes(value_ref.at[chan], 0, planes)
        left = residual(planes, [(diagonal(scale) / DAMPING) * scaled_ref[t] for t in range(count)], scale)
        if inside is not None:
            left = [r * mask for r, mask in zip(left, inside)]
        store_planes(resid_ref.at[chan], 0, left)
        north, south = load_planes(resid_ref.at[chan], 0, 2, window // 2)
        paired.append(north + south)
    coarse = pair_columns(paired, places)
    for chan in range(chans):
        low = 0.25 * coarse[chan]
        coarse_ref[chan] = low
        if parts != 2:
            continue
        packed_ref, east_ref, east_across, west_ref, west_across = sent_refs
        wide = value_ref.shape[1]
        value = [value_ref[chan, k] for k in range(wide)]
        right = [right_ref[chan, k] for k in range(wide)]
        low = tiles(low)
        north = place == 0
        value_border = [jnp.where(north, v[12:20], v[4:12]) for v in value]
        right_border = [jnp.where(north, b[13:17], b[8:12]) for b in right]
        for k, tile in enumerate(pack(value_border, right_border, low)):
            packed_ref[chan, k] = tile
        for east, west, fields in (
            (east_ref, west_ref, (value, right, low)),
            (east_across, west_across, (value_border, right_border, low)),
        ):
            east[chan] = bundle([eastward(f[-2], f[-1]) for f in fields], TO_EAST)
            west[chan] = bundle([westward(f[0], f[-1]) for f in fields], TO_WEST)


def down(parts, sweeps, target, grad_x, grad_y, labels):
    chans, rows, cols = target.shape
    window = window_of(rows, parts)
    wide, half = cols // LANES + 1, cols // 2 // LANES + 1
    spare = SUBLANES if window > rows else 0
    outs = [F32((chans, wide, window, LANES))] * 2 + [F32((chans, window // 2, half * LANES))]
    if parts == 2:
        outs.append(F32((chans, packed_tiles(wide - 1, half - 1), SUBLANES, LANES)))
        outs += [F32((chans, SUBLANES, LANES))] * 4
    return pl.pallas_call(
        functools.partial(down_kernel, parts),
        in_specs=[HBM] * 5,
        out_specs=[VMEM] * len(outs),
        out_shape=outs,
        scratch_shapes=[
            pltpu.SMEM(sweeps.shape, jnp.int32),
            SCRATCH(target.shape),
            SCRATCH(grad_x.shape),
            SCRATCH(grad_y.shape),
            pltpu.VMEM(labels.shape, jnp.int32),
            SCRATCH((chans, wide, window + spare, LANES)),
            SCRATCH((chans, wide, window + spare, LANES)),
            SCRATCH((window // SUBLANES, SUBLANES, wide * LANES)),
            SCRATCH((chans, wide, window, LANES)),
            pltpu.SemaphoreType.DMA((chans + 1, 3)),
        ],
        compiler_params=pltpu.CompilerParams(vmem_limit_bytes=32 * 2**20),
        name="down",
    )(*(in_hbm(a) for a in (sweeps, target, grad_x, grad_y, labels)))


def joined(place, own, other, height):
    gap = jnp.zeros((height - own.shape[0], own.shape[1]), jnp.float32)
    top, bottom = (lambda v: jnp.concatenate([v, gap], 0)), (lambda v: jnp.concatenate([gap, v], 0))
    return jnp.where(place == 0, top(own) + bottom(other), bottom(own) + top(other))


def up_kernel(parts, sweeps_hbm, value_ref, right_ref, coarse_ref, *refs):
    received = 5 if parts == 2 else 0
    packed_ref, *edge_refs = refs[:received] or [None]
    out_hbm, sweeps, v0_ref, b0_ref, k0_ref, b1_ref, k1_ref, k2_ref, fix_ref, out_ref, sems = refs[received:]
    sweeps_copy = pltpu.make_async_copy(sweeps_hbm, sweeps, sems.at[0])
    sweeps_copy.start()
    chans, rows, cols = out_ref.shape
    wide, window = value_ref.shape[1:3]
    half = coarse_ref.shape[2] // LANES
    full = parts * rows
    count0, count1, count2 = window // SUBLANES, max(1, full // 2 // SUBLANES), max(1, full // 4 // SUBLANES)
    place = lax.axis_index("lat")
    inside = band_masks(window, parts, place, rows)
    own_heights = (window, window, window // 2)

    def sides(chan, across):
        heights = ACROSS if across else own_heights
        from_west = unbundle(edge_refs[across][chan], heights, TO_EAST)
        from_east = unbundle(edge_refs[2 + across][chan], heights, TO_WEST)
        return list(zip(from_west, from_east))

    from_partner = []
    for chan in range(chans):
        low = coarse_ref[chan]
        if parts == 2:
            here, there = sides(chan, 0), sides(chan, 1)
            other = unpack(lambda k: packed_ref[chan, k], wide - 1, half - 1)
            value, right, other_low = (with_edges(f, *s) for f, s in zip(other, there))
            low = jnp.concatenate(with_edges(tiles(low), *here[2]), 1)
            low = joined(place, low, jnp.concatenate(other_low, 1), full // 2)
            for ref, own, side in ((v0_ref, value_ref, here[0]), (b0_ref, right_ref, here[1])):
                for k, tile in enumerate(with_edges([own[chan, k] for k in range(wide)], *side)):
                    ref[chan, k] = tile
            from_partner.append((value, right))
        else:
            v0_ref[chan] = value_ref[chan]
            b0_ref[chan] = right_ref[chan]
        for k, tile in enumerate(tiles(low)):
            b1_ref[chan, k] = tile

    def add_rows(value_at, right_at):
        for chan, (value, right) in enumerate(from_partner):
            for k in range(wide):
                v0_ref[chan, k, pl.ds(value_at, VALUE_ROWS), :] += value[k]
                b0_ref[chan, k, pl.ds(right_at, RIGHT_ROWS), :] += right[k]

    if parts == 2:
        pl.when(place == 0)(lambda: add_rows(12, 16))
        pl.when(place == 1)(lambda: add_rows(4, 5))

    def smoothed(fields, scaled_ref, count, scale):
        def step(_, fields):
            scaled = [[scaled_ref[i, t] for t in range(len(f))] for i, f in enumerate(fields)]
            return tuple(sweep(f, k, scale) for f, k in zip(fields, scaled))

        return lax.fori_loop(0, count, step, tuple(tuple(f) for f in fields))

    def from_zero(rights, scaled_ref, count, scale):
        first = [[(DAMPING / diagonal(scale)) * b for b in planes] for planes in rights]
        for i, planes in enumerate(first):
            for t, plane in enumerate(planes):
                scaled_ref[i, t] = plane
        return smoothed(first, scaled_ref, count - 1, scale)

    pair_places, spread_places = pairing(), spreading()
    height1 = full // 2 // count1
    right1 = [load_planes(b1_ref.at[i], 0, count1, height1) for i in range(chans)]
    sweeps_copy.wait()
    mid = from_zero(right1, k1_ref, sweeps[1], 0.25)
    left = [residual(f, load_planes(b1_ref.at[i], 0, count1, height1), 0.25) for i, f in enumerate(mid)]
    if count1 > 1:
        pairs = [f[t] + f[t + 1] for f in left for t in range(0, count1, 2)]
        low = [0.25 * v for v in pair_columns(pairs, pair_places)]
        right2 = [low[i * count2:(i + 1) * count2] for i in range(chans)]
    else:
        raise NotImplementedError("one part")
    fix2 = from_zero(right2, k2_ref, sweeps[2], 0.0625)
    mid = [[v + f for v, f in zip(planes, fix)] for planes, fix in zip(mid, prolong(fix2, spread_places))]
    mid = smoothed(mid, k1_ref, sweeps[1], 0.25)
    spare = (fix_ref.shape[2] - full) // 2
    for i, fix in enumerate(prolong(mid, spread_places)):
        store_planes(fix_ref.at[i], spare, fix)
    shown = pl.multiple_of((SUBLANES if parts == 2 else rows) * place, SUBLANES)
    start = own_start(parts, place)
    out_copies = []
    for i in range(chans):
        planes = load_planes(v0_ref.at[i], 0, count0, SUBLANES)
        fix = load_planes(fix_ref.at[i], shown, count0, SUBLANES)
        planes = tuple(v + f for v, f in zip(planes, fix))
        for t, b in enumerate(load_planes(b0_ref.at[i], 0, count0, SUBLANES)):
            k0_ref[t] = (DAMPING / diagonal(1.0)) * b

        def step(_, planes):
            return sweep(planes, [k0_ref[t] for t in range(count0)], 1.0, inside)

        planes = lax.fori_loop(0, sweeps[0], step, planes)
        store_planes(v0_ref.at[i], 0, planes)
        for k in range(cols // LANES):
            out_ref[i, :, k * LANES:(k + 1) * LANES] = v0_ref[i, k, pl.ds(start, rows), :]
        out_copies.append(pltpu.make_async_copy(out_ref.at[i], out_hbm.at[i], sems.at[1 + i]))
        out_copies[-1].start()
    for copy in out_copies:
        copy.wait()


def up(parts, shape, sweeps, value, right, coarse, *received):
    chans, rows, cols = shape
    wide, window = value.shape[1:3]
    full = parts * rows
    half, quarter = cols // 2 // LANES + 1, cols // 4 // LANES + 1
    count1, count2 = max(1, full // 2 // SUBLANES), max(1, full // 4 // SUBLANES)
    spare = 2 * SUBLANES if parts > 2 else 0
    return pl.pallas_call(
        functools.partial(up_kernel, parts),
        in_specs=[HBM] + [VMEM] * (3 + len(received)),
        out_specs=HBM,
        out_shape=F32(shape),
        scratch_shapes=[
            pltpu.SMEM(sweeps.shape, jnp.int32),
            SCRATCH(value.shape),
            SCRATCH(value.shape),
            SCRATCH((window // SUBLANES, SUBLANES, wide * LANES)),
            SCRATCH((chans, half, full // 2, LANES)),
            SCRATCH((chans, count1, full // 2 // count1, half * LANES)),
            SCRATCH((chans, count2, full // 4 // count2, quarter * LANES)),
            SCRATCH((chans, wide, full + spare, LANES)),
            SCRATCH(shape),
            pltpu.SemaphoreType.DMA((1 + chans,)),
        ],
        compiler_params=pltpu.CompilerParams(vmem_limit_bytes=48 * 2**20),
        name="up",
    )(in_hbm(sweeps), value, right, coarse, *received)


def local(target, grad_x, grad_y, labels, sweeps):
    parts, around_globe = lax.axis_size("lat"), lax.axis_size("lon")
    value, right, coarse, *sent = down(parts, sweeps, target, grad_x, grad_y, labels)
    eastward_pairs = [(i, (i + 1) % around_globe) for i in range(around_globe)]
    westward_pairs = [(j, i) for i, j in eastward_pairs]
    if parts == 2:
        def across(pairs):
            return [(2 * i + k, 2 * j + 1 - k) for i, j in pairs for k in range(2)]

        packed, east, east_across, west, west_across = sent
        packed = lax.ppermute(packed, "lat", [(0, 1), (1, 0)])
        from_west = lax.ppermute(east, "lon", eastward_pairs)
        across_west = lax.ppermute(east_across, ("lon", "lat"), across(eastward_pairs))
        from_east = lax.ppermute(west, "lon", westward_pairs)
        across_east = lax.ppermute(west_across, ("lon", "lat"), across(westward_pairs))
        received = (packed, from_west, across_west, from_east, across_east)
        return up(parts, target.shape, sweeps, value, right, coarse, *received)

    chans, half_rows = coarse.shape[:2]
    coarse = coarse.reshape(chans, half_rows, -1, LANES).transpose(0, 2, 1, 3)

    def shared_lon(field):
        parts_of = [field[:, k] for k in range(field.shape[1])]
        from_west = lax.ppermute(eastward(parts_of[-2], parts_of[-1]), "lon", eastward_pairs)
        from_east = lax.ppermute(westward(parts_of[0], parts_of[-1]), "lon", westward_pairs)
        return jnp.stack(with_edges(parts_of, from_west, from_east), 1)

    value, right, coarse = (shared_lon(f) for f in (value, right, coarse))
    if parts > 2:
        rows = target.shape[1]
        spare = 2 * SUBLANES
        southward = [(i, i + 1) for i in range(parts - 1)]
        northward = [(i + 1, i) for i in range(parts - 1)]

        def shared_lat(field):
            north = lax.ppermute(field[:, :, rows:], "lat", southward)
            south = lax.ppermute(field[:, :, :spare], "lat", northward)
            zeros = jnp.zeros_like(south)
            return field + jnp.concatenate([north, zeros], 2) + jnp.concatenate([zeros, south], 2)

        value, right = shared_lat(value), shared_lat(right)
        every = lax.all_gather(coarse, "lat")
        step = rows // 2
        total = jnp.zeros((chans, coarse.shape[1], parts * step + SUBLANES, LANES), jnp.float32)
        for i in range(parts):
            total = total.at[:, :, i * step:i * step + step + SUBLANES].add(every[i])
        coarse = total[:, :, 4:-4]
    coarse = coarse.transpose(0, 2, 1, 3).reshape(chans, coarse.shape[2], -1)
    return up(parts, target.shape, sweeps, value, right, coarse)


def solution(mesh):
    in_specs = (
        P(None, "lat", "lon"),
        P(None, None, "lat", "lon"),
        P(None, None, "lat", "lon"),
        P("lat", "lon"),
        P(),
    )
    out_specs = P(None, "lat", "lon")
    return jax.shard_map(local, mesh=mesh, in_specs=in_specs, out_specs=out_specs, check_vma=False)
```

```python
import functools

import jax
import jax.numpy as jnp
from jax import lax
from jax.experimental import pallas as pl
from jax.experimental.pallas import tpu as pltpu
from jax.sharding import PartitionSpec as P

SCREENING = 0.02
DAMPING = 0.8
LANES = 128
HALF = LANES // 2
SUBLANES = 8
VMEM = pl.BlockSpec(memory_space=pltpu.VMEM)
HBM = pl.BlockSpec(memory_space=pltpu.HBM)
F32 = functools.partial(jax.ShapeDtypeStruct, dtype=jnp.float32)
SCRATCH = functools.partial(pltpu.VMEM, dtype=jnp.float32)


def in_hbm(array):
    return pltpu.with_memory_space_constraint(array, pltpu.HBM)


def diagonal(scale):
    return SCREENING + 4.0 * scale


def rows_of(value):
    return lax.broadcasted_iota(jnp.int32, value.shape, 0)


def lanes_of(tile):
    return lax.broadcasted_iota(jnp.int32, tile.shape, len(tile.shape) - 1)


def tiles(value):
    return [value[:, k * LANES:(k + 1) * LANES] for k in range(value.shape[1] // LANES)]


def row_before(value):
    return jnp.where(rows_of(value) == 0, 0.0, pltpu.roll(value, 1, 0))


def row_after(value):
    last = value.shape[0] - 1
    return jnp.where(rows_of(value) == last, 0.0, pltpu.roll(value, last, 0))


def norths(planes):
    return [row_before(planes[-1])] + list(planes[:-1])


def souths(planes):
    return list(planes[1:]) + [row_after(planes[0])]


def west_of(value):
    return pltpu.roll(value, 1, 1)


def east_of(value):
    return pltpu.roll(value, value.shape[1] - 1, 1)


def around(planes):
    return [
        (north + south) + (west_of(value) + east_of(value))
        for value, north, south in zip(planes, norths(planes), souths(planes))
    ]


def sweep(planes, scaled, scale, inside=None):
    beside = DAMPING * scale / diagonal(scale)
    planes = [
        (1.0 - DAMPING) * value + (right + beside * total) for value, right, total in zip(planes, scaled, around(planes))
    ]
    return tuple(planes if inside is None else [value * mask for value, mask in zip(planes, inside)])


def residual(planes, right, scale):
    return [b - diagonal(scale) * value + scale * total for value, b, total in zip(planes, right, around(planes))]


def load_planes(ref, start, count, height):
    def plane(first):
        rows = pl.ds(first, height, stride=count) if count > 1 else pl.ds(first, height)
        return jnp.concatenate([ref[k, rows, :] for k in range(ref.shape[0])], 1)

    return [plane(start + t) for t in range(count)]


def store_planes(ref, start, planes):
    count, height = len(planes), planes[0].shape[0]
    for t, plane in enumerate(planes):
        rows = pl.ds(start + t, height, stride=count) if count > 1 else pl.ds(start + t, height)
        for k, tile in enumerate(tiles(plane)):
            ref[k, rows, :] = tile


def places_of(shape, wanted):
    source = lax.broadcasted_iota(jnp.int32, shape, 0)
    target = lax.broadcasted_iota(jnp.int32, shape, 1)
    return wanted(source, target).astype(jnp.float32).astype(jnp.bfloat16)


def halo_coarse(fine):
    return jnp.where(fine < HALF, fine // 2, HALF + fine // 2)


def pairing():
    own = places_of((2 * LANES, LANES), lambda source, target: source // 2 == target)
    halo = places_of((LANES, LANES), lambda source, target: halo_coarse(source) == target)
    return own, halo


def spreading():
    own = places_of((2 * LANES, 2 * LANES), lambda source, target: source == target // 2 + LANES * (target % 2))
    halo = places_of((2 * LANES, LANES), lambda source, target: source == halo_coarse(target) + LANES * (target % 2))
    return own, halo


def moved(value, places):
    high = value.astype(jnp.bfloat16)
    low = (value - high.astype(jnp.float32)).astype(jnp.bfloat16)
    dot = functools.partial(jnp.dot, preferred_element_type=jnp.float32)
    return dot(high, places) + dot(low, places)


def moved_blocks(own_blocks, halo_blocks, places):
    rows, count = halo_blocks[0].shape[0], len(own_blocks[0])
    packed = moved(jnp.concatenate([block for blocks in own_blocks for block in blocks], 0), places[0])
    edges = moved(jnp.concatenate(halo_blocks, 0), places[1])
    out = []
    for i in range(len(own_blocks)):
        parts = [packed[(i * count + k) * rows:(i * count + k + 1) * rows] for k in range(count)]
        out.append(jnp.concatenate(parts + [edges[i * rows:(i + 1) * rows]], 1))
    return out


def pair_columns(fields, places):
    cols = fields[0].shape[1] - LANES
    width = 2 * LANES
    own = [[f[:, k * width:(k + 1) * width] for k in range(cols // width)] for f in fields]
    return moved_blocks(own, [f[:, cols:] for f in fields], places)


def spread_columns(fields, places):
    cut = [list(zip(tiles(0.75 * f + 0.25 * west_of(f)), tiles(0.75 * f + 0.25 * east_of(f)))) for f in fields]
    blocks = [[jnp.concatenate(both, 1) for both in field] for field in cut]
    return moved_blocks([b[:-1] for b in blocks], [b[-1] for b in blocks], places)


def prolong(fields, places):
    halves = [
        half
        for planes in fields
        for value, north, south in zip(planes, norths(planes), souths(planes))
        for half in (0.75 * value + 0.25 * north, 0.75 * value + 0.25 * south)
    ]
    spread = spread_columns(halves, places)
    count = 2 * len(fields[0])
    return [spread[i * count:(i + 1) * count] for i in range(len(fields))]


def window_of(rows, parts):
    return rows + (2 * SUBLANES if parts > 2 else SUBLANES if parts == 2 else 0)


def own_start(parts, place):
    return 0 if parts == 1 else pl.multiple_of(SUBLANES * place, SUBLANES) if parts == 2 else SUBLANES


def band_masks(window, parts, place, rows):
    if parts <= 2:
        return None
    count = window // SUBLANES
    first = place * rows - SUBLANES
    row = [first + t + count * lax.broadcasted_iota(jnp.int32, (SUBLANES, 1), 0) for t in range(count)]
    return [((r >= 0) & (r < parts * rows)).astype(jnp.float32) for r in row]


def eastward(own_last, halo):
    return jnp.where(lanes_of(halo) < HALF, halo, own_last)


def westward(own_first, halo):
    return jnp.where(lanes_of(halo) < HALF, own_first, halo)


def with_edges(parts, from_west, from_east):
    inner = lanes_of(from_west) < HALF
    first = parts[0] + jnp.where(inner, from_west, 0.0)
    last = parts[-2] + jnp.where(inner, 0.0, from_east)
    halo = parts[-1] + jnp.where(inner, from_east, from_west)
    return [first] + list(parts[1:-2]) + [last, halo]


COARSE_WIDTH, FINE_WIDTH, REACH = 32, 8, 4
TO_EAST, TO_WEST = -24, -8


def in_window(lane, start, width):
    start = start % LANES
    end = start + width
    return (lane >= start) & (lane < end) if end <= LANES else (lane >= start) | (lane < end - LANES)


def slots(value_rows, right_rows, coarse_rows, coarse_start):
    out, at = [], 0
    for which, rows, start, width in (
        (2, coarse_rows, coarse_start, COARSE_WIDTH),
        (0, value_rows, -REACH, FINE_WIDTH),
        (1, right_rows, -REACH, FINE_WIDTH),
    ):
        for first in range(0, rows, SUBLANES):
            out.append((which, first, min(SUBLANES, rows - first), start, width, at))
            at += width
    assert at <= LANES
    return out


def bundle(fields, coarse_start):
    out = jnp.zeros((SUBLANES, LANES), jnp.float32)
    lane = lanes_of(out)
    for which, first, rows, start, width, at in slots(*(f.shape[0] for f in fields), coarse_start):
        piece = fields[which][first:first + rows]
        if rows < SUBLANES:
            piece = jnp.concatenate([piece, jnp.zeros((SUBLANES - rows, LANES), jnp.float32)], 0)
        out = jnp.where(in_window(lane, at, width), pltpu.roll(piece, (at - start) % LANES, 1), out)
    return out


def unbundle(tile, heights, coarse_start):
    lane = lanes_of(tile)
    pieces = ([], [], [])
    for which, first, rows, start, width, at in slots(*heights, coarse_start):
        piece = jnp.where(in_window(lane, start, width), pltpu.roll(tile, (start - at) % LANES, 1), 0.0)
        pieces[which].append(piece[:rows])
    return [jnp.concatenate(p, 0) if len(p) > 1 else p[0] for p in pieces]


VALUE_ROWS, RIGHT_ROWS, COARSE_ROWS = 8, 4, 12
ACROSS = (VALUE_ROWS, RIGHT_ROWS, COARSE_ROWS)


def pack(value, right, coarse):
    halves = right[:-1] + [c[SUBLANES:] for c in coarse[:-1]]
    joined = [jnp.concatenate(halves[k:k + 2], 0) for k in range(0, len(halves), 2)]
    return value[:-1] + [c[:SUBLANES] for c in coarse[:-1]] + joined + [bundle([value[-1], right[-1], coarse[-1]], TO_WEST)]


def packed_tiles(fine, coarse):
    return fine + coarse + (fine + coarse) // 2 + 1


def unpack(tile, fine, coarse):
    halves = []
    for k in range(fine + coarse, fine + coarse + (fine + coarse) // 2):
        both = tile(k)
        halves += [both[:4], both[4:]]
    value = [tile(k) for k in range(fine)]
    right = halves[:fine]
    low = [jnp.concatenate([tile(fine + k), halves[fine + k]], 0) for k in range(coarse)]
    ends = unbundle(tile(packed_tiles(fine, coarse) - 1), ACROSS, TO_WEST)
    return [field + [end] for field, end in zip((value, right, low), ends)]


def down_kernel(parts, sweeps_hbm, target, grad_x, grad_y, labels, *refs):
    sent = 5 if parts == 2 else 0
    value_ref, right_ref, coarse_ref = refs[:3]
    sent_refs = refs[3:3 + sent]
    sweeps, target_v, grad_x_v, grad_y_v, labels_v, v_ref, b_ref, scaled_ref, resid_ref, sems = refs[3 + sent:]
    chans, rows, cols = target.shape
    window = value_ref.shape[2]
    count = window // SUBLANES
    place = lax.axis_index("lat")
    start = own_start(parts, place)
    inside = band_masks(window, parts, place, rows)
    scale = 1.0

    first_copies = [
        pltpu.make_async_copy(labels, labels_v, sems.at[chans, 0]),
        pltpu.make_async_copy(sweeps_hbm, sweeps, sems.at[chans, 1]),
    ]
    for copy in first_copies:
        copy.start()
    copies = []
    for chan in range(chans):
        copies.append([
            pltpu.make_async_copy(target.at[chan], target_v.at[chan], sems.at[chan, 0]),
            pltpu.make_async_copy(grad_x.at[:, chan], grad_x_v.at[:, chan], sems.at[chan, 1]),
            pltpu.make_async_copy(grad_y.at[:, chan], grad_y_v.at[:, chan], sems.at[chan, 2]),
        ])
        for copy in copies[-1]:
            copy.start()
    if window > rows:
        v_ref[...] = jnp.zeros_like(v_ref)
        b_ref[...] = jnp.zeros_like(b_ref)
    places = pairing()
    for copy in first_copies:
        copy.wait()

    def chosen(grad, chan):
        marks = labels_v[...]
        out = jnp.zeros((rows, cols), jnp.float32)
        for source in range(grad.shape[0]):
            out = jnp.where(marks == source, grad[source, chan], out)
        return out

    blank = jnp.zeros((rows, LANES), jnp.float32)
    fields = []
    for chan in range(chans):
        for copy in copies[chan]:
            copy.wait()
    for chan in range(chans):
        own = jnp.concatenate([target_v[chan], blank], 1)
        sel_x = jnp.concatenate([chosen(grad_x_v, chan), blank], 1)
        sel_y = jnp.concatenate([chosen(grad_y_v, chan), blank], 1)
        right = SCREENING * own - ((sel_x - west_of(sel_x)) + (sel_y - row_before(sel_y)))
        below = pltpu.roll(sel_y[rows - SUBLANES:], 1, 0)
        below = jnp.where(rows_of(below) == 0, below, 0.0)
        for k, (v, b, s) in enumerate(zip(tiles(own), tiles(right), tiles(below))):
            v_ref[chan, k, pl.ds(start, rows), :] = v
            b_ref[chan, k, pl.ds(start, rows), :] = b
            if window > rows:
                b_ref[chan, k, pl.ds(start + rows, SUBLANES), :] = s
    for chan in range(chans):
        fields.append(tuple(load_planes(v_ref.at[chan], 0, count, SUBLANES)))
        right = load_planes(b_ref.at[chan], 0, count, SUBLANES)
        if inside is not None:
            right = [b * mask for b, mask in zip(right, inside)]
        store_planes(right_ref.at[chan], 0, right)
        for t in range(count):
            scaled_ref[chan, t] = (DAMPING / diagonal(scale)) * right[t]

    def step(_, fields):
        return tuple(
            sweep(planes, [scaled_ref[chan, t] for t in range(count)], scale, inside) for chan, planes in enumerate(fields)
        )

    fields = lax.fori_loop(0, sweeps[0], step, tuple(fields))
    paired = []
    for chan, planes in enumerate(fields):
        store_planes(value_ref.at[chan], 0, planes)
        left = residual(planes, [(diagonal(scale) / DAMPING) * scaled_ref[chan, t] for t in range(count)], scale)
        if inside is not None:
            left = [r * mask for r, mask in zip(left, inside)]
        store_planes(resid_ref.at[chan], 0, left)
    for chan in range(chans):
        north, south = load_planes(resid_ref.at[chan], 0, 2, window // 2)
        paired.append(north + south)
    coarse = pair_columns(paired, places)
    for chan in range(chans):
        low = 0.25 * coarse[chan]
        coarse_ref[chan] = low
        if parts != 2:
            continue
        packed_ref, east_ref, east_across, west_ref, west_across = sent_refs
        wide = value_ref.shape[1]
        value = [value_ref[chan, k] for k in range(wide)]
        right = [right_ref[chan, k] for k in range(wide)]
        low = tiles(low)
        north = place == 0
        value_border = [jnp.where(north, v[12:20], v[4:12]) for v in value]
        right_border = [jnp.where(north, b[13:17], b[8:12]) for b in right]
        for k, tile in enumerate(pack(value_border, right_border, low)):
            packed_ref[chan, k] = tile
        for east, west, fields in (
            (east_ref, west_ref, (value, right, low)),
            (east_across, west_across, (value_border, right_border, low)),
        ):
            east[chan] = bundle([eastward(f[-2], f[-1]) for f in fields], TO_EAST)
            west[chan] = bundle([westward(f[0], f[-1]) for f in fields], TO_WEST)


def down(parts, sweeps, target, grad_x, grad_y, labels):
    chans, rows, cols = target.shape
    window = window_of(rows, parts)
    wide, half = cols // LANES + 1, cols // 2 // LANES + 1
    spare = SUBLANES if window > rows else 0
    outs = [F32((chans, wide, window, LANES))] * 2 + [F32((chans, window // 2, half * LANES))]
    if parts == 2:
        outs.append(F32((chans, packed_tiles(wide - 1, half - 1), SUBLANES, LANES)))
        outs += [F32((chans, SUBLANES, LANES))] * 4
    return pl.pallas_call(
        functools.partial(down_kernel, parts),
        in_specs=[HBM] * 5,
        out_specs=[VMEM] * len(outs),
        out_shape=outs,
        scratch_shapes=[
            pltpu.SMEM(sweeps.shape, jnp.int32),
            SCRATCH(target.shape),
            SCRATCH(grad_x.shape),
            SCRATCH(grad_y.shape),
            pltpu.VMEM(labels.shape, jnp.int32),
            SCRATCH((chans, wide, window + spare, LANES)),
            SCRATCH((chans, wide, window + spare, LANES)),
            SCRATCH((chans, window // SUBLANES, SUBLANES, wide * LANES)),
            SCRATCH((chans, wide, window, LANES)),
            pltpu.SemaphoreType.DMA((chans + 1, 3)),
        ],
        compiler_params=pltpu.CompilerParams(vmem_limit_bytes=32 * 2**20),
        name="down",
    )(*(in_hbm(a) for a in (sweeps, target, grad_x, grad_y, labels)))


def joined(place, own, other, height):
    gap = jnp.zeros((height - own.shape[0], own.shape[1]), jnp.float32)
    top, bottom = (lambda v: jnp.concatenate([v, gap], 0)), (lambda v: jnp.concatenate([gap, v], 0))
    return jnp.where(place == 0, top(own) + bottom(other), bottom(own) + top(other))


def up_kernel(parts, sweeps_hbm, value_ref, right_ref, coarse_ref, *refs):
    received = 5 if parts == 2 else 0
    packed_ref, *edge_refs = refs[:received] or [None]
    out_hbm, sweeps, v0_ref, b0_ref, k0_ref, b1_ref, k1_ref, k2_ref, fix_ref, out_ref, sems = refs[received:]
    sweeps_copy = pltpu.make_async_copy(sweeps_hbm, sweeps, sems.at[0])
    sweeps_copy.start()
    chans, rows, cols = out_ref.shape
    wide, window = value_ref.shape[1:3]
    half = coarse_ref.shape[2] // LANES
    full = parts * rows
    count0, count1, count2 = window // SUBLANES, max(1, full // 2 // SUBLANES), max(1, full // 4 // SUBLANES)
    place = lax.axis_index("lat")
    inside = band_masks(window, parts, place, rows)
    own_heights = (window, window, window // 2)

    def sides(chan, across):
        heights = ACROSS if across else own_heights
        from_west = unbundle(edge_refs[across][chan], heights, TO_EAST)
        from_east = unbundle(edge_refs[2 + across][chan], heights, TO_WEST)
        return list(zip(from_west, from_east))

    from_partner = []
    for chan in range(chans):
        low = coarse_ref[chan]
        if parts == 2:
            here, there = sides(chan, 0), sides(chan, 1)
            other = unpack(lambda k: packed_ref[chan, k], wide - 1, half - 1)
            value, right, other_low = (with_edges(f, *s) for f, s in zip(other, there))
            low = jnp.concatenate(with_edges(tiles(low), *here[2]), 1)
            low = joined(place, low, jnp.concatenate(other_low, 1), full // 2)
            for ref, own, side in ((v0_ref, value_ref, here[0]), (b0_ref, right_ref, here[1])):
                for k, tile in enumerate(with_edges([own[chan, k] for k in range(wide)], *side)):
                    ref[chan, k] = tile
            from_partner.append((value, right))
        else:
            v0_ref[chan] = value_ref[chan]
            b0_ref[chan] = right_ref[chan]
        for k, tile in enumerate(tiles(low)):
            b1_ref[chan, k] = tile

    def add_rows(value_at, right_at):
        for chan, (value, right) in enumerate(from_partner):
            for k in range(wide):
                v0_ref[chan, k, pl.ds(value_at, VALUE_ROWS), :] += value[k]
                b0_ref[chan, k, pl.ds(right_at, RIGHT_ROWS), :] += right[k]

    if parts == 2:
        pl.when(place == 0)(lambda: add_rows(12, 16))
        pl.when(place == 1)(lambda: add_rows(4, 5))

    def smoothed(fields, scaled_ref, count, scale):
        def step(_, fields):
            scaled = [[scaled_ref[i, t] for t in range(len(f))] for i, f in enumerate(fields)]
            return tuple(sweep(f, k, scale) for f, k in zip(fields, scaled))

        return lax.fori_loop(0, count, step, tuple(tuple(f) for f in fields))

    def from_zero(rights, scaled_ref, count, scale):
        first = [[(DAMPING / diagonal(scale)) * b for b in planes] for planes in rights]
        for i, planes in enumerate(first):
            for t, plane in enumerate(planes):
                scaled_ref[i, t] = plane
        return smoothed(first, scaled_ref, count - 1, scale)

    pair_places, spread_places = pairing(), spreading()
    height1 = full // 2 // count1
    right1 = [load_planes(b1_ref.at[i], 0, count1, height1) for i in range(chans)]
    sweeps_copy.wait()
    mid = from_zero(right1, k1_ref, sweeps[1], 0.25)
    left = [residual(f, load_planes(b1_ref.at[i], 0, count1, height1), 0.25) for i, f in enumerate(mid)]
    if count1 > 1:
        pairs = [f[t] + f[t + 1] for f in left for t in range(0, count1, 2)]
        low = [0.25 * v for v in pair_columns(pairs, pair_places)]
        right2 = [low[i * count2:(i + 1) * count2] for i in range(chans)]
    else:
        raise NotImplementedError("one part")
    fix2 = from_zero(right2, k2_ref, sweeps[2], 0.0625)
    mid = [[v + f for v, f in zip(planes, fix)] for planes, fix in zip(mid, prolong(fix2, spread_places))]
    mid = smoothed(mid, k1_ref, sweeps[1], 0.25)
    spare = (fix_ref.shape[2] - full) // 2
    if spare:
        fix_ref[...] = jnp.zeros_like(fix_ref)
    for i, fix in enumerate(prolong(mid, spread_places)):
        store_planes(fix_ref.at[i], spare, fix)
    shown = pl.multiple_of((SUBLANES if parts == 2 else rows) * place, SUBLANES)
    start = own_start(parts, place)
    fields = []
    for i in range(chans):
        planes = load_planes(v0_ref.at[i], 0, count0, SUBLANES)
        fix = load_planes(fix_ref.at[i], shown, count0, SUBLANES)
        fields.append(tuple(v + f for v, f in zip(planes, fix)))
        for t, b in enumerate(load_planes(b0_ref.at[i], 0, count0, SUBLANES)):
            k0_ref[i, t] = (DAMPING / diagonal(1.0)) * b

    def step(_, fields):
        return tuple(
            sweep(planes, [k0_ref[i, t] for t in range(count0)], 1.0, inside) for i, planes in enumerate(fields)
        )

    fields = lax.fori_loop(0, sweeps[0], step, tuple(fields))
    out_copies = []
    for i, planes in enumerate(fields):
        store_planes(v0_ref.at[i], 0, planes)
        for k in range(cols // LANES):
            out_ref[i, :, k * LANES:(k + 1) * LANES] = v0_ref[i, k, pl.ds(start, rows), :]
        out_copies.append(pltpu.make_async_copy(out_ref.at[i], out_hbm.at[i], sems.at[1 + i]))
        out_copies[-1].start()
    for copy in out_copies:
        copy.wait()


def up(parts, shape, sweeps, value, right, coarse, *received):
    chans, rows, cols = shape
    wide, window = value.shape[1:3]
    full = parts * rows
    half, quarter = cols // 2 // LANES + 1, cols // 4 // LANES + 1
    count1, count2 = max(1, full // 2 // SUBLANES), max(1, full // 4 // SUBLANES)
    spare = 2 * SUBLANES if parts > 2 else 0
    return pl.pallas_call(
        functools.partial(up_kernel, parts),
        in_specs=[HBM] + [VMEM] * (3 + len(received)),
        out_specs=HBM,
        out_shape=F32(shape),
        scratch_shapes=[
            pltpu.SMEM(sweeps.shape, jnp.int32),
            SCRATCH(value.shape),
            SCRATCH(value.shape),
            SCRATCH((chans, window // SUBLANES, SUBLANES, wide * LANES)),
            SCRATCH((chans, half, full // 2, LANES)),
            SCRATCH((chans, count1, full // 2 // count1, half * LANES)),
            SCRATCH((chans, count2, full // 4 // count2, quarter * LANES)),
            SCRATCH((chans, wide, full + spare, LANES)),
            SCRATCH(shape),
            pltpu.SemaphoreType.DMA((1 + chans,)),
        ],
        compiler_params=pltpu.CompilerParams(vmem_limit_bytes=48 * 2**20),
        name="up",
    )(in_hbm(sweeps), value, right, coarse, *received)


def local(target, grad_x, grad_y, labels, sweeps):
    parts, around_globe = lax.axis_size("lat"), lax.axis_size("lon")
    value, right, coarse, *sent = down(parts, sweeps, target, grad_x, grad_y, labels)
    eastward_pairs = [(i, (i + 1) % around_globe) for i in range(around_globe)]
    westward_pairs = [(j, i) for i, j in eastward_pairs]
    if parts == 2:
        def across(pairs):
            return [(2 * i + k, 2 * j + 1 - k) for i, j in pairs for k in range(2)]

        packed, east, east_across, west, west_across = sent
        packed = lax.ppermute(packed, "lat", [(0, 1), (1, 0)])
        from_west = lax.ppermute(east, "lon", eastward_pairs)
        across_west = lax.ppermute(east_across, ("lon", "lat"), across(eastward_pairs))
        from_east = lax.ppermute(west, "lon", westward_pairs)
        across_east = lax.ppermute(west_across, ("lon", "lat"), across(westward_pairs))
        received = (packed, from_west, across_west, from_east, across_east)
        return up(parts, target.shape, sweeps, value, right, coarse, *received)

    chans, half_rows = coarse.shape[:2]
    coarse = coarse.reshape(chans, half_rows, -1, LANES).transpose(0, 2, 1, 3)

    def shared_lon(field):
        parts_of = [field[:, k] for k in range(field.shape[1])]
        from_west = lax.ppermute(eastward(parts_of[-2], parts_of[-1]), "lon", eastward_pairs)
        from_east = lax.ppermute(westward(parts_of[0], parts_of[-1]), "lon", westward_pairs)
        return jnp.stack(with_edges(parts_of, from_west, from_east), 1)

    value, right, coarse = (shared_lon(f) for f in (value, right, coarse))
    if parts > 2:
        rows = target.shape[1]
        spare = 2 * SUBLANES
        southward = [(i, i + 1) for i in range(parts - 1)]
        northward = [(i + 1, i) for i in range(parts - 1)]

        def shared_lat(field):
            north = lax.ppermute(field[:, :, rows:], "lat", southward)
            south = lax.ppermute(field[:, :, :spare], "lat", northward)
            zeros = jnp.zeros_like(south)
            return field + jnp.concatenate([north, zeros], 2) + jnp.concatenate([zeros, south], 2)

        value, right = shared_lat(value), shared_lat(right)
        every = lax.all_gather(coarse, "lat")
        step = rows // 2
        total = jnp.zeros((chans, coarse.shape[1], parts * step + SUBLANES, LANES), jnp.float32)
        for i in range(parts):
            total = total.at[:, :, i * step:i * step + step + SUBLANES].add(every[i])
        coarse = total[:, :, 4:-4]
    coarse = coarse.transpose(0, 2, 1, 3).reshape(chans, coarse.shape[2], -1)
    return up(parts, target.shape, sweeps, value, right, coarse)


def solution(mesh):
    in_specs = (
        P(None, "lat", "lon"),
        P(None, None, "lat", "lon"),
        P(None, None, "lat", "lon"),
        P("lat", "lon"),
        P(),
    )
    out_specs = P(None, "lat", "lon")
    return jax.shard_map(local, mesh=mesh, in_specs=in_specs, out_specs=out_specs, check_vma=False)
```

```python
import functools

import jax
import jax.numpy as jnp
from jax import lax
from jax.experimental import pallas as pl
from jax.experimental.pallas import tpu as pltpu
from jax.sharding import PartitionSpec as P

SCREENING = 0.02
DAMPING = 0.8
LANES = 128
HALF = LANES // 2
SUBLANES = 8
VMEM = pl.BlockSpec(memory_space=pltpu.VMEM)
HBM = pl.BlockSpec(memory_space=pltpu.HBM)
F32 = functools.partial(jax.ShapeDtypeStruct, dtype=jnp.float32)
SCRATCH = functools.partial(pltpu.VMEM, dtype=jnp.float32)


def in_hbm(array):
    return pltpu.with_memory_space_constraint(array, pltpu.HBM)


def diagonal(scale):
    return SCREENING + 4.0 * scale


def rows_of(value):
    return lax.broadcasted_iota(jnp.int32, value.shape, 0)


def lanes_of(tile):
    return lax.broadcasted_iota(jnp.int32, tile.shape, len(tile.shape) - 1)


def tiles(value):
    return [value[:, k * LANES:(k + 1) * LANES] for k in range(value.shape[1] // LANES)]


def row_before(value):
    return jnp.where(rows_of(value) == 0, 0.0, pltpu.roll(value, 1, 0))


def row_after(value):
    last = value.shape[0] - 1
    return jnp.where(rows_of(value) == last, 0.0, pltpu.roll(value, last, 0))


def norths(planes):
    return [row_before(planes[-1])] + list(planes[:-1])


def souths(planes):
    return list(planes[1:]) + [row_after(planes[0])]


def west_of(value):
    return pltpu.roll(value, 1, 1)


def east_of(value):
    return pltpu.roll(value, value.shape[1] - 1, 1)


def around(planes):
    return [
        (north + south) + (west_of(value) + east_of(value))
        for value, north, south in zip(planes, norths(planes), souths(planes))
    ]


def sweep(planes, scaled, scale, inside=None):
    beside = DAMPING * scale / diagonal(scale)
    totals = [beside * total for total in around(planes)]
    if scaled is not None:
        totals = [right + total for right, total in zip(scaled, totals)]
    planes = [(1.0 - DAMPING) * value + total for value, total in zip(planes, totals)]
    return tuple(planes if inside is None else [value * mask for value, mask in zip(planes, inside)])


def residual(planes, right, scale):
    return [b - diagonal(scale) * value + scale * total for value, b, total in zip(planes, right, around(planes))]


def load_planes(ref, start, count, height):
    def plane(first):
        rows = pl.ds(first, height, stride=count) if count > 1 else pl.ds(first, height)
        return jnp.concatenate([ref[k, rows, :] for k in range(ref.shape[0])], 1)

    return [plane(start + t) for t in range(count)]


def store_planes(ref, start, planes):
    count, height = len(planes), planes[0].shape[0]
    for t, plane in enumerate(planes):
        rows = pl.ds(start + t, height, stride=count) if count > 1 else pl.ds(start + t, height)
        for k, tile in enumerate(tiles(plane)):
            ref[k, rows, :] = tile


def places_of(shape, wanted):
    source = lax.broadcasted_iota(jnp.int32, shape, 0)
    target = lax.broadcasted_iota(jnp.int32, shape, 1)
    return wanted(source, target).astype(jnp.float32).astype(jnp.bfloat16)


def halo_coarse(fine):
    return jnp.where(fine < HALF, fine // 2, HALF + fine // 2)


def pairing():
    own = places_of((2 * LANES, LANES), lambda source, target: source // 2 == target)
    halo = places_of((LANES, LANES), lambda source, target: halo_coarse(source) == target)
    return own, halo


def spreading():
    own = places_of((2 * LANES, 2 * LANES), lambda source, target: source == target // 2 + LANES * (target % 2))
    halo = places_of((2 * LANES, LANES), lambda source, target: source == halo_coarse(target) + LANES * (target % 2))
    return own, halo


def moved(value, places):
    high = value.astype(jnp.bfloat16)
    low = (value - high.astype(jnp.float32)).astype(jnp.bfloat16)
    dot = functools.partial(jnp.dot, preferred_element_type=jnp.float32)
    return dot(high, places) + dot(low, places)


def moved_blocks(own_blocks, halo_blocks, places):
    rows, count = halo_blocks[0].shape[0], len(own_blocks[0])
    packed = moved(jnp.concatenate([block for blocks in own_blocks for block in blocks], 0), places[0])
    edges = moved(jnp.concatenate(halo_blocks, 0), places[1])
    out = []
    for i in range(len(own_blocks)):
        parts = [packed[(i * count + k) * rows:(i * count + k + 1) * rows] for k in range(count)]
        out.append(jnp.concatenate(parts + [edges[i * rows:(i + 1) * rows]], 1))
    return out


def pair_columns(fields, places):
    cols = fields[0].shape[1] - LANES
    width = 2 * LANES
    own = [[f[:, k * width:(k + 1) * width] for k in range(cols // width)] for f in fields]
    return moved_blocks(own, [f[:, cols:] for f in fields], places)


def spread_columns(fields, places):
    cut = [list(zip(tiles(0.75 * f + 0.25 * west_of(f)), tiles(0.75 * f + 0.25 * east_of(f)))) for f in fields]
    blocks = [[jnp.concatenate(both, 1) for both in field] for field in cut]
    return moved_blocks([b[:-1] for b in blocks], [b[-1] for b in blocks], places)


def prolong(fields, places):
    halves = [
        half
        for planes in fields
        for value, north, south in zip(planes, norths(planes), souths(planes))
        for half in (0.75 * value + 0.25 * north, 0.75 * value + 0.25 * south)
    ]
    spread = spread_columns(halves, places)
    count = 2 * len(fields[0])
    return [spread[i * count:(i + 1) * count] for i in range(len(fields))]


def window_of(rows, parts):
    return rows + (2 * SUBLANES if parts > 2 else SUBLANES if parts == 2 else 0)


def own_start(parts, place):
    return 0 if parts == 1 else pl.multiple_of(SUBLANES * place, SUBLANES) if parts == 2 else SUBLANES


def band_masks(window, parts, place, rows):
    if parts <= 2:
        return None
    count = window // SUBLANES
    first = place * rows - SUBLANES
    row = [first + t + count * lax.broadcasted_iota(jnp.int32, (SUBLANES, 1), 0) for t in range(count)]
    return [((r >= 0) & (r < parts * rows)).astype(jnp.float32) for r in row]


def eastward(own_last, halo):
    return jnp.where(lanes_of(halo) < HALF, halo, own_last)


def westward(own_first, halo):
    return jnp.where(lanes_of(halo) < HALF, own_first, halo)


def with_edges(parts, from_west, from_east):
    inner = lanes_of(from_west) < HALF
    first = parts[0] + jnp.where(inner, from_west, 0.0)
    last = parts[-2] + jnp.where(inner, 0.0, from_east)
    halo = parts[-1] + jnp.where(inner, from_east, from_west)
    return [first] + list(parts[1:-2]) + [last, halo]


COARSE_WIDTH, FINE_WIDTH = 32, 8
TO_EAST, TO_WEST = (-24, 0), (-8, -8)


def in_window(lane, start, width):
    start = start % LANES
    end = start + width
    return (lane >= start) & (lane < end) if end <= LANES else (lane >= start) | (lane < end - LANES)


def slots(heights, starts):
    out, at = [], 0
    for which, (rows, start, width) in enumerate(zip(heights, starts, (COARSE_WIDTH, FINE_WIDTH))):
        for first in range(0, rows, SUBLANES):
            out.append((which, first, min(SUBLANES, rows - first), start, width, at))
            at += width
    assert at <= LANES
    return out


def bundle(fields, starts):
    out = jnp.zeros((SUBLANES, LANES), jnp.float32)
    lane = lanes_of(out)
    for which, first, rows, start, width, at in slots([f.shape[0] for f in fields], starts):
        piece = fields[which][first:first + rows]
        if rows < SUBLANES:
            piece = jnp.concatenate([piece, jnp.zeros((SUBLANES - rows, LANES), jnp.float32)], 0)
        out = jnp.where(in_window(lane, at, width), pltpu.roll(piece, (at - start) % LANES, 1), out)
    return out


def unbundle(tile, heights, starts):
    lane = lanes_of(tile)
    pieces = [[] for _ in heights]
    for which, first, rows, start, width, at in slots(heights, starts):
        piece = jnp.where(in_window(lane, start, width), pltpu.roll(tile, (start - at) % LANES, 1), 0.0)
        pieces[which].append(piece[:rows])
    return [jnp.concatenate(p, 0) if len(p) > 1 else p[0] for p in pieces]


COARSE_ROWS, FINE_ROWS = 12, 8


def pack(coarse, fine):
    halves = [c[SUBLANES:] for c in coarse[:-1]]
    joined = [jnp.concatenate(halves[k:k + 2], 0) for k in range(0, len(halves), 2)]
    return fine + [c[:SUBLANES] for c in coarse[:-1]] + joined + [bundle([coarse[-1]], TO_WEST)]


def packed_tiles(coarse, fine):
    return fine + coarse + coarse // 2 + 1


def unpack_coarse(tile, coarse, fine):
    halves = []
    for k in range(fine + coarse, fine + coarse + coarse // 2):
        both = tile(k)
        halves += [both[:4], both[4:]]
    low = [jnp.concatenate([tile(fine + k), halves[k]], 0) for k in range(coarse)]
    return low + unbundle(tile(packed_tiles(coarse, fine) - 1), [COARSE_ROWS], TO_WEST)


def down_kernel(parts, sweeps_hbm, target, grad_x, grad_y, labels, *refs):
    sent = 5 if parts == 2 else 0
    fine_ref, coarse_ref = refs[:2]
    sent_refs = refs[2:2 + sent]
    sweeps, target_v, grad_x_v, grad_y_v, labels_v, v_ref, b_ref, scaled_ref, resid_ref, sems = refs[2 + sent:]
    chans, rows, cols = target.shape
    window = fine_ref.shape[2]
    count = window // SUBLANES
    place = lax.axis_index("lat")
    start = own_start(parts, place)
    inside = band_masks(window, parts, place, rows)
    scale = 1.0

    first_copies = [
        pltpu.make_async_copy(labels, labels_v, sems.at[chans, 0]),
        pltpu.make_async_copy(sweeps_hbm, sweeps, sems.at[chans, 1]),
    ]
    for copy in first_copies:
        copy.start()
    copies = []
    for chan in range(chans):
        copies.append([
            pltpu.make_async_copy(target.at[chan], target_v.at[chan], sems.at[chan, 0]),
            pltpu.make_async_copy(grad_x.at[:, chan], grad_x_v.at[:, chan], sems.at[chan, 1]),
            pltpu.make_async_copy(grad_y.at[:, chan], grad_y_v.at[:, chan], sems.at[chan, 2]),
        ])
        for copy in copies[-1]:
            copy.start()
    if window > rows:
        v_ref[...] = jnp.zeros_like(v_ref)
        b_ref[...] = jnp.zeros_like(b_ref)
    places = pairing()
    for copy in first_copies:
        copy.wait()

    def chosen(grad, chan):
        marks = labels_v[...]
        out = jnp.zeros((rows, cols), jnp.float32)
        for source in range(grad.shape[0]):
            out = jnp.where(marks == source, grad[source, chan], out)
        return out

    blank = jnp.zeros((rows, LANES), jnp.float32)
    fields = []
    for chan in range(chans):
        for copy in copies[chan]:
            copy.wait()
        own = jnp.concatenate([target_v[chan], blank], 1)
        sel_x = jnp.concatenate([chosen(grad_x_v, chan), blank], 1)
        sel_y = jnp.concatenate([chosen(grad_y_v, chan), blank], 1)
        right = SCREENING * own - ((sel_x - west_of(sel_x)) + (sel_y - row_before(sel_y)))
        below = pltpu.roll(sel_y[rows - SUBLANES:], 1, 0)
        below = jnp.where(rows_of(below) == 0, below, 0.0)
        for k, (v, b, s) in enumerate(zip(tiles(own), tiles(right), tiles(below))):
            v_ref[chan, k, pl.ds(start, rows), :] = v
            b_ref[chan, k, pl.ds(start, rows), :] = b
            if window > rows:
                b_ref[chan, k, pl.ds(start + rows, SUBLANES), :] = s
    for chan in range(chans):
        fields.append(tuple(load_planes(v_ref.at[chan], 0, count, SUBLANES)))
        right = load_planes(b_ref.at[chan], 0, count, SUBLANES)
        if inside is not None:
            right = [b * mask for b, mask in zip(right, inside)]
        for t in range(count):
            scaled_ref[chan, t] = (DAMPING / diagonal(scale)) * right[t]

    def step(_, fields):
        return tuple(
            sweep(planes, [scaled_ref[chan, t] for t in range(count)], scale, inside) for chan, planes in enumerate(fields)
        )

    fields = lax.fori_loop(0, sweeps[0], step, tuple(fields))
    paired = []
    for chan, planes in enumerate(fields):
        left = residual(planes, [(diagonal(scale) / DAMPING) * scaled_ref[chan, t] for t in range(count)], scale)
        if inside is not None:
            left = [r * mask for r, mask in zip(left, inside)]
        store_planes(resid_ref.at[chan], 0, left)
    for chan in range(chans):
        north, south = load_planes(resid_ref.at[chan], 0, 2, window // 2)
        paired.append(north + south)
    coarse = [0.25 * low for low in pair_columns(paired, places)]
    for chan in range(chans):
        coarse_ref[chan] = coarse[chan]
    fields = lax.fori_loop(0, sweeps[0], step, fields)
    for chan, planes in enumerate(fields):
        store_planes(fine_ref.at[chan], 0, planes)
    if parts != 2:
        return
    packed_ref, east_ref, east_across, west_ref, west_across = sent_refs
    wide = fine_ref.shape[1]
    for chan in range(chans):
        low = tiles(coarse[chan])
        over = [jnp.where(place == 0, fine_ref[chan, k, rows:], fine_ref[chan, k, :SUBLANES]) for k in range(wide)]
        for k, tile in enumerate(pack(low, over[:-1])):
            packed_ref[chan, k] = tile
        to_east, to_west = eastward(low[-2], low[-1]), westward(low[0], low[-1])
        beside = fine_ref[chan, wide - 1, pl.ds(start, rows), :]
        for ref, low_edge, fine_edge, starts in (
            (east_ref, to_east, beside, TO_EAST),
            (west_ref, to_west, beside, TO_WEST),
            (east_across, to_east, over[-1], TO_EAST),
            (west_across, to_west, over[-1], TO_WEST),
        ):
            ref[chan] = bundle([low_edge, fine_edge], starts)


def down(parts, sweeps, target, grad_x, grad_y, labels):
    chans, rows, cols = target.shape
    window = window_of(rows, parts)
    wide, half = cols // LANES + 1, cols // 2 // LANES + 1
    spare = SUBLANES if window > rows else 0
    outs = [F32((chans, wide, window, LANES)), F32((chans, window // 2, half * LANES))]
    if parts == 2:
        outs.append(F32((chans, packed_tiles(half - 1, wide - 1), SUBLANES, LANES)))
        outs += [F32((chans, SUBLANES, LANES))] * 4
    return pl.pallas_call(
        functools.partial(down_kernel, parts),
        in_specs=[HBM] * 5,
        out_specs=[VMEM] * len(outs),
        out_shape=outs,
        scratch_shapes=[
            pltpu.SMEM(sweeps.shape, jnp.int32),
            SCRATCH(target.shape),
            SCRATCH(grad_x.shape),
            SCRATCH(grad_y.shape),
            pltpu.VMEM(labels.shape, jnp.int32),
            SCRATCH((chans, wide, window + spare, LANES)),
            SCRATCH((chans, wide, window + spare, LANES)),
            SCRATCH((chans, window // SUBLANES, SUBLANES, wide * LANES)),
            SCRATCH((chans, wide, window, LANES)),
            pltpu.SemaphoreType.DMA((chans + 1, 3)),
        ],
        compiler_params=pltpu.CompilerParams(vmem_limit_bytes=32 * 2**20),
        name="down",
    )(*(in_hbm(a) for a in (sweeps, target, grad_x, grad_y, labels)))


def joined(place, own, other, height):
    gap = jnp.zeros((height - own.shape[0], own.shape[1]), jnp.float32)
    top, bottom = (lambda v: jnp.concatenate([v, gap], 0)), (lambda v: jnp.concatenate([gap, v], 0))
    return jnp.where(place == 0, top(own) + bottom(other), bottom(own) + top(other))


def up_kernel(parts, sweeps_hbm, fine_ref, coarse_ref, *refs):
    received = 5 if parts == 2 else 0
    packed_ref, *edge_refs = refs[:received] or [None]
    out_hbm, sweeps, b1_ref, k1_ref, k2_ref, fix_ref, out_ref, sems = refs[received:]
    sweeps_copy = pltpu.make_async_copy(sweeps_hbm, sweeps, sems.at[0])
    sweeps_copy.start()
    chans, rows, cols = out_ref.shape
    wide, half = cols // LANES, coarse_ref.shape[2] // LANES
    window = window_of(rows, parts)
    full = parts * rows
    count0, count1, count2 = window // SUBLANES, full // 2 // SUBLANES, full // 4 // SUBLANES
    place = lax.axis_index("lat")
    start = own_start(parts, place)
    inside = band_masks(window, parts, place, rows)

    def sides(chan, across):
        heights = (COARSE_ROWS, FINE_ROWS if across else rows)
        from_west = unbundle(edge_refs[across][chan], heights, TO_EAST)
        from_east = unbundle(edge_refs[2 + across][chan], heights, TO_WEST)
        return list(zip(from_west, from_east))

    def beside(parts_of, from_west, from_east):
        return [parts_of[0] + from_west] + parts_of[1:-1] + [parts_of[-1] + from_east]

    for chan in range(chans):
        low = coarse_ref[chan]
        fine = [fine_ref[chan, k, pl.ds(start, rows), :] for k in range(wide)]
        if parts == 2:
            here, there = sides(chan, 0), sides(chan, 1)
            other_low = with_edges(unpack_coarse(lambda k: packed_ref[chan, k], half - 1, wide), *there[0])
            low = jnp.concatenate(with_edges(tiles(low), *here[0]), 1)
            low = joined(place, low, jnp.concatenate(other_low, 1), full // 2)
            fine = beside(fine, *here[1])
            other = beside([packed_ref[chan, k] for k in range(wide)], *there[1])
        for k, tile in enumerate(tiles(low)):
            b1_ref[chan, k] = tile
        for k in range(wide):
            span = slice(k * LANES, (k + 1) * LANES)
            out_ref[chan, :, span] = fine[k]
            if parts == 2:
                out_ref[chan, pl.ds(SUBLANES - start, SUBLANES), span] += other[k]

    def smoothed(fields, scaled_ref, count, scale):
        def step(_, fields):
            scaled = [[scaled_ref[i, t] for t in range(len(f))] for i, f in enumerate(fields)]
            return tuple(sweep(f, k, scale) for f, k in zip(fields, scaled))

        return lax.fori_loop(0, count, step, tuple(tuple(f) for f in fields))

    def from_zero(rights, scaled_ref, count, scale):
        first = [[(DAMPING / diagonal(scale)) * b for b in planes] for planes in rights]
        for i, planes in enumerate(first):
            for t, plane in enumerate(planes):
                scaled_ref[i, t] = plane
        return smoothed(first, scaled_ref, count - 1, scale)

    pair_places, spread_places = pairing(), spreading()
    right1 = [load_planes(b1_ref.at[i], 0, count1, SUBLANES) for i in range(chans)]
    sweeps_copy.wait()
    mid = from_zero(right1, k1_ref, sweeps[1], 0.25)
    left = [residual(f, load_planes(b1_ref.at[i], 0, count1, SUBLANES), 0.25) for i, f in enumerate(mid)]
    pairs = [f[t] + f[t + 1] for f in left for t in range(0, count1, 2)]
    low = [0.25 * v for v in pair_columns(pairs, pair_places)]
    right2 = [low[i * count2:(i + 1) * count2] for i in range(chans)]
    fix2 = from_zero(right2, k2_ref, sweeps[2], 0.0625)
    mid = [[v + f for v, f in zip(planes, fix)] for planes, fix in zip(mid, prolong(fix2, spread_places))]
    mid = smoothed(mid, k1_ref, sweeps[1], 0.25)
    spare = (fix_ref.shape[2] - full) // 2
    if spare:
        fix_ref[...] = jnp.zeros_like(fix_ref)
    for i, fix in enumerate(prolong(mid, spread_places)):
        store_planes(fix_ref.at[i], spare, fix)
    shown = pl.multiple_of((SUBLANES if parts == 2 else rows) * place, SUBLANES)
    start = own_start(parts, place)
    fields = [tuple(load_planes(fix_ref.at[i], shown, count0, SUBLANES)) for i in range(chans)]

    def step(_, fields):
        return tuple(sweep(planes, None, 1.0, inside) for planes in fields)

    fields = lax.fori_loop(0, sweeps[0], step, tuple(fields))
    out_copies = []
    for i, planes in enumerate(fields):
        store_planes(fix_ref.at[i], 0, planes)
        for k in range(wide):
            out_ref[i, :, k * LANES:(k + 1) * LANES] += fix_ref[i, k, pl.ds(start, rows), :]
        out_copies.append(pltpu.make_async_copy(out_ref.at[i], out_hbm.at[i], sems.at[1 + i]))
        out_copies[-1].start()
    for copy in out_copies:
        copy.wait()


def up(parts, shape, sweeps, fine, coarse, *received):
    chans, rows, cols = shape
    full = parts * rows
    wide, half, quarter = cols // LANES + 1, cols // 2 // LANES + 1, cols // 4 // LANES + 1
    count1, count2 = full // 2 // SUBLANES, full // 4 // SUBLANES
    spare = 2 * SUBLANES if parts > 2 else 0
    return pl.pallas_call(
        functools.partial(up_kernel, parts),
        in_specs=[HBM] + [VMEM] * (2 + len(received)),
        out_specs=HBM,
        out_shape=F32(shape),
        scratch_shapes=[
            pltpu.SMEM(sweeps.shape, jnp.int32),
            SCRATCH((chans, half, full // 2, LANES)),
            SCRATCH((chans, count1, SUBLANES, half * LANES)),
            SCRATCH((chans, count2, SUBLANES, quarter * LANES)),
            SCRATCH((chans, wide, full + spare, LANES)),
            SCRATCH(shape),
            pltpu.SemaphoreType.DMA((1 + chans,)),
        ],
        compiler_params=pltpu.CompilerParams(vmem_limit_bytes=48 * 2**20),
        name="up",
    )(in_hbm(sweeps), fine, coarse, *received)


def local(target, grad_x, grad_y, labels, sweeps):
    parts, around_globe = lax.axis_size("lat"), lax.axis_size("lon")
    if parts < 2:
        raise NotImplementedError
    fine, coarse, *sent = down(parts, sweeps, target, grad_x, grad_y, labels)
    eastward_pairs = [(i, (i + 1) % around_globe) for i in range(around_globe)]
    westward_pairs = [(j, i) for i, j in eastward_pairs]
    if parts == 2:
        def across(pairs):
            return [(2 * i + k, 2 * j + 1 - k) for i, j in pairs for k in range(2)]

        packed, east, east_across, west, west_across = sent
        packed = lax.ppermute(packed, "lat", [(0, 1), (1, 0)])
        from_west = lax.ppermute(east, "lon", eastward_pairs)
        across_west = lax.ppermute(east_across, ("lon", "lat"), across(eastward_pairs))
        from_east = lax.ppermute(west, "lon", westward_pairs)
        across_east = lax.ppermute(west_across, ("lon", "lat"), across(westward_pairs))
        received = (packed, from_west, across_west, from_east, across_east)
        return up(parts, target.shape, sweeps, fine, coarse, *received)

    chans, half_rows = coarse.shape[:2]
    coarse = coarse.reshape(chans, half_rows, -1, LANES).transpose(0, 2, 1, 3)

    def shared_lon(field):
        parts_of = [field[:, k] for k in range(field.shape[1])]
        from_west = lax.ppermute(eastward(parts_of[-2], parts_of[-1]), "lon", eastward_pairs)
        from_east = lax.ppermute(westward(parts_of[0], parts_of[-1]), "lon", westward_pairs)
        return jnp.stack(with_edges(parts_of, from_west, from_east), 1)

    fine, coarse = shared_lon(fine), shared_lon(coarse)
    rows = target.shape[1]
    spare = 2 * SUBLANES
    southward = [(i, i + 1) for i in range(parts - 1)]
    northward = [(i + 1, i) for i in range(parts - 1)]
    north = lax.ppermute(fine[:, :, rows:], "lat", southward)
    south = lax.ppermute(fine[:, :, :spare], "lat", northward)
    zeros = jnp.zeros_like(south)
    fine = fine + jnp.concatenate([north, zeros], 2) + jnp.concatenate([zeros, south], 2)
    every = lax.all_gather(coarse, "lat")
    step = rows // 2
    total = jnp.zeros((chans, coarse.shape[1], parts * step + SUBLANES, LANES), jnp.float32)
    for i in range(parts):
        total = total.at[:, :, i * step:i * step + step + SUBLANES].add(every[i])
    coarse = total[:, :, 4:-4].transpose(0, 2, 1, 3).reshape(chans, parts * step, -1)
    return up(parts, target.shape, sweeps, fine, coarse)


def solution(mesh):
    in_specs = (
        P(None, "lat", "lon"),
        P(None, None, "lat", "lon"),
        P(None, None, "lat", "lon"),
        P("lat", "lon"),
        P(),
    )
    out_specs = P(None, "lat", "lon")
    return jax.shard_map(local, mesh=mesh, in_specs=in_specs, out_specs=out_specs, check_vma=False)
```

```python
import functools

import jax
import jax.numpy as jnp
from jax import lax
from jax.experimental import pallas as pl
from jax.experimental.pallas import tpu as pltpu
from jax.sharding import PartitionSpec as P

SCREENING = 0.02
DAMPING = 0.8
LANES = 128
HALF = LANES // 2
SUBLANES = 8
VMEM = pl.BlockSpec(memory_space=pltpu.VMEM)
HBM = pl.BlockSpec(memory_space=pltpu.HBM)
F32 = functools.partial(jax.ShapeDtypeStruct, dtype=jnp.float32)
SCRATCH = functools.partial(pltpu.VMEM, dtype=jnp.float32)


def in_hbm(array):
    return pltpu.with_memory_space_constraint(array, pltpu.HBM)


def diagonal(scale):
    return SCREENING + 4.0 * scale


def rows_of(value):
    return lax.broadcasted_iota(jnp.int32, value.shape, 0)


def lanes_of(tile):
    return lax.broadcasted_iota(jnp.int32, tile.shape, len(tile.shape) - 1)


def tiles(value):
    return [value[:, k * LANES:(k + 1) * LANES] for k in range(value.shape[1] // LANES)]


def row_before(value):
    return jnp.where(rows_of(value) == 0, 0.0, pltpu.roll(value, 1, 0))


def row_after(value):
    last = value.shape[0] - 1
    return jnp.where(rows_of(value) == last, 0.0, pltpu.roll(value, last, 0))


def norths(planes):
    return [row_before(planes[-1])] + list(planes[:-1])


def souths(planes):
    return list(planes[1:]) + [row_after(planes[0])]


def west_of(value):
    return pltpu.roll(value, 1, 1)


def east_of(value):
    return pltpu.roll(value, value.shape[1] - 1, 1)


def around(planes):
    return [
        (north + south) + (west_of(value) + east_of(value))
        for value, north, south in zip(planes, norths(planes), souths(planes))
    ]


def sweep(planes, scaled, scale, inside=None):
    beside = DAMPING * scale / diagonal(scale)
    planes = [
        (1.0 - DAMPING) * value + (right + beside * total) for value, right, total in zip(planes, scaled, around(planes))
    ]
    return tuple(planes if inside is None else [value * mask for value, mask in zip(planes, inside)])


def residual(planes, right, scale):
    return [b - diagonal(scale) * value + scale * total for value, b, total in zip(planes, right, around(planes))]


def load_planes(ref, start, count, height):
    def plane(first):
        rows = pl.ds(first, height, stride=count) if count > 1 else pl.ds(first, height)
        return jnp.concatenate([ref[k, rows, :] for k in range(ref.shape[0])], 1)

    return [plane(start + t) for t in range(count)]


def store_planes(ref, start, planes):
    count, height = len(planes), planes[0].shape[0]
    for t, plane in enumerate(planes):
        rows = pl.ds(start + t, height, stride=count) if count > 1 else pl.ds(start + t, height)
        for k, tile in enumerate(tiles(plane)):
            ref[k, rows, :] = tile


def places_of(shape, wanted):
    source = lax.broadcasted_iota(jnp.int32, shape, 0)
    target = lax.broadcasted_iota(jnp.int32, shape, 1)
    return wanted(source, target).astype(jnp.float32).astype(jnp.bfloat16)


def halo_coarse(fine):
    return jnp.where(fine < HALF, fine // 2, HALF + fine // 2)


def pairing():
    own = places_of((2 * LANES, LANES), lambda source, target: source // 2 == target)
    halo = places_of((LANES, LANES), lambda source, target: halo_coarse(source) == target)
    return own, halo


def spreading():
    own = places_of((2 * LANES, 2 * LANES), lambda source, target: source == target // 2 + LANES * (target % 2))
    halo = places_of((2 * LANES, LANES), lambda source, target: source == halo_coarse(target) + LANES * (target % 2))
    return own, halo


def moved(value, places):
    high = value.astype(jnp.bfloat16)
    low = (value - high.astype(jnp.float32)).astype(jnp.bfloat16)
    dot = functools.partial(jnp.dot, preferred_element_type=jnp.float32)
    return dot(high, places) + dot(low, places)


def moved_blocks(own_blocks, halo_blocks, places):
    rows, count = halo_blocks[0].shape[0], len(own_blocks[0])
    packed = moved(jnp.concatenate([block for blocks in own_blocks for block in blocks], 0), places[0])
    edges = moved(jnp.concatenate(halo_blocks, 0), places[1])
    out = []
    for i in range(len(own_blocks)):
        parts = [packed[(i * count + k) * rows:(i * count + k + 1) * rows] for k in range(count)]
        out.append(jnp.concatenate(parts + [edges[i * rows:(i + 1) * rows]], 1))
    return out


def pair_columns(fields, places):
    cols = fields[0].shape[1] - LANES
    width = 2 * LANES
    own = [[f[:, k * width:(k + 1) * width] for k in range(cols // width)] for f in fields]
    return moved_blocks(own, [f[:, cols:] for f in fields], places)


def spread_columns(fields, places):
    cut = [list(zip(tiles(0.75 * f + 0.25 * west_of(f)), tiles(0.75 * f + 0.25 * east_of(f)))) for f in fields]
    blocks = [[jnp.concatenate(both, 1) for both in field] for field in cut]
    return moved_blocks([b[:-1] for b in blocks], [b[-1] for b in blocks], places)


def prolong(fields, places):
    halves = [
        half
        for planes in fields
        for value, north, south in zip(planes, norths(planes), souths(planes))
        for half in (0.75 * value + 0.25 * north, 0.75 * value + 0.25 * south)
    ]
    spread = spread_columns(halves, places)
    count = 2 * len(fields[0])
    return [spread[i * count:(i + 1) * count] for i in range(len(fields))]


def window_of(rows, parts):
    return rows + (2 * SUBLANES if parts > 2 else SUBLANES if parts == 2 else 0)


def own_start(parts, place):
    return 0 if parts == 1 else pl.multiple_of(SUBLANES * place, SUBLANES) if parts == 2 else SUBLANES


def band_masks(window, parts, place, rows):
    if parts <= 2:
        return None
    count = window // SUBLANES
    first = place * rows - SUBLANES
    row = [first + t + count * lax.broadcasted_iota(jnp.int32, (SUBLANES, 1), 0) for t in range(count)]
    return [((r >= 0) & (r < parts * rows)).astype(jnp.float32) for r in row]


def eastward(own_last, halo):
    return jnp.where(lanes_of(halo) < HALF, halo, own_last)


def westward(own_first, halo):
    return jnp.where(lanes_of(halo) < HALF, own_first, halo)


def with_edges(parts, from_west, from_east):
    inner = lanes_of(from_west) < HALF
    first = parts[0] + jnp.where(inner, from_west, 0.0)
    last = parts[-2] + jnp.where(inner, 0.0, from_east)
    halo = parts[-1] + jnp.where(inner, from_east, from_west)
    return [first] + list(parts[1:-2]) + [last, halo]


COARSE_WIDTH, FINE_WIDTH, REACH = 32, 8, 4
TO_EAST, TO_WEST = -24, -8


def in_window(lane, start, width):
    start = start % LANES
    end = start + width
    return (lane >= start) & (lane < end) if end <= LANES else (lane >= start) | (lane < end - LANES)


def slots(value_rows, right_rows, coarse_rows, coarse_start):
    out, at = [], 0
    for which, rows, start, width in (
        (2, coarse_rows, coarse_start, COARSE_WIDTH),
        (0, value_rows, -REACH, FINE_WIDTH),
        (1, right_rows, -REACH, FINE_WIDTH),
    ):
        for first in range(0, rows, SUBLANES):
            out.append((which, first, min(SUBLANES, rows - first), start, width, at))
            at += width
    assert at <= LANES
    return out


def bundle(fields, coarse_start):
    out = jnp.zeros((SUBLANES, LANES), jnp.float32)
    lane = lanes_of(out)
    for which, first, rows, start, width, at in slots(*(f.shape[0] for f in fields), coarse_start):
        piece = fields[which][first:first + rows]
        if rows < SUBLANES:
            piece = jnp.concatenate([piece, jnp.zeros((SUBLANES - rows, LANES), jnp.float32)], 0)
        out = jnp.where(in_window(lane, at, width), pltpu.roll(piece, (at - start) % LANES, 1), out)
    return out


def unbundle(tile, heights, coarse_start):
    lane = lanes_of(tile)
    pieces = ([], [], [])
    for which, first, rows, start, width, at in slots(*heights, coarse_start):
        piece = jnp.where(in_window(lane, start, width), pltpu.roll(tile, (start - at) % LANES, 1), 0.0)
        pieces[which].append(piece[:rows])
    return [jnp.concatenate(p, 0) if len(p) > 1 else p[0] for p in pieces]


VALUE_ROWS, RIGHT_ROWS, COARSE_ROWS = 8, 4, 12
ACROSS = (VALUE_ROWS, RIGHT_ROWS, COARSE_ROWS)


def pack(value, right, coarse):
    halves = right[:-1] + [c[SUBLANES:] for c in coarse[:-1]]
    joined = [jnp.concatenate(halves[k:k + 2], 0) for k in range(0, len(halves), 2)]
    return value[:-1] + [c[:SUBLANES] for c in coarse[:-1]] + joined + [bundle([value[-1], right[-1], coarse[-1]], TO_WEST)]


def packed_tiles(fine, coarse):
    return fine + coarse + (fine + coarse) // 2 + 1


def unpack(tile, fine, coarse):
    halves = []
    for k in range(fine + coarse, fine + coarse + (fine + coarse) // 2):
        both = tile(k)
        halves += [both[:4], both[4:]]
    value = [tile(k) for k in range(fine)]
    right = halves[:fine]
    low = [jnp.concatenate([tile(fine + k), halves[fine + k]], 0) for k in range(coarse)]
    ends = unbundle(tile(packed_tiles(fine, coarse) - 1), ACROSS, TO_WEST)
    return [field + [end] for field, end in zip((value, right, low), ends)]


def down_kernel(parts, sweeps_hbm, target, grad_x, grad_y, labels, *refs):
    sent = 5 if parts == 2 else 0
    value_ref, right_ref, coarse_ref = refs[:3]
    sent_refs = refs[3:3 + sent]
    sweeps, target_v, grad_x_v, grad_y_v, labels_v, v_ref, b_ref, scaled_ref, resid_ref, sems = refs[3 + sent:]
    chans, rows, cols = target.shape
    window = value_ref.shape[2]
    count = window // SUBLANES
    place = lax.axis_index("lat")
    start = own_start(parts, place)
    inside = band_masks(window, parts, place, rows)
    scale = 1.0

    first_copies = [
        pltpu.make_async_copy(labels, labels_v, sems.at[chans, 0]),
        pltpu.make_async_copy(sweeps_hbm, sweeps, sems.at[chans, 1]),
    ]
    for copy in first_copies:
        copy.start()
    copies = []
    for chan in range(chans):
        copies.append([
            pltpu.make_async_copy(target.at[chan], target_v.at[chan], sems.at[chan, 0]),
            pltpu.make_async_copy(grad_x.at[:, chan], grad_x_v.at[:, chan], sems.at[chan, 1]),
            pltpu.make_async_copy(grad_y.at[:, chan], grad_y_v.at[:, chan], sems.at[chan, 2]),
        ])
        for copy in copies[-1]:
            copy.start()
    if window > rows:
        v_ref[...] = jnp.zeros_like(v_ref)
        b_ref[...] = jnp.zeros_like(b_ref)
    places = pairing()
    for copy in first_copies:
        copy.wait()

    def chosen(grad, chan):
        marks = labels_v[...]
        out = jnp.zeros((rows, cols), jnp.float32)
        for source in range(grad.shape[0]):
            out = jnp.where(marks == source, grad[source, chan], out)
        return out

    blank = jnp.zeros((rows, LANES), jnp.float32)
    fields = []
    for chan in range(chans):
        for copy in copies[chan]:
            copy.wait()
        own = jnp.concatenate([target_v[chan], blank], 1)
        sel_x = jnp.concatenate([chosen(grad_x_v, chan), blank], 1)
        sel_y = jnp.concatenate([chosen(grad_y_v, chan), blank], 1)
        right = SCREENING * own - ((sel_x - west_of(sel_x)) + (sel_y - row_before(sel_y)))
        below = pltpu.roll(sel_y[rows - SUBLANES:], 1, 0)
        below = jnp.where(rows_of(below) == 0, below, 0.0)
        for k, (v, b, s) in enumerate(zip(tiles(own), tiles(right), tiles(below))):
            v_ref[chan, k, pl.ds(start, rows), :] = v
            b_ref[chan, k, pl.ds(start, rows), :] = b
            if window > rows:
                b_ref[chan, k, pl.ds(start + rows, SUBLANES), :] = s
    for chan in range(chans):
        fields.append(tuple(load_planes(v_ref.at[chan], 0, count, SUBLANES)))
        right = load_planes(b_ref.at[chan], 0, count, SUBLANES)
        if inside is not None:
            right = [b * mask for b, mask in zip(right, inside)]
        store_planes(right_ref.at[chan], 0, right)
        for t in range(count):
            scaled_ref[chan, t] = (DAMPING / diagonal(scale)) * right[t]

    def step(_, fields):
        return tuple(
            sweep(planes, [scaled_ref[chan, t] for t in range(count)], scale, inside) for chan, planes in enumerate(fields)
        )

    fields = lax.fori_loop(0, sweeps[0], step, tuple(fields))
    paired = []
    for chan, planes in enumerate(fields):
        store_planes(value_ref.at[chan], 0, planes)
        left = residual(planes, [(diagonal(scale) / DAMPING) * scaled_ref[chan, t] for t in range(count)], scale)
        if inside is not None:
            left = [r * mask for r, mask in zip(left, inside)]
        store_planes(resid_ref.at[chan], 0, left)
    for chan in range(chans):
        north, south = load_planes(resid_ref.at[chan], 0, 2, window // 2)
        paired.append(north + south)
    coarse = pair_columns(paired, places)
    for chan in range(chans):
        low = 0.25 * coarse[chan]
        coarse_ref[chan] = low
        if parts != 2:
            continue
        packed_ref, east_across, east_ref, west_across, west_ref = sent_refs
        wide = value_ref.shape[1]
        value = [value_ref[chan, k] for k in range(wide)]
        right = [right_ref[chan, k] for k in range(wide)]
        low = tiles(low)
        north = place == 0
        value_border = [jnp.where(north, v[12:20], v[4:12]) for v in value]
        right_border = [jnp.where(north, b[13:17], b[8:12]) for b in right]
        for k, tile in enumerate(pack(value_border, right_border, low)):
            packed_ref[chan, k] = tile
        for east, west, fields in (
            (east_ref, west_ref, (value, right, low)),
            (east_across, west_across, (value_border, right_border, low)),
        ):
            east[chan] = bundle([eastward(f[-2], f[-1]) for f in fields], TO_EAST)
            west[chan] = bundle([westward(f[0], f[-1]) for f in fields], TO_WEST)


def down(parts, sweeps, target, grad_x, grad_y, labels):
    chans, rows, cols = target.shape
    window = window_of(rows, parts)
    wide, half = cols // LANES + 1, cols // 2 // LANES + 1
    spare = SUBLANES if window > rows else 0
    outs = [F32((chans, wide, window, LANES))] * 2 + [F32((chans, window // 2, half * LANES))]
    if parts == 2:
        outs.append(F32((chans, packed_tiles(wide - 1, half - 1), SUBLANES, LANES)))
        outs += [F32((chans, SUBLANES, LANES))] * 4
    return pl.pallas_call(
        functools.partial(down_kernel, parts),
        in_specs=[HBM] * 5,
        out_specs=[VMEM] * len(outs),
        out_shape=outs,
        scratch_shapes=[
            pltpu.SMEM(sweeps.shape, jnp.int32),
            SCRATCH(target.shape),
            SCRATCH(grad_x.shape),
            SCRATCH(grad_y.shape),
            pltpu.VMEM(labels.shape, jnp.int32),
            SCRATCH((chans, wide, window + spare, LANES)),
            SCRATCH((chans, wide, window + spare, LANES)),
            SCRATCH((chans, window // SUBLANES, SUBLANES, wide * LANES)),
            SCRATCH((chans, wide, window, LANES)),
            pltpu.SemaphoreType.DMA((chans + 1, 3)),
        ],
        compiler_params=pltpu.CompilerParams(vmem_limit_bytes=32 * 2**20),
        name="down",
    )(*(in_hbm(a) for a in (sweeps, target, grad_x, grad_y, labels)))


def joined(place, own, other, height):
    gap = jnp.zeros((height - own.shape[0], own.shape[1]), jnp.float32)
    top, bottom = (lambda v: jnp.concatenate([v, gap], 0)), (lambda v: jnp.concatenate([gap, v], 0))
    return jnp.where(place == 0, top(own) + bottom(other), bottom(own) + top(other))


def up_kernel(parts, sweeps_hbm, value_ref, right_ref, coarse_ref, *refs):
    received = 5 if parts == 2 else 0
    packed_ref, *edge_refs = refs[:received] or [None]
    out_hbm, sweeps, v0_ref, b0_ref, k0_ref, b1_ref, k1_ref, k2_ref, fix_ref, out_ref, sems = refs[received:]
    sweeps_copy = pltpu.make_async_copy(sweeps_hbm, sweeps, sems.at[0])
    sweeps_copy.start()
    chans, rows, cols = out_ref.shape
    wide, window = value_ref.shape[1:3]
    half = coarse_ref.shape[2] // LANES
    full = parts * rows
    count0, count1, count2 = window // SUBLANES, max(1, full // 2 // SUBLANES), max(1, full // 4 // SUBLANES)
    place = lax.axis_index("lat")
    inside = band_masks(window, parts, place, rows)
    own_heights = (window, window, window // 2)

    def sides(chan, across):
        heights = ACROSS if across else own_heights
        from_west = unbundle(edge_refs[1 - across][chan], heights, TO_EAST)
        from_east = unbundle(edge_refs[3 - across][chan], heights, TO_WEST)
        return list(zip(from_west, from_east))

    from_partner = []
    for chan in range(chans):
        low = coarse_ref[chan]
        if parts == 2:
            here, there = sides(chan, 0), sides(chan, 1)
            other = unpack(lambda k: packed_ref[chan, k], wide - 1, half - 1)
            value, right, other_low = (with_edges(f, *s) for f, s in zip(other, there))
            low = jnp.concatenate(with_edges(tiles(low), *here[2]), 1)
            low = joined(place, low, jnp.concatenate(other_low, 1), full // 2)
            for ref, own, side in ((v0_ref, value_ref, here[0]), (b0_ref, right_ref, here[1])):
                for k, tile in enumerate(with_edges([own[chan, k] for k in range(wide)], *side)):
                    ref[chan, k] = tile
            from_partner.append((value, right))
        else:
            v0_ref[chan] = value_ref[chan]
            b0_ref[chan] = right_ref[chan]
        for k, tile in enumerate(tiles(low)):
            b1_ref[chan, k] = tile

    def add_rows(value_at, right_at):
        for chan, (value, right) in enumerate(from_partner):
            for k in range(wide):
                v0_ref[chan, k, pl.ds(value_at, VALUE_ROWS), :] += value[k]
                b0_ref[chan, k, pl.ds(right_at, RIGHT_ROWS), :] += right[k]

    if parts == 2:
        pl.when(place == 0)(lambda: add_rows(12, 16))
        pl.when(place == 1)(lambda: add_rows(4, 5))

    def smoothed(fields, scaled_ref, count, scale):
        def step(_, fields):
            scaled = [[scaled_ref[i, t] for t in range(len(f))] for i, f in enumerate(fields)]
            return tuple(sweep(f, k, scale) for f, k in zip(fields, scaled))

        return lax.fori_loop(0, count, step, tuple(tuple(f) for f in fields))

    def from_zero(rights, scaled_ref, count, scale):
        first = [[(DAMPING / diagonal(scale)) * b for b in planes] for planes in rights]
        for i, planes in enumerate(first):
            for t, plane in enumerate(planes):
                scaled_ref[i, t] = plane
        return smoothed(first, scaled_ref, count - 1, scale)

    pair_places, spread_places = pairing(), spreading()
    height1 = full // 2 // count1
    right1 = [load_planes(b1_ref.at[i], 0, count1, height1) for i in range(chans)]
    sweeps_copy.wait()
    mid = from_zero(right1, k1_ref, sweeps[1], 0.25)
    left = [residual(f, load_planes(b1_ref.at[i], 0, count1, height1), 0.25) for i, f in enumerate(mid)]
    if count1 > 1:
        pairs = [f[t] + f[t + 1] for f in left for t in range(0, count1, 2)]
        low = [0.25 * v for v in pair_columns(pairs, pair_places)]
        right2 = [low[i * count2:(i + 1) * count2] for i in range(chans)]
    else:
        raise NotImplementedError("one part")
    fix2 = from_zero(right2, k2_ref, sweeps[2], 0.0625)
    mid = [[v + f for v, f in zip(planes, fix)] for planes, fix in zip(mid, prolong(fix2, spread_places))]
    mid = smoothed(mid, k1_ref, sweeps[1], 0.25)
    spare = (fix_ref.shape[2] - full) // 2
    if spare:
        fix_ref[...] = jnp.zeros_like(fix_ref)
    for i, fix in enumerate(prolong(mid, spread_places)):
        store_planes(fix_ref.at[i], spare, fix)
    shown = pl.multiple_of((SUBLANES if parts == 2 else rows) * place, SUBLANES)
    start = own_start(parts, place)
    fields = []
    for i in range(chans):
        planes = load_planes(v0_ref.at[i], 0, count0, SUBLANES)
        fix = load_planes(fix_ref.at[i], shown, count0, SUBLANES)
        fields.append(tuple(v + f for v, f in zip(planes, fix)))
        for t, b in enumerate(load_planes(b0_ref.at[i], 0, count0, SUBLANES)):
            k0_ref[i, t] = (DAMPING / diagonal(1.0)) * b

    def step(_, fields):
        return tuple(
            sweep(planes, [k0_ref[i, t] for t in range(count0)], 1.0, inside) for i, planes in enumerate(fields)
        )

    fields = lax.fori_loop(0, sweeps[0], step, tuple(fields))
    out_copies = []
    for i, planes in enumerate(fields):
        store_planes(v0_ref.at[i], 0, planes)
        for k in range(cols // LANES):
            out_ref[i, :, k * LANES:(k + 1) * LANES] = v0_ref[i, k, pl.ds(start, rows), :]
        out_copies.append(pltpu.make_async_copy(out_ref.at[i], out_hbm.at[i], sems.at[1 + i]))
        out_copies[-1].start()
    for copy in out_copies:
        copy.wait()


def up(parts, shape, sweeps, value, right, coarse, *received):
    chans, rows, cols = shape
    wide, window = value.shape[1:3]
    full = parts * rows
    half, quarter = cols // 2 // LANES + 1, cols // 4 // LANES + 1
    count1, count2 = max(1, full // 2 // SUBLANES), max(1, full // 4 // SUBLANES)
    spare = 2 * SUBLANES if parts > 2 else 0
    return pl.pallas_call(
        functools.partial(up_kernel, parts),
        in_specs=[HBM] + [VMEM] * (3 + len(received)),
        out_specs=HBM,
        out_shape=F32(shape),
        scratch_shapes=[
            pltpu.SMEM(sweeps.shape, jnp.int32),
            SCRATCH(value.shape),
            SCRATCH(value.shape),
            SCRATCH((chans, window // SUBLANES, SUBLANES, wide * LANES)),
            SCRATCH((chans, half, full // 2, LANES)),
            SCRATCH((chans, count1, full // 2 // count1, half * LANES)),
            SCRATCH((chans, count2, full // 4 // count2, quarter * LANES)),
            SCRATCH((chans, wide, full + spare, LANES)),
            SCRATCH(shape),
            pltpu.SemaphoreType.DMA((1 + chans,)),
        ],
        compiler_params=pltpu.CompilerParams(vmem_limit_bytes=48 * 2**20),
        name="up",
    )(in_hbm(sweeps), value, right, coarse, *received)


def local(target, grad_x, grad_y, labels, sweeps):
    parts, around_globe = lax.axis_size("lat"), lax.axis_size("lon")
    value, right, coarse, *sent = down(parts, sweeps, target, grad_x, grad_y, labels)
    eastward_pairs = [(i, (i + 1) % around_globe) for i in range(around_globe)]
    westward_pairs = [(j, i) for i, j in eastward_pairs]
    if parts < 2:
        raise NotImplementedError
    if parts == 2:
        def across(pairs):
            return [(2 * i + k, 2 * j + 1 - k) for i, j in pairs for k in range(2)]

        packed, east_across, east, west_across, west = sent
        packed = lax.ppermute(packed, "lat", [(0, 1), (1, 0)])
        across_west = lax.ppermute(east_across, ("lon", "lat"), across(eastward_pairs))
        from_west = lax.ppermute(east, "lon", eastward_pairs)
        across_east = lax.ppermute(west_across, ("lon", "lat"), across(westward_pairs))
        from_east = lax.ppermute(west, "lon", westward_pairs)
        received = (packed, across_west, from_west, across_east, from_east)
        return up(parts, target.shape, sweeps, value, right, coarse, *received)

    chans, half_rows = coarse.shape[:2]
    coarse = coarse.reshape(chans, half_rows, -1, LANES).transpose(0, 2, 1, 3)

    def shared_lon(field):
        parts_of = [field[:, k] for k in range(field.shape[1])]
        from_west = lax.ppermute(eastward(parts_of[-2], parts_of[-1]), "lon", eastward_pairs)
        from_east = lax.ppermute(westward(parts_of[0], parts_of[-1]), "lon", westward_pairs)
        return jnp.stack(with_edges(parts_of, from_west, from_east), 1)

    value, right, coarse = (shared_lon(f) for f in (value, right, coarse))
    if parts > 2:
        rows = target.shape[1]
        spare = 2 * SUBLANES
        southward = [(i, i + 1) for i in range(parts - 1)]
        northward = [(i + 1, i) for i in range(parts - 1)]

        def shared_lat(field):
            north = lax.ppermute(field[:, :, rows:], "lat", southward)
            south = lax.ppermute(field[:, :, :spare], "lat", northward)
            zeros = jnp.zeros_like(south)
            return field + jnp.concatenate([north, zeros], 2) + jnp.concatenate([zeros, south], 2)

        value, right = shared_lat(value), shared_lat(right)
        every = lax.all_gather(coarse, "lat")
        step = rows // 2
        total = jnp.zeros((chans, coarse.shape[1], parts * step + SUBLANES, LANES), jnp.float32)
        for i in range(parts):
            total = total.at[:, :, i * step:i * step + step + SUBLANES].add(every[i])
        coarse = total[:, :, 4:-4]
    coarse = coarse.transpose(0, 2, 1, 3).reshape(chans, coarse.shape[2], -1)
    return up(parts, target.shape, sweeps, value, right, coarse)


def solution(mesh):
    in_specs = (
        P(None, "lat", "lon"),
        P(None, None, "lat", "lon"),
        P(None, None, "lat", "lon"),
        P("lat", "lon"),
        P(),
    )
    out_specs = P(None, "lat", "lon")
    return jax.shard_map(local, mesh=mesh, in_specs=in_specs, out_specs=out_specs, check_vma=False)
```

```python
import functools

import jax
import jax.numpy as jnp
from jax import lax
from jax.experimental import pallas as pl
from jax.experimental.pallas import tpu as pltpu
from jax.sharding import PartitionSpec as P

SCREENING = 0.02
DAMPING = 0.8
LANES = 128
HALF = LANES // 2
SUBLANES = 8
VMEM = pl.BlockSpec(memory_space=pltpu.VMEM)
HBM = pl.BlockSpec(memory_space=pltpu.HBM)
F32 = functools.partial(jax.ShapeDtypeStruct, dtype=jnp.float32)
SCRATCH = functools.partial(pltpu.VMEM, dtype=jnp.float32)


def in_hbm(array):
    return pltpu.with_memory_space_constraint(array, pltpu.HBM)


def diagonal(scale):
    return SCREENING + 4.0 * scale


def rows_of(value):
    return lax.broadcasted_iota(jnp.int32, value.shape, 0)


def lanes_of(tile):
    return lax.broadcasted_iota(jnp.int32, tile.shape, len(tile.shape) - 1)


def tiles(value):
    return [value[:, k * LANES:(k + 1) * LANES] for k in range(value.shape[1] // LANES)]


def row_before(value):
    return jnp.where(rows_of(value) == 0, 0.0, pltpu.roll(value, 1, 0))


def row_after(value):
    last = value.shape[0] - 1
    return jnp.where(rows_of(value) == last, 0.0, pltpu.roll(value, last, 0))


def norths(planes):
    return [row_before(planes[-1])] + list(planes[:-1])


def souths(planes):
    return list(planes[1:]) + [row_after(planes[0])]


def west_of(value):
    return pltpu.roll(value, 1, 1)


def east_of(value):
    return pltpu.roll(value, value.shape[1] - 1, 1)


def neighbours(planes, combine):
    cut = [tiles(plane) for plane in planes]
    count, wide = len(cut), len(cut[0])
    lane = lanes_of(cut[0][0])
    out = []
    for t in range(count):
        westward = [None] * wide
        eastward = [None] * wide

        def rolled(known, k, shift):
            k %= wide
            if known[k] is None:
                known[k] = pltpu.roll(cut[t][k], shift, 1)
            return known[k]

        done = []
        for k in range(wide):
            north = cut[t - 1][k] if t else row_before(cut[-1][k])
            south = cut[t + 1][k] if t + 1 < count else row_after(cut[0][k])
            west = jnp.where(lane == 0, rolled(westward, k - 1, 1), rolled(westward, k, 1))
            east = jnp.where(lane == LANES - 1, rolled(eastward, k + 1, LANES - 1), rolled(eastward, k, LANES - 1))
            done.append(combine(t, k, cut[t][k], (north + south) + (west + east)))
        out.append(jnp.concatenate(done, 1))
    return out


def sweep(planes, scaled, scale, inside=None):
    beside = DAMPING * scale / diagonal(scale)

    def combine(t, k, value, total):
        value = (1.0 - DAMPING) * value + (scaled(t, k) + beside * total)
        return value if inside is None else value * inside[t]

    return tuple(neighbours(planes, combine))


def residual(planes, right, scale):
    return neighbours(planes, lambda t, k, value, total: right(t, k) - diagonal(scale) * value + scale * total)


def span(k):
    return slice(k * LANES, (k + 1) * LANES)


def load_planes(ref, start, count, height):
    def plane(first):
        rows = pl.ds(first, height, stride=count) if count > 1 else pl.ds(first, height)
        return jnp.concatenate([ref[k, rows, :] for k in range(ref.shape[0])], 1)

    return [plane(start + t) for t in range(count)]


def store_planes(ref, start, planes):
    count, height = len(planes), planes[0].shape[0]
    for t, plane in enumerate(planes):
        rows = pl.ds(start + t, height, stride=count) if count > 1 else pl.ds(start + t, height)
        for k, tile in enumerate(tiles(plane)):
            ref[k, rows, :] = tile


def places_of(shape, wanted):
    source = lax.broadcasted_iota(jnp.int32, shape, 0)
    target = lax.broadcasted_iota(jnp.int32, shape, 1)
    return wanted(source, target).astype(jnp.float32).astype(jnp.bfloat16)


def halo_coarse(fine):
    return jnp.where(fine < HALF, fine // 2, HALF + fine // 2)


def pairing():
    own = places_of((2 * LANES, LANES), lambda source, target: source // 2 == target)
    halo = places_of((LANES, LANES), lambda source, target: halo_coarse(source) == target)
    return own, halo


def spreading():
    own = places_of((2 * LANES, 2 * LANES), lambda source, target: source == target // 2 + LANES * (target % 2))
    halo = places_of((2 * LANES, LANES), lambda source, target: source == halo_coarse(target) + LANES * (target % 2))
    return own, halo


def moved(value, places):
    high = value.astype(jnp.bfloat16)
    low = (value - high.astype(jnp.float32)).astype(jnp.bfloat16)
    dot = functools.partial(jnp.dot, preferred_element_type=jnp.float32)
    return dot(high, places) + dot(low, places)


def moved_blocks(own_blocks, halo_blocks, places):
    rows, count = halo_blocks[0].shape[0], len(own_blocks[0])
    packed = moved(jnp.concatenate([block for blocks in own_blocks for block in blocks], 0), places[0])
    edges = moved(jnp.concatenate(halo_blocks, 0), places[1])
    out = []
    for i in range(len(own_blocks)):
        parts = [packed[(i * count + k) * rows:(i * count + k + 1) * rows] for k in range(count)]
        out.append(jnp.concatenate(parts + [edges[i * rows:(i + 1) * rows]], 1))
    return out


def pair_columns(fields, places):
    cols = fields[0].shape[1] - LANES
    width = 2 * LANES
    own = [[f[:, k * width:(k + 1) * width] for k in range(cols // width)] for f in fields]
    return moved_blocks(own, [f[:, cols:] for f in fields], places)


def spread_columns(fields, places):
    cut = [list(zip(tiles(0.75 * f + 0.25 * west_of(f)), tiles(0.75 * f + 0.25 * east_of(f)))) for f in fields]
    blocks = [[jnp.concatenate(both, 1) for both in field] for field in cut]
    return moved_blocks([b[:-1] for b in blocks], [b[-1] for b in blocks], places)


def prolong(fields, places):
    halves = [
        half
        for planes in fields
        for value, north, south in zip(planes, norths(planes), souths(planes))
        for half in (0.75 * value + 0.25 * north, 0.75 * value + 0.25 * south)
    ]
    spread = spread_columns(halves, places)
    count = 2 * len(fields[0])
    return [spread[i * count:(i + 1) * count] for i in range(len(fields))]


def window_of(rows, parts):
    return rows + (2 * SUBLANES if parts > 2 else SUBLANES if parts == 2 else 0)


def own_start(parts, place):
    return 0 if parts == 1 else pl.multiple_of(SUBLANES * place, SUBLANES) if parts == 2 else SUBLANES


def band_masks(window, parts, place, rows):
    if parts <= 2:
        return None
    count = window // SUBLANES
    first = place * rows - SUBLANES
    row = [first + t + count * lax.broadcasted_iota(jnp.int32, (SUBLANES, 1), 0) for t in range(count)]
    return [((r >= 0) & (r < parts * rows)).astype(jnp.float32) for r in row]


def eastward(own_last, halo):
    return jnp.where(lanes_of(halo) < HALF, halo, own_last)


def westward(own_first, halo):
    return jnp.where(lanes_of(halo) < HALF, own_first, halo)


def with_edges(parts, from_west, from_east):
    inner = lanes_of(from_west) < HALF
    first = parts[0] + jnp.where(inner, from_west, 0.0)
    last = parts[-2] + jnp.where(inner, 0.0, from_east)
    halo = parts[-1] + jnp.where(inner, from_east, from_west)
    return [first] + list(parts[1:-2]) + [last, halo]


COARSE_WIDTH, FINE_WIDTH, REACH = 32, 8, 4
TO_EAST, TO_WEST = -24, -8


def in_window(lane, start, width):
    start = start % LANES
    end = start + width
    return (lane >= start) & (lane < end) if end <= LANES else (lane >= start) | (lane < end - LANES)


def slots(value_rows, right_rows, coarse_rows, coarse_start):
    out, at = [], 0
    for which, rows, start, width in (
        (2, coarse_rows, coarse_start, COARSE_WIDTH),
        (0, value_rows, -REACH, FINE_WIDTH),
        (1, right_rows, -REACH, FINE_WIDTH),
    ):
        for first in range(0, rows, SUBLANES):
            out.append((which, first, min(SUBLANES, rows - first), start, width, at))
            at += width
    assert at <= LANES
    return out


def bundle(fields, coarse_start):
    out = jnp.zeros((SUBLANES, LANES), jnp.float32)
    lane = lanes_of(out)
    for which, first, rows, start, width, at in slots(*(f.shape[0] for f in fields), coarse_start):
        piece = fields[which][first:first + rows]
        if rows < SUBLANES:
            piece = jnp.concatenate([piece, jnp.zeros((SUBLANES - rows, LANES), jnp.float32)], 0)
        out = jnp.where(in_window(lane, at, width), pltpu.roll(piece, (at - start) % LANES, 1), out)
    return out


def unbundle(tile, heights, coarse_start):
    lane = lanes_of(tile)
    pieces = ([], [], [])
    for which, first, rows, start, width, at in slots(*heights, coarse_start):
        piece = jnp.where(in_window(lane, start, width), pltpu.roll(tile, (start - at) % LANES, 1), 0.0)
        pieces[which].append(piece[:rows])
    return [jnp.concatenate(p, 0) if len(p) > 1 else p[0] for p in pieces]


VALUE_ROWS, RIGHT_ROWS, COARSE_ROWS = 8, 4, 12
ACROSS = (VALUE_ROWS, RIGHT_ROWS, COARSE_ROWS)


def pack(value, right, coarse):
    halves = right[:-1] + [c[SUBLANES:] for c in coarse[:-1]]
    joined = [jnp.concatenate(halves[k:k + 2], 0) for k in range(0, len(halves), 2)]
    return value[:-1] + [c[:SUBLANES] for c in coarse[:-1]] + joined + [bundle([value[-1], right[-1], coarse[-1]], TO_WEST)]


def packed_tiles(fine, coarse):
    return fine + coarse + (fine + coarse) // 2 + 1


def unpack(tile, fine, coarse):
    halves = []
    for k in range(fine + coarse, fine + coarse + (fine + coarse) // 2):
        both = tile(k)
        halves += [both[:4], both[4:]]
    value = [tile(k) for k in range(fine)]
    right = halves[:fine]
    low = [jnp.concatenate([tile(fine + k), halves[fine + k]], 0) for k in range(coarse)]
    ends = unbundle(tile(packed_tiles(fine, coarse) - 1), ACROSS, TO_WEST)
    return [field + [end] for field, end in zip((value, right, low), ends)]


def down_kernel(parts, sweeps_hbm, target, grad_x, grad_y, labels, *refs):
    sent = 5 if parts == 2 else 0
    value_ref, right_ref, coarse_ref = refs[:3]
    sent_refs = refs[3:3 + sent]
    sweeps, target_v, grad_x_v, grad_y_v, labels_v, v_ref, b_ref, scaled_ref, resid_ref, sems = refs[3 + sent:]
    chans, rows, cols = target.shape
    window = value_ref.shape[2]
    count = window // SUBLANES
    place = lax.axis_index("lat")
    start = own_start(parts, place)
    inside = band_masks(window, parts, place, rows)
    scale = 1.0

    first_copies = [
        pltpu.make_async_copy(labels, labels_v, sems.at[chans, 0]),
        pltpu.make_async_copy(sweeps_hbm, sweeps, sems.at[chans, 1]),
    ]
    for copy in first_copies:
        copy.start()
    copies = []
    for chan in range(chans):
        copies.append([
            pltpu.make_async_copy(target.at[chan], target_v.at[chan], sems.at[chan, 0]),
            pltpu.make_async_copy(grad_x.at[:, chan], grad_x_v.at[:, chan], sems.at[chan, 1]),
            pltpu.make_async_copy(grad_y.at[:, chan], grad_y_v.at[:, chan], sems.at[chan, 2]),
        ])
        for copy in copies[-1]:
            copy.start()
    if window > rows:
        v_ref[...] = jnp.zeros_like(v_ref)
        b_ref[...] = jnp.zeros_like(b_ref)
    places = pairing()
    for copy in first_copies:
        copy.wait()

    def chosen(grad, chan):
        marks = labels_v[...]
        out = jnp.zeros((rows, cols), jnp.float32)
        for source in range(grad.shape[0]):
            out = jnp.where(marks == source, grad[source, chan], out)
        return out

    blank = jnp.zeros((rows, LANES), jnp.float32)
    fields = []
    for chan in range(chans):
        for copy in copies[chan]:
            copy.wait()
        own = jnp.concatenate([target_v[chan], blank], 1)
        sel_x = jnp.concatenate([chosen(grad_x_v, chan), blank], 1)
        sel_y = jnp.concatenate([chosen(grad_y_v, chan), blank], 1)
        right = SCREENING * own - ((sel_x - west_of(sel_x)) + (sel_y - row_before(sel_y)))
        below = pltpu.roll(sel_y[rows - SUBLANES:], 1, 0)
        below = jnp.where(rows_of(below) == 0, below, 0.0)
        for k, (v, b, s) in enumerate(zip(tiles(own), tiles(right), tiles(below))):
            v_ref[chan, k, pl.ds(start, rows), :] = v
            b_ref[chan, k, pl.ds(start, rows), :] = b
            if window > rows:
                b_ref[chan, k, pl.ds(start + rows, SUBLANES), :] = s
    for chan in range(chans):
        fields.append(tuple(load_planes(v_ref.at[chan], 0, count, SUBLANES)))
        right = load_planes(b_ref.at[chan], 0, count, SUBLANES)
        if inside is not None:
            right = [b * mask for b, mask in zip(right, inside)]
        store_planes(right_ref.at[chan], 0, right)
        for t in range(count):
            scaled_ref[chan, t] = (DAMPING / diagonal(scale)) * right[t]

    def step(_, fields):
        return tuple(
            sweep(planes, lambda t, k, chan=chan: scaled_ref[chan, t, :, span(k)], scale, inside)
            for chan, planes in enumerate(fields)
        )

    fields = lax.fori_loop(0, sweeps[0], step, tuple(fields))
    paired = []
    for chan, planes in enumerate(fields):
        store_planes(value_ref.at[chan], 0, planes)
        back = diagonal(scale) / DAMPING
        left = residual(planes, lambda t, k, chan=chan: back * scaled_ref[chan, t, :, span(k)], scale)
        if inside is not None:
            left = [r * mask for r, mask in zip(left, inside)]
        store_planes(resid_ref.at[chan], 0, left)
    for chan in range(chans):
        north, south = load_planes(resid_ref.at[chan], 0, 2, window // 2)
        paired.append(north + south)
    coarse = pair_columns(paired, places)
    for chan in range(chans):
        low = 0.25 * coarse[chan]
        coarse_ref[chan] = low
        if parts != 2:
            continue
        packed_ref, east_across, east_ref, west_across, west_ref = sent_refs
        wide = value_ref.shape[1]
        value = [value_ref[chan, k] for k in range(wide)]
        right = [right_ref[chan, k] for k in range(wide)]
        low = tiles(low)
        north = place == 0
        value_border = [jnp.where(north, v[12:20], v[4:12]) for v in value]
        right_border = [jnp.where(north, b[13:17], b[8:12]) for b in right]
        for k, tile in enumerate(pack(value_border, right_border, low)):
            packed_ref[chan, k] = tile
        for east, west, fields in (
            (east_ref, west_ref, (value, right, low)),
            (east_across, west_across, (value_border, right_border, low)),
        ):
            east[chan] = bundle([eastward(f[-2], f[-1]) for f in fields], TO_EAST)
            west[chan] = bundle([westward(f[0], f[-1]) for f in fields], TO_WEST)


def down(parts, sweeps, target, grad_x, grad_y, labels):
    chans, rows, cols = target.shape
    window = window_of(rows, parts)
    wide, half = cols // LANES + 1, cols // 2 // LANES + 1
    spare = SUBLANES if window > rows else 0
    outs = [F32((chans, wide, window, LANES))] * 2 + [F32((chans, window // 2, half * LANES))]
    if parts == 2:
        outs.append(F32((chans, packed_tiles(wide - 1, half - 1), SUBLANES, LANES)))
        outs += [F32((chans, SUBLANES, LANES))] * 4
    return pl.pallas_call(
        functools.partial(down_kernel, parts),
        in_specs=[HBM] * 5,
        out_specs=[VMEM] * len(outs),
        out_shape=outs,
        scratch_shapes=[
            pltpu.SMEM(sweeps.shape, jnp.int32),
            SCRATCH(target.shape),
            SCRATCH(grad_x.shape),
            SCRATCH(grad_y.shape),
            pltpu.VMEM(labels.shape, jnp.int32),
            SCRATCH((chans, wide, window + spare, LANES)),
            SCRATCH((chans, wide, window + spare, LANES)),
            SCRATCH((chans, window // SUBLANES, SUBLANES, wide * LANES)),
            SCRATCH((chans, wide, window, LANES)),
            pltpu.SemaphoreType.DMA((chans + 1, 3)),
        ],
        compiler_params=pltpu.CompilerParams(vmem_limit_bytes=32 * 2**20),
        name="down",
    )(*(in_hbm(a) for a in (sweeps, target, grad_x, grad_y, labels)))


def joined(place, own, other, height):
    gap = jnp.zeros((height - own.shape[0], own.shape[1]), jnp.float32)
    top, bottom = (lambda v: jnp.concatenate([v, gap], 0)), (lambda v: jnp.concatenate([gap, v], 0))
    return jnp.where(place == 0, top(own) + bottom(other), bottom(own) + top(other))


def up_kernel(parts, sweeps_hbm, value_ref, right_ref, coarse_ref, *refs):
    received = 5 if parts == 2 else 0
    packed_ref, *edge_refs = refs[:received] or [None]
    out_hbm, sweeps, v0_ref, b0_ref, k0_ref, b1_ref, k1_ref, k2_ref, fix_ref, out_ref, sems = refs[received:]
    sweeps_copy = pltpu.make_async_copy(sweeps_hbm, sweeps, sems.at[0])
    sweeps_copy.start()
    chans, rows, cols = out_ref.shape
    wide, window = value_ref.shape[1:3]
    half = coarse_ref.shape[2] // LANES
    full = parts * rows
    count0, count1, count2 = window // SUBLANES, max(1, full // 2 // SUBLANES), max(1, full // 4 // SUBLANES)
    place = lax.axis_index("lat")
    inside = band_masks(window, parts, place, rows)
    own_heights = (window, window, window // 2)

    def sides(chan, across):
        heights = ACROSS if across else own_heights
        from_west = unbundle(edge_refs[1 - across][chan], heights, TO_EAST)
        from_east = unbundle(edge_refs[3 - across][chan], heights, TO_WEST)
        return list(zip(from_west, from_east))

    from_partner = []
    for chan in range(chans):
        low = coarse_ref[chan]
        if parts == 2:
            here, there = sides(chan, 0), sides(chan, 1)
            other = unpack(lambda k: packed_ref[chan, k], wide - 1, half - 1)
            value, right, other_low = (with_edges(f, *s) for f, s in zip(other, there))
            low = jnp.concatenate(with_edges(tiles(low), *here[2]), 1)
            low = joined(place, low, jnp.concatenate(other_low, 1), full // 2)
            for ref, own, side in ((v0_ref, value_ref, here[0]), (b0_ref, right_ref, here[1])):
                for k, tile in enumerate(with_edges([own[chan, k] for k in range(wide)], *side)):
                    ref[chan, k] = tile
            from_partner.append((value, right))
        else:
            v0_ref[chan] = value_ref[chan]
            b0_ref[chan] = right_ref[chan]
        for k, tile in enumerate(tiles(low)):
            b1_ref[chan, k] = tile

    def add_rows(value_at, right_at):
        for chan, (value, right) in enumerate(from_partner):
            for k in range(wide):
                v0_ref[chan, k, pl.ds(value_at, VALUE_ROWS), :] += value[k]
                b0_ref[chan, k, pl.ds(right_at, RIGHT_ROWS), :] += right[k]

    if parts == 2:
        pl.when(place == 0)(lambda: add_rows(12, 16))
        pl.when(place == 1)(lambda: add_rows(4, 5))

    def smoothed(fields, scaled_ref, count, scale):
        def step(_, fields):
            return tuple(
                sweep(planes, lambda t, k, i=i: scaled_ref[i, t, :, span(k)], scale) for i, planes in enumerate(fields)
            )

        return lax.fori_loop(0, count, step, tuple(tuple(f) for f in fields))

    def from_zero(rights, scaled_ref, count, scale):
        first = [[(DAMPING / diagonal(scale)) * b for b in planes] for planes in rights]
        for i, planes in enumerate(first):
            for t, plane in enumerate(planes):
                scaled_ref[i, t] = plane
        return smoothed(first, scaled_ref, count - 1, scale)

    pair_places, spread_places = pairing(), spreading()
    height1 = full // 2 // count1
    right1 = [load_planes(b1_ref.at[i], 0, count1, height1) for i in range(chans)]
    sweeps_copy.wait()
    mid = from_zero(right1, k1_ref, sweeps[1], 0.25)
    back = diagonal(0.25) / DAMPING
    left = [residual(f, lambda t, k, i=i: back * k1_ref[i, t, :, span(k)], 0.25) for i, f in enumerate(mid)]
    pairs = [f[t] + f[t + 1] for f in left for t in range(0, count1, 2)]
    low = [0.25 * v for v in pair_columns(pairs, pair_places)]
    right2 = [low[i * count2:(i + 1) * count2] for i in range(chans)]
    fix2 = from_zero(right2, k2_ref, sweeps[2], 0.0625)
    mid = [[v + f for v, f in zip(planes, fix)] for planes, fix in zip(mid, prolong(fix2, spread_places))]
    mid = smoothed(mid, k1_ref, sweeps[1], 0.25)
    spare = (fix_ref.shape[2] - full) // 2
    if spare:
        fix_ref[...] = jnp.zeros_like(fix_ref)
    for i, fix in enumerate(prolong(mid, spread_places)):
        store_planes(fix_ref.at[i], spare, fix)
    shown = pl.multiple_of((SUBLANES if parts == 2 else rows) * place, SUBLANES)
    start = own_start(parts, place)
    fields = []
    for i in range(chans):
        planes = load_planes(v0_ref.at[i], 0, count0, SUBLANES)
        fix = load_planes(fix_ref.at[i], shown, count0, SUBLANES)
        fields.append(tuple(v + f for v, f in zip(planes, fix)))
        for t, b in enumerate(load_planes(b0_ref.at[i], 0, count0, SUBLANES)):
            k0_ref[i, t] = (DAMPING / diagonal(1.0)) * b

    def step(_, fields):
        return tuple(
            sweep(planes, lambda t, k, i=i: k0_ref[i, t, :, span(k)], 1.0, inside) for i, planes in enumerate(fields)
        )

    fields = lax.fori_loop(0, sweeps[0], step, tuple(fields))
    out_copies = []
    for i, planes in enumerate(fields):
        store_planes(v0_ref.at[i], 0, planes)
        for k in range(cols // LANES):
            out_ref[i, :, k * LANES:(k + 1) * LANES] = v0_ref[i, k, pl.ds(start, rows), :]
        out_copies.append(pltpu.make_async_copy(out_ref.at[i], out_hbm.at[i], sems.at[1 + i]))
        out_copies[-1].start()
    for copy in out_copies:
        copy.wait()


def up(parts, shape, sweeps, value, right, coarse, *received):
    chans, rows, cols = shape
    wide, window = value.shape[1:3]
    full = parts * rows
    half, quarter = cols // 2 // LANES + 1, cols // 4 // LANES + 1
    count1, count2 = max(1, full // 2 // SUBLANES), max(1, full // 4 // SUBLANES)
    spare = 2 * SUBLANES if parts > 2 else 0
    return pl.pallas_call(
        functools.partial(up_kernel, parts),
        in_specs=[HBM] + [VMEM] * (3 + len(received)),
        out_specs=HBM,
        out_shape=F32(shape),
        scratch_shapes=[
            pltpu.SMEM(sweeps.shape, jnp.int32),
            SCRATCH(value.shape),
            SCRATCH(value.shape),
            SCRATCH((chans, window // SUBLANES, SUBLANES, wide * LANES)),
            SCRATCH((chans, half, full // 2, LANES)),
            SCRATCH((chans, count1, full // 2 // count1, half * LANES)),
            SCRATCH((chans, count2, full // 4 // count2, quarter * LANES)),
            SCRATCH((chans, wide, full + spare, LANES)),
            SCRATCH(shape),
            pltpu.SemaphoreType.DMA((1 + chans,)),
        ],
        compiler_params=pltpu.CompilerParams(vmem_limit_bytes=48 * 2**20),
        name="up",
    )(in_hbm(sweeps), value, right, coarse, *received)


def local(target, grad_x, grad_y, labels, sweeps):
    parts, around_globe = lax.axis_size("lat"), lax.axis_size("lon")
    value, right, coarse, *sent = down(parts, sweeps, target, grad_x, grad_y, labels)
    eastward_pairs = [(i, (i + 1) % around_globe) for i in range(around_globe)]
    westward_pairs = [(j, i) for i, j in eastward_pairs]
    if parts < 2:
        raise NotImplementedError
    if parts == 2:
        def across(pairs):
            return [(2 * i + k, 2 * j + 1 - k) for i, j in pairs for k in range(2)]

        packed, east_across, east, west_across, west = sent
        packed = lax.ppermute(packed, "lat", [(0, 1), (1, 0)])
        across_west = lax.ppermute(east_across, ("lon", "lat"), across(eastward_pairs))
        from_west = lax.ppermute(east, "lon", eastward_pairs)
        across_east = lax.ppermute(west_across, ("lon", "lat"), across(westward_pairs))
        from_east = lax.ppermute(west, "lon", westward_pairs)
        received = (packed, across_west, from_west, across_east, from_east)
        return up(parts, target.shape, sweeps, value, right, coarse, *received)

    chans, half_rows = coarse.shape[:2]
    coarse = coarse.reshape(chans, half_rows, -1, LANES).transpose(0, 2, 1, 3)

    def shared_lon(field):
        parts_of = [field[:, k] for k in range(field.shape[1])]
        from_west = lax.ppermute(eastward(parts_of[-2], parts_of[-1]), "lon", eastward_pairs)
        from_east = lax.ppermute(westward(parts_of[0], parts_of[-1]), "lon", westward_pairs)
        return jnp.stack(with_edges(parts_of, from_west, from_east), 1)

    value, right, coarse = (shared_lon(f) for f in (value, right, coarse))
    if parts > 2:
        rows = target.shape[1]
        spare = 2 * SUBLANES
        southward = [(i, i + 1) for i in range(parts - 1)]
        northward = [(i + 1, i) for i in range(parts - 1)]

        def shared_lat(field):
            north = lax.ppermute(field[:, :, rows:], "lat", southward)
            south = lax.ppermute(field[:, :, :spare], "lat", northward)
            zeros = jnp.zeros_like(south)
            return field + jnp.concatenate([north, zeros], 2) + jnp.concatenate([zeros, south], 2)

        value, right = shared_lat(value), shared_lat(right)
        every = lax.all_gather(coarse, "lat")
        step = rows // 2
        total = jnp.zeros((chans, coarse.shape[1], parts * step + SUBLANES, LANES), jnp.float32)
        for i in range(parts):
            total = total.at[:, :, i * step:i * step + step + SUBLANES].add(every[i])
        coarse = total[:, :, 4:-4]
    coarse = coarse.transpose(0, 2, 1, 3).reshape(chans, coarse.shape[2], -1)
    return up(parts, target.shape, sweeps, value, right, coarse)


def solution(mesh):
    in_specs = (
        P(None, "lat", "lon"),
        P(None, None, "lat", "lon"),
        P(None, None, "lat", "lon"),
        P("lat", "lon"),
        P(),
    )
    out_specs = P(None, "lat", "lon")
    return jax.shard_map(local, mesh=mesh, in_specs=in_specs, out_specs=out_specs, check_vma=False)
```

```python
import functools

import jax
import jax.numpy as jnp
from jax import lax
from jax.experimental import pallas as pl
from jax.experimental.pallas import tpu as pltpu
from jax.sharding import PartitionSpec as P

SCREENING = 0.02
DAMPING = 0.8
LANES = 128
HALF = LANES // 2
SUBLANES = 8
VMEM = pl.BlockSpec(memory_space=pltpu.VMEM)
HBM = pl.BlockSpec(memory_space=pltpu.HBM)
F32 = functools.partial(jax.ShapeDtypeStruct, dtype=jnp.float32)
SCRATCH = functools.partial(pltpu.VMEM, dtype=jnp.float32)


def in_hbm(array):
    return pltpu.with_memory_space_constraint(array, pltpu.HBM)


def diagonal(scale):
    return SCREENING + 4.0 * scale


def rows_of(value):
    return lax.broadcasted_iota(jnp.int32, value.shape, 0)


def lanes_of(tile):
    return lax.broadcasted_iota(jnp.int32, tile.shape, len(tile.shape) - 1)


def tiles(value):
    return [value[:, k * LANES:(k + 1) * LANES] for k in range(value.shape[1] // LANES)]


def row_before(value):
    return jnp.where(rows_of(value) == 0, 0.0, pltpu.roll(value, 1, 0))


def row_after(value):
    last = value.shape[0] - 1
    return jnp.where(rows_of(value) == last, 0.0, pltpu.roll(value, last, 0))


def norths(planes):
    return [row_before(planes[-1])] + list(planes[:-1])


def souths(planes):
    return list(planes[1:]) + [row_after(planes[0])]


def west_of(value):
    return pltpu.roll(value, 1, 1)


def east_of(value):
    return pltpu.roll(value, value.shape[1] - 1, 1)


def neighbours(planes, combine):
    cut = [tiles(plane) for plane in planes]
    count, wide = len(cut), len(cut[0])
    lane = lanes_of(cut[0][0])
    out = []
    for t in range(count):
        westward = [None] * wide
        eastward = [None] * wide

        def rolled(known, k, shift):
            k %= wide
            if known[k] is None:
                known[k] = pltpu.roll(cut[t][k], shift, 1)
            return known[k]

        done = []
        for k in range(wide):
            north = cut[t - 1][k] if t else row_before(cut[-1][k])
            south = cut[t + 1][k] if t + 1 < count else row_after(cut[0][k])
            west = jnp.where(lane == 0, rolled(westward, k - 1, 1), rolled(westward, k, 1))
            east = jnp.where(lane == LANES - 1, rolled(eastward, k + 1, LANES - 1), rolled(eastward, k, LANES - 1))
            done.append(combine(t, k, cut[t][k], (north + south) + (west + east)))
        out.append(jnp.concatenate(done, 1))
    return out


def sweep(planes, scaled, scale, inside=None):
    beside = DAMPING * scale / diagonal(scale)

    def combine(t, k, value, total):
        value = (1.0 - DAMPING) * value + (scaled(t, k) + beside * total)
        return value if inside is None else value * inside[t]

    return tuple(neighbours(planes, combine))


def residual(planes, right, scale):
    return neighbours(planes, lambda t, k, value, total: right(t, k) - diagonal(scale) * value + scale * total)


def span(k):
    return slice(k * LANES, (k + 1) * LANES)


def load_planes(ref, start, count, height):
    def plane(first):
        rows = pl.ds(first, height, stride=count) if count > 1 else pl.ds(first, height)
        return jnp.concatenate([ref[k, rows, :] for k in range(ref.shape[0])], 1)

    return [plane(start + t) for t in range(count)]


def store_planes(ref, start, planes):
    count, height = len(planes), planes[0].shape[0]
    for t, plane in enumerate(planes):
        rows = pl.ds(start + t, height, stride=count) if count > 1 else pl.ds(start + t, height)
        for k, tile in enumerate(tiles(plane)):
            ref[k, rows, :] = tile


def places_of(shape, wanted):
    source = lax.broadcasted_iota(jnp.int32, shape, 0)
    target = lax.broadcasted_iota(jnp.int32, shape, 1)
    return wanted(source, target).astype(jnp.float32).astype(jnp.bfloat16)


def halo_coarse(fine):
    return jnp.where(fine < HALF, fine // 2, HALF + fine // 2)


def pairing():
    own = places_of((2 * LANES, LANES), lambda source, target: source // 2 == target)
    halo = places_of((LANES, LANES), lambda source, target: halo_coarse(source) == target)
    return own, halo


def spreading():
    own = places_of((2 * LANES, 2 * LANES), lambda source, target: source == target // 2 + LANES * (target % 2))
    halo = places_of((2 * LANES, LANES), lambda source, target: source == halo_coarse(target) + LANES * (target % 2))
    return own, halo


def moved(value, places):
    high = value.astype(jnp.bfloat16)
    low = (value - high.astype(jnp.float32)).astype(jnp.bfloat16)
    dot = functools.partial(jnp.dot, preferred_element_type=jnp.float32)
    return dot(high, places) + dot(low, places)


def moved_blocks(own_blocks, halo_blocks, places):
    rows, count = halo_blocks[0].shape[0], len(own_blocks[0])
    packed = moved(jnp.concatenate([block for blocks in own_blocks for block in blocks], 0), places[0])
    edges = moved(jnp.concatenate(halo_blocks, 0), places[1])
    out = []
    for i in range(len(own_blocks)):
        parts = [packed[(i * count + k) * rows:(i * count + k + 1) * rows] for k in range(count)]
        out.append(jnp.concatenate(parts + [edges[i * rows:(i + 1) * rows]], 1))
    return out


def pair_columns(fields, places):
    cols = fields[0].shape[1] - LANES
    width = 2 * LANES
    own = [[f[:, k * width:(k + 1) * width] for k in range(cols // width)] for f in fields]
    return moved_blocks(own, [f[:, cols:] for f in fields], places)


def spread_columns(fields, places):
    cut = [list(zip(tiles(0.75 * f + 0.25 * west_of(f)), tiles(0.75 * f + 0.25 * east_of(f)))) for f in fields]
    blocks = [[jnp.concatenate(both, 1) for both in field] for field in cut]
    return moved_blocks([b[:-1] for b in blocks], [b[-1] for b in blocks], places)


def prolong(fields, places):
    halves = [
        half
        for planes in fields
        for value, north, south in zip(planes, norths(planes), souths(planes))
        for half in (0.75 * value + 0.25 * north, 0.75 * value + 0.25 * south)
    ]
    spread = spread_columns(halves, places)
    count = 2 * len(fields[0])
    return [spread[i * count:(i + 1) * count] for i in range(len(fields))]


def window_of(rows, parts):
    return rows + (2 * SUBLANES if parts > 2 else SUBLANES if parts == 2 else 0)


def own_start(parts, place):
    return 0 if parts == 1 else pl.multiple_of(SUBLANES * place, SUBLANES) if parts == 2 else SUBLANES


def band_masks(window, parts, place, rows):
    if parts <= 2:
        return None
    count = window // SUBLANES
    first = place * rows - SUBLANES
    row = [first + t + count * lax.broadcasted_iota(jnp.int32, (SUBLANES, 1), 0) for t in range(count)]
    return [((r >= 0) & (r < parts * rows)).astype(jnp.float32) for r in row]


def eastward(own_last, halo):
    return jnp.where(lanes_of(halo) < HALF, halo, own_last)


def westward(own_first, halo):
    return jnp.where(lanes_of(halo) < HALF, own_first, halo)


def with_edges(parts, from_west, from_east):
    inner = lanes_of(from_west) < HALF
    first = parts[0] + jnp.where(inner, from_west, 0.0)
    last = parts[-2] + jnp.where(inner, 0.0, from_east)
    halo = parts[-1] + jnp.where(inner, from_east, from_west)
    return [first] + list(parts[1:-2]) + [last, halo]


COARSE_WIDTH, FINE_WIDTH, REACH = 32, 8, 4
TO_EAST, TO_WEST = -24, -8


def in_window(lane, start, width):
    start = start % LANES
    end = start + width
    return (lane >= start) & (lane < end) if end <= LANES else (lane >= start) | (lane < end - LANES)


def slots(value_rows, right_rows, coarse_rows, coarse_start):
    out, at = [], 0
    for which, rows, start, width in (
        (2, coarse_rows, coarse_start, COARSE_WIDTH),
        (0, value_rows, -REACH, FINE_WIDTH),
        (1, right_rows, -REACH, FINE_WIDTH),
    ):
        for first in range(0, rows, SUBLANES):
            out.append((which, first, min(SUBLANES, rows - first), start, width, at))
            at += width
    assert at <= LANES
    return out


def bundle(fields, coarse_start):
    out = jnp.zeros((SUBLANES, LANES), jnp.float32)
    lane = lanes_of(out)
    for which, first, rows, start, width, at in slots(*(f.shape[0] for f in fields), coarse_start):
        piece = fields[which][first:first + rows]
        if rows < SUBLANES:
            piece = jnp.concatenate([piece, jnp.zeros((SUBLANES - rows, LANES), jnp.float32)], 0)
        out = jnp.where(in_window(lane, at, width), pltpu.roll(piece, (at - start) % LANES, 1), out)
    return out


def unbundle(tile, heights, coarse_start):
    lane = lanes_of(tile)
    pieces = ([], [], [])
    for which, first, rows, start, width, at in slots(*heights, coarse_start):
        piece = jnp.where(in_window(lane, start, width), pltpu.roll(tile, (start - at) % LANES, 1), 0.0)
        pieces[which].append(piece[:rows])
    return [jnp.concatenate(p, 0) if len(p) > 1 else p[0] for p in pieces]


VALUE_ROWS, RIGHT_ROWS, COARSE_ROWS = 8, 4, 12
ACROSS = (VALUE_ROWS, RIGHT_ROWS, COARSE_ROWS)


def pack(value, right, coarse):
    halves = right[:-1] + [c[SUBLANES:] for c in coarse[:-1]]
    joined = [jnp.concatenate(halves[k:k + 2], 0) for k in range(0, len(halves), 2)]
    return value[:-1] + [c[:SUBLANES] for c in coarse[:-1]] + joined + [bundle([value[-1], right[-1], coarse[-1]], TO_WEST)]


def packed_tiles(fine, coarse):
    return fine + coarse + (fine + coarse) // 2 + 1


def unpack(tile, fine, coarse):
    halves = []
    for k in range(fine + coarse, fine + coarse + (fine + coarse) // 2):
        both = tile(k)
        halves += [both[:4], both[4:]]
    value = [tile(k) for k in range(fine)]
    right = halves[:fine]
    low = [jnp.concatenate([tile(fine + k), halves[fine + k]], 0) for k in range(coarse)]
    ends = unbundle(tile(packed_tiles(fine, coarse) - 1), ACROSS, TO_WEST)
    return [field + [end] for field, end in zip((value, right, low), ends)]


def down_kernel(parts, sweeps_hbm, target, grad_x, grad_y, labels, *refs):
    sent = 5 if parts == 2 else 0
    value_ref, right_ref, coarse_ref = refs[:3]
    sent_refs = refs[3:3 + sent]
    sweeps, target_v, grad_x_v, grad_y_v, labels_v, v_ref, b_ref, scaled_ref, resid_ref, sems = refs[3 + sent:]
    chans, rows, cols = target.shape
    window = value_ref.shape[2]
    count = window // SUBLANES
    place = lax.axis_index("lat")
    start = own_start(parts, place)
    inside = band_masks(window, parts, place, rows)
    scale = 1.0

    first_copies = [
        pltpu.make_async_copy(labels, labels_v, sems.at[chans, 0]),
        pltpu.make_async_copy(sweeps_hbm, sweeps, sems.at[chans, 1]),
    ]
    for copy in first_copies:
        copy.start()
    copies = []
    for chan in range(chans):
        copies.append([
            pltpu.make_async_copy(target.at[chan], target_v.at[chan], sems.at[chan, 0]),
            pltpu.make_async_copy(grad_x.at[:, chan], grad_x_v.at[:, chan], sems.at[chan, 1]),
            pltpu.make_async_copy(grad_y.at[:, chan], grad_y_v.at[:, chan], sems.at[chan, 2]),
        ])
        for copy in copies[-1]:
            copy.start()
    if window > rows:
        v_ref[...] = jnp.zeros_like(v_ref)
        b_ref[...] = jnp.zeros_like(b_ref)
    places = pairing()
    for copy in first_copies:
        copy.wait()

    def chosen(grad, chan):
        marks = labels_v[...]
        out = jnp.zeros((rows, cols), jnp.float32)
        for source in range(grad.shape[0]):
            out = jnp.where(marks == source, grad[source, chan], out)
        return out

    blank = jnp.zeros((rows, LANES), jnp.float32)
    fields = []
    for chan in range(chans):
        for copy in copies[chan]:
            copy.wait()
        own = jnp.concatenate([target_v[chan], blank], 1)
        sel_x = jnp.concatenate([chosen(grad_x_v, chan), blank], 1)
        sel_y = jnp.concatenate([chosen(grad_y_v, chan), blank], 1)
        right = SCREENING * own - ((sel_x - west_of(sel_x)) + (sel_y - row_before(sel_y)))
        below = pltpu.roll(sel_y[rows - SUBLANES:], 1, 0)
        below = jnp.where(rows_of(below) == 0, below, 0.0)
        for k, (v, b, s) in enumerate(zip(tiles(own), tiles(right), tiles(below))):
            v_ref[chan, k, pl.ds(start, rows), :] = v
            b_ref[chan, k, pl.ds(start, rows), :] = b
            if window > rows:
                b_ref[chan, k, pl.ds(start + rows, SUBLANES), :] = s
    for chan in range(chans):
        fields.append(tuple(load_planes(v_ref.at[chan], 0, count, SUBLANES)))
        right = load_planes(b_ref.at[chan], 0, count, SUBLANES)
        if inside is not None:
            right = [b * mask for b, mask in zip(right, inside)]
        store_planes(right_ref.at[chan], 0, right)
        for t in range(count):
            scaled_ref[chan, t] = (DAMPING / diagonal(scale)) * right[t]

    def step(_, fields):
        return tuple(
            sweep(planes, lambda t, k, chan=chan: scaled_ref[chan, t, :, span(k)], scale, inside)
            for chan, planes in enumerate(fields)
        )

    fields = lax.fori_loop(0, sweeps[0], step, tuple(fields))
    paired = []
    for chan, planes in enumerate(fields):
        store_planes(value_ref.at[chan], 0, planes)
        back = diagonal(scale) / DAMPING
        left = residual(planes, lambda t, k, chan=chan: back * scaled_ref[chan, t, :, span(k)], scale)
        if inside is not None:
            left = [r * mask for r, mask in zip(left, inside)]
        store_planes(resid_ref.at[chan], 0, left)
    for chan in range(chans):
        north, south = load_planes(resid_ref.at[chan], 0, 2, window // 2)
        paired.append(north + south)
    coarse = pair_columns(paired, places)
    for chan in range(chans):
        low = 0.25 * coarse[chan]
        coarse_ref[chan] = low
        if parts != 2:
            continue
        packed_ref, east_across, east_ref, west_across, west_ref = sent_refs
        wide = value_ref.shape[1]
        value = [value_ref[chan, k] for k in range(wide)]
        right = [right_ref[chan, k] for k in range(wide)]
        low = tiles(low)
        north = place == 0
        value_border = [jnp.where(north, v[12:20], v[4:12]) for v in value]
        right_border = [jnp.where(north, b[13:17], b[8:12]) for b in right]
        for k, tile in enumerate(pack(value_border, right_border, low)):
            packed_ref[chan, k] = tile
        for east, west, fields in (
            (east_ref, west_ref, (value, right, low)),
            (east_across, west_across, (value_border, right_border, low)),
        ):
            east[chan] = bundle([eastward(f[-2], f[-1]) for f in fields], TO_EAST)
            west[chan] = bundle([westward(f[0], f[-1]) for f in fields], TO_WEST)


def down(parts, sweeps, target, grad_x, grad_y, labels):
    chans, rows, cols = target.shape
    window = window_of(rows, parts)
    wide, half = cols // LANES + 1, cols // 2 // LANES + 1
    spare = SUBLANES if window > rows else 0
    outs = [F32((chans, wide, window, LANES))] * 2 + [F32((chans, window // 2, half * LANES))]
    if parts == 2:
        outs.append(F32((chans, packed_tiles(wide - 1, half - 1), SUBLANES, LANES)))
        outs += [F32((chans, SUBLANES, LANES))] * 4
    return pl.pallas_call(
        functools.partial(down_kernel, parts),
        in_specs=[HBM] * 5,
        out_specs=[VMEM] * len(outs),
        out_shape=outs,
        scratch_shapes=[
            pltpu.SMEM(sweeps.shape, jnp.int32),
            SCRATCH(target.shape),
            SCRATCH(grad_x.shape),
            SCRATCH(grad_y.shape),
            pltpu.VMEM(labels.shape, jnp.int32),
            SCRATCH((chans, wide, window + spare, LANES)),
            SCRATCH((chans, wide, window + spare, LANES)),
            SCRATCH((chans, window // SUBLANES, SUBLANES, wide * LANES)),
            SCRATCH((chans, wide, window, LANES)),
            pltpu.SemaphoreType.DMA((chans + 1, 3)),
        ],
        compiler_params=pltpu.CompilerParams(vmem_limit_bytes=32 * 2**20),
        name="down",
    )(*(in_hbm(a) for a in (sweeps, target, grad_x, grad_y, labels)))


def joined(place, own, other, height):
    gap = jnp.zeros((height - own.shape[0], own.shape[1]), jnp.float32)
    top, bottom = (lambda v: jnp.concatenate([v, gap], 0)), (lambda v: jnp.concatenate([gap, v], 0))
    return jnp.where(place == 0, top(own) + bottom(other), bottom(own) + top(other))


def up_kernel(parts, sweeps_hbm, value_ref, right_ref, coarse_ref, *refs):
    received = 7 if parts == 2 else 0
    packed_ref, *edge_refs = refs[:received] or [None]
    out_hbm, sweeps, v0_ref, b0_ref, k0_ref, b1_ref, k1_ref, k2_ref, fix_ref, out_ref, sems = refs[received:]
    sweeps_copy = pltpu.make_async_copy(sweeps_hbm, sweeps, sems.at[0])
    sweeps_copy.start()
    chans, rows, cols = out_ref.shape
    wide, window = value_ref.shape[1:3]
    half = coarse_ref.shape[2] // LANES
    full = parts * rows
    count0, count1, count2 = window // SUBLANES, max(1, full // 2 // SUBLANES), max(1, full // 4 // SUBLANES)
    place = lax.axis_index("lat")
    inside = band_masks(window, parts, place, rows)
    own_heights = (window, window, window // 2)

    def sides(chan, across):
        heights = ACROSS if across else own_heights
        from_west = unbundle(edge_refs[1 - across][chan], heights, TO_EAST)
        from_east = unbundle(edge_refs[3 - across][chan] + edge_refs[5 - across][chan], heights, TO_WEST)
        return list(zip(from_west, from_east))

    from_partner = []
    for chan in range(chans):
        low = coarse_ref[chan]
        if parts == 2:
            here, there = sides(chan, 0), sides(chan, 1)
            other = unpack(lambda k: packed_ref[chan, k], wide - 1, half - 1)
            value, right, other_low = (with_edges(f, *s) for f, s in zip(other, there))
            low = jnp.concatenate(with_edges(tiles(low), *here[2]), 1)
            low = joined(place, low, jnp.concatenate(other_low, 1), full // 2)
            for ref, own, side in ((v0_ref, value_ref, here[0]), (b0_ref, right_ref, here[1])):
                for k, tile in enumerate(with_edges([own[chan, k] for k in range(wide)], *side)):
                    ref[chan, k] = tile
            from_partner.append((value, right))
        else:
            v0_ref[chan] = value_ref[chan]
            b0_ref[chan] = right_ref[chan]
        for k, tile in enumerate(tiles(low)):
            b1_ref[chan, k] = tile

    def add_rows(value_at, right_at):
        for chan, (value, right) in enumerate(from_partner):
            for k in range(wide):
                v0_ref[chan, k, pl.ds(value_at, VALUE_ROWS), :] += value[k]
                b0_ref[chan, k, pl.ds(right_at, RIGHT_ROWS), :] += right[k]

    if parts == 2:
        pl.when(place == 0)(lambda: add_rows(12, 16))
        pl.when(place == 1)(lambda: add_rows(4, 5))

    def smoothed(fields, scaled_ref, count, scale):
        def step(_, fields):
            return tuple(
                sweep(planes, lambda t, k, i=i: scaled_ref[i, t, :, span(k)], scale) for i, planes in enumerate(fields)
            )

        return lax.fori_loop(0, count, step, tuple(tuple(f) for f in fields))

    def from_zero(rights, scaled_ref, count, scale):
        first = [[(DAMPING / diagonal(scale)) * b for b in planes] for planes in rights]
        for i, planes in enumerate(first):
            for t, plane in enumerate(planes):
                scaled_ref[i, t] = plane
        return smoothed(first, scaled_ref, count - 1, scale)

    pair_places, spread_places = pairing(), spreading()
    height1 = full // 2 // count1
    right1 = [load_planes(b1_ref.at[i], 0, count1, height1) for i in range(chans)]
    sweeps_copy.wait()
    mid = from_zero(right1, k1_ref, sweeps[1], 0.25)
    back = diagonal(0.25) / DAMPING
    left = [residual(f, lambda t, k, i=i: back * k1_ref[i, t, :, span(k)], 0.25) for i, f in enumerate(mid)]
    pairs = [f[t] + f[t + 1] for f in left for t in range(0, count1, 2)]
    low = [0.25 * v for v in pair_columns(pairs, pair_places)]
    right2 = [low[i * count2:(i + 1) * count2] for i in range(chans)]
    fix2 = from_zero(right2, k2_ref, sweeps[2], 0.0625)
    mid = [[v + f for v, f in zip(planes, fix)] for planes, fix in zip(mid, prolong(fix2, spread_places))]
    mid = smoothed(mid, k1_ref, sweeps[1], 0.25)
    spare = (fix_ref.shape[2] - full) // 2
    if spare:
        fix_ref[...] = jnp.zeros_like(fix_ref)
    for i, fix in enumerate(prolong(mid, spread_places)):
        store_planes(fix_ref.at[i], spare, fix)
    shown = pl.multiple_of((SUBLANES if parts == 2 else rows) * place, SUBLANES)
    start = own_start(parts, place)
    fields = []
    for i in range(chans):
        planes = load_planes(v0_ref.at[i], 0, count0, SUBLANES)
        fix = load_planes(fix_ref.at[i], shown, count0, SUBLANES)
        fields.append(tuple(v + f for v, f in zip(planes, fix)))
        for t, b in enumerate(load_planes(b0_ref.at[i], 0, count0, SUBLANES)):
            k0_ref[i, t] = (DAMPING / diagonal(1.0)) * b

    def step(_, fields):
        return tuple(
            sweep(planes, lambda t, k, i=i: k0_ref[i, t, :, span(k)], 1.0, inside) for i, planes in enumerate(fields)
        )

    fields = lax.fori_loop(0, sweeps[0], step, tuple(fields))
    out_copies = []
    for i, planes in enumerate(fields):
        store_planes(v0_ref.at[i], 0, planes)
        for k in range(cols // LANES):
            out_ref[i, :, k * LANES:(k + 1) * LANES] = v0_ref[i, k, pl.ds(start, rows), :]
        out_copies.append(pltpu.make_async_copy(out_ref.at[i], out_hbm.at[i], sems.at[1 + i]))
        out_copies[-1].start()
    for copy in out_copies:
        copy.wait()


def up(parts, shape, sweeps, value, right, coarse, *received):
    chans, rows, cols = shape
    wide, window = value.shape[1:3]
    full = parts * rows
    half, quarter = cols // 2 // LANES + 1, cols // 4 // LANES + 1
    count1, count2 = max(1, full // 2 // SUBLANES), max(1, full // 4 // SUBLANES)
    spare = 2 * SUBLANES if parts > 2 else 0
    return pl.pallas_call(
        functools.partial(up_kernel, parts),
        in_specs=[HBM] + [VMEM] * (3 + len(received)),
        out_specs=HBM,
        out_shape=F32(shape),
        scratch_shapes=[
            pltpu.SMEM(sweeps.shape, jnp.int32),
            SCRATCH(value.shape),
            SCRATCH(value.shape),
            SCRATCH((chans, window // SUBLANES, SUBLANES, wide * LANES)),
            SCRATCH((chans, half, full // 2, LANES)),
            SCRATCH((chans, count1, full // 2 // count1, half * LANES)),
            SCRATCH((chans, count2, full // 4 // count2, quarter * LANES)),
            SCRATCH((chans, wide, full + spare, LANES)),
            SCRATCH(shape),
            pltpu.SemaphoreType.DMA((1 + chans,)),
        ],
        compiler_params=pltpu.CompilerParams(vmem_limit_bytes=48 * 2**20),
        name="up",
    )(in_hbm(sweeps), value, right, coarse, *received)


def local(target, grad_x, grad_y, labels, sweeps):
    parts, around_globe = lax.axis_size("lat"), lax.axis_size("lon")
    value, right, coarse, *sent = down(parts, sweeps, target, grad_x, grad_y, labels)
    eastward_pairs = [(i, (i + 1) % around_globe) for i in range(around_globe)]
    westward_pairs = [(j, i) for i, j in eastward_pairs]
    if parts < 2:
        raise NotImplementedError
    if parts == 2:
        def across(pairs):
            return [(2 * i + k, 2 * j + 1 - k) for i, j in pairs for k in range(2)]

        packed, east_across, east, west_across, west = sent
        packed = lax.ppermute(packed, "lat", [(0, 1), (1, 0)])
        across_west = lax.ppermute(east_across, ("lon", "lat"), across(eastward_pairs))
        from_west = lax.ppermute(east, "lon", eastward_pairs)
        inner = [(i, j) for i, j in westward_pairs if i]
        around = [(i, j) for i, j in westward_pairs if not i]
        across_east = lax.ppermute(west_across, ("lon", "lat"), across(inner))
        from_east = lax.ppermute(west, "lon", inner)
        across_around = lax.ppermute(west_across, ("lon", "lat"), across(around))
        from_around = lax.ppermute(west, "lon", around)
        received = (packed, across_west, from_west, across_east, from_east, across_around, from_around)
        return up(parts, target.shape, sweeps, value, right, coarse, *received)

    chans, half_rows = coarse.shape[:2]
    coarse = coarse.reshape(chans, half_rows, -1, LANES).transpose(0, 2, 1, 3)

    def shared_lon(field):
        parts_of = [field[:, k] for k in range(field.shape[1])]
        from_west = lax.ppermute(eastward(parts_of[-2], parts_of[-1]), "lon", eastward_pairs)
        from_east = lax.ppermute(westward(parts_of[0], parts_of[-1]), "lon", westward_pairs)
        return jnp.stack(with_edges(parts_of, from_west, from_east), 1)

    value, right, coarse = (shared_lon(f) for f in (value, right, coarse))
    if parts > 2:
        rows = target.shape[1]
        spare = 2 * SUBLANES
        southward = [(i, i + 1) for i in range(parts - 1)]
        northward = [(i + 1, i) for i in range(parts - 1)]

        def shared_lat(field):
            north = lax.ppermute(field[:, :, rows:], "lat", southward)
            south = lax.ppermute(field[:, :, :spare], "lat", northward)
            zeros = jnp.zeros_like(south)
            return field + jnp.concatenate([north, zeros], 2) + jnp.concatenate([zeros, south], 2)

        value, right = shared_lat(value), shared_lat(right)
        every = lax.all_gather(coarse, "lat")
        step = rows // 2
        total = jnp.zeros((chans, coarse.shape[1], parts * step + SUBLANES, LANES), jnp.float32)
        for i in range(parts):
            total = total.at[:, :, i * step:i * step + step + SUBLANES].add(every[i])
        coarse = total[:, :, 4:-4]
    coarse = coarse.transpose(0, 2, 1, 3).reshape(chans, coarse.shape[2], -1)
    return up(parts, target.shape, sweeps, value, right, coarse)


def solution(mesh):
    in_specs = (
        P(None, "lat", "lon"),
        P(None, None, "lat", "lon"),
        P(None, None, "lat", "lon"),
        P("lat", "lon"),
        P(),
    )
    out_specs = P(None, "lat", "lon")
    return jax.shard_map(local, mesh=mesh, in_specs=in_specs, out_specs=out_specs, check_vma=False)
```

```python
import functools

import jax
import jax.numpy as jnp
from jax import lax
from jax.experimental import pallas as pl
from jax.experimental.pallas import tpu as pltpu
from jax.sharding import PartitionSpec as P

SCREENING = 0.02
DAMPING = 0.8
LEAST_SWEEPS = 2
LANES = 128
HALF = LANES // 2
SUBLANES = 8
VMEM = pl.BlockSpec(memory_space=pltpu.VMEM)
HBM = pl.BlockSpec(memory_space=pltpu.HBM)
F32 = functools.partial(jax.ShapeDtypeStruct, dtype=jnp.float32)
SCRATCH = functools.partial(pltpu.VMEM, dtype=jnp.float32)


def in_hbm(array):
    return pltpu.with_memory_space_constraint(array, pltpu.HBM)


def diagonal(scale):
    return SCREENING + 4.0 * scale


def rows_of(value):
    return lax.broadcasted_iota(jnp.int32, value.shape, 0)


def lanes_of(tile):
    return lax.broadcasted_iota(jnp.int32, tile.shape, len(tile.shape) - 1)


def tiles(value):
    return [value[:, k * LANES:(k + 1) * LANES] for k in range(value.shape[1] // LANES)]


def row_before(value):
    return jnp.where(rows_of(value) == 0, 0.0, pltpu.roll(value, 1, 0))


def row_after(value):
    last = value.shape[0] - 1
    return jnp.where(rows_of(value) == last, 0.0, pltpu.roll(value, last, 0))


def norths(planes):
    return [row_before(planes[-1])] + list(planes[:-1])


def souths(planes):
    return list(planes[1:]) + [row_after(planes[0])]


def west_of(value):
    return pltpu.roll(value, 1, 1)


def east_of(value):
    return pltpu.roll(value, value.shape[1] - 1, 1)


def neighbours(planes, combine):
    cut = [tiles(plane) for plane in planes]
    count, wide = len(cut), len(cut[0])
    lane = lanes_of(cut[0][0])
    out = []
    for t in range(count):
        westward = [None] * wide
        eastward = [None] * wide

        def rolled(known, k, shift):
            k %= wide
            if known[k] is None:
                known[k] = pltpu.roll(cut[t][k], shift, 1)
            return known[k]

        done = []
        for k in range(wide):
            north = cut[t - 1][k] if t else row_before(cut[-1][k])
            south = cut[t + 1][k] if t + 1 < count else row_after(cut[0][k])
            west = jnp.where(lane == 0, rolled(westward, k - 1, 1), rolled(westward, k, 1))
            east = jnp.where(lane == LANES - 1, rolled(eastward, k + 1, LANES - 1), rolled(eastward, k, LANES - 1))
            done.append(combine(t, k, cut[t][k], (north + south) + (west + east)))
        out.append(jnp.concatenate(done, 1))
    return out


def sweep(planes, scaled, scale, inside=None):
    beside = DAMPING * scale / diagonal(scale)

    def combine(t, k, value, total):
        value = (1.0 - DAMPING) * value + (scaled(t, k) + beside * total)
        return value if inside is None else value * inside[t]

    return tuple(neighbours(planes, combine))


def residual(planes, right, scale):
    return neighbours(planes, lambda t, k, value, total: right(t, k) - diagonal(scale) * value + scale * total)


def span(k):
    return slice(k * LANES, (k + 1) * LANES)


def repeat(step, sweeps, level, fields, written, ready=lambda: None):
    for i in range(written):
        fields = step(i, fields)
    ready()
    return lax.fori_loop(LEAST_SWEEPS, sweeps[level], step, fields)


def load_planes(ref, start, count, height):
    def plane(first):
        rows = pl.ds(first, height, stride=count) if count > 1 else pl.ds(first, height)
        return jnp.concatenate([ref[k, rows, :] for k in range(ref.shape[0])], 1)

    return [plane(start + t) for t in range(count)]


def store_planes(ref, start, planes):
    count, height = len(planes), planes[0].shape[0]
    for t, plane in enumerate(planes):
        rows = pl.ds(start + t, height, stride=count) if count > 1 else pl.ds(start + t, height)
        for k, tile in enumerate(tiles(plane)):
            ref[k, rows, :] = tile


def places_of(shape, wanted):
    source = lax.broadcasted_iota(jnp.int32, shape, 0)
    target = lax.broadcasted_iota(jnp.int32, shape, 1)
    return wanted(source, target).astype(jnp.float32).astype(jnp.bfloat16)


def halo_coarse(fine):
    return jnp.where(fine < HALF, fine // 2, HALF + fine // 2)


def pairing():
    own = places_of((2 * LANES, LANES), lambda source, target: source // 2 == target)
    halo = places_of((LANES, LANES), lambda source, target: halo_coarse(source) == target)
    return own, halo


def spreading():
    own = places_of((2 * LANES, 2 * LANES), lambda source, target: source == target // 2 + LANES * (target % 2))
    halo = places_of((2 * LANES, LANES), lambda source, target: source == halo_coarse(target) + LANES * (target % 2))
    return own, halo


def moved(value, places):
    high = value.astype(jnp.bfloat16)
    low = (value - high.astype(jnp.float32)).astype(jnp.bfloat16)
    dot = functools.partial(jnp.dot, preferred_element_type=jnp.float32)
    return dot(high, places) + dot(low, places)


def moved_blocks(own_blocks, halo_blocks, places):
    rows, count = halo_blocks[0].shape[0], len(own_blocks[0])
    packed = moved(jnp.concatenate([block for blocks in own_blocks for block in blocks], 0), places[0])
    edges = moved(jnp.concatenate(halo_blocks, 0), places[1])
    out = []
    for i in range(len(own_blocks)):
        parts = [packed[(i * count + k) * rows:(i * count + k + 1) * rows] for k in range(count)]
        out.append(jnp.concatenate(parts + [edges[i * rows:(i + 1) * rows]], 1))
    return out


def pair_columns(fields, places):
    cols = fields[0].shape[1] - LANES
    width = 2 * LANES
    own = [[f[:, k * width:(k + 1) * width] for k in range(cols // width)] for f in fields]
    return moved_blocks(own, [f[:, cols:] for f in fields], places)


def spread_columns(fields, places):
    cut = [list(zip(tiles(0.75 * f + 0.25 * west_of(f)), tiles(0.75 * f + 0.25 * east_of(f)))) for f in fields]
    blocks = [[jnp.concatenate(both, 1) for both in field] for field in cut]
    return moved_blocks([b[:-1] for b in blocks], [b[-1] for b in blocks], places)


def prolong(fields, places):
    halves = [
        half
        for planes in fields
        for value, north, south in zip(planes, norths(planes), souths(planes))
        for half in (0.75 * value + 0.25 * north, 0.75 * value + 0.25 * south)
    ]
    spread = spread_columns(halves, places)
    count = 2 * len(fields[0])
    return [spread[i * count:(i + 1) * count] for i in range(len(fields))]


def window_of(rows, parts):
    return rows + (2 * SUBLANES if parts > 2 else SUBLANES if parts == 2 else 0)


def own_start(parts, place):
    return 0 if parts == 1 else pl.multiple_of(SUBLANES * place, SUBLANES) if parts == 2 else SUBLANES


def band_masks(window, parts, place, rows):
    if parts <= 2:
        return None
    count = window // SUBLANES
    first = place * rows - SUBLANES
    row = [first + t + count * lax.broadcasted_iota(jnp.int32, (SUBLANES, 1), 0) for t in range(count)]
    return [((r >= 0) & (r < parts * rows)).astype(jnp.float32) for r in row]


def eastward(own_last, halo):
    return jnp.where(lanes_of(halo) < HALF, halo, own_last)


def westward(own_first, halo):
    return jnp.where(lanes_of(halo) < HALF, own_first, halo)


def with_edges(parts, from_west, from_east):
    inner = lanes_of(from_west) < HALF
    first = parts[0] + jnp.where(inner, from_west, 0.0)
    last = parts[-2] + jnp.where(inner, 0.0, from_east)
    halo = parts[-1] + jnp.where(inner, from_east, from_west)
    return [first] + list(parts[1:-2]) + [last, halo]


COARSE_WIDTH, FINE_WIDTH, REACH = 32, 8, 4
TO_EAST, TO_WEST = -24, -8


def in_window(lane, start, width):
    start = start % LANES
    end = start + width
    return (lane >= start) & (lane < end) if end <= LANES else (lane >= start) | (lane < end - LANES)


def slots(value_rows, right_rows, coarse_rows, coarse_start):
    out, at = [], 0
    for which, rows, start, width in (
        (2, coarse_rows, coarse_start, COARSE_WIDTH),
        (0, value_rows, -REACH, FINE_WIDTH),
        (1, right_rows, -REACH, FINE_WIDTH),
    ):
        for first in range(0, rows, SUBLANES):
            out.append((which, first, min(SUBLANES, rows - first), start, width, at))
            at += width
    assert at <= LANES
    return out


def bundle(fields, coarse_start):
    out = jnp.zeros((SUBLANES, LANES), jnp.float32)
    lane = lanes_of(out)
    for which, first, rows, start, width, at in slots(*(f.shape[0] for f in fields), coarse_start):
        piece = fields[which][first:first + rows]
        if rows < SUBLANES:
            piece = jnp.concatenate([piece, jnp.zeros((SUBLANES - rows, LANES), jnp.float32)], 0)
        out = jnp.where(in_window(lane, at, width), pltpu.roll(piece, (at - start) % LANES, 1), out)
    return out


def unbundle(tile, heights, coarse_start):
    lane = lanes_of(tile)
    pieces = ([], [], [])
    for which, first, rows, start, width, at in slots(*heights, coarse_start):
        piece = jnp.where(in_window(lane, start, width), pltpu.roll(tile, (start - at) % LANES, 1), 0.0)
        pieces[which].append(piece[:rows])
    return [jnp.concatenate(p, 0) if len(p) > 1 else p[0] for p in pieces]


VALUE_ROWS, RIGHT_ROWS, COARSE_ROWS = 8, 4, 12
ACROSS = (VALUE_ROWS, RIGHT_ROWS, COARSE_ROWS)


def pack(value, right, coarse):
    halves = right[:-1] + [c[SUBLANES:] for c in coarse[:-1]]
    joined = [jnp.concatenate(halves[k:k + 2], 0) for k in range(0, len(halves), 2)]
    return value[:-1] + [c[:SUBLANES] for c in coarse[:-1]] + joined + [bundle([value[-1], right[-1], coarse[-1]], TO_WEST)]


def packed_tiles(fine, coarse):
    return fine + coarse + (fine + coarse) // 2 + 1


def unpack(tile, fine, coarse):
    halves = []
    for k in range(fine + coarse, fine + coarse + (fine + coarse) // 2):
        both = tile(k)
        halves += [both[:4], both[4:]]
    value = [tile(k) for k in range(fine)]
    right = halves[:fine]
    low = [jnp.concatenate([tile(fine + k), halves[fine + k]], 0) for k in range(coarse)]
    ends = unbundle(tile(packed_tiles(fine, coarse) - 1), ACROSS, TO_WEST)
    return [field + [end] for field, end in zip((value, right, low), ends)]


def down_kernel(parts, sweeps_hbm, target, grad_x, grad_y, labels, *refs):
    sent = 5 if parts == 2 else 0
    value_ref, right_ref, coarse_ref = refs[:3]
    sent_refs = refs[3:3 + sent]
    sweeps, target_v, grad_x_v, grad_y_v, labels_v, v_ref, b_ref, scaled_ref, resid_ref, sems = refs[3 + sent:]
    chans, rows, cols = target.shape
    window = value_ref.shape[2]
    count = window // SUBLANES
    place = lax.axis_index("lat")
    start = own_start(parts, place)
    inside = band_masks(window, parts, place, rows)
    scale = 1.0

    first_copies = [
        pltpu.make_async_copy(labels, labels_v, sems.at[chans, 0]),
        pltpu.make_async_copy(sweeps_hbm, sweeps, sems.at[chans, 1]),
    ]
    for copy in first_copies:
        copy.start()
    copies = []
    for chan in range(chans):
        copies.append([
            pltpu.make_async_copy(target.at[chan], target_v.at[chan], sems.at[chan, 0]),
            pltpu.make_async_copy(grad_x.at[:, chan], grad_x_v.at[:, chan], sems.at[chan, 1]),
            pltpu.make_async_copy(grad_y.at[:, chan], grad_y_v.at[:, chan], sems.at[chan, 2]),
        ])
        for copy in copies[-1]:
            copy.start()
    if window > rows:
        v_ref[...] = jnp.zeros_like(v_ref)
        b_ref[...] = jnp.zeros_like(b_ref)
    places = pairing()
    for copy in first_copies:
        copy.wait()

    def chosen(grad, chan):
        marks = labels_v[...]
        out = jnp.zeros((rows, cols), jnp.float32)
        for source in range(grad.shape[0]):
            out = jnp.where(marks == source, grad[source, chan], out)
        return out

    blank = jnp.zeros((rows, LANES), jnp.float32)
    fields = []
    for chan in range(chans):
        for copy in copies[chan]:
            copy.wait()
        own = jnp.concatenate([target_v[chan], blank], 1)
        sel_x = jnp.concatenate([chosen(grad_x_v, chan), blank], 1)
        sel_y = jnp.concatenate([chosen(grad_y_v, chan), blank], 1)
        right = SCREENING * own - ((sel_x - west_of(sel_x)) + (sel_y - row_before(sel_y)))
        below = pltpu.roll(sel_y[rows - SUBLANES:], 1, 0)
        below = jnp.where(rows_of(below) == 0, below, 0.0)
        for k, (v, b, s) in enumerate(zip(tiles(own), tiles(right), tiles(below))):
            v_ref[chan, k, pl.ds(start, rows), :] = v
            b_ref[chan, k, pl.ds(start, rows), :] = b
            if window > rows:
                b_ref[chan, k, pl.ds(start + rows, SUBLANES), :] = s
    for chan in range(chans):
        fields.append(tuple(load_planes(v_ref.at[chan], 0, count, SUBLANES)))
        right = load_planes(b_ref.at[chan], 0, count, SUBLANES)
        if inside is not None:
            right = [b * mask for b, mask in zip(right, inside)]
        store_planes(right_ref.at[chan], 0, right)
        for t in range(count):
            scaled_ref[chan, t] = (DAMPING / diagonal(scale)) * right[t]

    def step(_, fields):
        return tuple(
            sweep(planes, lambda t, k, chan=chan: scaled_ref[chan, t, :, span(k)], scale, inside)
            for chan, planes in enumerate(fields)
        )

    fields = repeat(step, sweeps, 0, tuple(fields), LEAST_SWEEPS)
    paired = []
    for chan, planes in enumerate(fields):
        store_planes(value_ref.at[chan], 0, planes)
        back = diagonal(scale) / DAMPING
        left = residual(planes, lambda t, k, chan=chan: back * scaled_ref[chan, t, :, span(k)], scale)
        if inside is not None:
            left = [r * mask for r, mask in zip(left, inside)]
        store_planes(resid_ref.at[chan], 0, left)
    for chan in range(chans):
        north, south = load_planes(resid_ref.at[chan], 0, 2, window // 2)
        paired.append(north + south)
    coarse = pair_columns(paired, places)
    for chan in range(chans):
        low = 0.25 * coarse[chan]
        coarse_ref[chan] = low
        if parts != 2:
            continue
        packed_ref, east_across, east_ref, west_across, west_ref = sent_refs
        wide = value_ref.shape[1]
        value = [value_ref[chan, k] for k in range(wide)]
        right = [right_ref[chan, k] for k in range(wide)]
        low = tiles(low)
        north = place == 0
        value_border = [jnp.where(north, v[12:20], v[4:12]) for v in value]
        right_border = [jnp.where(north, b[13:17], b[8:12]) for b in right]
        for k, tile in enumerate(pack(value_border, right_border, low)):
            packed_ref[chan, k] = tile
        for east, west, fields in (
            (east_ref, west_ref, (value, right, low)),
            (east_across, west_across, (value_border, right_border, low)),
        ):
            east[chan] = bundle([eastward(f[-2], f[-1]) for f in fields], TO_EAST)
            west[chan] = bundle([westward(f[0], f[-1]) for f in fields], TO_WEST)


def down(parts, sweeps, target, grad_x, grad_y, labels):
    chans, rows, cols = target.shape
    window = window_of(rows, parts)
    wide, half = cols // LANES + 1, cols // 2 // LANES + 1
    spare = SUBLANES if window > rows else 0
    outs = [F32((chans, wide, window, LANES))] * 2 + [F32((chans, window // 2, half * LANES))]
    if parts == 2:
        outs.append(F32((chans, packed_tiles(wide - 1, half - 1), SUBLANES, LANES)))
        outs += [F32((chans, SUBLANES, LANES))] * 4
    return pl.pallas_call(
        functools.partial(down_kernel, parts),
        in_specs=[HBM] * 5,
        out_specs=[VMEM] * len(outs),
        out_shape=outs,
        scratch_shapes=[
            pltpu.SMEM(sweeps.shape, jnp.int32),
            SCRATCH(target.shape),
            SCRATCH(grad_x.shape),
            SCRATCH(grad_y.shape),
            pltpu.VMEM(labels.shape, jnp.int32),
            SCRATCH((chans, wide, window + spare, LANES)),
            SCRATCH((chans, wide, window + spare, LANES)),
            SCRATCH((chans, window // SUBLANES, SUBLANES, wide * LANES)),
            SCRATCH((chans, wide, window, LANES)),
            pltpu.SemaphoreType.DMA((chans + 1, 3)),
        ],
        compiler_params=pltpu.CompilerParams(vmem_limit_bytes=32 * 2**20),
        name="down",
    )(*(in_hbm(a) for a in (sweeps, target, grad_x, grad_y, labels)))


def joined(place, own, other, height):
    gap = jnp.zeros((height - own.shape[0], own.shape[1]), jnp.float32)
    top, bottom = (lambda v: jnp.concatenate([v, gap], 0)), (lambda v: jnp.concatenate([gap, v], 0))
    return jnp.where(place == 0, top(own) + bottom(other), bottom(own) + top(other))


def up_kernel(parts, sweeps_hbm, value_ref, right_ref, coarse_ref, *refs):
    received = 5 if parts == 2 else 0
    packed_ref, *edge_refs = refs[:received] or [None]
    out_hbm, sweeps, v0_ref, b0_ref, k0_ref, b1_ref, k1_ref, k2_ref, fix_ref, out_ref, sems = refs[received:]
    sweeps_copy = pltpu.make_async_copy(sweeps_hbm, sweeps, sems.at[0])
    sweeps_copy.start()
    chans, rows, cols = out_ref.shape
    wide, window = value_ref.shape[1:3]
    half = coarse_ref.shape[2] // LANES
    full = parts * rows
    count0, count1, count2 = window // SUBLANES, max(1, full // 2 // SUBLANES), max(1, full // 4 // SUBLANES)
    place = lax.axis_index("lat")
    inside = band_masks(window, parts, place, rows)
    own_heights = (window, window, window // 2)

    def sides(chan, across):
        heights = ACROSS if across else own_heights
        from_west = unbundle(edge_refs[1 - across][chan], heights, TO_EAST)
        from_east = unbundle(edge_refs[3 - across][chan], heights, TO_WEST)
        return list(zip(from_west, from_east))

    from_partner = []
    for chan in range(chans):
        low = coarse_ref[chan]
        if parts == 2:
            here, there = sides(chan, 0), sides(chan, 1)
            other = unpack(lambda k: packed_ref[chan, k], wide - 1, half - 1)
            value, right, other_low = (with_edges(f, *s) for f, s in zip(other, there))
            low = jnp.concatenate(with_edges(tiles(low), *here[2]), 1)
            low = joined(place, low, jnp.concatenate(other_low, 1), full // 2)
            for ref, own, side in ((v0_ref, value_ref, here[0]), (b0_ref, right_ref, here[1])):
                for k, tile in enumerate(with_edges([own[chan, k] for k in range(wide)], *side)):
                    ref[chan, k] = tile
            from_partner.append((value, right))
        else:
            v0_ref[chan] = value_ref[chan]
            b0_ref[chan] = right_ref[chan]
        for k, tile in enumerate(tiles(low)):
            b1_ref[chan, k] = tile

    def add_rows(value_at, right_at):
        for chan, (value, right) in enumerate(from_partner):
            for k in range(wide):
                v0_ref[chan, k, pl.ds(value_at, VALUE_ROWS), :] += value[k]
                b0_ref[chan, k, pl.ds(right_at, RIGHT_ROWS), :] += right[k]

    if parts == 2:
        pl.when(place == 0)(lambda: add_rows(12, 16))
        pl.when(place == 1)(lambda: add_rows(4, 5))

    def smoothed(fields, scaled_ref, level, written=LEAST_SWEEPS, ready=lambda: None):
        def step(_, fields):
            return tuple(
                sweep(planes, lambda t, k, i=i: scaled_ref[i, t, :, span(k)], 0.25**level)
                for i, planes in enumerate(fields)
            )

        return repeat(step, sweeps, level, tuple(tuple(f) for f in fields), written, ready)

    def from_zero(rights, scaled_ref, level, ready=lambda: None):
        first = [[(DAMPING / diagonal(0.25**level)) * b for b in planes] for planes in rights]
        for i, planes in enumerate(first):
            for t, plane in enumerate(planes):
                scaled_ref[i, t] = plane
        return smoothed(first, scaled_ref, level, LEAST_SWEEPS - 1, ready)

    pair_places, spread_places = pairing(), spreading()
    height1 = full // 2 // count1
    right1 = [load_planes(b1_ref.at[i], 0, count1, height1) for i in range(chans)]
    mid = from_zero(right1, k1_ref, 1, sweeps_copy.wait)
    back = diagonal(0.25) / DAMPING
    left = [residual(f, lambda t, k, i=i: back * k1_ref[i, t, :, span(k)], 0.25) for i, f in enumerate(mid)]
    pairs = [f[t] + f[t + 1] for f in left for t in range(0, count1, 2)]
    low = [0.25 * v for v in pair_columns(pairs, pair_places)]
    right2 = [low[i * count2:(i + 1) * count2] for i in range(chans)]
    fix2 = from_zero(right2, k2_ref, 2)
    mid = [[v + f for v, f in zip(planes, fix)] for planes, fix in zip(mid, prolong(fix2, spread_places))]
    mid = smoothed(mid, k1_ref, 1)
    spare = (fix_ref.shape[2] - full) // 2
    if spare:
        fix_ref[...] = jnp.zeros_like(fix_ref)
    for i, fix in enumerate(prolong(mid, spread_places)):
        store_planes(fix_ref.at[i], spare, fix)
    shown = pl.multiple_of((SUBLANES if parts == 2 else rows) * place, SUBLANES)
    start = own_start(parts, place)
    fields = []
    for i in range(chans):
        planes = load_planes(v0_ref.at[i], 0, count0, SUBLANES)
        fix = load_planes(fix_ref.at[i], shown, count0, SUBLANES)
        fields.append(tuple(v + f for v, f in zip(planes, fix)))
        for t, b in enumerate(load_planes(b0_ref.at[i], 0, count0, SUBLANES)):
            k0_ref[i, t] = (DAMPING / diagonal(1.0)) * b

    def step(_, fields):
        return tuple(
            sweep(planes, lambda t, k, i=i: k0_ref[i, t, :, span(k)], 1.0, inside) for i, planes in enumerate(fields)
        )

    fields = repeat(step, sweeps, 0, tuple(fields), LEAST_SWEEPS)
    out_copies = []
    for i, planes in enumerate(fields):
        store_planes(v0_ref.at[i], 0, planes)
        for k in range(cols // LANES):
            out_ref[i, :, k * LANES:(k + 1) * LANES] = v0_ref[i, k, pl.ds(start, rows), :]
        out_copies.append(pltpu.make_async_copy(out_ref.at[i], out_hbm.at[i], sems.at[1 + i]))
        out_copies[-1].start()
    for copy in out_copies:
        copy.wait()


def up(parts, shape, sweeps, value, right, coarse, *received):
    chans, rows, cols = shape
    wide, window = value.shape[1:3]
    full = parts * rows
    half, quarter = cols // 2 // LANES + 1, cols // 4 // LANES + 1
    count1, count2 = max(1, full // 2 // SUBLANES), max(1, full // 4 // SUBLANES)
    spare = 2 * SUBLANES if parts > 2 else 0
    return pl.pallas_call(
        functools.partial(up_kernel, parts),
        in_specs=[HBM] + [VMEM] * (3 + len(received)),
        out_specs=HBM,
        out_shape=F32(shape),
        scratch_shapes=[
            pltpu.SMEM(sweeps.shape, jnp.int32),
            SCRATCH(value.shape),
            SCRATCH(value.shape),
            SCRATCH((chans, window // SUBLANES, SUBLANES, wide * LANES)),
            SCRATCH((chans, half, full // 2, LANES)),
            SCRATCH((chans, count1, full // 2 // count1, half * LANES)),
            SCRATCH((chans, count2, full // 4 // count2, quarter * LANES)),
            SCRATCH((chans, wide, full + spare, LANES)),
            SCRATCH(shape),
            pltpu.SemaphoreType.DMA((1 + chans,)),
        ],
        compiler_params=pltpu.CompilerParams(vmem_limit_bytes=48 * 2**20),
        name="up",
    )(in_hbm(sweeps), value, right, coarse, *received)


def local(target, grad_x, grad_y, labels, sweeps):
    parts, around_globe = lax.axis_size("lat"), lax.axis_size("lon")
    value, right, coarse, *sent = down(parts, sweeps, target, grad_x, grad_y, labels)
    eastward_pairs = [(i, (i + 1) % around_globe) for i in range(around_globe)]
    westward_pairs = [(j, i) for i, j in eastward_pairs]
    if parts < 2:
        raise NotImplementedError
    if parts == 2:
        def across(pairs):
            return [(2 * i + k, 2 * j + 1 - k) for i, j in pairs for k in range(2)]

        packed, east_across, east, west_across, west = sent
        packed = lax.ppermute(packed, "lat", [(0, 1), (1, 0)])
        across_west = lax.ppermute(east_across, ("lon", "lat"), across(eastward_pairs))
        from_west = lax.ppermute(east, "lon", eastward_pairs)
        across_east = lax.ppermute(west_across, ("lon", "lat"), across(westward_pairs))
        from_east = lax.ppermute(west, "lon", westward_pairs)
        received = (packed, across_west, from_west, across_east, from_east)
        return up(parts, target.shape, sweeps, value, right, coarse, *received)

    chans, half_rows = coarse.shape[:2]
    coarse = coarse.reshape(chans, half_rows, -1, LANES).transpose(0, 2, 1, 3)

    def shared_lon(field):
        parts_of = [field[:, k] for k in range(field.shape[1])]
        from_west = lax.ppermute(eastward(parts_of[-2], parts_of[-1]), "lon", eastward_pairs)
        from_east = lax.ppermute(westward(parts_of[0], parts_of[-1]), "lon", westward_pairs)
        return jnp.stack(with_edges(parts_of, from_west, from_east), 1)

    value, right, coarse = (shared_lon(f) for f in (value, right, coarse))
    if parts > 2:
        rows = target.shape[1]
        spare = 2 * SUBLANES
        southward = [(i, i + 1) for i in range(parts - 1)]
        northward = [(i + 1, i) for i in range(parts - 1)]

        def shared_lat(field):
            north = lax.ppermute(field[:, :, rows:], "lat", southward)
            south = lax.ppermute(field[:, :, :spare], "lat", northward)
            zeros = jnp.zeros_like(south)
            return field + jnp.concatenate([north, zeros], 2) + jnp.concatenate([zeros, south], 2)

        value, right = shared_lat(value), shared_lat(right)
        every = lax.all_gather(coarse, "lat")
        step = rows // 2
        total = jnp.zeros((chans, coarse.shape[1], parts * step + SUBLANES, LANES), jnp.float32)
        for i in range(parts):
            total = total.at[:, :, i * step:i * step + step + SUBLANES].add(every[i])
        coarse = total[:, :, 4:-4]
    coarse = coarse.transpose(0, 2, 1, 3).reshape(chans, coarse.shape[2], -1)
    return up(parts, target.shape, sweeps, value, right, coarse)


def solution(mesh):
    in_specs = (
        P(None, "lat", "lon"),
        P(None, None, "lat", "lon"),
        P(None, None, "lat", "lon"),
        P("lat", "lon"),
        P(),
    )
    out_specs = P(None, "lat", "lon")
    return jax.shard_map(local, mesh=mesh, in_specs=in_specs, out_specs=out_specs, check_vma=False)
```

```python
import functools

import jax
import jax.numpy as jnp
from jax import lax
from jax.experimental import pallas as pl
from jax.experimental.pallas import tpu as pltpu
from jax.sharding import PartitionSpec as P

SCREENING = 0.02
DAMPING = 0.8
LEAST_SWEEPS = 2
LANES = 128
HALF = LANES // 2
SUBLANES = 8
VMEM = pl.BlockSpec(memory_space=pltpu.VMEM)
HBM = pl.BlockSpec(memory_space=pltpu.HBM)
F32 = functools.partial(jax.ShapeDtypeStruct, dtype=jnp.float32)
SCRATCH = functools.partial(pltpu.VMEM, dtype=jnp.float32)


def in_hbm(array):
    return pltpu.with_memory_space_constraint(array, pltpu.HBM)


def diagonal(scale):
    return SCREENING + 4.0 * scale


def rows_of(value):
    return lax.broadcasted_iota(jnp.int32, value.shape, 0)


def lanes_of(tile):
    return lax.broadcasted_iota(jnp.int32, tile.shape, len(tile.shape) - 1)


def tiles(value):
    return [value[:, k * LANES:(k + 1) * LANES] for k in range(value.shape[1] // LANES)]


def row_before(value):
    return jnp.where(rows_of(value) == 0, 0.0, pltpu.roll(value, 1, 0))


def row_after(value):
    last = value.shape[0] - 1
    return jnp.where(rows_of(value) == last, 0.0, pltpu.roll(value, last, 0))


def norths(planes):
    return [row_before(planes[-1])] + list(planes[:-1])


def souths(planes):
    return list(planes[1:]) + [row_after(planes[0])]


def west_of(value):
    return pltpu.roll(value, 1, 1)


def east_of(value):
    return pltpu.roll(value, value.shape[1] - 1, 1)


def neighbours(groups, combine):
    cut = [[tiles(plane) for plane in planes] for planes in groups]
    count, wide = len(cut[0]), len(cut[0][0])
    lane = lanes_of(cut[0][0][0])
    known = {}

    def rolled(g, t, k, shift):
        place = (g, t, k % wide, shift)
        if place not in known:
            known[place] = pltpu.roll(cut[g][t][k % wide], shift, 1)
        return known[place]

    def west(g, t, k):
        if g:
            return cut[0][t][k]
        g = len(cut) - 1
        return jnp.where(lane == 0, rolled(g, t, k - 1, 1), rolled(g, t, k, 1))

    def east(g, t, k):
        if g + 1 < len(cut):
            return cut[1][t][k]
        return jnp.where(lane == LANES - 1, rolled(0, t, k + 1, LANES - 1), rolled(0, t, k, LANES - 1))

    out = []
    for g in range(len(cut)):
        group = []
        for t in range(count):
            done = []
            for k in range(wide):
                north = cut[g][t - 1][k] if t else row_before(cut[g][-1][k])
                south = cut[g][t + 1][k] if t + 1 < count else row_after(cut[g][0][k])
                done.append(combine(g, t, k, cut[g][t][k], (north + south) + (west(g, t, k) + east(g, t, k))))
            group.append(jnp.concatenate(done, 1))
        out.append(tuple(group))
    return tuple(out)


def sweep(groups, scaled, scale, inside=None):
    beside = DAMPING * scale / diagonal(scale)

    def combine(g, t, k, value, total):
        value = (1.0 - DAMPING) * value + (scaled(g, t, k) + beside * total)
        return value if inside is None else value * inside[t]

    return neighbours(groups, combine)


def residual(groups, scaled, scale):
    back = diagonal(scale) / DAMPING
    return neighbours(
        groups, lambda g, t, k, value, total: back * scaled(g, t, k) - diagonal(scale) * value + scale * total
    )


def span(k):
    return slice(k * LANES, (k + 1) * LANES)


def repeat(step, sweeps, level, fields, written, ready=lambda: None):
    for i in range(written):
        fields = step(i, fields)
    ready()
    return lax.fori_loop(LEAST_SWEEPS, sweeps[level], step, fields)


def load_planes(ref, start, count, height):
    def plane(first):
        rows = pl.ds(first, height, stride=count) if count > 1 else pl.ds(first, height)
        return jnp.concatenate([ref[k, rows, :] for k in range(ref.shape[0])], 1)

    return [plane(start + t) for t in range(count)]


def store_planes(ref, start, planes):
    count, height = len(planes), planes[0].shape[0]
    for t, plane in enumerate(planes):
        rows = pl.ds(start + t, height, stride=count) if count > 1 else pl.ds(start + t, height)
        for k, tile in enumerate(tiles(plane)):
            ref[k, rows, :] = tile


def places_of(shape, wanted):
    source = lax.broadcasted_iota(jnp.int32, shape, 0)
    target = lax.broadcasted_iota(jnp.int32, shape, 1)
    return wanted(source, target).astype(jnp.float32).astype(jnp.bfloat16)


def halo_quarter(fine):
    return jnp.where(fine < HALF, fine // 4, LANES - LANES // 4 + fine // 4)


def pairing():
    own = places_of((4 * LANES, 2 * LANES), lambda f, target: f // 4 + LANES * (f // 2 % 2) == target)
    halo = places_of((LANES, 2 * LANES), lambda f, target: halo_quarter(f) + LANES * (f // 2 % 2) == target)
    return own, halo


def merging():
    own = places_of((4 * LANES, 4 * LANES), lambda source, f: source == f // 4 + LANES * (f % 4))
    halo = places_of((4 * LANES, LANES), lambda source, f: source == halo_quarter(f) + LANES * (f % 4))
    return own, halo


def moved(value, places):
    high = value.astype(jnp.bfloat16)
    low = (value - high.astype(jnp.float32)).astype(jnp.bfloat16)
    dot = functools.partial(jnp.dot, preferred_element_type=jnp.float32)
    return dot(high, places) + dot(low, places)


def moved_blocks(own_blocks, halo_blocks, places):
    rows, count = halo_blocks[0].shape[0], len(own_blocks[0])
    packed = moved(jnp.concatenate([block for blocks in own_blocks for block in blocks], 0), places[0])
    edges = moved(jnp.concatenate(halo_blocks, 0), places[1])
    cut = lambda value, i: value[i * rows:(i + 1) * rows]
    return [[cut(packed, i * count + k) for k in range(count)] + [cut(edges, i)] for i in range(len(own_blocks))]


def pair_columns(fields, places):
    cols, width = fields[0].shape[1] - LANES, 4 * LANES
    own = [[f[:, k * width:(k + 1) * width] for k in range(cols // width)] for f in fields]
    moved_to = moved_blocks(own, [f[:, cols:] for f in fields], places)
    return [[[block[:, span(g)] for block in blocks] for g in range(2)] for blocks in moved_to]


def spread_rows(planes):
    return [
        half
        for value, north, south in zip(planes, norths(planes), souths(planes))
        for half in (0.75 * value + 0.25 * north, 0.75 * value + 0.25 * south)
    ]


def prolong(planes):
    planes = spread_rows(planes)
    return [
        [0.75 * value + 0.25 * west_of(value) for value in planes],
        [0.75 * value + 0.25 * east_of(value) for value in planes],
    ]


def prolong_merged(fields, places):
    own, halo = [], []
    for even, odd in fields:
        for e, o in zip(spread_rows(even), spread_rows(odd)):
            quarters = (
                0.75 * e + 0.25 * west_of(o),
                0.75 * e + 0.25 * o,
                0.75 * o + 0.25 * e,
                0.75 * o + 0.25 * east_of(e),
            )
            blocks = [jnp.concatenate(four, 1) for four in zip(*(tiles(q) for q in quarters))]
            own.append(blocks[:-1])
            halo.append(blocks[-1])
    planes = [jnp.concatenate(blocks, 1) for blocks in moved_blocks(own, halo, places)]
    count = len(planes) // len(fields)
    return [planes[i * count:(i + 1) * count] for i in range(len(fields))]


def window_of(rows, parts):
    return rows + (2 * SUBLANES if parts > 2 else SUBLANES if parts == 2 else 0)


def own_start(parts, place):
    return 0 if parts == 1 else pl.multiple_of(SUBLANES * place, SUBLANES) if parts == 2 else SUBLANES


def band_masks(window, parts, place, rows):
    if parts <= 2:
        return None
    count = window // SUBLANES
    first = place * rows - SUBLANES
    row = [first + t + count * lax.broadcasted_iota(jnp.int32, (SUBLANES, 1), 0) for t in range(count)]
    return [((r >= 0) & (r < parts * rows)).astype(jnp.float32) for r in row]


def eastward(own_last, halo):
    return jnp.where(lanes_of(halo) < HALF, halo, own_last)


def westward(own_first, halo):
    return jnp.where(lanes_of(halo) < HALF, own_first, halo)


def with_edges(parts, from_west, from_east):
    inner = lanes_of(from_west) < HALF
    first = parts[0] + jnp.where(inner, from_west, 0.0)
    last = parts[-2] + jnp.where(inner, 0.0, from_east)
    halo = parts[-1] + jnp.where(inner, from_east, from_west)
    return [first] + list(parts[1:-2]) + [last, halo]


COARSE_WIDTH, FINE_WIDTH, REACH = 16, 8, 4
TO_EAST, TO_WEST = -12, -4


def in_window(lane, start, width):
    start = start % LANES
    end = start + width
    return (lane >= start) & (lane < end) if end <= LANES else (lane >= start) | (lane < end - LANES)


def slots(heights, coarse_start):
    out, at = [], 0
    for which, rows in enumerate(heights):
        start, width = (-REACH, FINE_WIDTH) if which < 2 else (coarse_start, COARSE_WIDTH)
        for first in range(0, rows, SUBLANES):
            out.append((which, first, min(SUBLANES, rows - first), start, width, at))
            at += width
    assert at <= LANES
    return out


def bundle(fields, coarse_start):
    out = jnp.zeros((SUBLANES, LANES), jnp.float32)
    lane = lanes_of(out)
    for which, first, rows, start, width, at in slots([f.shape[0] for f in fields], coarse_start):
        piece = fields[which][first:first + rows]
        if rows < SUBLANES:
            piece = jnp.concatenate([piece, jnp.zeros((SUBLANES - rows, LANES), jnp.float32)], 0)
        out = jnp.where(in_window(lane, at, width), pltpu.roll(piece, (at - start) % LANES, 1), out)
    return out


def unbundle(tile, heights, coarse_start):
    lane = lanes_of(tile)
    pieces = [[] for _ in heights]
    for which, first, rows, start, width, at in slots(heights, coarse_start):
        piece = jnp.where(in_window(lane, start, width), pltpu.roll(tile, (start - at) % LANES, 1), 0.0)
        pieces[which].append(piece[:rows])
    return [jnp.concatenate(p, 0) if len(p) > 1 else p[0] for p in pieces]


COARSE_ROWS = 12
ACROSS = (SUBLANES, SUBLANES, COARSE_ROWS, COARSE_ROWS)


def border_rows(place):
    north, south = (pl.multiple_of(SUBLANES * (n - place), SUBLANES) for n in (1, 2))
    return pl.ds(north, SUBLANES), pl.ds(south, SUBLANES)


def border_value(place, ref):
    north, south = (ref[rows, :] for rows in border_rows(place))
    return jnp.where(rows_of(north) >= 4, north, south)


def border_right(place, ref):
    north, south = (ref[rows, :] for rows in border_rows(place))
    return jnp.where((place == 0) & (rows_of(north) != 4), north, pltpu.roll(south, 4, 0))


def add_border(place, value_ref, right_ref, value, right):
    row = rows_of(value)
    north, south = border_rows(place)
    value_ref[north, :] += jnp.where(row >= 4, value, 0.0)
    value_ref[south, :] += jnp.where(row < 4, value, 0.0)
    right_ref[north, :] += jnp.where((place == 1) & (row > 4), right, 0.0)
    right_ref[south, :] += jnp.where(row < jnp.where(place == 1, 1, 4), pltpu.roll(right, 4, 0), 0.0)


def half_tiles(lower, upper):
    return jnp.where(rows_of(lower) >= 4, lower, pltpu.roll(upper, 4, 0))


def pack(value, right, coarse):
    low = [tile for group in coarse for tile in group[:-1]]
    joined = [half_tiles(right[k], right[k + 1]) for k in range(0, len(right) - 1, 2)]
    joined += [jnp.concatenate([low[k][SUBLANES:], low[k + 1][SUBLANES:]], 0) for k in range(0, len(low), 2)]
    ends = bundle([value[-1], right[-1]] + [group[-1] for group in coarse], TO_WEST)
    return value[:-1] + [tile[:SUBLANES] for tile in low] + joined + [ends]


def packed_tiles(fine, coarse):
    return fine + coarse + (fine + coarse) // 2 + 1


def unpack(tile, fine, coarse):
    value = [tile(k) for k in range(fine)]
    right, low = [], []
    for k in range(fine // 2):
        both = tile(fine + coarse + k)
        right += [both, pltpu.roll(both, 4, 0)]
    for k in range(coarse // 2):
        both = tile(fine + coarse + fine // 2 + k)
        low += [jnp.concatenate([tile(fine + 2 * k + j), both[4 * j:4 * j + 4]], 0) for j in range(2)]
    ends = unbundle(tile(packed_tiles(fine, coarse) - 1), ACROSS, TO_WEST)
    fields = (value, right, low[:coarse // 2], low[coarse // 2:])
    return [field + [end] for field, end in zip(fields, ends)]


def down_kernel(parts, sweeps_hbm, target, grad_x, grad_y, labels, *refs):
    sent = 5 if parts == 2 else 0
    value_ref, right_ref, coarse_ref, merge_ref, merge_halo_ref = refs[:5]
    sent_refs = refs[5:5 + sent]
    sweeps, target_v, grad_x_v, grad_y_v, labels_v, v_ref, b_ref, scaled_ref, resid_ref, sems = refs[5 + sent:]
    chans, rows, cols = target.shape
    window = value_ref.shape[2]
    count = window // SUBLANES
    place = lax.axis_index("lat")
    start = own_start(parts, place)
    inside = band_masks(window, parts, place, rows)
    scale = 1.0

    first_copies = [
        pltpu.make_async_copy(labels, labels_v, sems.at[chans, 0]),
        pltpu.make_async_copy(sweeps_hbm, sweeps, sems.at[chans, 1]),
    ]
    for copy in first_copies:
        copy.start()
    copies = []
    for chan in range(chans):
        copies.append([
            pltpu.make_async_copy(target.at[chan], target_v.at[chan], sems.at[chan, 0]),
            pltpu.make_async_copy(grad_x.at[:, chan], grad_x_v.at[:, chan], sems.at[chan, 1]),
            pltpu.make_async_copy(grad_y.at[:, chan], grad_y_v.at[:, chan], sems.at[chan, 2]),
        ])
        for copy in copies[-1]:
            copy.start()
    if window > rows:
        v_ref[...] = jnp.zeros_like(v_ref)
        b_ref[...] = jnp.zeros_like(b_ref)
    places = pairing()
    merge_ref[...], merge_halo_ref[...] = merging()
    for copy in first_copies:
        copy.wait()

    def chosen(grad, chan):
        marks = labels_v[...]
        out = jnp.zeros((rows, cols), jnp.float32)
        for source in range(grad.shape[0]):
            out = jnp.where(marks == source, grad[source, chan], out)
        return out

    blank = jnp.zeros((rows, LANES), jnp.float32)
    fields = []
    for chan in range(chans):
        for copy in copies[chan]:
            copy.wait()
        own = jnp.concatenate([target_v[chan], blank], 1)
        sel_x = jnp.concatenate([chosen(grad_x_v, chan), blank], 1)
        sel_y = jnp.concatenate([chosen(grad_y_v, chan), blank], 1)
        right = SCREENING * own - ((sel_x - west_of(sel_x)) + (sel_y - row_before(sel_y)))
        below = pltpu.roll(sel_y[rows - SUBLANES:], 1, 0)
        below = jnp.where(rows_of(below) == 0, below, 0.0)
        for k, (v, b, s) in enumerate(zip(tiles(own), tiles(right), tiles(below))):
            v_ref[chan, k, pl.ds(start, rows), :] = v
            b_ref[chan, k, pl.ds(start, rows), :] = b
            if window > rows:
                b_ref[chan, k, pl.ds(start + rows, SUBLANES), :] = s
    for chan in range(chans):
        fields.append((tuple(load_planes(v_ref.at[chan], 0, count, SUBLANES)),))
        right = load_planes(b_ref.at[chan], 0, count, SUBLANES)
        if inside is not None:
            right = [b * mask for b, mask in zip(right, inside)]
        store_planes(right_ref.at[chan], 0, right)
        for t in range(count):
            scaled_ref[chan, t] = (DAMPING / diagonal(scale)) * right[t]

    def scaled(chan):
        return lambda g, t, k: scaled_ref[chan, t, :, span(k)]

    def step(_, fields):
        return tuple(sweep(field, scaled(chan), scale, inside) for chan, field in enumerate(fields))

    fields = repeat(step, sweeps, 0, tuple(fields), LEAST_SWEEPS)
    paired = []
    for chan, field in enumerate(fields):
        store_planes(value_ref.at[chan], 0, field[0])
        left = residual(field, scaled(chan), scale)[0]
        if inside is not None:
            left = [r * mask for r, mask in zip(left, inside)]
        store_planes(resid_ref.at[chan], 0, left)
    for chan in range(chans):
        north, south = load_planes(resid_ref.at[chan], 0, 2, window // 2)
        paired.append(north + south)
    coarse = pair_columns(paired, places)
    for chan in range(chans):
        low = [[0.25 * tile for tile in group] for group in coarse[chan]]
        coarse_ref[chan] = jnp.concatenate(low[0] + low[1], 1)
        if parts != 2:
            continue
        packed_ref, east_across, east_ref, west_across, west_ref = sent_refs
        wide = value_ref.shape[1]
        value = [value_ref[chan, k] for k in range(wide)]
        right = [right_ref[chan, k] for k in range(wide)]
        value_border = [border_value(place, value_ref.at[chan, k]) for k in range(wide)]
        right_border = [border_right(place, right_ref.at[chan, k]) for k in range(wide)]
        for k, tile in enumerate(pack(value_border, right_border, low)):
            packed_ref[chan, k] = tile
        for east, west, fields in (
            (east_ref, west_ref, (value, right, *low)),
            (east_across, west_across, (value_border, right_border, *low)),
        ):
            east[chan] = bundle([eastward(f[-2], f[-1]) for f in fields], TO_EAST)
            west[chan] = bundle([westward(f[0], f[-1]) for f in fields], TO_WEST)


def down(parts, sweeps, target, grad_x, grad_y, labels):
    chans, rows, cols = target.shape
    window = window_of(rows, parts)
    wide, quarter = cols // LANES + 1, cols // 4 // LANES + 1
    spare = SUBLANES if window > rows else 0
    outs = [F32((chans, wide, window, LANES))] * 2 + [F32((chans, window // 2, 2 * quarter * LANES))]
    outs += [jax.ShapeDtypeStruct((4 * LANES, n * LANES), jnp.bfloat16) for n in (4, 1)]
    if parts == 2:
        outs.append(F32((chans, packed_tiles(wide - 1, 2 * (quarter - 1)), SUBLANES, LANES)))
        outs += [F32((chans, SUBLANES, LANES))] * 4
    return pl.pallas_call(
        functools.partial(down_kernel, parts),
        in_specs=[HBM] * 5,
        out_specs=[VMEM] * len(outs),
        out_shape=outs,
        scratch_shapes=[
            pltpu.SMEM(sweeps.shape, jnp.int32),
            SCRATCH(target.shape),
            SCRATCH(grad_x.shape),
            SCRATCH(grad_y.shape),
            pltpu.VMEM(labels.shape, jnp.int32),
            SCRATCH((chans, wide, window + spare, LANES)),
            SCRATCH((chans, wide, window + spare, LANES)),
            SCRATCH((chans, window // SUBLANES, SUBLANES, wide * LANES)),
            SCRATCH((chans, wide, window, LANES)),
            pltpu.SemaphoreType.DMA((chans + 1, 3)),
        ],
        compiler_params=pltpu.CompilerParams(vmem_limit_bytes=32 * 2**20),
        name="down",
    )(*(in_hbm(a) for a in (sweeps, target, grad_x, grad_y, labels)))


def joined(place, own, other, height):
    gap = jnp.zeros((height - own.shape[0], own.shape[1]), jnp.float32)
    top, bottom = (lambda v: jnp.concatenate([v, gap], 0)), (lambda v: jnp.concatenate([gap, v], 0))
    return jnp.where(place == 0, top(own) + bottom(other), bottom(own) + top(other))


def up_kernel(parts, sweeps_hbm, value_ref, right_ref, coarse_ref, merge_ref, merge_halo_ref, *refs):
    received = 5 if parts == 2 else 0
    packed_ref, *edge_refs = refs[:received] or [None]
    out_hbm, sweeps, v0_ref, b0_ref, k0_ref, b1_ref, k1_ref, k2_ref, fix_ref, out_ref, sems = refs[received:]
    sweeps_copy = pltpu.make_async_copy(sweeps_hbm, sweeps, sems.at[0])
    sweeps_copy.start()
    chans, rows, cols = out_ref.shape
    wide, window = value_ref.shape[1:3]
    quarter = b1_ref.shape[2]
    full = parts * rows
    count0, count1 = window // SUBLANES, full // 2 // SUBLANES
    place = lax.axis_index("lat")
    inside = band_masks(window, parts, place, rows)
    own_heights = (window, window, window // 2, window // 2)

    def sides(chan, across):
        heights = ACROSS if across else own_heights
        from_west = unbundle(edge_refs[1 - across][chan], heights, TO_EAST)
        from_east = unbundle(edge_refs[3 - across][chan], heights, TO_WEST)
        return list(zip(from_west, from_east))

    for chan in range(chans):
        low = tiles(coarse_ref[chan])
        low = [low[:quarter], low[quarter:]]
        if parts == 2:
            here, there = sides(chan, 0), sides(chan, 1)
            other = unpack(lambda k: packed_ref[chan, k], wide - 1, 2 * (quarter - 1))
            value, right, *other_low = (with_edges(f, *s) for f, s in zip(other, there))
            low = [with_edges(f, *s) for f, s in zip(low, here[2:])]
            low = [[joined(place, a, b, full // 2) for a, b in zip(*both)] for both in zip(low, other_low)]
            for ref, own, side in ((v0_ref, value_ref, here[0]), (b0_ref, right_ref, here[1])):
                for k, tile in enumerate(with_edges([own[chan, k] for k in range(wide)], *side)):
                    ref[chan, k] = tile
            for k in range(wide):
                add_border(place, v0_ref.at[chan, k], b0_ref.at[chan, k], value[k], right[k])
        else:
            v0_ref[chan] = value_ref[chan]
            b0_ref[chan] = right_ref[chan]
        for g, group in enumerate(low):
            for k, tile in enumerate(group):
                b1_ref[chan, g, k] = tile

    def smoothed(fields, scaled_ref, level, written=LEAST_SWEEPS, ready=lambda: None):
        def step(_, fields):
            return tuple(
                sweep(field, lambda g, t, k, i=i: scaled_ref[i, g, t, :, span(k)], 0.25**level)
                for i, field in enumerate(fields)
            )

        fields = tuple(tuple(tuple(planes) for planes in field) for field in fields)
        return repeat(step, sweeps, level, fields, written, ready)

    def from_zero(rights, scaled_ref, level, ready=lambda: None):
        first = [[[(DAMPING / diagonal(0.25**level)) * b for b in planes] for planes in field] for field in rights]
        for i, field in enumerate(first):
            for g, planes in enumerate(field):
                for t, plane in enumerate(planes):
                    scaled_ref[i, g, t] = plane
        return smoothed(first, scaled_ref, level, LEAST_SWEEPS - 1, ready)

    right1 = [[load_planes(b1_ref.at[i, g], 0, count1, SUBLANES) for g in range(2)] for i in range(chans)]
    mid = from_zero(right1, k1_ref, 1, sweeps_copy.wait)
    right2 = []
    for i, field in enumerate(mid):
        even, odd = residual(field, lambda g, t, k, i=i: k1_ref[i, g, t, :, span(k)], 0.25)
        both = [a + b for a, b in zip(even, odd)]
        right2.append([[0.25 * (both[t] + both[t + 1]) for t in range(0, count1, 2)]])
    fix2 = from_zero(right2, k2_ref, 2)
    mid = [
        [[v + f for v, f in zip(planes, more)] for planes, more in zip(field, prolong(fix[0]))]
        for field, fix in zip(mid, fix2)
    ]
    mid = smoothed(mid, k1_ref, 1)
    spare = (fix_ref.shape[2] - full) // 2
    if spare:
        fix_ref[...] = jnp.zeros_like(fix_ref)
    for i, fix in enumerate(prolong_merged(mid, (merge_ref[...], merge_halo_ref[...]))):
        store_planes(fix_ref.at[i], spare, fix)
    shown = pl.multiple_of((SUBLANES if parts == 2 else rows) * place, SUBLANES)
    start = own_start(parts, place)
    fields = []
    for i in range(chans):
        planes = load_planes(v0_ref.at[i], 0, count0, SUBLANES)
        fix = load_planes(fix_ref.at[i], shown, count0, SUBLANES)
        fields.append((tuple(v + f for v, f in zip(planes, fix)),))
        for t, b in enumerate(load_planes(b0_ref.at[i], 0, count0, SUBLANES)):
            k0_ref[i, t] = (DAMPING / diagonal(1.0)) * b

    def step(_, fields):
        return tuple(
            sweep(field, lambda g, t, k, i=i: k0_ref[i, t, :, span(k)], 1.0, inside) for i, field in enumerate(fields)
        )

    fields = repeat(step, sweeps, 0, tuple(fields), LEAST_SWEEPS)
    out_copies = []
    for i, field in enumerate(fields):
        store_planes(v0_ref.at[i], 0, field[0])
        for k in range(cols // LANES):
            out_ref[i, :, k * LANES:(k + 1) * LANES] = v0_ref[i, k, pl.ds(start, rows), :]
        out_copies.append(pltpu.make_async_copy(out_ref.at[i], out_hbm.at[i], sems.at[1 + i]))
        out_copies[-1].start()
    for copy in out_copies:
        copy.wait()


def up(parts, shape, sweeps, value, right, coarse, *more):
    chans, rows, cols = shape
    wide, window = value.shape[1:3]
    full = parts * rows
    quarter = cols // 4 // LANES + 1
    count1, count2 = full // 2 // SUBLANES, full // 4 // SUBLANES
    spare = 2 * SUBLANES if parts > 2 else 0
    return pl.pallas_call(
        functools.partial(up_kernel, parts),
        in_specs=[HBM] + [VMEM] * (3 + len(more)),
        out_specs=HBM,
        out_shape=F32(shape),
        scratch_shapes=[
            pltpu.SMEM(sweeps.shape, jnp.int32),
            SCRATCH(value.shape),
            SCRATCH(value.shape),
            SCRATCH((chans, window // SUBLANES, SUBLANES, wide * LANES)),
            SCRATCH((chans, 2, quarter, full // 2, LANES)),
            SCRATCH((chans, 2, count1, SUBLANES, quarter * LANES)),
            SCRATCH((chans, 1, count2, SUBLANES, quarter * LANES)),
            SCRATCH((chans, wide, full + spare, LANES)),
            SCRATCH(shape),
            pltpu.SemaphoreType.DMA((1 + chans,)),
        ],
        compiler_params=pltpu.CompilerParams(vmem_limit_bytes=48 * 2**20),
        name="up",
    )(in_hbm(sweeps), value, right, coarse, *more)


def local(target, grad_x, grad_y, labels, sweeps):
    parts, around_globe = lax.axis_size("lat"), lax.axis_size("lon")
    value, right, coarse, merge, merge_halo, *sent = down(parts, sweeps, target, grad_x, grad_y, labels)
    eastward_pairs = [(i, (i + 1) % around_globe) for i in range(around_globe)]
    westward_pairs = [(j, i) for i, j in eastward_pairs]
    if parts < 2:
        raise NotImplementedError
    if parts == 2:
        def across(pairs):
            return [(2 * i + k, 2 * j + 1 - k) for i, j in pairs for k in range(2)]

        packed, east_across, east, west_across, west = sent
        packed = lax.ppermute(packed, "lat", [(0, 1), (1, 0)])
        across_west = lax.ppermute(east_across, ("lon", "lat"), across(eastward_pairs))
        from_west = lax.ppermute(east, "lon", eastward_pairs)
        across_east = lax.ppermute(west_across, ("lon", "lat"), across(westward_pairs))
        from_east = lax.ppermute(west, "lon", westward_pairs)
        received = (packed, across_west, from_west, across_east, from_east)
        return up(parts, target.shape, sweeps, value, right, coarse, merge, merge_halo, *received)

    chans, half_rows = coarse.shape[:2]
    coarse = coarse.reshape(chans, half_rows, -1, LANES).transpose(0, 2, 1, 3)

    def shared_lon(field):
        parts_of = [field[:, k] for k in range(field.shape[1])]
        from_west = lax.ppermute(eastward(parts_of[-2], parts_of[-1]), "lon", eastward_pairs)
        from_east = lax.ppermute(westward(parts_of[0], parts_of[-1]), "lon", westward_pairs)
        return jnp.stack(with_edges(parts_of, from_west, from_east), 1)

    value, right = shared_lon(value), shared_lon(right)
    halves = jnp.split(coarse, 2, axis=1)
    coarse = jnp.concatenate([shared_lon(f) for f in halves], 1)
    if parts > 2:
        rows = target.shape[1]
        spare = 2 * SUBLANES
        southward = [(i, i + 1) for i in range(parts - 1)]
        northward = [(i + 1, i) for i in range(parts - 1)]

        def shared_lat(field):
            north = lax.ppermute(field[:, :, rows:], "lat", southward)
            south = lax.ppermute(field[:, :, :spare], "lat", northward)
            zeros = jnp.zeros_like(south)
            return field + jnp.concatenate([north, zeros], 2) + jnp.concatenate([zeros, south], 2)

        value, right = shared_lat(value), shared_lat(right)
        every = lax.all_gather(coarse, "lat")
        step = rows // 2
        total = jnp.zeros((chans, coarse.shape[1], parts * step + SUBLANES, LANES), jnp.float32)
        for i in range(parts):
            total = total.at[:, :, i * step:i * step + step + SUBLANES].add(every[i])
        coarse = total[:, :, 4:-4]
    coarse = coarse.transpose(0, 2, 1, 3).reshape(chans, coarse.shape[2], -1)
    return up(parts, target.shape, sweeps, value, right, coarse, merge, merge_halo)


def solution(mesh):
    in_specs = (
        P(None, "lat", "lon"),
        P(None, None, "lat", "lon"),
        P(None, None, "lat", "lon"),
        P("lat", "lon"),
        P(),
    )
    out_specs = P(None, "lat", "lon")
    return jax.shard_map(local, mesh=mesh, in_specs=in_specs, out_specs=out_specs, check_vma=False)
```

```python
import functools

import jax
import jax.numpy as jnp
from jax import lax
from jax.experimental import pallas as pl
from jax.experimental.pallas import tpu as pltpu
from jax.sharding import PartitionSpec as P

SCREENING = 0.02
DAMPING = 0.8
LEAST_SWEEPS, MOST_SWEEPS = 2, 4
LANES = 128
HALF = LANES // 2
SUBLANES = 8
VMEM = pl.BlockSpec(memory_space=pltpu.VMEM)
HBM = pl.BlockSpec(memory_space=pltpu.HBM)
F32 = functools.partial(jax.ShapeDtypeStruct, dtype=jnp.float32)
SCRATCH = functools.partial(pltpu.VMEM, dtype=jnp.float32)


def in_hbm(array):
    return pltpu.with_memory_space_constraint(array, pltpu.HBM)


def diagonal(scale):
    return SCREENING + 4.0 * scale


def rows_of(value):
    return lax.broadcasted_iota(jnp.int32, value.shape, 0)


def lanes_of(tile):
    return lax.broadcasted_iota(jnp.int32, tile.shape, len(tile.shape) - 1)


def tiles(value):
    return [value[:, k * LANES:(k + 1) * LANES] for k in range(value.shape[1] // LANES)]


def row_before(value):
    return jnp.where(rows_of(value) == 0, 0.0, pltpu.roll(value, 1, 0))


def row_after(value):
    last = value.shape[0] - 1
    return jnp.where(rows_of(value) == last, 0.0, pltpu.roll(value, last, 0))


def norths(planes):
    return [row_before(planes[-1])] + list(planes[:-1])


def souths(planes):
    return list(planes[1:]) + [row_after(planes[0])]


def west_of(value):
    return pltpu.roll(value, 1, 1)


def east_of(value):
    return pltpu.roll(value, value.shape[1] - 1, 1)


def neighbours(groups, combine):
    cut = [[tiles(plane) for plane in planes] for planes in groups]
    count, wide = len(cut[0]), len(cut[0][0])
    lane = lanes_of(cut[0][0][0])
    known = {}

    def rolled(g, t, k, shift):
        place = (g, t, k % wide, shift)
        if place not in known:
            known[place] = pltpu.roll(cut[g][t][k % wide], shift, 1)
        return known[place]

    def west(g, t, k):
        if g:
            return cut[0][t][k]
        g = len(cut) - 1
        return jnp.where(lane == 0, rolled(g, t, k - 1, 1), rolled(g, t, k, 1))

    def east(g, t, k):
        if g + 1 < len(cut):
            return cut[1][t][k]
        return jnp.where(lane == LANES - 1, rolled(0, t, k + 1, LANES - 1), rolled(0, t, k, LANES - 1))

    out = []
    for g in range(len(cut)):
        group = []
        for t in range(count):
            done = []
            for k in range(wide):
                north = cut[g][t - 1][k] if t else row_before(cut[g][-1][k])
                south = cut[g][t + 1][k] if t + 1 < count else row_after(cut[g][0][k])
                done.append(combine(g, t, k, cut[g][t][k], (north + south) + (west(g, t, k) + east(g, t, k))))
            group.append(jnp.concatenate(done, 1))
        out.append(tuple(group))
    return tuple(out)


def sweep(groups, scaled, scale, inside=None):
    beside = DAMPING * scale / diagonal(scale)

    def combine(g, t, k, value, total):
        value = (1.0 - DAMPING) * value + (scaled(g, t, k) + beside * total)
        return value if inside is None else value * inside[t]

    return neighbours(groups, combine)


def residual(groups, scaled, scale):
    back = diagonal(scale) / DAMPING
    return neighbours(
        groups, lambda g, t, k, value, total: back * scaled(g, t, k) - diagonal(scale) * value + scale * total
    )


def span(k):
    return slice(k * LANES, (k + 1) * LANES)


def repeat(step, sweeps, level, fields, written, ready=lambda: None):
    def steps(count):
        def run(fields):
            for i in range(count):
                fields = step(i, fields)
            return fields

        return run

    fields = steps(written)(fields)
    ready()
    cases = [steps(more) for more in range(MOST_SWEEPS - LEAST_SWEEPS + 1)]
    return lax.switch(sweeps[level] - LEAST_SWEEPS, cases, fields)


def load_planes(ref, start, count, height):
    def plane(first):
        rows = pl.ds(first, height, stride=count) if count > 1 else pl.ds(first, height)
        return jnp.concatenate([ref[k, rows, :] for k in range(ref.shape[0])], 1)

    return [plane(start + t) for t in range(count)]


def store_planes(ref, start, planes):
    count, height = len(planes), planes[0].shape[0]
    for t, plane in enumerate(planes):
        rows = pl.ds(start + t, height, stride=count) if count > 1 else pl.ds(start + t, height)
        for k, tile in enumerate(tiles(plane)):
            ref[k, rows, :] = tile


def places_of(shape, wanted):
    source = lax.broadcasted_iota(jnp.int32, shape, 0)
    target = lax.broadcasted_iota(jnp.int32, shape, 1)
    return wanted(source, target).astype(jnp.float32).astype(jnp.bfloat16)


def halo_quarter(fine):
    return jnp.where(fine < HALF, fine // 4, LANES - LANES // 4 + fine // 4)


def pairing():
    own = places_of((4 * LANES, 2 * LANES), lambda f, target: f // 4 + LANES * (f // 2 % 2) == target)
    halo = places_of((LANES, 2 * LANES), lambda f, target: halo_quarter(f) + LANES * (f // 2 % 2) == target)
    return own, halo


def merging():
    own = places_of((4 * LANES, 4 * LANES), lambda source, f: source == f // 4 + LANES * (f % 4))
    halo = places_of((4 * LANES, LANES), lambda source, f: source == halo_quarter(f) + LANES * (f % 4))
    return own, halo


def moved(value, places):
    high = value.astype(jnp.bfloat16)
    low = (value - high.astype(jnp.float32)).astype(jnp.bfloat16)
    dot = functools.partial(jnp.dot, preferred_element_type=jnp.float32)
    return dot(high, places) + dot(low, places)


def moved_blocks(own_blocks, halo_blocks, places):
    rows, count = halo_blocks[0].shape[0], len(own_blocks[0])
    packed = moved(jnp.concatenate([block for blocks in own_blocks for block in blocks], 0), places[0])
    edges = moved(jnp.concatenate(halo_blocks, 0), places[1])
    cut = lambda value, i: value[i * rows:(i + 1) * rows]
    return [[cut(packed, i * count + k) for k in range(count)] + [cut(edges, i)] for i in range(len(own_blocks))]


def pair_columns(fields, places):
    cols, width = fields[0].shape[1] - LANES, 4 * LANES
    own = [[f[:, k * width:(k + 1) * width] for k in range(cols // width)] for f in fields]
    moved_to = moved_blocks(own, [f[:, cols:] for f in fields], places)
    return [[[block[:, span(g)] for block in blocks] for g in range(2)] for blocks in moved_to]


def spread_rows(planes):
    return [
        half
        for value, north, south in zip(planes, norths(planes), souths(planes))
        for half in (0.75 * value + 0.25 * north, 0.75 * value + 0.25 * south)
    ]


def prolong(planes):
    planes = spread_rows(planes)
    return [
        [0.75 * value + 0.25 * west_of(value) for value in planes],
        [0.75 * value + 0.25 * east_of(value) for value in planes],
    ]


def prolong_merged(fields, places):
    own, halo = [], []
    for even, odd in fields:
        for e, o in zip(spread_rows(even), spread_rows(odd)):
            quarters = (
                0.75 * e + 0.25 * west_of(o),
                0.75 * e + 0.25 * o,
                0.75 * o + 0.25 * e,
                0.75 * o + 0.25 * east_of(e),
            )
            blocks = [jnp.concatenate(four, 1) for four in zip(*(tiles(q) for q in quarters))]
            own.append(blocks[:-1])
            halo.append(blocks[-1])
    planes = [jnp.concatenate(blocks, 1) for blocks in moved_blocks(own, halo, places)]
    count = len(planes) // len(fields)
    return [planes[i * count:(i + 1) * count] for i in range(len(fields))]


def window_of(rows, parts):
    return rows + (2 * SUBLANES if parts > 2 else SUBLANES if parts == 2 else 0)


def own_start(parts, place):
    return 0 if parts == 1 else pl.multiple_of(SUBLANES * place, SUBLANES) if parts == 2 else SUBLANES


def band_masks(window, parts, place, rows):
    if parts <= 2:
        return None
    count = window // SUBLANES
    first = place * rows - SUBLANES
    row = [first + t + count * lax.broadcasted_iota(jnp.int32, (SUBLANES, 1), 0) for t in range(count)]
    return [((r >= 0) & (r < parts * rows)).astype(jnp.float32) for r in row]


def eastward(own_last, halo):
    return jnp.where(lanes_of(halo) < HALF, halo, own_last)


def westward(own_first, halo):
    return jnp.where(lanes_of(halo) < HALF, own_first, halo)


def with_edges(parts, from_west, from_east):
    inner = lanes_of(from_west) < HALF
    first = parts[0] + jnp.where(inner, from_west, 0.0)
    last = parts[-2] + jnp.where(inner, 0.0, from_east)
    halo = parts[-1] + jnp.where(inner, from_east, from_west)
    return [first] + list(parts[1:-2]) + [last, halo]


COARSE_WIDTH, FINE_WIDTH, REACH = 16, 8, 4
TO_EAST, TO_WEST = -12, -4


def in_window(lane, start, width):
    start = start % LANES
    end = start + width
    return (lane >= start) & (lane < end) if end <= LANES else (lane >= start) | (lane < end - LANES)


def slots(heights, coarse_start):
    out, at = [], 0
    for which, rows in enumerate(heights):
        start, width = (-REACH, FINE_WIDTH) if which < 2 else (coarse_start, COARSE_WIDTH)
        for first in range(0, rows, SUBLANES):
            out.append((which, first, min(SUBLANES, rows - first), start, width, at))
            at += width
    assert at <= LANES
    return out


def bundle(fields, coarse_start):
    out = jnp.zeros((SUBLANES, LANES), jnp.float32)
    lane = lanes_of(out)
    for which, first, rows, start, width, at in slots([f.shape[0] for f in fields], coarse_start):
        piece = fields[which][first:first + rows]
        if rows < SUBLANES:
            piece = jnp.concatenate([piece, jnp.zeros((SUBLANES - rows, LANES), jnp.float32)], 0)
        out = jnp.where(in_window(lane, at, width), pltpu.roll(piece, (at - start) % LANES, 1), out)
    return out


def unbundle(tile, heights, coarse_start):
    lane = lanes_of(tile)
    pieces = [[] for _ in heights]
    for which, first, rows, start, width, at in slots(heights, coarse_start):
        piece = jnp.where(in_window(lane, start, width), pltpu.roll(tile, (start - at) % LANES, 1), 0.0)
        pieces[which].append(piece[:rows])
    return [jnp.concatenate(p, 0) if len(p) > 1 else p[0] for p in pieces]


COARSE_ROWS = 12
ACROSS = (SUBLANES, SUBLANES, COARSE_ROWS, COARSE_ROWS)


def border_rows(place):
    north, south = (pl.multiple_of(SUBLANES * (n - place), SUBLANES) for n in (1, 2))
    return pl.ds(north, SUBLANES), pl.ds(south, SUBLANES)


def border_value(place, ref):
    north, south = (ref[rows, :] for rows in border_rows(place))
    return jnp.where(rows_of(north) >= 4, north, south)


def border_right(place, ref):
    north, south = (ref[rows, :] for rows in border_rows(place))
    return jnp.where((place == 0) & (rows_of(north) != 4), north, pltpu.roll(south, 4, 0))


def add_border(place, value_ref, right_ref, value, right):
    row = rows_of(value)
    north, south = border_rows(place)
    value_ref[north, :] += jnp.where(row >= 4, value, 0.0)
    value_ref[south, :] += jnp.where(row < 4, value, 0.0)
    right_ref[north, :] += jnp.where((place == 1) & (row > 4), right, 0.0)
    right_ref[south, :] += jnp.where(row < jnp.where(place == 1, 1, 4), pltpu.roll(right, 4, 0), 0.0)


def half_tiles(lower, upper):
    return jnp.where(rows_of(lower) >= 4, lower, pltpu.roll(upper, 4, 0))


def pack(value, right, coarse):
    low = [tile for group in coarse for tile in group[:-1]]
    joined = [half_tiles(right[k], right[k + 1]) for k in range(0, len(right) - 1, 2)]
    joined += [jnp.concatenate([low[k][SUBLANES:], low[k + 1][SUBLANES:]], 0) for k in range(0, len(low), 2)]
    ends = bundle([value[-1], right[-1]] + [group[-1] for group in coarse], TO_WEST)
    return value[:-1] + [tile[:SUBLANES] for tile in low] + joined + [ends]


def packed_tiles(fine, coarse):
    return fine + coarse + (fine + coarse) // 2 + 1


def unpack(tile, fine, coarse):
    value = [tile(k) for k in range(fine)]
    right, low = [], []
    for k in range(fine // 2):
        both = tile(fine + coarse + k)
        right += [both, pltpu.roll(both, 4, 0)]
    for k in range(coarse // 2):
        both = tile(fine + coarse + fine // 2 + k)
        low += [jnp.concatenate([tile(fine + 2 * k + j), both[4 * j:4 * j + 4]], 0) for j in range(2)]
    ends = unbundle(tile(packed_tiles(fine, coarse) - 1), ACROSS, TO_WEST)
    fields = (value, right, low[:coarse // 2], low[coarse // 2:])
    return [field + [end] for field, end in zip(fields, ends)]


def down_kernel(parts, sweeps_hbm, target, grad_x, grad_y, labels, *refs):
    sent = 5 if parts == 2 else 0
    value_ref, right_ref, coarse_ref, merge_ref, merge_halo_ref = refs[:5]
    sent_refs = refs[5:5 + sent]
    sweeps, target_v, grad_x_v, grad_y_v, labels_v, v_ref, b_ref, scaled_ref, resid_ref, sems = refs[5 + sent:]
    chans, rows, cols = target.shape
    window = value_ref.shape[2]
    count = window // SUBLANES
    place = lax.axis_index("lat")
    start = own_start(parts, place)
    inside = band_masks(window, parts, place, rows)
    scale = 1.0

    first_copies = [
        pltpu.make_async_copy(labels, labels_v, sems.at[chans, 0]),
        pltpu.make_async_copy(sweeps_hbm, sweeps, sems.at[chans, 1]),
    ]
    for copy in first_copies:
        copy.start()
    copies = []
    for chan in range(chans):
        copies.append([
            pltpu.make_async_copy(target.at[chan], target_v.at[chan], sems.at[chan, 0]),
            pltpu.make_async_copy(grad_x.at[:, chan], grad_x_v.at[:, chan], sems.at[chan, 1]),
            pltpu.make_async_copy(grad_y.at[:, chan], grad_y_v.at[:, chan], sems.at[chan, 2]),
        ])
        for copy in copies[-1]:
            copy.start()
    if window > rows:
        v_ref[...] = jnp.zeros_like(v_ref)
        b_ref[...] = jnp.zeros_like(b_ref)
    places = pairing()
    merge_ref[...], merge_halo_ref[...] = merging()
    for copy in first_copies:
        copy.wait()

    def chosen(grad, chan):
        marks = labels_v[...]
        out = jnp.zeros((rows, cols), jnp.float32)
        for source in range(grad.shape[0]):
            out = jnp.where(marks == source, grad[source, chan], out)
        return out

    blank = jnp.zeros((rows, LANES), jnp.float32)
    fields = []
    for chan in range(chans):
        for copy in copies[chan]:
            copy.wait()
        own = jnp.concatenate([target_v[chan], blank], 1)
        sel_x = jnp.concatenate([chosen(grad_x_v, chan), blank], 1)
        sel_y = jnp.concatenate([chosen(grad_y_v, chan), blank], 1)
        right = SCREENING * own - ((sel_x - west_of(sel_x)) + (sel_y - row_before(sel_y)))
        below = pltpu.roll(sel_y[rows - SUBLANES:], 1, 0)
        below = jnp.where(rows_of(below) == 0, below, 0.0)
        for k, (v, b, s) in enumerate(zip(tiles(own), tiles(right), tiles(below))):
            v_ref[chan, k, pl.ds(start, rows), :] = v
            b_ref[chan, k, pl.ds(start, rows), :] = b
            if window > rows:
                b_ref[chan, k, pl.ds(start + rows, SUBLANES), :] = s
    for chan in range(chans):
        fields.append((tuple(load_planes(v_ref.at[chan], 0, count, SUBLANES)),))
        right = load_planes(b_ref.at[chan], 0, count, SUBLANES)
        if inside is not None:
            right = [b * mask for b, mask in zip(right, inside)]
        store_planes(right_ref.at[chan], 0, right)
        for t in range(count):
            scaled_ref[chan, t] = (DAMPING / diagonal(scale)) * right[t]

    def scaled(chan):
        return lambda g, t, k: scaled_ref[chan, t, :, span(k)]

    def step(_, fields):
        return tuple(sweep(field, scaled(chan), scale, inside) for chan, field in enumerate(fields))

    fields = repeat(step, sweeps, 0, tuple(fields), LEAST_SWEEPS)
    paired = []
    for chan, field in enumerate(fields):
        store_planes(value_ref.at[chan], 0, field[0])
        left = residual(field, scaled(chan), scale)[0]
        if inside is not None:
            left = [r * mask for r, mask in zip(left, inside)]
        store_planes(resid_ref.at[chan], 0, left)
    for chan in range(chans):
        north, south = load_planes(resid_ref.at[chan], 0, 2, window // 2)
        paired.append(north + south)
    coarse = pair_columns(paired, places)
    for chan in range(chans):
        low = [[0.25 * tile for tile in group] for group in coarse[chan]]
        coarse_ref[chan] = jnp.concatenate(low[0] + low[1], 1)
        if parts != 2:
            continue
        packed_ref, east_across, east_ref, west_across, west_ref = sent_refs
        wide = value_ref.shape[1]
        value = [value_ref[chan, k] for k in range(wide)]
        right = [right_ref[chan, k] for k in range(wide)]
        value_border = [border_value(place, value_ref.at[chan, k]) for k in range(wide)]
        right_border = [border_right(place, right_ref.at[chan, k]) for k in range(wide)]
        for k, tile in enumerate(pack(value_border, right_border, low)):
            packed_ref[chan, k] = tile
        for east, west, fields in (
            (east_ref, west_ref, (value, right, *low)),
            (east_across, west_across, (value_border, right_border, *low)),
        ):
            east[chan] = bundle([eastward(f[-2], f[-1]) for f in fields], TO_EAST)
            west[chan] = bundle([westward(f[0], f[-1]) for f in fields], TO_WEST)


def down(parts, sweeps, target, grad_x, grad_y, labels):
    chans, rows, cols = target.shape
    window = window_of(rows, parts)
    wide, quarter = cols // LANES + 1, cols // 4 // LANES + 1
    spare = SUBLANES if window > rows else 0
    outs = [F32((chans, wide, window, LANES))] * 2 + [F32((chans, window // 2, 2 * quarter * LANES))]
    outs += [jax.ShapeDtypeStruct((4 * LANES, n * LANES), jnp.bfloat16) for n in (4, 1)]
    if parts == 2:
        outs.append(F32((chans, packed_tiles(wide - 1, 2 * (quarter - 1)), SUBLANES, LANES)))
        outs += [F32((chans, SUBLANES, LANES))] * 4
    return pl.pallas_call(
        functools.partial(down_kernel, parts),
        in_specs=[HBM] * 5,
        out_specs=[VMEM] * len(outs),
        out_shape=outs,
        scratch_shapes=[
            pltpu.SMEM(sweeps.shape, jnp.int32),
            SCRATCH(target.shape),
            SCRATCH(grad_x.shape),
            SCRATCH(grad_y.shape),
            pltpu.VMEM(labels.shape, jnp.int32),
            SCRATCH((chans, wide, window + spare, LANES)),
            SCRATCH((chans, wide, window + spare, LANES)),
            SCRATCH((chans, window // SUBLANES, SUBLANES, wide * LANES)),
            SCRATCH((chans, wide, window, LANES)),
            pltpu.SemaphoreType.DMA((chans + 1, 3)),
        ],
        compiler_params=pltpu.CompilerParams(vmem_limit_bytes=32 * 2**20),
        name="down",
    )(*(in_hbm(a) for a in (sweeps, target, grad_x, grad_y, labels)))


def joined(place, own, other, height):
    gap = jnp.zeros((height - own.shape[0], own.shape[1]), jnp.float32)
    top, bottom = (lambda v: jnp.concatenate([v, gap], 0)), (lambda v: jnp.concatenate([gap, v], 0))
    return jnp.where(place == 0, top(own) + bottom(other), bottom(own) + top(other))


def up_kernel(parts, sweeps_hbm, value_ref, right_ref, coarse_ref, merge_ref, merge_halo_ref, *refs):
    received = 5 if parts == 2 else 0
    packed_ref, *edge_refs = refs[:received] or [None]
    out_hbm, sweeps, v0_ref, b0_ref, k0_ref, b1_ref, k1_ref, k2_ref, fix_ref, out_ref, sems = refs[received:]
    sweeps_copy = pltpu.make_async_copy(sweeps_hbm, sweeps, sems.at[0])
    sweeps_copy.start()
    chans, rows, cols = out_ref.shape
    wide, window = value_ref.shape[1:3]
    quarter = b1_ref.shape[2]
    full = parts * rows
    count0, count1 = window // SUBLANES, full // 2 // SUBLANES
    place = lax.axis_index("lat")
    inside = band_masks(window, parts, place, rows)
    own_heights = (window, window, window // 2, window // 2)

    def sides(chan, across):
        heights = ACROSS if across else own_heights
        from_west = unbundle(edge_refs[1 - across][chan], heights, TO_EAST)
        from_east = unbundle(edge_refs[3 - across][chan], heights, TO_WEST)
        return list(zip(from_west, from_east))

    for chan in range(chans):
        low = tiles(coarse_ref[chan])
        low = [low[:quarter], low[quarter:]]
        if parts == 2:
            here, there = sides(chan, 0), sides(chan, 1)
            other = unpack(lambda k: packed_ref[chan, k], wide - 1, 2 * (quarter - 1))
            value, right, *other_low = (with_edges(f, *s) for f, s in zip(other, there))
            low = [with_edges(f, *s) for f, s in zip(low, here[2:])]
            low = [[joined(place, a, b, full // 2) for a, b in zip(*both)] for both in zip(low, other_low)]
            for ref, own, side in ((v0_ref, value_ref, here[0]), (b0_ref, right_ref, here[1])):
                for k, tile in enumerate(with_edges([own[chan, k] for k in range(wide)], *side)):
                    ref[chan, k] = tile
            for k in range(wide):
                add_border(place, v0_ref.at[chan, k], b0_ref.at[chan, k], value[k], right[k])
        else:
            v0_ref[chan] = value_ref[chan]
            b0_ref[chan] = right_ref[chan]
        for g, group in enumerate(low):
            for k, tile in enumerate(group):
                b1_ref[chan, g, k] = tile

    def smoothed(fields, scaled_ref, level, written=LEAST_SWEEPS, ready=lambda: None):
        def step(_, fields):
            return tuple(
                sweep(field, lambda g, t, k, i=i: scaled_ref[i, g, t, :, span(k)], 0.25**level)
                for i, field in enumerate(fields)
            )

        fields = tuple(tuple(tuple(planes) for planes in field) for field in fields)
        return repeat(step, sweeps, level, fields, written, ready)

    def from_zero(rights, scaled_ref, level, ready=lambda: None):
        first = [[[(DAMPING / diagonal(0.25**level)) * b for b in planes] for planes in field] for field in rights]
        for i, field in enumerate(first):
            for g, planes in enumerate(field):
                for t, plane in enumerate(planes):
                    scaled_ref[i, g, t] = plane
        return smoothed(first, scaled_ref, level, LEAST_SWEEPS - 1, ready)

    right1 = [[load_planes(b1_ref.at[i, g], 0, count1, SUBLANES) for g in range(2)] for i in range(chans)]
    mid = from_zero(right1, k1_ref, 1, sweeps_copy.wait)
    right2 = []
    for i, field in enumerate(mid):
        even, odd = residual(field, lambda g, t, k, i=i: k1_ref[i, g, t, :, span(k)], 0.25)
        both = [a + b for a, b in zip(even, odd)]
        right2.append([[0.25 * (both[t] + both[t + 1]) for t in range(0, count1, 2)]])
    fix2 = from_zero(right2, k2_ref, 2)
    mid = [
        [[v + f for v, f in zip(planes, more)] for planes, more in zip(field, prolong(fix[0]))]
        for field, fix in zip(mid, fix2)
    ]
    mid = smoothed(mid, k1_ref, 1)
    spare = (fix_ref.shape[2] - full) // 2
    if spare:
        fix_ref[...] = jnp.zeros_like(fix_ref)
    for i, fix in enumerate(prolong_merged(mid, (merge_ref[...], merge_halo_ref[...]))):
        store_planes(fix_ref.at[i], spare, fix)
    shown = pl.multiple_of((SUBLANES if parts == 2 else rows) * place, SUBLANES)
    start = own_start(parts, place)
    fields = []
    for i in range(chans):
        planes = load_planes(v0_ref.at[i], 0, count0, SUBLANES)
        fix = load_planes(fix_ref.at[i], shown, count0, SUBLANES)
        fields.append((tuple(v + f for v, f in zip(planes, fix)),))
        for t, b in enumerate(load_planes(b0_ref.at[i], 0, count0, SUBLANES)):
            k0_ref[i, t] = (DAMPING / diagonal(1.0)) * b

    def step(_, fields):
        return tuple(
            sweep(field, lambda g, t, k, i=i: k0_ref[i, t, :, span(k)], 1.0, inside) for i, field in enumerate(fields)
        )

    fields = repeat(step, sweeps, 0, tuple(fields), LEAST_SWEEPS)
    out_copies = []
    for i, field in enumerate(fields):
        store_planes(v0_ref.at[i], 0, field[0])
        for k in range(cols // LANES):
            out_ref[i, :, k * LANES:(k + 1) * LANES] = v0_ref[i, k, pl.ds(start, rows), :]
        out_copies.append(pltpu.make_async_copy(out_ref.at[i], out_hbm.at[i], sems.at[1 + i]))
        out_copies[-1].start()
    for copy in out_copies:
        copy.wait()


def up(parts, shape, sweeps, value, right, coarse, *more):
    chans, rows, cols = shape
    wide, window = value.shape[1:3]
    full = parts * rows
    quarter = cols // 4 // LANES + 1
    count1, count2 = full // 2 // SUBLANES, full // 4 // SUBLANES
    spare = 2 * SUBLANES if parts > 2 else 0
    return pl.pallas_call(
        functools.partial(up_kernel, parts),
        in_specs=[HBM] + [VMEM] * (3 + len(more)),
        out_specs=HBM,
        out_shape=F32(shape),
        scratch_shapes=[
            pltpu.SMEM(sweeps.shape, jnp.int32),
            SCRATCH(value.shape),
            SCRATCH(value.shape),
            SCRATCH((chans, window // SUBLANES, SUBLANES, wide * LANES)),
            SCRATCH((chans, 2, quarter, full // 2, LANES)),
            SCRATCH((chans, 2, count1, SUBLANES, quarter * LANES)),
            SCRATCH((chans, 1, count2, SUBLANES, quarter * LANES)),
            SCRATCH((chans, wide, full + spare, LANES)),
            SCRATCH(shape),
            pltpu.SemaphoreType.DMA((1 + chans,)),
        ],
        compiler_params=pltpu.CompilerParams(vmem_limit_bytes=48 * 2**20),
        name="up",
    )(in_hbm(sweeps), value, right, coarse, *more)


def local(target, grad_x, grad_y, labels, sweeps):
    parts, around_globe = lax.axis_size("lat"), lax.axis_size("lon")
    value, right, coarse, merge, merge_halo, *sent = down(parts, sweeps, target, grad_x, grad_y, labels)
    eastward_pairs = [(i, (i + 1) % around_globe) for i in range(around_globe)]
    westward_pairs = [(j, i) for i, j in eastward_pairs]
    if parts < 2:
        raise NotImplementedError
    if parts == 2:
        def across(pairs):
            return [(2 * i + k, 2 * j + 1 - k) for i, j in pairs for k in range(2)]

        packed, east_across, east, west_across, west = sent
        packed = lax.ppermute(packed, "lat", [(0, 1), (1, 0)])
        across_west = lax.ppermute(east_across, ("lon", "lat"), across(eastward_pairs))
        from_west = lax.ppermute(east, "lon", eastward_pairs)
        across_east = lax.ppermute(west_across, ("lon", "lat"), across(westward_pairs))
        from_east = lax.ppermute(west, "lon", westward_pairs)
        received = (packed, across_west, from_west, across_east, from_east)
        return up(parts, target.shape, sweeps, value, right, coarse, merge, merge_halo, *received)

    chans, half_rows = coarse.shape[:2]
    coarse = coarse.reshape(chans, half_rows, -1, LANES).transpose(0, 2, 1, 3)

    def shared_lon(field):
        parts_of = [field[:, k] for k in range(field.shape[1])]
        from_west = lax.ppermute(eastward(parts_of[-2], parts_of[-1]), "lon", eastward_pairs)
        from_east = lax.ppermute(westward(parts_of[0], parts_of[-1]), "lon", westward_pairs)
        return jnp.stack(with_edges(parts_of, from_west, from_east), 1)

    value, right = shared_lon(value), shared_lon(right)
    halves = jnp.split(coarse, 2, axis=1)
    coarse = jnp.concatenate([shared_lon(f) for f in halves], 1)
    if parts > 2:
        rows = target.shape[1]
        spare = 2 * SUBLANES
        southward = [(i, i + 1) for i in range(parts - 1)]
        northward = [(i + 1, i) for i in range(parts - 1)]

        def shared_lat(field):
            north = lax.ppermute(field[:, :, rows:], "lat", southward)
            south = lax.ppermute(field[:, :, :spare], "lat", northward)
            zeros = jnp.zeros_like(south)
            return field + jnp.concatenate([north, zeros], 2) + jnp.concatenate([zeros, south], 2)

        value, right = shared_lat(value), shared_lat(right)
        every = lax.all_gather(coarse, "lat")
        step = rows // 2
        total = jnp.zeros((chans, coarse.shape[1], parts * step + SUBLANES, LANES), jnp.float32)
        for i in range(parts):
            total = total.at[:, :, i * step:i * step + step + SUBLANES].add(every[i])
        coarse = total[:, :, 4:-4]
    coarse = coarse.transpose(0, 2, 1, 3).reshape(chans, coarse.shape[2], -1)
    return up(parts, target.shape, sweeps, value, right, coarse, merge, merge_halo)


def solution(mesh):
    in_specs = (
        P(None, "lat", "lon"),
        P(None, None, "lat", "lon"),
        P(None, None, "lat", "lon"),
        P("lat", "lon"),
        P(),
    )
    out_specs = P(None, "lat", "lon")
    return jax.shard_map(local, mesh=mesh, in_specs=in_specs, out_specs=out_specs, check_vma=False)
```

```python
import functools

import jax
import jax.numpy as jnp
from jax import lax
from jax.experimental import pallas as pl
from jax.experimental.pallas import tpu as pltpu
from jax.sharding import PartitionSpec as P

SCREENING = 0.02
DAMPING = 0.8
LEAST_SWEEPS, MOST_SWEEPS = 2, 4
LANES = 128
HALF = LANES // 2
SUBLANES = 8
VMEM = pl.BlockSpec(memory_space=pltpu.VMEM)
HBM = pl.BlockSpec(memory_space=pltpu.HBM)
F32 = functools.partial(jax.ShapeDtypeStruct, dtype=jnp.float32)
SCRATCH = functools.partial(pltpu.VMEM, dtype=jnp.float32)


def in_hbm(array):
    return pltpu.with_memory_space_constraint(array, pltpu.HBM)


def diagonal(scale):
    return SCREENING + 4.0 * scale


def rows_of(value):
    return lax.broadcasted_iota(jnp.int32, value.shape, 0)


def lanes_of(tile):
    return lax.broadcasted_iota(jnp.int32, tile.shape, len(tile.shape) - 1)


def tiles(value):
    return [value[:, k * LANES:(k + 1) * LANES] for k in range(value.shape[1] // LANES)]


def row_before(value):
    return jnp.where(rows_of(value) == 0, 0.0, pltpu.roll(value, 1, 0))


def row_after(value):
    last = value.shape[0] - 1
    return jnp.where(rows_of(value) == last, 0.0, pltpu.roll(value, last, 0))


def norths(planes):
    return [row_before(planes[-1])] + list(planes[:-1])


def souths(planes):
    return list(planes[1:]) + [row_after(planes[0])]


def west_of(value):
    return pltpu.roll(value, 1, 1)


def east_of(value):
    return pltpu.roll(value, value.shape[1] - 1, 1)


def neighbours(groups, combine):
    cut = [[tiles(plane) for plane in planes] for planes in groups]
    count, wide = len(cut[0]), len(cut[0][0])
    lane = lanes_of(cut[0][0][0])
    known = {}

    def rolled(g, t, k, shift):
        place = (g, t, k % wide, shift)
        if place not in known:
            known[place] = pltpu.roll(cut[g][t][k % wide], shift, 1)
        return known[place]

    def west(g, t, k):
        if g:
            return cut[0][t][k]
        g = len(cut) - 1
        return jnp.where(lane == 0, rolled(g, t, k - 1, 1), rolled(g, t, k, 1))

    def east(g, t, k):
        if g + 1 < len(cut):
            return cut[1][t][k]
        return jnp.where(lane == LANES - 1, rolled(0, t, k + 1, LANES - 1), rolled(0, t, k, LANES - 1))

    out = []
    for g in range(len(cut)):
        group = []
        for t in range(count):
            done = []
            for k in range(wide):
                north = cut[g][t - 1][k] if t else row_before(cut[g][-1][k])
                south = cut[g][t + 1][k] if t + 1 < count else row_after(cut[g][0][k])
                done.append(combine(g, t, k, cut[g][t][k], (north + south) + (west(g, t, k) + east(g, t, k))))
            group.append(jnp.concatenate(done, 1))
        out.append(tuple(group))
    return tuple(out)


def sweep(groups, scaled, scale, inside=None):
    beside = DAMPING * scale / diagonal(scale)

    def combine(g, t, k, value, total):
        value = (1.0 - DAMPING) * value + (scaled(g, t, k) + beside * total)
        return value if inside is None else value * inside[t]

    return neighbours(groups, combine)


def residual(groups, scaled, scale):
    back = diagonal(scale) / DAMPING
    return neighbours(
        groups, lambda g, t, k, value, total: back * scaled(g, t, k) - diagonal(scale) * value + scale * total
    )


def span(k):
    return slice(k * LANES, (k + 1) * LANES)


def repeat(step, sweeps, level, fields, written, ready=lambda: None):
    def steps(count):
        def run(fields):
            for i in range(count):
                fields = step(i, fields)
            return fields

        return run

    fields = steps(written)(fields)
    ready()
    cases = [steps(more) for more in range(MOST_SWEEPS - LEAST_SWEEPS + 1)]
    return lax.switch(sweeps[level] - LEAST_SWEEPS, cases, fields)


def load_planes(ref, start, count, height):
    def plane(first):
        rows = pl.ds(first, height, stride=count) if count > 1 else pl.ds(first, height)
        return jnp.concatenate([ref[k, rows, :] for k in range(ref.shape[0])], 1)

    return [plane(start + t) for t in range(count)]


def store_planes(ref, start, planes):
    count, height = len(planes), planes[0].shape[0]
    for t, plane in enumerate(planes):
        rows = pl.ds(start + t, height, stride=count) if count > 1 else pl.ds(start + t, height)
        for k, tile in enumerate(tiles(plane)):
            ref[k, rows, :] = tile


def places_of(shape, wanted):
    source = lax.broadcasted_iota(jnp.int32, shape, 0)
    target = lax.broadcasted_iota(jnp.int32, shape, 1)
    return wanted(source, target).astype(jnp.float32).astype(jnp.bfloat16)


def halo_quarter(fine):
    return jnp.where(fine < HALF, fine // 4, LANES - LANES // 4 + fine // 4)


def pairing():
    own = places_of((4 * LANES, 2 * LANES), lambda f, target: f // 4 + LANES * (f // 2 % 2) == target)
    halo = places_of((LANES, 2 * LANES), lambda f, target: halo_quarter(f) + LANES * (f // 2 % 2) == target)
    return own, halo


def merging():
    own = places_of((4 * LANES, 4 * LANES), lambda source, f: source == f // 4 + LANES * (f % 4))
    halo = places_of((4 * LANES, LANES), lambda source, f: source == halo_quarter(f) + LANES * (f % 4))
    return own, halo


def moved(value, places):
    high = value.astype(jnp.bfloat16)
    low = (value - high.astype(jnp.float32)).astype(jnp.bfloat16)
    dot = functools.partial(jnp.dot, preferred_element_type=jnp.float32)
    return dot(high, places) + dot(low, places)


def moved_blocks(own_blocks, halo_blocks, places):
    rows, count = halo_blocks[0].shape[0], len(own_blocks[0])
    packed = moved(jnp.concatenate([block for blocks in own_blocks for block in blocks], 0), places[0])
    edges = moved(jnp.concatenate(halo_blocks, 0), places[1])
    cut = lambda value, i: value[i * rows:(i + 1) * rows]
    return [[cut(packed, i * count + k) for k in range(count)] + [cut(edges, i)] for i in range(len(own_blocks))]


def pair_columns(fields, places):
    cols, width = fields[0].shape[1] - LANES, 4 * LANES
    own = [[f[:, k * width:(k + 1) * width] for k in range(cols // width)] for f in fields]
    moved_to = moved_blocks(own, [f[:, cols:] for f in fields], places)
    return [[[block[:, span(g)] for block in blocks] for g in range(2)] for blocks in moved_to]


def spread_rows(planes):
    return [
        half
        for value, north, south in zip(planes, norths(planes), souths(planes))
        for half in (0.75 * value + 0.25 * north, 0.75 * value + 0.25 * south)
    ]


def prolong(planes):
    planes = spread_rows(planes)
    return [
        [0.75 * value + 0.25 * west_of(value) for value in planes],
        [0.75 * value + 0.25 * east_of(value) for value in planes],
    ]


def prolong_merged(fields, places):
    own, halo = [], []
    for even, odd in fields:
        for e, o in zip(spread_rows(even), spread_rows(odd)):
            quarters = (
                0.75 * e + 0.25 * west_of(o),
                0.75 * e + 0.25 * o,
                0.75 * o + 0.25 * e,
                0.75 * o + 0.25 * east_of(e),
            )
            blocks = [jnp.concatenate(four, 1) for four in zip(*(tiles(q) for q in quarters))]
            own.append(blocks[:-1])
            halo.append(blocks[-1])
    planes = [jnp.concatenate(blocks, 1) for blocks in moved_blocks(own, halo, places)]
    count = len(planes) // len(fields)
    return [planes[i * count:(i + 1) * count] for i in range(len(fields))]


def window_of(rows, parts):
    return rows + (2 * SUBLANES if parts > 2 else SUBLANES if parts == 2 else 0)


def own_start(parts, place):
    return 0 if parts == 1 else pl.multiple_of(SUBLANES * place, SUBLANES) if parts == 2 else SUBLANES


def band_masks(window, parts, place, rows):
    if parts <= 2:
        return None
    count = window // SUBLANES
    first = place * rows - SUBLANES
    row = [first + t + count * lax.broadcasted_iota(jnp.int32, (SUBLANES, 1), 0) for t in range(count)]
    return [((r >= 0) & (r < parts * rows)).astype(jnp.float32) for r in row]


def eastward(own_last, halo):
    return jnp.where(lanes_of(halo) < HALF, halo, own_last)


def westward(own_first, halo):
    return jnp.where(lanes_of(halo) < HALF, own_first, halo)


def with_edges(parts, from_west, from_east):
    inner = lanes_of(from_west) < HALF
    first = parts[0] + jnp.where(inner, from_west, 0.0)
    last = parts[-2] + jnp.where(inner, 0.0, from_east)
    halo = parts[-1] + jnp.where(inner, from_east, from_west)
    return [first] + list(parts[1:-2]) + [last, halo]


COARSE_WIDTH, FINE_WIDTH, REACH = 16, 8, 4
TO_EAST, TO_WEST = -12, -4


def in_window(lane, start, width):
    start = start % LANES
    end = start + width
    return (lane >= start) & (lane < end) if end <= LANES else (lane >= start) | (lane < end - LANES)


def slots(heights, coarse_start):
    out, at = [], 0
    for which, rows in enumerate(heights):
        start, width = (-REACH, FINE_WIDTH) if which < 2 else (coarse_start, COARSE_WIDTH)
        for first in range(0, rows, SUBLANES):
            out.append((which, first, min(SUBLANES, rows - first), start, width, at))
            at += width
    assert at <= LANES
    return out


def bundle(fields, coarse_start):
    out = jnp.zeros((SUBLANES, LANES), jnp.float32)
    lane = lanes_of(out)
    for which, first, rows, start, width, at in slots([f.shape[0] for f in fields], coarse_start):
        piece = fields[which][first:first + rows]
        if rows < SUBLANES:
            piece = jnp.concatenate([piece, jnp.zeros((SUBLANES - rows, LANES), jnp.float32)], 0)
        out = jnp.where(in_window(lane, at, width), pltpu.roll(piece, (at - start) % LANES, 1), out)
    return out


def unbundle(tile, heights, coarse_start):
    lane = lanes_of(tile)
    pieces = [[] for _ in heights]
    for which, first, rows, start, width, at in slots(heights, coarse_start):
        piece = jnp.where(in_window(lane, start, width), pltpu.roll(tile, (start - at) % LANES, 1), 0.0)
        pieces[which].append(piece[:rows])
    return [jnp.concatenate(p, 0) if len(p) > 1 else p[0] for p in pieces]


COARSE_ROWS = 12
ACROSS = (SUBLANES, SUBLANES, COARSE_ROWS, COARSE_ROWS)


def border_rows(place):
    north, south = (pl.multiple_of(SUBLANES * (n - place), SUBLANES) for n in (1, 2))
    return pl.ds(north, SUBLANES), pl.ds(south, SUBLANES)


def border_value(place, ref):
    north, south = (ref[rows, :] for rows in border_rows(place))
    return jnp.where(rows_of(north) >= 4, north, south)


def border_right(place, ref):
    north, south = (ref[rows, :] for rows in border_rows(place))
    return jnp.where((place == 0) & (rows_of(north) != 4), north, pltpu.roll(south, 4, 0))


def add_border(place, value_ref, right_ref, value, right):
    row = rows_of(value)
    north, south = border_rows(place)
    value_ref[north, :] += jnp.where(row >= 4, value, 0.0)
    value_ref[south, :] += jnp.where(row < 4, value, 0.0)
    right_ref[north, :] += jnp.where((place == 1) & (row > 4), right, 0.0)
    right_ref[south, :] += jnp.where(row < jnp.where(place == 1, 1, 4), pltpu.roll(right, 4, 0), 0.0)


def half_tiles(lower, upper):
    return jnp.where(rows_of(lower) >= 4, lower, pltpu.roll(upper, 4, 0))


def pack(value, right, coarse):
    low = [tile for group in coarse for tile in group[:-1]]
    joined = [half_tiles(right[k], right[k + 1]) for k in range(0, len(right) - 1, 2)]
    joined += [jnp.concatenate([low[k][SUBLANES:], low[k + 1][SUBLANES:]], 0) for k in range(0, len(low), 2)]
    ends = bundle([value[-1], right[-1]] + [group[-1] for group in coarse], TO_WEST)
    return value[:-1] + [tile[:SUBLANES] for tile in low] + joined + [ends]


def packed_tiles(fine, coarse):
    return fine + coarse + (fine + coarse) // 2 + 1


def unpack(tile, fine, coarse):
    value = [tile(k) for k in range(fine)]
    right, low = [], []
    for k in range(fine // 2):
        both = tile(fine + coarse + k)
        right += [both, pltpu.roll(both, 4, 0)]
    for k in range(coarse // 2):
        both = tile(fine + coarse + fine // 2 + k)
        low += [jnp.concatenate([tile(fine + 2 * k + j), both[4 * j:4 * j + 4]], 0) for j in range(2)]
    ends = unbundle(tile(packed_tiles(fine, coarse) - 1), ACROSS, TO_WEST)
    fields = (value, right, low[:coarse // 2], low[coarse // 2:])
    return [field + [end] for field, end in zip(fields, ends)]


def merging_kernel(own_ref, halo_ref):
    own_ref[...], halo_ref[...] = merging()


def merging_places():
    return pl.pallas_call(
        merging_kernel,
        out_specs=[VMEM] * 2,
        out_shape=[jax.ShapeDtypeStruct((4 * LANES, n * LANES), jnp.bfloat16) for n in (4, 1)],
        cost_estimate=pl.CostEstimate(flops=10**6, bytes_accessed=10**6, transcendentals=0),
        name="merging",
    )()


def down_kernel(parts, sweeps_hbm, target, grad_x, grad_y, labels, *refs):
    sent = 5 if parts == 2 else 0
    value_ref, right_ref, coarse_ref = refs[:3]
    sent_refs = refs[3:3 + sent]
    sweeps, target_v, grad_x_v, grad_y_v, labels_v, v_ref, b_ref, scaled_ref, resid_ref, sems = refs[3 + sent:]
    chans, rows, cols = target.shape
    sources = grad_x.shape[0]
    window = value_ref.shape[2]
    count = window // SUBLANES
    place = lax.axis_index("lat")
    start = own_start(parts, place)
    inside = band_masks(window, parts, place, rows)
    scale = 1.0

    first_copies = [
        pltpu.make_async_copy(labels, labels_v, sems.at[chans, 0]),
        pltpu.make_async_copy(sweeps_hbm, sweeps, sems.at[chans, 1]),
    ]
    for copy in first_copies:
        copy.start()
    copies = []
    for chan in range(chans):
        copies.append([pltpu.make_async_copy(target.at[chan], target_v.at[chan], sems.at[chan, 0])])
        for source in range(sources):
            for i, (grad, here) in enumerate(((grad_x, grad_x_v), (grad_y, grad_y_v))):
                sem = sems.at[chan, 1 + 2 * source + i]
                copies[-1].append(pltpu.make_async_copy(grad.at[source, chan], here.at[source, chan], sem))
        for copy in copies[-1]:
            copy.start()
    if window > rows:
        v_ref[...] = jnp.zeros_like(v_ref)
        b_ref[...] = jnp.zeros_like(b_ref)
    places = pairing()
    for copy in first_copies:
        copy.wait()

    def chosen(grad, chan):
        marks = labels_v[...]
        out = jnp.zeros((rows, cols), jnp.float32)
        for source in range(grad.shape[0]):
            out = jnp.where(marks == source, grad[source, chan], out)
        return out

    blank = jnp.zeros((rows, LANES), jnp.float32)
    fields = []
    for chan in range(chans):
        for copy in copies[chan]:
            copy.wait()
        own = jnp.concatenate([target_v[chan], blank], 1)
        sel_x = jnp.concatenate([chosen(grad_x_v, chan), blank], 1)
        sel_y = jnp.concatenate([chosen(grad_y_v, chan), blank], 1)
        right = SCREENING * own - ((sel_x - west_of(sel_x)) + (sel_y - row_before(sel_y)))
        below = pltpu.roll(sel_y[rows - SUBLANES:], 1, 0)
        below = jnp.where(rows_of(below) == 0, below, 0.0)
        for k, (v, b, s) in enumerate(zip(tiles(own), tiles(right), tiles(below))):
            v_ref[chan, k, pl.ds(start, rows), :] = v
            b_ref[chan, k, pl.ds(start, rows), :] = b
            if window > rows:
                b_ref[chan, k, pl.ds(start + rows, SUBLANES), :] = s
    for chan in range(chans):
        fields.append((tuple(load_planes(v_ref.at[chan], 0, count, SUBLANES)),))
        right = load_planes(b_ref.at[chan], 0, count, SUBLANES)
        if inside is not None:
            right = [b * mask for b, mask in zip(right, inside)]
        store_planes(right_ref.at[chan], 0, right)
        for t in range(count):
            scaled_ref[chan, t] = (DAMPING / diagonal(scale)) * right[t]

    def scaled(chan):
        return lambda g, t, k: scaled_ref[chan, t, :, span(k)]

    def step(_, fields):
        return tuple(sweep(field, scaled(chan), scale, inside) for chan, field in enumerate(fields))

    fields = repeat(step, sweeps, 0, tuple(fields), LEAST_SWEEPS)
    paired = []
    for chan, field in enumerate(fields):
        store_planes(value_ref.at[chan], 0, field[0])
        left = residual(field, scaled(chan), scale)[0]
        if inside is not None:
            left = [r * mask for r, mask in zip(left, inside)]
        store_planes(resid_ref.at[chan], 0, left)
    for chan in range(chans):
        north, south = load_planes(resid_ref.at[chan], 0, 2, window // 2)
        paired.append(north + south)
    coarse = pair_columns(paired, places)
    for chan in range(chans):
        low = [[0.25 * tile for tile in group] for group in coarse[chan]]
        coarse_ref[chan] = jnp.concatenate(low[0] + low[1], 1)
        if parts != 2:
            continue
        packed_ref, east_across, east_ref, west_across, west_ref = sent_refs
        wide = value_ref.shape[1]
        value = [value_ref[chan, k] for k in range(wide)]
        right = [right_ref[chan, k] for k in range(wide)]
        value_border = [border_value(place, value_ref.at[chan, k]) for k in range(wide)]
        right_border = [border_right(place, right_ref.at[chan, k]) for k in range(wide)]
        for k, tile in enumerate(pack(value_border, right_border, low)):
            packed_ref[chan, k] = tile
        for east, west, fields in (
            (east_ref, west_ref, (value, right, *low)),
            (east_across, west_across, (value_border, right_border, *low)),
        ):
            east[chan] = bundle([eastward(f[-2], f[-1]) for f in fields], TO_EAST)
            west[chan] = bundle([westward(f[0], f[-1]) for f in fields], TO_WEST)


def down(parts, sweeps, target, grad_x, grad_y, labels):
    chans, rows, cols = target.shape
    window = window_of(rows, parts)
    wide, quarter = cols // LANES + 1, cols // 4 // LANES + 1
    spare = SUBLANES if window > rows else 0
    outs = [F32((chans, wide, window, LANES))] * 2 + [F32((chans, window // 2, 2 * quarter * LANES))]
    if parts == 2:
        outs.append(F32((chans, packed_tiles(wide - 1, 2 * (quarter - 1)), SUBLANES, LANES)))
        outs += [F32((chans, SUBLANES, LANES))] * 4
    return pl.pallas_call(
        functools.partial(down_kernel, parts),
        in_specs=[HBM] * 5,
        out_specs=[VMEM] * len(outs),
        out_shape=outs,
        scratch_shapes=[
            pltpu.SMEM(sweeps.shape, jnp.int32),
            SCRATCH(target.shape),
            SCRATCH(grad_x.shape),
            SCRATCH(grad_y.shape),
            pltpu.VMEM(labels.shape, jnp.int32),
            SCRATCH((chans, wide, window + spare, LANES)),
            SCRATCH((chans, wide, window + spare, LANES)),
            SCRATCH((chans, window // SUBLANES, SUBLANES, wide * LANES)),
            SCRATCH((chans, wide, window, LANES)),
            pltpu.SemaphoreType.DMA((chans + 1, 1 + 2 * grad_x.shape[0])),
        ],
        compiler_params=pltpu.CompilerParams(vmem_limit_bytes=32 * 2**20),
        name="down",
    )(*(in_hbm(a) for a in (sweeps, target, grad_x, grad_y, labels)))


def joined(place, own, other, height):
    gap = jnp.zeros((height - own.shape[0], own.shape[1]), jnp.float32)
    top, bottom = (lambda v: jnp.concatenate([v, gap], 0)), (lambda v: jnp.concatenate([gap, v], 0))
    return jnp.where(place == 0, top(own) + bottom(other), bottom(own) + top(other))


def up_kernel(parts, sweeps_hbm, value_ref, right_ref, coarse_ref, merge_ref, merge_halo_ref, *refs):
    received = 5 if parts == 2 else 0
    packed_ref, *edge_refs = refs[:received] or [None]
    out_hbm, sweeps, v0_ref, b0_ref, k0_ref, b1_ref, k1_ref, k2_ref, fix_ref, out_ref, sems = refs[received:]
    sweeps_copy = pltpu.make_async_copy(sweeps_hbm, sweeps, sems.at[0])
    sweeps_copy.start()
    chans, rows, cols = out_ref.shape
    wide, window = value_ref.shape[1:3]
    quarter = b1_ref.shape[2]
    full = parts * rows
    count0, count1 = window // SUBLANES, full // 2 // SUBLANES
    place = lax.axis_index("lat")
    inside = band_masks(window, parts, place, rows)
    own_heights = (window, window, window // 2, window // 2)

    def sides(chan, across):
        heights = ACROSS if across else own_heights
        from_west = unbundle(edge_refs[1 - across][chan], heights, TO_EAST)
        from_east = unbundle(edge_refs[3 - across][chan], heights, TO_WEST)
        return list(zip(from_west, from_east))

    for chan in range(chans):
        low = tiles(coarse_ref[chan])
        low = [low[:quarter], low[quarter:]]
        if parts == 2:
            here, there = sides(chan, 0), sides(chan, 1)
            other = unpack(lambda k: packed_ref[chan, k], wide - 1, 2 * (quarter - 1))
            value, right, *other_low = (with_edges(f, *s) for f, s in zip(other, there))
            low = [with_edges(f, *s) for f, s in zip(low, here[2:])]
            low = [[joined(place, a, b, full // 2) for a, b in zip(*both)] for both in zip(low, other_low)]
            for ref, own, side in ((v0_ref, value_ref, here[0]), (b0_ref, right_ref, here[1])):
                for k, tile in enumerate(with_edges([own[chan, k] for k in range(wide)], *side)):
                    ref[chan, k] = tile
            for k in range(wide):
                add_border(place, v0_ref.at[chan, k], b0_ref.at[chan, k], value[k], right[k])
        else:
            v0_ref[chan] = value_ref[chan]
            b0_ref[chan] = right_ref[chan]
        for g, group in enumerate(low):
            for k, tile in enumerate(group):
                b1_ref[chan, g, k] = tile

    def smoothed(fields, scaled_ref, level, written=LEAST_SWEEPS, ready=lambda: None):
        def step(_, fields):
            return tuple(
                sweep(field, lambda g, t, k, i=i: scaled_ref[i, g, t, :, span(k)], 0.25**level)
                for i, field in enumerate(fields)
            )

        fields = tuple(tuple(tuple(planes) for planes in field) for field in fields)
        return repeat(step, sweeps, level, fields, written, ready)

    def from_zero(rights, scaled_ref, level, ready=lambda: None):
        first = [[[(DAMPING / diagonal(0.25**level)) * b for b in planes] for planes in field] for field in rights]
        for i, field in enumerate(first):
            for g, planes in enumerate(field):
                for t, plane in enumerate(planes):
                    scaled_ref[i, g, t] = plane
        return smoothed(first, scaled_ref, level, LEAST_SWEEPS - 1, ready)

    right1 = [[load_planes(b1_ref.at[i, g], 0, count1, SUBLANES) for g in range(2)] for i in range(chans)]
    mid = from_zero(right1, k1_ref, 1, sweeps_copy.wait)
    right2 = []
    for i, field in enumerate(mid):
        even, odd = residual(field, lambda g, t, k, i=i: k1_ref[i, g, t, :, span(k)], 0.25)
        both = [a + b for a, b in zip(even, odd)]
        right2.append([[0.25 * (both[t] + both[t + 1]) for t in range(0, count1, 2)]])
    fix2 = from_zero(right2, k2_ref, 2)
    mid = [
        [[v + f for v, f in zip(planes, more)] for planes, more in zip(field, prolong(fix[0]))]
        for field, fix in zip(mid, fix2)
    ]
    mid = smoothed(mid, k1_ref, 1)
    spare = (fix_ref.shape[2] - full) // 2
    if spare:
        fix_ref[...] = jnp.zeros_like(fix_ref)
    for i, fix in enumerate(prolong_merged(mid, (merge_ref[...], merge_halo_ref[...]))):
        store_planes(fix_ref.at[i], spare, fix)
    shown = pl.multiple_of((SUBLANES if parts == 2 else rows) * place, SUBLANES)
    start = own_start(parts, place)
    fields = []
    for i in range(chans):
        planes = load_planes(v0_ref.at[i], 0, count0, SUBLANES)
        fix = load_planes(fix_ref.at[i], shown, count0, SUBLANES)
        fields.append((tuple(v + f for v, f in zip(planes, fix)),))
        for t, b in enumerate(load_planes(b0_ref.at[i], 0, count0, SUBLANES)):
            k0_ref[i, t] = (DAMPING / diagonal(1.0)) * b

    def step(_, fields):
        return tuple(
            sweep(field, lambda g, t, k, i=i: k0_ref[i, t, :, span(k)], 1.0, inside) for i, field in enumerate(fields)
        )

    fields = repeat(step, sweeps, 0, tuple(fields), LEAST_SWEEPS)
    out_copies = []
    for i, field in enumerate(fields):
        store_planes(v0_ref.at[i], 0, field[0])
        for k in range(cols // LANES):
            out_ref[i, :, k * LANES:(k + 1) * LANES] = v0_ref[i, k, pl.ds(start, rows), :]
        out_copies.append(pltpu.make_async_copy(out_ref.at[i], out_hbm.at[i], sems.at[1 + i]))
        out_copies[-1].start()
    for copy in out_copies:
        copy.wait()


def up(parts, shape, sweeps, value, right, coarse, *more):
    chans, rows, cols = shape
    wide, window = value.shape[1:3]
    full = parts * rows
    quarter = cols // 4 // LANES + 1
    count1, count2 = full // 2 // SUBLANES, full // 4 // SUBLANES
    spare = 2 * SUBLANES if parts > 2 else 0
    return pl.pallas_call(
        functools.partial(up_kernel, parts),
        in_specs=[HBM] + [VMEM] * (3 + len(more)),
        out_specs=HBM,
        out_shape=F32(shape),
        scratch_shapes=[
            pltpu.SMEM(sweeps.shape, jnp.int32),
            SCRATCH(value.shape),
            SCRATCH(value.shape),
            SCRATCH((chans, window // SUBLANES, SUBLANES, wide * LANES)),
            SCRATCH((chans, 2, quarter, full // 2, LANES)),
            SCRATCH((chans, 2, count1, SUBLANES, quarter * LANES)),
            SCRATCH((chans, 1, count2, SUBLANES, quarter * LANES)),
            SCRATCH((chans, wide, full + spare, LANES)),
            SCRATCH(shape),
            pltpu.SemaphoreType.DMA((1 + chans,)),
        ],
        compiler_params=pltpu.CompilerParams(vmem_limit_bytes=48 * 2**20),
        name="up",
    )(in_hbm(sweeps), value, right, coarse, *more)


def local(target, grad_x, grad_y, labels, sweeps):
    parts, around_globe = lax.axis_size("lat"), lax.axis_size("lon")
    value, right, coarse, *sent = down(parts, sweeps, target, grad_x, grad_y, labels)
    merge, merge_halo = merging_places()
    eastward_pairs = [(i, (i + 1) % around_globe) for i in range(around_globe)]
    westward_pairs = [(j, i) for i, j in eastward_pairs]
    if parts < 2:
        raise NotImplementedError
    if parts == 2:
        def across(pairs):
            return [(2 * i + k, 2 * j + 1 - k) for i, j in pairs for k in range(2)]

        packed, east_across, east, west_across, west = sent
        packed = lax.ppermute(packed, "lat", [(0, 1), (1, 0)])
        across_west = lax.ppermute(east_across, ("lon", "lat"), across(eastward_pairs))
        from_west = lax.ppermute(east, "lon", eastward_pairs)
        across_east = lax.ppermute(west_across, ("lon", "lat"), across(westward_pairs))
        from_east = lax.ppermute(west, "lon", westward_pairs)
        received = (packed, across_west, from_west, across_east, from_east)
        return up(parts, target.shape, sweeps, value, right, coarse, merge, merge_halo, *received)

    chans, half_rows = coarse.shape[:2]
    coarse = coarse.reshape(chans, half_rows, -1, LANES).transpose(0, 2, 1, 3)

    def shared_lon(field):
        parts_of = [field[:, k] for k in range(field.shape[1])]
        from_west = lax.ppermute(eastward(parts_of[-2], parts_of[-1]), "lon", eastward_pairs)
        from_east = lax.ppermute(westward(parts_of[0], parts_of[-1]), "lon", westward_pairs)
        return jnp.stack(with_edges(parts_of, from_west, from_east), 1)

    value, right = shared_lon(value), shared_lon(right)
    halves = jnp.split(coarse, 2, axis=1)
    coarse = jnp.concatenate([shared_lon(f) for f in halves], 1)
    if parts > 2:
        rows = target.shape[1]
        spare = 2 * SUBLANES
        southward = [(i, i + 1) for i in range(parts - 1)]
        northward = [(i + 1, i) for i in range(parts - 1)]

        def shared_lat(field):
            north = lax.ppermute(field[:, :, rows:], "lat", southward)
            south = lax.ppermute(field[:, :, :spare], "lat", northward)
            zeros = jnp.zeros_like(south)
            return field + jnp.concatenate([north, zeros], 2) + jnp.concatenate([zeros, south], 2)

        value, right = shared_lat(value), shared_lat(right)
        every = lax.all_gather(coarse, "lat")
        step = rows // 2
        total = jnp.zeros((chans, coarse.shape[1], parts * step + SUBLANES, LANES), jnp.float32)
        for i in range(parts):
            total = total.at[:, :, i * step:i * step + step + SUBLANES].add(every[i])
        coarse = total[:, :, 4:-4]
    coarse = coarse.transpose(0, 2, 1, 3).reshape(chans, coarse.shape[2], -1)
    return up(parts, target.shape, sweeps, value, right, coarse, merge, merge_halo)


def solution(mesh):
    in_specs = (
        P(None, "lat", "lon"),
        P(None, None, "lat", "lon"),
        P(None, None, "lat", "lon"),
        P("lat", "lon"),
        P(),
    )
    out_specs = P(None, "lat", "lon")
    return jax.shard_map(local, mesh=mesh, in_specs=in_specs, out_specs=out_specs, check_vma=False)
```
